32 devices in a mesh: pat: 4 (over z), seq: 8 (over y, x, core).
Axes of the slice: x: 2, y: 2, z: 4, core: 2. Of those that a mesh axis runs over, the one named last changes fastest.
Arguments:
- inputs: bfloat16 [2, 3072, 768], P(None, 'seq'), may hold values from -6 to 6
- lengths: int32 [2], replicated, may hold values from 768 to 3072, as said below
- gain_one: float32 [768], replicated, may hold values from 0.5 to 1.5
- shift_one: float32 [768], replicated, may hold values from -3 to 3
- w_query: bfloat16 [768, 768], P(None, 'pat'), may hold values from -0.21875 to 0.21875
- b_query: float32 [768], P('pat'), may hold values from -3 to 3
- w_key: bfloat16 [768, 768], P(None, 'pat'), may hold values from -0.21875 to 0.21875
- w_value: bfloat16 [768, 768], P(None, 'pat'), may hold values from -0.21875 to 0.21875
- b_value: float32 [768], P('pat'), may hold values from -3 to 3
- w_out: bfloat16 [768, 768], P('pat'), may hold values from -1.25 to 1.25
- b_out: float32 [768], replicated, may hold values from -3 to 3
- gain_two: float32 [768], replicated, may hold values from 0.5 to 1.5
- shift_two: float32 [768], replicated, may hold values from -3 to 3
- w_up: bfloat16 [768, 3072], P(None, 'pat'), may hold values from -0.21875 to 0.21875
- b_up: float32 [3072], P('pat'), may hold values from -3 to 3
- w_down: bfloat16 [3072, 768], P('pat'), may hold values from -0.4375 to 0.4375
- b_down: float32 [768], replicated, may hold values from -3 to 3
- d_output: bfloat16 [2, 3072, 768], P(None, 'seq'), may hold values from -6 to 6
Outputs:
- outputs: bfloat16 [2, 3072, 768], P(None, 'seq')
- grad_inputs: bfloat16 [2, 3072, 768], P(None, 'seq')
- grad_gain_one: float32 [768], replicated
- grad_shift_one: float32 [768], replicated
- grad_query: float32 [768, 768], P(None, 'pat')
- grad_bquery: float32 [768], P('pat')
- grad_key: float32 [768, 768], P(None, 'pat')
- grad_value: float32 [768, 768], P(None, 'pat')
- grad_bvalue: float32 [768], P('pat')
- grad_out: float32 [768, 768], P('pat')
- grad_bout: float32 [768], replicated
- grad_gain_two: float32 [768], replicated
- grad_shift_two: float32 [768], replicated
- grad_up: float32 [768, 3072], P(None, 'pat')
- grad_bup: float32 [3072], P('pat')
- grad_down: float32 [3072, 768], P('pat')
- grad_bdown: float32 [768], replicated
The draws below stay inside these ranges and needn't reach their ends.
Inputs may be any that keep to these rules, and one draw needn't show every extreme that they name: `lengths`: each row's valid length; in every draw one row, drawn from the seed, is full (3072).
All inputs are finite; a program needn't handle non-finite values.
Results may differ from the reference program's by a relative error of at most 0.04.
Values may be sent and summed in bfloat16 or wider, within the bound.
A program may use at most 320 MiB of HBM per device.

```python
import jax
import jax.numpy as jnp
from jax import lax

D = 768
H = 12
HD = 64
FF = 3072
BLOCK = 384
MB = 2
SPAN1 = 4
SPAN2 = 8
SPAN3 = 16
SPAN4 = 32
SPAN5 = 64
ROW = 3072


def draw_lengths(key, part):
    key = jax.random.fold_in(key, 7)
    first, second = jax.random.split(key)
    random_lengths = jax.random.randint(first, (MB,), ROW // 4, ROW + 1)
    full_row = jax.random.randint(second, (), 0, MB)
    return jnp.where(jnp.arange(MB) == full_row, ROW, random_lengths).astype(jnp.int32)


def levels(rng, dims, pieces, smallest, top_value):
    def one(position, parts):
        heights = jax.random.uniform(jax.random.fold_in(jax.random.fold_in(rng, 6), position), (parts,), jnp.float32, smallest / len(pieces), top_value / len(pieces))
        return jnp.repeat(jnp.exp(heights), dims[position] // parts).reshape((-1,) + (1,) * (len(dims) - position - 1))

    level = one(*pieces[0])
    for cut in pieces[1:]:
        level = level * one(*cut)
    return level


def bell_draw(key, dims, width, limit, shards=(), held_as=jnp.bfloat16):
    drawn = jax.random.normal(key, dims, jnp.float32) * width
    if len(shards) > 0:
        drawn = levels(key, dims, shards, -0.22, 0.18) * drawn
    return jnp.clip(drawn, min=-limit, max=limit).astype(held_as)


def setup_inputs(seed: int = 0) -> dict:
    key_list = jax.random.split(jax.random.key(seed), 19)
    return {
        "inputs": bell_draw(key_list[0], (MB, ROW, D), 1.0, 6.0, ((1, 8),)),
        "lengths": draw_lengths(jax.random.fold_in(key_list[18], 71), 0),
        "gain_one": jnp.clip(1.0 + 0.1 * jax.random.normal(key_list[2], (D,), jnp.float32), 0.5, 1.5),
        "shift_one": bell_draw(key_list[3], (D,), 0.3, 3.0, (), jnp.float32),
        "w_query": bell_draw(key_list[4], (D, D), D ** -0.5, 0.21875, ((1, 4),)),
        "b_query": bell_draw(key_list[5], (D,), 0.3, 3.0, ((0, 4),), jnp.float32),
        "w_key": bell_draw(key_list[6], (D, D), D ** -0.5, 0.21875, ((1, 4),)),
        "w_value": bell_draw(key_list[7], (D, D), D ** -0.5, 0.21875, ((1, 4),)),
        "b_value": bell_draw(key_list[8], (D,), 0.3, 3.0, ((0, 4),), jnp.float32),
        "w_out": bell_draw(key_list[9], (D, D), (D // 32) ** -0.5, 1.25, ((0, 4),)),
        "b_out": bell_draw(key_list[10], (D,), 0.3, 3.0, (), jnp.float32),
        "gain_two": jnp.clip(1.0 + 0.1 * jax.random.normal(key_list[11], (D,), jnp.float32), 0.5, 1.5),
        "shift_two": bell_draw(key_list[12], (D,), 0.3, 3.0, (), jnp.float32),
        "w_up": bell_draw(key_list[13], (D, FF), D ** -0.5, 0.21875, ((1, 4),)),
        "b_up": bell_draw(key_list[14], (FF,), 0.3, 3.0, ((0, 4),), jnp.float32),
        "w_down": bell_draw(key_list[15], (FF, D), (FF // 16) ** -0.5, 0.4375, ((0, 4),)),
        "b_down": bell_draw(key_list[16], (D,), 0.3, 3.0, (), jnp.float32),
        "d_output": bell_draw(key_list[17], (MB, ROW, D), 1.0, 6.0, ((1, 8),)),
    }


@jax.custom_vjp
def low(v):
    return lax.optimization_barrier(v.astype(jnp.bfloat16)).astype(jnp.float32)

@jax.custom_vjp
def low_back(v):
    return v

def low_keep(v):
    return (low(v), None)

def low_pass(kept, grad):
    return (grad,)

def back_keep(v):
    return (v, None)

def back_low(kept, grad):
    return (low(grad),)
low.defvjp(low_keep, low_pass)
low_back.defvjp(back_keep, back_low)
dilations = (1, 2, 4, 6, 12)
epsilon = 1e-05
highest = lax.Precision.HIGHEST

def layer_norm(values, gain, shift):
    mean = lax.optimization_barrier(jnp.mean(values, -1, keepdims=True))
    centred = values - mean
    spread = lax.optimization_barrier(jnp.mean(centred * centred, -1, keepdims=True))
    return centred * lax.rsqrt(spread + epsilon) * gain + shift

def both_ways(values):
    return low(low_back(values))

def matmul(left, right):
    return jnp.einsum('btd,de->bte', left, right, precision=highest)

def pick_table(step):
    offsets = jnp.arange(H, dtype=jnp.int32) % step
    table = (jnp.arange(step, dtype=jnp.int32)[:, None] == offsets[None, :]).astype(jnp.float32)
    return (offsets, table)

def thin_rows(values, table):
    step, heads = table.shape
    shape = values.shape
    split = values.reshape((shape[0] // step, step) + shape[1:])
    mask = table.reshape((1, step, heads) + (1,) * (len(shape) - 2))
    return lax.optimization_barrier(jnp.sum(split * mask, axis=1))

def widen_rows(values, table):
    step, heads = table.shape
    shape = values.shape
    mask = table.reshape((1, step, heads) + (1,) * (len(shape) - 2))
    spread = values[:, None] * mask
    return spread.reshape((shape[0] * step,) + shape[1:])

def make_block(keys, values, key_places, span_rows, length):
    scale = HD ** (-0.5)

    def one_block(args):
        queries, query_places = args
        raw = jnp.einsum('qhd,khd->hqk', queries, keys, precision=highest) * scale
        score = low_back(raw)
        near = query_places.T[:, :, None]
        far = key_places.T[:, None, :]
        live = (near // span_rows == far // span_rows) & (far <= near) & ((far < length) | (far == near))
        weight = jnp.where(live, jnp.exp(jnp.where(live, score, 0.0)), 0.0)
        numerator = jnp.einsum('hqk,khd->qhd', low(weight), values, precision=highest)
        return (numerator, lax.optimization_barrier(jnp.sum(weight, -1)).T)
    return jax.checkpoint(one_block)

def attend_row(query, key, value, length):
    spans = (SPAN1, SPAN2, SPAN3, SPAN4, SPAN5)
    numerator = jnp.zeros((ROW, H, HD), jnp.float32)
    denominator = jnp.zeros((ROW, H), jnp.float32)
    for number, step in enumerate(dilations):
        offsets, table = pick_table(step)
        count = ROW // step
        blocks = max(1, count // 512)
        while count % blocks:
            blocks -= 1
        thin_query = thin_rows(query, table).reshape(blocks, count // blocks, H, HD)
        thin_key = thin_rows(key, table)
        thin_value = thin_rows(value, table)
        places = jnp.arange(count, dtype=jnp.int32)[:, None] * step + offsets[None, :]
        block_places = places.reshape(blocks, count // blocks, H)
        worker = make_block(thin_key, thin_value, places, spans[number] * BLOCK, length)
        part_num, part_den = lax.map(worker, (thin_query, block_places))
        numerator = numerator + widen_rows(part_num.reshape(count, H, HD), table)
        denominator = denominator + widen_rows(part_den.reshape(count, H), table)
    return (numerator, denominator)

def forward(inputs, gain_one, shift_one, w_query, b_query, w_key, w_value, b_value, w_out, b_out, gain_two, shift_two, w_up, b_up, w_down, b_down, lengths):
    norm_one = low(layer_norm(inputs, gain_one, shift_one))
    query = both_ways(matmul(norm_one, w_query) + b_query)
    key = both_ways(matmul(norm_one, w_key))
    value = both_ways(matmul(norm_one, w_value) + b_value)
    rows_out = []
    for batch in range(MB):
        numerator, denominator = attend_row(query[batch].reshape(ROW, H, HD), key[batch].reshape(ROW, H, HD), value[batch].reshape(ROW, H, HD), lengths[batch])
        attended = low(low_back(numerator) / denominator[..., None])
        rows_out.append(attended.reshape(ROW, D))
    attended = jnp.stack(rows_out)
    state_two = inputs + (low_back(matmul(attended, w_out)) + b_out)
    norm_two = low(layer_norm(state_two, gain_two, shift_two))
    hidden = low_back(matmul(norm_two, w_up) + b_up)
    active = low(jax.nn.gelu(hidden))
    return state_two + matmul(active, w_down) + b_down

def reference(inputs, lengths, gain_one, shift_one, w_query, b_query, w_key, w_value, b_value, w_out, b_out, gain_two, shift_two, w_up, b_up, w_down, b_down, d_output):
    params = tuple((item.astype(jnp.float32) for item in (inputs, gain_one, shift_one, w_query, b_query, w_key, w_value, b_value, w_out, b_out, gain_two, shift_two, w_up, b_up, w_down, b_down)))

    def run(*args):
        return forward(*args, lengths)
    outputs, pullback = jax.vjp(run, *params)
    grads = pullback(d_output.astype(jnp.float32))
    return (outputs.astype(jnp.bfloat16), grads[0].astype(jnp.bfloat16), grads[1], grads[2], grads[3], grads[4], grads[5], grads[6], grads[7], grads[8], grads[9], grads[10], grads[11], grads[12], grads[13], grads[14], grads[15])
```

```python
import functools

import jax
import jax.numpy as jnp
import numpy as np
from jax import lax
from jax.experimental import pallas as pl
from jax.experimental.pallas import tpu as pltpu
from jax.sharding import PartitionSpec as P

HD = 64
SPAN1 = 4
DILATIONS = (1, 2, 4, 6, 12)
CYCLE = 12
EPS = 1e-05
NEG = -1e30
LEN_LANE = 24
COR_LANE = 25
MESH = pl.DeviceIdType.MESH
BF = jnp.bfloat16
F32 = jnp.float32
ROOT = float(np.sqrt(2.0 / np.pi))


def nn(a, b):
    return lax.dot_general(a, b, (((1,), (0,)), ((), ())), preferred_element_type=F32)


def nt(a, b):
    return lax.dot_general(a, b, (((1,), (1,)), ((), ())), preferred_element_type=F32)


def tn(a, b):
    return lax.dot_general(a, b, (((0,), (0,)), ((), ())), preferred_element_type=F32)


def exact_nt(a, b):
    return lax.dot_general(
        a, b, (((1,), (1,)), ((), ())), preferred_element_type=F32, precision=lax.Precision.HIGHEST
    )


def exact_nn(a, b):
    return lax.dot_general(
        a, b, (((1,), (0,)), ((), ())), preferred_element_type=F32, precision=lax.Precision.HIGHEST
    )


def remote(src, dst, send, recv, device):
    return pltpu.make_async_remote_copy(
        src_ref=src,
        dst_ref=dst,
        send_sem=send,
        recv_sem=recv,
        device_id=device,
        device_id_type=MESH,
    )


def when(cond, fn):
    pl.when(cond)(fn)


def rows_of(start, size):
    return pl.ds(pl.multiple_of(start, 16), size)


def orders(shard):
    p = np.arange(shard)
    return 2 * (p % (shard // 2)) + p // (shard // 2)


def perm_matrix(shard):
    token = orders(shard)
    m = np.zeros((shard, shard), np.float32)
    m[np.arange(shard), token] = 1.0
    return m


def query_ext(shard):
    cls = orders(shard) % CYCLE
    m = np.zeros((shard, 128), np.float32)
    m[np.arange(shard), cls] = 1.0
    m[np.arange(shard), CYCLE + cls] = 1.0
    m[:, LEN_LANE] = 1.0
    return m


def key_tables(shard, heads, levels):
    cls = orders(shard) % CYCLE
    out = np.zeros((heads, levels, shard, 128), np.float32)
    for h in range(heads):
        for level in range(levels):
            count = np.zeros((CYCLE, CYCLE))
            for r in DILATIONS[level:]:
                on = (np.arange(CYCLE) % r == h % r).astype(np.float64)
                count += on[:, None] * on[None, :]
            with np.errstate(divide="ignore"):
                log = np.log(count)
            high = np.where(count > 0, log, NEG).astype(np.float32).astype(jnp.bfloat16)
            low = np.where(count > 0, log - high.astype(np.float64), 0.0)
            out[h, level, :, :CYCLE] = high.astype(np.float32)[:, cls].T
            out[h, level, :, CYCLE : 2 * CYCLE] = low[:, cls].T
            out[h, level, :, COR_LANE] = 1.0
            out[h, level, :, COR_LANE + 1] = 1.0
    return out.astype(jnp.bfloat16)


class Place:
    def __init__(self, n, pat):
        self.n, self.pat = n, pat
        self.z = lax.axis_index("pat")
        self.s = lax.axis_index("seq")
        self.core = lax.rem(self.s, 2)
        self.chip = lax.div(self.s, 2)
        self.seg = lax.div(self.s, SPAN1)
        self.pos = lax.rem(self.s, SPAN1)
        self.sib = self.s + 1 - 2 * self.core
        self.even = lax.rem(self.chip, 2) == 0

    def other_z(self, k):
        return lax.rem(self.z + k, self.pat)

    def greet(self, z_axis, same_core, all_seq=False):
        bar = pltpu.get_barrier_semaphore()
        count = 0
        if z_axis:
            for k in range(1, self.pat):
                pl.semaphore_signal(
                    bar, inc=1, device_id=(self.other_z(k), self.s), device_id_type=MESH
                )
                count += 1
        if all_seq:
            for k in range(1, self.n):
                to = lax.rem(self.s + k, self.n)
                pl.semaphore_signal(bar, inc=1, device_id=(self.z, to), device_id_type=MESH)
                count += 1
        elif same_core:
            pl.semaphore_signal(bar, inc=1, device_id=(self.z, self.sib), device_id_type=MESH)
            count += 1
            for k in range(1, self.n // 2):
                to = lax.rem(self.s + 2 * k, self.n)
                pl.semaphore_signal(bar, inc=1, device_id=(self.z, to), device_id_type=MESH)
                count += 1
        return bar, count


def lane_masks():
    lane = lax.broadcasted_iota(jnp.int32, (1, 128), 1)
    low = jnp.where(lane < HD, 1.0, 0.0)
    return low.astype(BF), (1.0 - low).astype(BF)


def token_of(index, shard):
    half = jnp.where(index >= shard // 2, 1, 0)
    return 2 * (index - half * (shard // 2)) + half


def length_lane(positions, length, rows):
    lane = lax.broadcasted_iota(jnp.int32, (rows, 128), 1)
    hit = jnp.logical_and(lane == LEN_LANE, positions >= length)
    return jnp.where(hit, NEG, 0.0).astype(BF)


def dense_positions(device, shard):
    row = lax.broadcasted_iota(jnp.int32, (shard, 128), 0)
    return device * shard + token_of(row, shard)


def thin_positions(first_device, parity, shard, blocks):
    half = shard // 2
    row = lax.broadcasted_iota(jnp.int32, (blocks * half, 128), 0)
    block = lax.div(row, half)
    return (first_device + block) * shard + 2 * (row - block * half) + parity


def level_of(seg_a, seg_b, levels):
    level = jnp.int32(1)
    size = 2
    for _ in range(2, levels):
        apart = lax.div(seg_a, size) != lax.div(seg_b, size)
        level = level + jnp.where(apart, 1, 0)
        size *= 2
    return level


class Shares:
    def __init__(self, place, shard, forward, dense, thin, dense_sems, thin_sems):
        self.p, self.shard, self.forward = place, shard, forward
        self.dense, self.thin = dense, thin
        self.ds, self.ts = dense_sems, thin_sems
        p = place
        self.chips = p.n // 2
        if forward:
            self.sib_sends, self.sib_gets = p.core == 0, p.core == 1
            self.x_sends, self.x_gets = p.even, jnp.logical_not(p.even)
            self.x_to, self.x_slot = p.s + 2, p.pos - 2
        else:
            self.sib_sends, self.sib_gets = p.core == 1, p.core == 0
            self.x_sends, self.x_gets = jnp.logical_not(p.even), p.even
            self.x_to, self.x_slot = p.s - 2, p.pos + 2
        self.sib_pos = p.pos + 1 - 2 * p.core
        self.x_sib_slot = self.x_slot + 1 - 2 * p.core

    def sib_copy(self, slot):
        p = self.p
        return remote(
            self.dense(slot), self.dense(slot), self.ds[0].at[0], self.ds[1].at[0], (p.z, p.sib)
        )

    def x_copy(self, slot):
        p = self.p
        to = jnp.where(self.x_sends, self.x_to, p.sib)
        return remote(
            self.dense(slot), self.dense(slot), self.ds[0].at[1], self.ds[1].at[1], (p.z, to)
        )

    def hand_copy(self, slot):
        p = self.p
        return remote(
            self.dense(slot), self.dense(slot), self.ds[0].at[2], self.ds[1].at[2], (p.z, p.sib)
        )

    def thin_to(self, chip):
        seg = chip // 2
        return (seg > self.p.seg) if self.forward else (seg < self.p.seg)

    def thin_from(self, chip):
        seg = chip // 2
        return (seg < self.p.seg) if self.forward else (seg > self.p.seg)

    def thin_copy(self, chip):
        p = self.p
        return remote(
            self.thin(p.s),
            self.thin(p.s),
            self.ts[0].at[chip],
            self.ts[1].at[p.chip],
            (p.z, 2 * chip + p.core),
        )

    def thin_got(self, chip):
        p = self.p
        slot = 2 * chip + p.core
        return remote(
            self.thin(slot), self.thin(slot), self.ts[0].at[chip], self.ts[1].at[chip], (p.z, p.sib)
        )

    def thin_hand(self, chip, mine):
        p = self.p
        slot = 2 * chip + (p.core if mine else 1 - p.core)
        return remote(
            self.thin(slot), self.thin(slot), self.ts[2].at[chip], self.ts[3].at[chip], (p.z, p.sib)
        )

    def start(self):
        p = self.p
        when(self.x_sends, lambda: self.x_copy(p.pos).start())
        for chip in range(self.chips):
            when(self.thin_to(chip), lambda chip=chip: self.thin_copy(chip).start())
        when(self.sib_sends, lambda: self.sib_copy(p.pos).start())

    def pass_on(self):
        def dense_part():
            self.x_copy(self.x_slot).wait_recv()
            self.hand_copy(self.x_slot).start()

        when(self.x_gets, dense_part)
        for chip in range(self.chips):

            def thin_part(chip=chip):
                self.thin_got(chip).wait_recv()
                self.thin_hand(chip, True).start()

            when(self.thin_from(chip), thin_part)

    def arrive(self):
        when(self.sib_gets, lambda: self.sib_copy(self.sib_pos).wait_recv())
        when(self.x_gets, lambda: self.hand_copy(self.x_sib_slot).wait_recv())
        for chip in range(self.chips):
            when(
                self.thin_from(chip),
                lambda chip=chip: self.thin_hand(chip, False).wait_recv(),
            )

    def finish(self):
        p = self.p
        when(self.x_sends, lambda: self.x_copy(p.pos).wait_send())
        when(self.sib_sends, lambda: self.sib_copy(p.pos).wait_send())
        when(self.x_gets, lambda: self.hand_copy(self.x_slot).wait_send())
        for chip in range(self.chips):
            when(self.thin_to(chip), lambda chip=chip: self.thin_copy(chip).wait_send())
            when(self.thin_from(chip), lambda chip=chip: self.thin_hand(chip, True).wait_send())


def dense_sems(batches):
    return [pltpu.SemaphoreType.DMA((batches, 3))] * 2


def thin_sems(batches, chips):
    return [pltpu.SemaphoreType.DMA((batches, chips))] * 4


class Spread:
    def __init__(self, place, send, recv):
        self.p, self.send, self.recv = place, send, recv

    def copy_to(self, k, src, dst):
        p = self.p
        return remote(src, dst, self.send.at[k - 1], self.recv.at[k - 1], (p.other_z(k), p.s))


def forward_kernel(
    n,
    pat,
    levels,
    lens,
    x_ref,
    gain,
    shift,
    wq,
    bq,
    wkv,
    bkv,
    wout,
    perm,
    qext,
    ktab,
    xp,
    n1,
    qp,
    kvd,
    kvt,
    attf,
    wofp,
    attw,
    den,
    tab,
    acc,
    tab_sem,
    w_send,
    w_recv,
    a_send,
    a_recv,
    ds0,
    ds1,
    ts0,
    ts1,
    ts2,
    ts3,
):
    batches, shard, width = x_ref.shape
    half = shard // 2
    heads = wout.shape[0] // HD
    units = batches * heads
    p = Place(n, pat)
    bar, greeted = p.greet(True, True)
    low, high = lane_masks()

    def tab_copy(i):
        return pltpu.make_async_copy(ktab.at[heads * p.z + i], tab.at[i], tab_sem.at[i])

    for i in range(heads):
        tab_copy(i).start()
    for z in range(pat):
        wofp[z, 0:HD, :] = jnp.zeros((HD, width), BF)
        wofp[z, HD + heads * HD : 2 * HD + heads * HD, :] = jnp.zeros((HD, width), BF)
    wofp[p.z, HD : HD + heads * HD, :] = wout[...]
    for b in range(batches):
        xb = nn(perm[...], x_ref[b])
        xp[b] = xb.astype(BF)
        mean = jnp.mean(xb, -1, keepdims=True)
        cen = xb - mean
        var = jnp.mean(cen * cen, -1, keepdims=True)
        n1[b] = (cen * lax.rsqrt(var + EPS) * gain[...] + shift[...]).astype(BF)

    shares = [
        Shares(
            p,
            shard,
            True,
            lambda slot, b=b: kvd.at[pl.ds(heads * b, heads), rows_of(slot * shard, shard), :],
            lambda dev, b=b: kvt.at[pl.ds(heads * b, heads), rows_of(dev * half, half), :],
            [ds0.at[b], ds1.at[b]],
            [ts0.at[b], ts1.at[b], ts2.at[b], ts3.at[b]],
        )
        for b in range(batches)
    ]
    parity = [lax.rem(heads * p.z + i, 2) for i in range(heads)]
    for b in range(batches):
        q = ((nn(n1[b], wq[...]) + bq[...]).astype(BF)) * jnp.asarray(HD**-0.5, BF)
        kv = (nn(n1[b], wkv[...]) + bkv[...]).astype(BF)
        for i in range(heads):
            qp[heads * b + i] = q[:, i * 128 : (i + 1) * 128]
            kvd[heads * b + i, rows_of(p.pos * shard, shard), :] = kv[:, i * 128 : (i + 1) * 128]
        for i in range(heads):
            kvt[heads * b + i, rows_of(p.s * half, half), :] = kvd[
                heads * b + i, rows_of(p.pos * shard + parity[i] * half, half), :
            ]
        if b == 0:
            pl.semaphore_wait(bar, greeted)
        shares[b].start()
    w_spread = Spread(p, w_send, w_recv)

    def w_slot(z):
        return wofp.at[z, HD : HD + heads * HD, :]

    for k in range(1, pat):
        w_spread.copy_to(k, w_slot(p.z), w_slot(p.z)).start()
    for i in range(heads):
        tab_copy(i).wait()

    def attend(qx, kv, ext, bias):
        s = nt(qx, jnp.concatenate([kv, ext], 1))
        if bias is not None:
            s = s + bias
        return nn(jnp.exp(s).astype(BF), kv * high + low)

    own = rows_of(p.pos * shard, shard)
    qi = lax.broadcasted_iota(jnp.int32, (shard, shard), 0)
    ki = lax.broadcasted_iota(jnp.int32, (shard, shard), 1)
    qt, kt = token_of(qi, shard), token_of(ki, shard)
    for b in range(batches):
        live = jnp.logical_or(
            jnp.logical_and(kt < qt, kt + p.s * shard < lens[b]), kt == qt
        )
        bias = jnp.where(live, 0.0, NEG)
        for i in range(heads):
            u = heads * b + i
            qx = jnp.concatenate([qp[u], qext[...]], 1)
            acc[u] = attend(qx, kvd[u, own, :], tab[i, 0], bias)

    att_spread = [Spread(p, a_send.at[t], a_recv.at[t]) for t in range(units // 2)]
    lane = lax.broadcasted_iota(jnp.int32, (shard, 128), 1)
    for b in range(batches):
        shares[b].pass_on()
        shares[b].arrive()

        def dense(j, carry, b=b):
            lenl = length_lane(dense_positions(p.seg * SPAN1 + j, shard), lens[b], shard)
            for i in range(heads):
                u = heads * b + i
                qx = jnp.concatenate([qp[u], qext[...]], 1)
                kv = kvd[u, rows_of(j * shard, shard), :]
                acc[u] += attend(qx, kv, tab[i, 0] + lenl, None)
            return carry

        lax.fori_loop(0, p.pos, dense, 0)

        def thin(sg, carry, b=b):
            level = level_of(sg, p.seg, levels)
            for i in range(heads):
                u = heads * b + i
                mine = rows_of(parity[i] * half, half)
                places = thin_positions(sg * SPAN1, parity[i], shard, SPAN1)
                lenl = length_lane(places, lens[b], SPAN1 * half)
                ext = jnp.concatenate([tab[i, level, mine, :]] * SPAN1, 0) + lenl
                qx = jnp.concatenate([qp[u, mine, :], qext[mine, :]], 1)
                kv = kvt[u, rows_of(sg * SPAN1 * half, SPAN1 * half), :]
                acc[u, mine, :] += attend(qx, kv, ext, None)
            return carry

        lax.fori_loop(0, p.seg, thin, 0)
        for t in range(units // 2):
            if (2 * t + 1) // heads != b:
                continue
            even, odd = acc[2 * t], acc[2 * t + 1]
            num = jnp.where(lane < HD, pltpu.roll(even, HD, 1), odd)
            dn = jnp.where(lane < HD, even, pltpu.roll(odd, HD, 1))
            wide = num / dn
            den[t] = dn
            attw[t] = wide
            attf[p.z, t] = wide.astype(BF)
            for k in range(1, pat):
                att_spread[t].copy_to(k, attf.at[p.z, t], attf.at[p.z, t]).start()
    for k in range(1, pat):
        frm = lax.rem(p.z + pat - k, pat)
        w_spread.copy_to(k, w_slot(p.z), w_slot(p.z)).wait_send()
        w_spread.copy_to(k, w_slot(frm), w_slot(frm)).wait_recv()
        for t in range(units // 2):
            att_spread[t].copy_to(k, attf.at[p.z, t], attf.at[p.z, t]).wait_send()
            att_spread[t].copy_to(k, attf.at[frm, t], attf.at[frm, t]).wait_recv()
    for b in range(batches):
        shares[b].finish()


def middle_kernel(
    n,
    pat,
    xp,
    attf,
    wofp,
    bout,
    gain,
    shift,
    wup,
    bup,
    wdown,
    dout,
    perm,
    gud,
    fd,
    dsf,
    dst,
    sto,
    vecs,
    state,
    n2,
    act,
    dop,
    dh,
    dns,
    dno,
    dnr,
    r_send,
    r_recv,
    g_send,
    g_recv,
):
    batches, shard, width = xp.shape
    quarter = shard // pat
    p = Place(n, pat)
    bar, greeted = p.greet(True, False)
    rs = [Spread(p, r_send.at[b], r_recv.at[b]) for b in range(batches)]
    ag = [Spread(p, g_send.at[b], g_recv.at[b]) for b in range(batches)]
    bup_sum = jnp.zeros((1, width), F32)
    bdown_sum = jnp.zeros((1, width), F32)
    for b in range(batches):
        mixed = jnp.zeros((shard, width), F32)
        for z in range(pat):
            pair = jnp.concatenate([attf[z, b], attf[z, b + 1]], 1)
            weight = wofp[z, HD : HD + 256, :] if b == 0 else wofp[z, 0:256, :]
            mixed = mixed + nn(pair, weight)
        st = xp[b].astype(F32) + mixed + bout[...]
        state[b] = st
        mean = jnp.mean(st, -1, keepdims=True)
        cen = st - mean
        var = jnp.mean(cen * cen, -1, keepdims=True)
        norm = (cen * lax.rsqrt(var + EPS) * gain[...] + shift[...]).astype(BF)
        n2[b] = norm
        dob = nn(perm[...], dout[b])
        dop[b] = dob.astype(BF)
        bdown_sum = bdown_sum + jnp.sum(dob, 0, keepdims=True)
        hid = nn(norm, wup[...]) + bup[...]
        cube = hid * hid * hid
        th = jnp.tanh(ROOT * (hid + 0.044715 * cube))
        act[b] = (0.5 * hid * (1.0 + th)).astype(BF)
        slope = 0.5 * (1.0 + th) + 0.5 * hid * (1.0 - th * th) * (
            ROOT * (1.0 + 3.0 * 0.044715 * hid * hid)
        )
        dhid = (nt(dop[b], wdown[...]) * slope).astype(BF)
        dh[b] = dhid
        bup_sum = bup_sum + jnp.sum(dhid.astype(F32), 0, keepdims=True)
        dn = nt(dhid, wup[...])
        for z in range(pat):
            dns[b, z] = dn[z * quarter : (z + 1) * quarter].astype(BF)
        if b == 0:
            pl.semaphore_wait(bar, greeted)
        for k in range(1, pat):
            rs[b].copy_to(k, dns.at[b, p.other_z(k)], dnr.at[b, k - 1]).start()
    vecs[...] = jnp.zeros(vecs.shape, F32)
    for b in range(batches):
        fd[b] = nn(act[b], wdown[...]).astype(BF)
    bout_sum = jnp.zeros((1, width), F32)
    gain_sum = jnp.zeros((1, width), F32)
    shift_sum = jnp.zeros((1, width), F32)
    mine = rows_of(p.z * quarter, quarter)
    for b in range(batches):
        total = dns[b, p.z].astype(F32)
        for k in range(1, pat):
            rs[b].copy_to(k, dns.at[b, p.other_z(k)], dnr.at[b, k - 1]).wait_recv()
            total = total + dnr[b, k - 1].astype(F32)
        st = state[b, mine, :]
        sto[b] = st
        mean = jnp.mean(st, -1, keepdims=True)
        cen = st - mean
        inv = lax.rsqrt(jnp.mean(cen * cen, -1, keepdims=True) + EPS)
        hat = cen * inv
        gain_sum = gain_sum + jnp.sum(total * hat, 0, keepdims=True)
        shift_sum = shift_sum + jnp.sum(total, 0, keepdims=True)
        dhat = total * gain[...]
        back = inv * (
            dhat
            - jnp.mean(dhat, -1, keepdims=True)
            - hat * jnp.mean(dhat * hat, -1, keepdims=True)
        )
        ds = dop[b, mine, :].astype(F32) + back
        dst[b] = ds
        bout_sum = bout_sum + jnp.sum(ds, 0, keepdims=True)
        dsf[b, mine, :] = ds.astype(BF)
        for k in range(1, pat):
            ag[b].copy_to(k, dsf.at[b, mine, :], dsf.at[b, mine, :]).start()
    vecs[2:3, :] = bout_sum
    vecs[3:4, :] = gain_sum
    vecs[4:5, :] = shift_sum
    vecs[5:6, :] = bup_sum
    vecs[6:7, :] = bdown_sum
    up = tn(n2[0], dh[0])
    for b in range(1, batches):
        up = up + tn(n2[b], dh[b])
    gud[0:width, :] = up.astype(BF)
    down = tn(act[0], dop[0])
    for b in range(1, batches):
        down = down + tn(act[b], dop[b])
    gud[width : 2 * width, :] = down.astype(BF)
    for b in range(batches):
        for k in range(1, pat):
            frm = lax.rem(p.z + pat - k, pat)
            theirs = dsf.at[b, rows_of(frm * quarter, quarter), :]
            rs[b].copy_to(k, dns.at[b, p.other_z(k)], dnr.at[b, k - 1]).wait_send()
            ag[b].copy_to(k, dsf.at[b, mine, :], dsf.at[b, mine, :]).wait_send()
            ag[b].copy_to(k, theirs, theirs).wait_recv()


def backward_kernel(
    n,
    pat,
    levels,
    lens,
    dsf,
    wofp,
    attf,
    attw,
    den,
    qp,
    kvd,
    kvt,
    tab,
    qext,
    fd,
    sto,
    bdown,
    permt,
    dq,
    dkv,
    gout,
    outp,
    qud,
    qut,
    crd,
    crt,
    uext,
    acq,
    ack,
    fdr,
    outf,
    f_send,
    f_recv,
    o_send,
    o_recv,
    ds0,
    ds1,
    ts0,
    ts1,
    ts2,
    ts3,
    cd0,
    cd1,
    ct0,
    ct1,
    ct2,
    ct3,
):
    batches, shard, width = dsf.shape
    half = shard // 2
    quarter = shard // pat
    units = qp.shape[0]
    heads = units // batches
    p = Place(n, pat)
    bar, greeted = p.greet(True, True)
    low, high = lane_masks()
    parity = [lax.rem(heads * p.z + i, 2) for i in range(heads)]
    own = rows_of(p.pos * shard, shard)
    lane = lax.broadcasted_iota(jnp.int32, (shard, 128), 1)
    row8 = lax.broadcasted_iota(jnp.int32, (8, 128), 0)
    lane8 = lax.broadcasted_iota(jnp.int32, (8, 128), 1)
    pick = jnp.where(row8 == lax.div(lane8, HD), 1.0, 0.0).astype(F32)
    ri = lax.broadcasted_iota(jnp.int32, (128, 128), 0)
    ci = lax.broadcasted_iota(jnp.int32, (128, 128), 1)
    same = jnp.where(lax.div(ri, HD) == lax.div(ci, HD), 1.0, 0.0).astype(F32)

    wide = [
        nt(dsf[b], wofp[p.z, HD : HD + 256, :] if b == 0 else wofp[p.z, 0:256, :])
        for b in range(batches)
    ]
    tiles = [wide[0][:, 0:128], wide[0][:, 128:256] + wide[1][:, 0:128], wide[1][:, 128:256]]
    crd[p.pos] = jnp.zeros(crd.shape[1:], F32)
    crt[p.s] = jnp.zeros(crt.shape[1:], F32)
    for t in range(units // 2):
        dn = den[t]
        up = tiles[t] / dn
        prod = tiles[t] * attw[t] / dn
        cor = exact_nn(prod, same)
        cor_rows = exact_nt(pick, prod)
        for e in range(2):
            u = 2 * t + e
            i = u % heads
            part = up if e == 1 else pltpu.roll(up, HD, 1)
            mixed = jnp.where(lane < HD, qp[u].astype(F32), part).astype(BF)
            qud[u, own, :] = mixed
            qut[u, rows_of(p.s * half, half), :] = qud[
                u, rows_of(p.pos * shard + parity[i] * half, half), :
            ]
            crd[p.pos, u : u + 1, :] = cor_rows[e : e + 1, :]
            col = -cor[:, e * HD : e * HD + 1]
            first = col.astype(BF).astype(F32)
            ue = jnp.where(lane == COR_LANE, first, 0.0) + jnp.where(
                lane == COR_LANE + 1, col - first, 0.0
            )
            uext[u] = ue.astype(BF)
            thin_cor = jnp.where(parity[i] == 0, cor_rows[e : e + 1, 0:half], cor_rows[e : e + 1, half:shard])
            crt[p.s, u : u + 1, :] = thin_cor
    pl.semaphore_wait(bar, greeted)
    cors = Shares(
        p,
        shard,
        False,
        lambda slot: crd.at[slot],
        lambda dev: crt.at[dev],
        [cd0, cd1],
        [ct0, ct1, ct2, ct3],
    )
    shares = [
        Shares(
            p,
            shard,
            False,
            lambda slot, b=b: qud.at[pl.ds(heads * b, heads), rows_of(slot * shard, shard), :],
            lambda dev, b=b: qut.at[pl.ds(heads * b, heads), rows_of(dev * half, half), :],
            [ds0.at[b], ds1.at[b]],
            [ts0.at[b], ts1.at[b], ts2.at[b], ts3.at[b]],
        )
        for b in range(batches)
    ]
    cors.start()
    for b in range(batches):
        shares[b].start()
    fs = [Spread(p, f_send.at[b], f_recv.at[b]) for b in range(batches)]
    og = [Spread(p, o_send.at[b], o_recv.at[b]) for b in range(batches)]

    def fd_src(b, k):
        return fd.at[b, rows_of(p.other_z(k) * quarter, quarter), :]

    for b in range(batches):
        for k in range(1, pat):
            fs[b].copy_to(k, fd_src(b, k), fdr.at[b, k - 1]).start()

    def query_side(qu, qe, ue, kv, ext, bias):
        kvx = jnp.concatenate([kv, ext], 1)
        s = nt(jnp.concatenate([qu * low, qe], 1), kvx)
        if bias is not None:
            s = s + bias
        dp = nt(jnp.concatenate([qu * high, ue], 1), kvx)
        return nn((jnp.exp(s) * dp).astype(BF), kv)

    def key_side(qu, qe, cor, kv, ext, bias):
        s = nt(jnp.concatenate([kv, ext], 1), jnp.concatenate([qu * low, qe], 1))
        if bias is not None:
            s = s + bias
        w = jnp.exp(s)
        dp = nt(kv, qu * high) - cor
        return nn((w * dp).astype(BF), qu * low) + nn(w.astype(BF), qu * high)

    qi = lax.broadcasted_iota(jnp.int32, (shard, shard), 0)
    ki = lax.broadcasted_iota(jnp.int32, (shard, shard), 1)
    ti, tj = token_of(qi, shard), token_of(ki, shard)
    for b in range(batches):
        bias = jnp.where(
            jnp.logical_or(jnp.logical_and(tj < ti, tj + p.s * shard < lens[b]), tj == ti), 0.0, NEG
        )
        biast = jnp.where(
            jnp.logical_or(jnp.logical_and(ti < tj, ti + p.s * shard < lens[b]), tj == ti), 0.0, NEG
        )
        for i in range(heads):
            u = heads * b + i
            kv = kvd[u, own, :]
            qu = qud[u, own, :]
            acq[u] = query_side(qu, qext[...], uext[u], kv, tab[i, 0], bias)
            ack[u] = key_side(qu, qext[...], crd[p.pos, u : u + 1, :], kv, tab[i, 0], biast)

    for b in range(batches):

        def dense_q(j, carry, b=b):
            lenl = length_lane(dense_positions(p.seg * SPAN1 + j, shard), lens[b], shard)
            for i in range(heads):
                u = heads * b + i
                kv = kvd[u, rows_of(j * shard, shard), :]
                acq[u] += query_side(
                    qud[u, own, :], qext[...], uext[u], kv, tab[i, 0] + lenl, None
                )
            return carry

        lax.fori_loop(0, p.pos, dense_q, 0)

        def thin_q(sg, carry, b=b):
            level = level_of(sg, p.seg, levels)
            for i in range(heads):
                u = heads * b + i
                mine = rows_of(parity[i] * half, half)
                places = thin_positions(sg * SPAN1, parity[i], shard, SPAN1)
                lenl = length_lane(places, lens[b], SPAN1 * half)
                ext = jnp.concatenate([tab[i, level, mine, :]] * SPAN1, 0) + lenl
                kv = kvt[u, rows_of(sg * SPAN1 * half, SPAN1 * half), :]
                qu = qut[u, rows_of(p.s * half, half), :]
                acq[u, mine, :] += query_side(
                    qu, qext[mine, :], uext[u, mine, :], kv, ext, None
                )
            return carry

        lax.fori_loop(0, p.seg, thin_q, 0)

    zrows = rows_of(p.z * quarter, quarter)
    for b in range(batches):
        total = fd[b, zrows, :].astype(F32)
        for k in range(1, pat):
            fs[b].copy_to(k, fd_src(b, k), fdr.at[b, k - 1]).wait_recv()
            total = total + fdr[b, k - 1].astype(F32)
        outf[b, zrows, :] = (sto[b] + total + bdown[...]).astype(BF)
        for k in range(1, pat):
            og[b].copy_to(k, outf.at[b, zrows, :], outf.at[b, zrows, :]).start()
    left = tn(jnp.concatenate([attf[p.z, 0], attf[p.z, 1]], 1), dsf[0])
    right = tn(jnp.concatenate([attf[p.z, 1], attf[p.z, 2]], 1), dsf[1])
    gout[...] = (left[0 : heads * HD] + right[HD : HD + heads * HD]).astype(BF)

    cors.pass_on()
    cors.arrive()
    for b in range(batches):
        shares[b].pass_on()
        shares[b].arrive()
        lenl = length_lane(dense_positions(p.s, shard), lens[b], shard)

        def dense_k(j, carry, b=b, lenl=lenl):
            for i in range(heads):
                u = heads * b + i
                qu = qud[u, rows_of(j * shard, shard), :]
                ack[u] += key_side(
                    qu, qext[...], crd[j, u : u + 1, :], kvd[u, own, :], tab[i, 0] + lenl, None
                )
            return carry

        lax.fori_loop(p.pos + 1, SPAN1, dense_k, 0)

        def thin_k(dev, carry, b=b):
            level = level_of(lax.div(dev, SPAN1), p.seg, levels)
            for i in range(heads):
                u = heads * b + i
                mine = rows_of(parity[i] * half, half)
                ext = tab[i, level, mine, :] + length_lane(
                    thin_positions(p.s, parity[i], shard, 1), lens[b], half
                )
                kv = kvt[u, rows_of(p.s * half, half), :]
                qu = qut[u, rows_of(dev * half, half), :]
                ack[u, mine, :] += key_side(
                    qu, qext[mine, :], crt[dev, u : u + 1, :], kv, ext, None
                )
            return carry

        lax.fori_loop(SPAN1 * (p.seg + 1), n, thin_k, 0)
        for i in range(heads):
            u = heads * b + i
            lanes = slice(i * 128, (i + 1) * 128)
            dq[b, :, lanes] = (acq[u] * HD**-0.5).astype(BF)
            dkv[b, :, lanes] = ack[u].astype(BF)

    for b in range(batches):
        for k in range(1, pat):
            frm = lax.rem(p.z + pat - k, pat)
            theirs = outf.at[b, rows_of(frm * quarter, quarter), :]
            og[b].copy_to(k, theirs, theirs).wait_recv()
            og[b].copy_to(k, outf.at[b, zrows, :], outf.at[b, zrows, :]).wait_send()
            fs[b].copy_to(k, fd_src(b, k), fdr.at[b, k - 1]).wait_send()
        outp[b] = nn(permt[...], outf[b]).astype(BF)
    cors.finish()
    for b in range(batches):
        shares[b].finish()


def tail_kernel(
    n,
    pat,
    xp,
    n1,
    dq,
    dkv,
    wq,
    wkv,
    gain,
    dst,
    vecs,
    gud,
    gout,
    permt,
    ginp,
    vout,
    gup,
    gdown,
    goutf,
    gq,
    gk,
    gv,
    dns,
    dnr,
    gif,
    grad,
    gsum,
    r1,
    r2,
    r3,
    v0,
    vz,
    vs,
    r_send,
    r_recv,
    g_send,
    g_recv,
    s_send,
    s_recv,
    z_send,
    z_recv,
    v_send,
    v_recv,
):
    batches, shard, width = xp.shape
    quarter = shard // pat
    cols = gout.shape[0]
    heads = cols // HD
    p = Place(n, pat)
    bar, greeted = p.greet(True, False, True)
    rs = [Spread(p, r_send.at[b], r_recv.at[b]) for b in range(batches)]
    ag = [Spread(p, g_send.at[b], g_recv.at[b]) for b in range(batches)]
    for b in range(batches):
        part = nt(dq[b], wq[...]) + nt(dkv[b], wkv[...])
        for z in range(pat):
            dns[b, z] = part[z * quarter : (z + 1) * quarter].astype(BF)
        if b == 0:
            pl.semaphore_wait(bar, greeted)
        for k in range(1, pat):
            rs[b].copy_to(k, dns.at[b, p.other_z(k)], dnr.at[b, k - 1]).start()
    qsum = jnp.zeros((1, heads * 128), F32)
    vsum = jnp.zeros((1, heads * 128), F32)
    for b in range(batches):
        qsum = qsum + jnp.sum(dq[b].astype(F32), 0, keepdims=True)
        vsum = vsum + jnp.sum(dkv[b].astype(F32), 0, keepdims=True)
    grad[0 : 2 * width, :] = gud[...]
    base = 2 * width
    for i in range(heads):
        lanes = slice(i * 128, (i + 1) * 128)
        a = tn(dq[0, :, lanes], n1[0])
        c = tn(dkv[0, :, lanes], n1[0])
        for b in range(1, batches):
            a = a + tn(dq[b, :, lanes], n1[b])
            c = c + tn(dkv[b, :, lanes], n1[b])
        grad[base + i * HD : base + (i + 1) * HD, :] = a[0:HD].astype(BF)
        grad[base + cols + i * HD : base + cols + (i + 1) * HD, :] = c[0:HD].astype(BF)
        grad[base + 2 * cols + i * HD : base + 2 * cols + (i + 1) * HD, :] = c[HD:].astype(BF)
    grad[base + 3 * cols : base + 4 * cols, :] = gout[...]

    size = grad.shape[0]
    bit_x = lax.rem(lax.div(p.s, 2), 2)
    bit_y = lax.div(p.s, 4)
    to_x = p.s + 2 - 4 * bit_x
    to_y = p.s + 4 - 8 * bit_y
    first = p.core == 0
    stages = [
        (p.core, p.sib, r1),
        (jnp.where(first, bit_x, bit_y), jnp.where(first, to_x, to_y), r2),
        (jnp.where(first, bit_y, bit_x), jnp.where(first, to_y, to_x), r3),
    ]
    offs = [jnp.int32(0)]
    sizes = [size]

    def red_copy(d):
        bit, to, buf = stages[d]
        h = sizes[d] // 2
        src = grad.at[rows_of(offs[d] + (1 - bit) * h, h), :]
        return remote(src, buf, s_send.at[d], s_recv.at[d], (p.z, to))

    def back_copy(d, got):
        bit, to, _ = stages[d]
        h = sizes[d] // 2
        rows = rows_of(offs[d] + ((1 - bit) if got else bit) * h, h)
        return remote(
            gsum.at[rows, :], gsum.at[rows, :], s_send.at[3 + d], s_recv.at[3 + d], (p.z, to)
        )

    for d in range(3):
        bit, _, buf = stages[d]
        h = sizes[d] // 2
        offs.append(offs[d] + bit * h)
        sizes.append(h)

    red_copy(0).start()

    def norm_back(b, gain_sum, shift_sum):
        zrows = rows_of(p.z * quarter, quarter)
        total = dns[b, p.z].astype(F32)
        for k in range(1, pat):
            rs[b].copy_to(k, dns.at[b, p.other_z(k)], dnr.at[b, k - 1]).wait_recv()
            total = total + dnr[b, k - 1].astype(F32)
        st = xp[b, zrows, :].astype(F32)
        mean = jnp.mean(st, -1, keepdims=True)
        cen = st - mean
        inv = lax.rsqrt(jnp.mean(cen * cen, -1, keepdims=True) + EPS)
        hat = cen * inv
        gain_sum = gain_sum + jnp.sum(total * hat, 0, keepdims=True)
        shift_sum = shift_sum + jnp.sum(total, 0, keepdims=True)
        dhat = total * gain[...]
        back = inv * (
            dhat
            - jnp.mean(dhat, -1, keepdims=True)
            - hat * jnp.mean(dhat * hat, -1, keepdims=True)
        )
        gif[b, zrows, :] = (dst[b] + back).astype(BF)
        for k in range(1, pat):
            ag[b].copy_to(k, gif.at[b, zrows, :], gif.at[b, zrows, :]).start()
        return gain_sum, shift_sum

    def reduce_stage(d):
        rows = rows_of(offs[d + 1], sizes[d + 1])
        red_copy(d).wait_recv()
        total = grad[rows, :].astype(F32) + stages[d][2][...].astype(F32)
        return rows, total.astype(BF)

    rows, total = reduce_stage(0)
    grad[rows, :] = total
    red_copy(1).start()
    zero = jnp.zeros((1, width), F32)
    gain_sum, shift_sum = norm_back(0, zero, zero)
    rows, total = reduce_stage(1)
    grad[rows, :] = total
    red_copy(2).start()
    for b in range(1, batches):
        gain_sum, shift_sum = norm_back(b, gain_sum, shift_sum)
    v0[...] = vecs[...]
    v0[0:1, :] = gain_sum
    v0[1:2, :] = shift_sum
    zsp = Spread(p, z_send, z_recv)
    for k in range(1, pat):
        zsp.copy_to(k, v0, vz.at[k - 1]).start()
    rows, total = reduce_stage(2)
    gsum[rows, :] = total
    back_copy(2, False).start()
    for k in range(1, pat):
        zsp.copy_to(k, v0, vz.at[k - 1]).wait_recv()
    row = lax.broadcasted_iota(jnp.int32, (8, width), 0)
    extra = vz[0]
    for k in range(2, pat):
        extra = extra + vz[k - 1]
    vs[0, 0:8, :] = v0[...] + jnp.where(row < 5, extra, 0.0)
    vs[0, 8:16, :] = jnp.zeros((8, width), F32)
    vs[0, 8:9, 0 : heads * 128] = qsum
    vs[0, 9:10, 0 : heads * 128] = vsum

    def vec_copy(k):
        to = lax.rem(p.s + k, n)
        return remote(vs.at[0], vs.at[k], v_send.at[k - 1], v_recv.at[k - 1], (p.z, to))

    for k in range(1, n):
        vec_copy(k).start()
    back_copy(2, True).wait_recv()
    back_copy(1, False).start()
    for k in range(1, n):
        vec_copy(k).wait_recv()
    allv = vs[0]
    for k in range(1, n):
        allv = allv + vs[k]
    vout[...] = allv
    back_copy(1, True).wait_recv()
    back_copy(0, False).start()
    for b in range(batches):
        for k in range(1, pat):
            frm = lax.rem(p.z + pat - k, pat)
            theirs = gif.at[b, rows_of(frm * quarter, quarter), :]
            ag[b].copy_to(k, theirs, theirs).wait_recv()
        ginp[b] = nn(permt[...], gif[b]).astype(BF)
    back_copy(0, True).wait_recv()
    gup[...] = gsum[0:width, :].astype(F32)
    gdown[...] = gsum[width : 2 * width, :].astype(F32)
    gq[...] = jnp.transpose(gsum[base : base + cols, :].astype(F32))
    gk[...] = jnp.transpose(gsum[base + cols : base + 2 * cols, :].astype(F32))
    gv[...] = jnp.transpose(gsum[base + 2 * cols : base + 3 * cols, :].astype(F32))
    goutf[...] = gsum[base + 3 * cols : base + 4 * cols, :].astype(F32)
    zrows = rows_of(p.z * quarter, quarter)
    for b in range(batches):
        for k in range(1, pat):
            rs[b].copy_to(k, dns.at[b, p.other_z(k)], dnr.at[b, k - 1]).wait_send()
            ag[b].copy_to(k, gif.at[b, zrows, :], gif.at[b, zrows, :]).wait_send()
    for d in range(3):
        red_copy(d).wait_send()
        back_copy(d, False).wait_send()
    for k in range(1, pat):
        zsp.copy_to(k, v0, vz.at[k - 1]).wait_send()
    for k in range(1, n):
        vec_copy(k).wait_send()


def call(kernel, name, outs, scratch, specs, number):
    return pl.pallas_call(
        kernel,
        name=name,
        out_shape=[jax.ShapeDtypeStruct(s, d) for s, d in outs],
        in_specs=[pl.BlockSpec(memory_space=m) for m in specs],
        out_specs=[pl.BlockSpec(memory_space=pltpu.VMEM)] * len(outs),
        scratch_shapes=scratch,
        compiler_params=pltpu.CompilerParams(
            collective_id=number, has_side_effects=True, vmem_limit_bytes=62 << 20
        ),
    )


def shards(
    n,
    pat,
    inputs,
    lengths,
    gain_one,
    shift_one,
    w_query,
    b_query,
    w_key,
    w_value,
    b_value,
    w_out,
    b_out,
    gain_two,
    shift_two,
    w_up,
    b_up,
    w_down,
    b_down,
    d_output,
):
    batches, shard, width = inputs.shape
    cols = w_query.shape[1]
    heads = cols // HD
    units = batches * heads
    chips = n // 2
    half = shard // 2
    quarter = shard // pat
    levels = 1
    while SPAN1 << (levels - 1) < n:
        levels += 1
    perm = jnp.asarray(perm_matrix(shard), BF)
    permt = jnp.asarray(perm_matrix(shard).T, BF)
    qext = jnp.asarray(query_ext(shard), BF)
    ktab = jnp.asarray(key_tables(shard, heads * pat, levels))
    row = lambda v: v.reshape(1, -1)
    by_head = lambda w: w.reshape(w.shape[0], heads, HD)
    pack = lambda a, b: jnp.concatenate([by_head(a), by_head(b)], 2).reshape(a.shape[0], 2 * cols)
    wq = pack(w_query, jnp.zeros_like(w_query))
    wkv = pack(w_key, w_value)
    bq = pack(row(b_query), jnp.zeros((1, cols), F32))
    bkv = pack(jnp.zeros((1, cols), F32), row(b_value))
    vm, sm, anyv = pltpu.VMEM, pltpu.SMEM, pl.ANY
    dma = pltpu.SemaphoreType.DMA
    tiles = units // 2

    xp, n1, qp, kvd, kvt, attf, wofp, attw, den, tab = call(
        functools.partial(forward_kernel, n, pat, levels),
        "attention_forward",
        [
            ((batches, shard, width), BF),
            ((batches, shard, width), BF),
            ((units, shard, 128), BF),
            ((units, SPAN1 * shard, 128), BF),
            ((units, n * half, 128), BF),
            ((pat, tiles, shard, 128), BF),
            ((pat, cols + 2 * HD, width), BF),
            ((tiles, shard, 128), F32),
            ((tiles, shard, 128), F32),
            ((heads, levels, shard, 128), BF),
        ],
        [
            pltpu.VMEM((units, shard, 128), F32),
            dma((heads,)),
            dma((pat - 1,)),
            dma((pat - 1,)),
            dma((tiles, pat - 1)),
            dma((tiles, pat - 1)),
        ]
        + dense_sems(batches)
        + thin_sems(batches, chips),
        [sm] + [vm] * 10 + [anyv],
        0,
    )(lengths, inputs, row(gain_one), row(shift_one), wq, bq, wkv, bkv, w_out, perm, qext, ktab)

    gud, fd, dsf, dst, sto, vecs = call(
        functools.partial(middle_kernel, n, pat),
        "feed_forward",
        [
            ((2 * width, width), BF),
            ((batches, shard, width), BF),
            ((batches, shard, width), BF),
            ((batches, quarter, width), F32),
            ((batches, quarter, width), F32),
            ((8, width), F32),
        ],
        [
            pltpu.VMEM((batches, shard, width), F32),
            pltpu.VMEM((batches, shard, width), BF),
            pltpu.VMEM((batches, shard, width), BF),
            pltpu.VMEM((batches, shard, width), BF),
            pltpu.VMEM((batches, shard, width), BF),
            pltpu.VMEM((batches, pat, quarter, width), BF),
            pltpu.VMEM((batches, quarter, width), F32),
            pltpu.VMEM((batches, pat - 1, quarter, width), BF),
        ]
        + [dma((batches, pat - 1))] * 4,
        [vm] * 11,
        1,
    )(
        xp,
        attf,
        wofp,
        row(b_out),
        row(gain_two),
        row(shift_two),
        w_up,
        row(b_up),
        w_down,
        d_output,
        perm,
    )

    dq, dkv, gout, outputs = call(
        functools.partial(backward_kernel, n, pat, levels),
        "attention_backward",
        [
            ((batches, shard, 2 * cols), BF),
            ((batches, shard, 2 * cols), BF),
            ((cols, width), BF),
            ((batches, shard, width), BF),
        ],
        [
            pltpu.VMEM((units, SPAN1 * shard, 128), BF),
            pltpu.VMEM((units, n * half, 128), BF),
            pltpu.VMEM((SPAN1, 8, shard), F32),
            pltpu.VMEM((n, 8, half), F32),
            pltpu.VMEM((units, shard, 128), BF),
            pltpu.VMEM((units, shard, 128), F32),
            pltpu.VMEM((units, shard, 128), F32),
            pltpu.VMEM((batches, pat - 1, quarter, width), BF),
            pltpu.VMEM((batches, shard, width), BF),
        ]
        + [dma((batches, pat - 1))] * 4
        + dense_sems(batches)
        + thin_sems(batches, chips)
        + [dma((3,))] * 2
        + [dma((chips,))] * 4,
        [sm] + [vm] * 14,
        2,
    )(lengths, dsf, wofp, attf, attw, den, qp, kvd, kvt, tab, qext, fd, sto, row(b_down), permt)

    rows = 2 * width + 4 * cols
    grad_inputs, vout, g_up, g_down, g_out, g_q, g_k, g_v = call(
        functools.partial(tail_kernel, n, pat),
        "gradient_sums",
        [
            ((batches, shard, width), BF),
            ((16, width), F32),
            ((width, width), F32),
            ((width, width), F32),
            ((cols, width), F32),
            ((width, cols), F32),
            ((width, cols), F32),
            ((width, cols), F32),
        ],
        [
            pltpu.VMEM((batches, pat, quarter, width), BF),
            pltpu.VMEM((batches, pat - 1, quarter, width), BF),
            pltpu.VMEM((batches, shard, width), BF),
            pltpu.VMEM((rows, width), BF),
            pltpu.VMEM((rows, width), BF),
            pltpu.VMEM((rows // 2, width), BF),
            pltpu.VMEM((rows // 4, width), BF),
            pltpu.VMEM((rows // 8, width), BF),
            pltpu.VMEM((8, width), F32),
            pltpu.VMEM((pat - 1, 8, width), F32),
            pltpu.VMEM((n, 16, width), F32),
        ]
        + [dma((batches, pat - 1))] * 4
        + [dma((6,))] * 2
        + [dma((pat - 1,))] * 2
        + [dma((n - 1,))] * 2,
        [vm] * 12,
        3,
    )(xp, n1, dq, dkv, wq, wkv, row(gain_one), dst, vecs, gud, gout, permt)
    q_row = vout[8, : 2 * cols].reshape(heads, 2, HD)
    v_row = vout[9, : 2 * cols].reshape(heads, 2, HD)
    return (
        outputs,
        grad_inputs,
        vout[0],
        vout[1],
        g_q,
        q_row[:, 0].reshape(cols),
        g_k,
        g_v,
        v_row[:, 1].reshape(cols),
        g_out,
        vout[2],
        vout[3],
        vout[4],
        g_up,
        vout[5],
        g_down,
        vout[6],
    )


def solution(mesh):
    token = P(None, "seq", None)
    in_specs = (
        token,
        P(),
        P(),
        P(),
        P(None, "pat"),
        P("pat"),
        P(None, "pat"),
        P(None, "pat"),
        P("pat"),
        P("pat", None),
        P(),
        P(),
        P(),
        P(None, "pat"),
        P("pat"),
        P("pat", None),
        P(),
        token,
    )
    out_specs = (
        token,
        token,
        P(),
        P(),
        P(None, "pat"),
        P("pat"),
        P(None, "pat"),
        P(None, "pat"),
        P("pat"),
        P("pat", None),
        P(),
        P(),
        P(),
        P(None, "pat"),
        P("pat"),
        P("pat", None),
        P(),
    )
    body = functools.partial(shards, mesh.shape["seq"], mesh.shape["pat"])
    return jax.shard_map(body, mesh=mesh, in_specs=in_specs, out_specs=out_specs, check_vma=False)
```

```python
import functools

import jax
import jax.numpy as jnp
import numpy as np
from jax import lax
from jax.experimental import pallas as pl
from jax.experimental.pallas import tpu as pltpu
from jax.sharding import PartitionSpec as P

HD = 64
SPAN1 = 4
DILATIONS = (1, 2, 4, 6, 12)
CYCLE = 12
EPS = 1e-05
NEG = -1e30
LEN_LANE = 24
COR_LANE = 25
MESH = pl.DeviceIdType.MESH
BF = jnp.bfloat16
F32 = jnp.float32
ROOT = float(np.sqrt(2.0 / np.pi))


def nn(a, b):
    return lax.dot_general(a, b, (((1,), (0,)), ((), ())), preferred_element_type=F32)


def nt(a, b):
    return lax.dot_general(a, b, (((1,), (1,)), ((), ())), preferred_element_type=F32)


def tn(a, b):
    return lax.dot_general(a, b, (((0,), (0,)), ((), ())), preferred_element_type=F32)


def exact_nt(a, b):
    return lax.dot_general(
        a, b, (((1,), (1,)), ((), ())), preferred_element_type=F32, precision=lax.Precision.HIGHEST
    )


def exact_nn(a, b):
    return lax.dot_general(
        a, b, (((1,), (0,)), ((), ())), preferred_element_type=F32, precision=lax.Precision.HIGHEST
    )


def remote(src, dst, send, recv, device):
    return pltpu.make_async_remote_copy(
        src_ref=src,
        dst_ref=dst,
        send_sem=send,
        recv_sem=recv,
        device_id=device,
        device_id_type=MESH,
    )


def when(cond, fn):
    pl.when(cond)(fn)


def rows_of(start, size):
    return pl.ds(pl.multiple_of(start, 16), size)


def orders(shard):
    p = np.arange(shard)
    return 2 * (p % (shard // 2)) + p // (shard // 2)


def perm_matrix(shard):
    token = orders(shard)
    m = np.zeros((shard, shard), np.float32)
    m[np.arange(shard), token] = 1.0
    return m


def query_ext(shard):
    cls = orders(shard) % CYCLE
    m = np.zeros((shard, 128), np.float32)
    m[np.arange(shard), cls] = 1.0
    m[np.arange(shard), CYCLE + cls] = 1.0
    m[:, LEN_LANE] = 1.0
    return m


def key_tables(shard, heads, levels):
    cls = orders(shard) % CYCLE
    out = np.zeros((heads, levels, shard, 128), np.float32)
    for h in range(heads):
        for level in range(levels):
            count = np.zeros((CYCLE, CYCLE))
            for r in DILATIONS[level:]:
                on = (np.arange(CYCLE) % r == h % r).astype(np.float64)
                count += on[:, None] * on[None, :]
            with np.errstate(divide="ignore"):
                log = np.log(count)
            high = np.where(count > 0, log, NEG).astype(np.float32).astype(jnp.bfloat16)
            low = np.where(count > 0, log - high.astype(np.float64), 0.0)
            out[h, level, :, :CYCLE] = high.astype(np.float32)[:, cls].T
            out[h, level, :, CYCLE : 2 * CYCLE] = low[:, cls].T
            out[h, level, :, COR_LANE] = 1.0
            out[h, level, :, COR_LANE + 1] = 1.0
    return out.astype(jnp.bfloat16)


class Place:
    def __init__(self, n, pat):
        self.n, self.pat = n, pat
        self.z = lax.axis_index("pat")
        self.s = lax.axis_index("seq")
        self.core = lax.rem(self.s, 2)
        self.chip = lax.div(self.s, 2)
        self.seg = lax.div(self.s, SPAN1)
        self.pos = lax.rem(self.s, SPAN1)
        self.sib = self.s + 1 - 2 * self.core
        self.even = lax.rem(self.chip, 2) == 0

    def other_z(self, k):
        return lax.rem(self.z + k, self.pat)

    def greet(self, z_axis, same_core, all_seq=False):
        bar = pltpu.get_barrier_semaphore()
        count = 0
        if z_axis:
            for k in range(1, self.pat):
                pl.semaphore_signal(
                    bar, inc=1, device_id=(self.other_z(k), self.s), device_id_type=MESH
                )
                count += 1
        if all_seq:
            for k in range(1, self.n):
                to = lax.rem(self.s + k, self.n)
                pl.semaphore_signal(bar, inc=1, device_id=(self.z, to), device_id_type=MESH)
                count += 1
        elif same_core:
            pl.semaphore_signal(bar, inc=1, device_id=(self.z, self.sib), device_id_type=MESH)
            count += 1
            for k in range(1, self.n // 2):
                to = lax.rem(self.s + 2 * k, self.n)
                pl.semaphore_signal(bar, inc=1, device_id=(self.z, to), device_id_type=MESH)
                count += 1
        return bar, count


def lane_masks():
    lane = lax.broadcasted_iota(jnp.int32, (1, 128), 1)
    low = jnp.where(lane < HD, 1.0, 0.0)
    return low.astype(BF), (1.0 - low).astype(BF)


def token_of(index, shard):
    half = jnp.where(index >= shard // 2, 1, 0)
    return 2 * (index - half * (shard // 2)) + half


def length_lane(positions, length, rows):
    lane = lax.broadcasted_iota(jnp.int32, (rows, 128), 1)
    hit = jnp.logical_and(lane == LEN_LANE, positions >= length)
    return jnp.where(hit, NEG, 0.0).astype(BF)


def dense_positions(device, shard):
    row = lax.broadcasted_iota(jnp.int32, (shard, 128), 0)
    return device * shard + token_of(row, shard)


def thin_positions(first_device, parity, shard, blocks):
    half = shard // 2
    row = lax.broadcasted_iota(jnp.int32, (blocks * half, 128), 0)
    block = lax.div(row, half)
    return (first_device + block) * shard + 2 * (row - block * half) + parity


def level_of(seg_a, seg_b, levels):
    level = jnp.int32(1)
    size = 2
    for _ in range(2, levels):
        apart = lax.div(seg_a, size) != lax.div(seg_b, size)
        level = level + jnp.where(apart, 1, 0)
        size *= 2
    return level


class Shares:
    def __init__(self, place, shard, forward, dense, thin, dense_sems, thin_sems):
        self.p, self.shard, self.forward = place, shard, forward
        self.dense, self.thin = dense, thin
        self.ds, self.ts = dense_sems, thin_sems
        p = place
        self.chips = p.n // 2
        if forward:
            self.sib_sends, self.sib_gets = p.core == 0, p.core == 1
            self.x_sends, self.x_gets = p.even, jnp.logical_not(p.even)
            self.x_to, self.x_slot = p.s + 2, p.pos - 2
        else:
            self.sib_sends, self.sib_gets = p.core == 1, p.core == 0
            self.x_sends, self.x_gets = jnp.logical_not(p.even), p.even
            self.x_to, self.x_slot = p.s - 2, p.pos + 2
        self.sib_pos = p.pos + 1 - 2 * p.core
        self.x_sib_slot = self.x_slot + 1 - 2 * p.core

    def sib_copy(self, slot):
        p = self.p
        return remote(
            self.dense(slot), self.dense(slot), self.ds[0].at[0], self.ds[1].at[0], (p.z, p.sib)
        )

    def x_copy(self, slot):
        p = self.p
        to = jnp.where(self.x_sends, self.x_to, p.sib)
        return remote(
            self.dense(slot), self.dense(slot), self.ds[0].at[1], self.ds[1].at[1], (p.z, to)
        )

    def hand_copy(self, slot):
        p = self.p
        return remote(
            self.dense(slot), self.dense(slot), self.ds[0].at[2], self.ds[1].at[2], (p.z, p.sib)
        )

    def thin_to(self, chip):
        seg = chip // 2
        return (seg > self.p.seg) if self.forward else (seg < self.p.seg)

    def thin_from(self, chip):
        seg = chip // 2
        return (seg < self.p.seg) if self.forward else (seg > self.p.seg)

    def thin_copy(self, chip):
        p = self.p
        return remote(
            self.thin(p.s),
            self.thin(p.s),
            self.ts[0].at[chip],
            self.ts[1].at[p.chip],
            (p.z, 2 * chip + p.core),
        )

    def thin_got(self, chip):
        p = self.p
        slot = 2 * chip + p.core
        return remote(
            self.thin(slot), self.thin(slot), self.ts[0].at[chip], self.ts[1].at[chip], (p.z, p.sib)
        )

    def thin_hand(self, chip, mine):
        p = self.p
        slot = 2 * chip + (p.core if mine else 1 - p.core)
        return remote(
            self.thin(slot), self.thin(slot), self.ts[2].at[chip], self.ts[3].at[chip], (p.z, p.sib)
        )

    def start(self):
        p = self.p
        when(self.x_sends, lambda: self.x_copy(p.pos).start())
        for chip in range(self.chips):
            when(self.thin_to(chip), lambda chip=chip: self.thin_copy(chip).start())
        when(self.sib_sends, lambda: self.sib_copy(p.pos).start())

    def pass_on(self):
        def dense_part():
            self.x_copy(self.x_slot).wait_recv()
            self.hand_copy(self.x_slot).start()

        when(self.x_gets, dense_part)
        for chip in range(self.chips):

            def thin_part(chip=chip):
                self.thin_got(chip).wait_recv()
                self.thin_hand(chip, True).start()

            when(self.thin_from(chip), thin_part)

    def arrive(self):
        when(self.sib_gets, lambda: self.sib_copy(self.sib_pos).wait_recv())
        when(self.x_gets, lambda: self.hand_copy(self.x_sib_slot).wait_recv())
        for chip in range(self.chips):
            when(
                self.thin_from(chip),
                lambda chip=chip: self.thin_hand(chip, False).wait_recv(),
            )

    def finish(self):
        p = self.p
        when(self.x_sends, lambda: self.x_copy(p.pos).wait_send())
        when(self.sib_sends, lambda: self.sib_copy(p.pos).wait_send())
        when(self.x_gets, lambda: self.hand_copy(self.x_slot).wait_send())
        for chip in range(self.chips):
            when(self.thin_to(chip), lambda chip=chip: self.thin_copy(chip).wait_send())
            when(self.thin_from(chip), lambda chip=chip: self.thin_hand(chip, True).wait_send())


def dense_sems(batches):
    return [pltpu.SemaphoreType.DMA((batches, 3))] * 2


def thin_sems(batches, chips):
    return [pltpu.SemaphoreType.DMA((batches, chips))] * 4


class Spread:
    def __init__(self, place, send, recv):
        self.p, self.send, self.recv = place, send, recv

    def copy_to(self, k, src, dst):
        p = self.p
        return remote(src, dst, self.send.at[k - 1], self.recv.at[k - 1], (p.other_z(k), p.s))


def forward_kernel(
    n,
    pat,
    levels,
    lens,
    x_ref,
    gain,
    shift,
    wq,
    bq,
    wkv,
    bkv,
    wout,
    perm,
    qext,
    ktab,
    xp,
    n1,
    qp,
    kvd,
    kvt,
    attf,
    wofp,
    attw,
    den,
    tab,
    acc,
    tab_sem,
    w_send,
    w_recv,
    a_send,
    a_recv,
    ds0,
    ds1,
    ts0,
    ts1,
    ts2,
    ts3,
):
    batches, shard, width = x_ref.shape
    half = shard // 2
    heads = wout.shape[0] // HD
    units = batches * heads
    p = Place(n, pat)
    bar, greeted = p.greet(True, True)
    low, high = lane_masks()

    def tab_copy(i):
        return pltpu.make_async_copy(ktab.at[heads * p.z + i], tab.at[i], tab_sem.at[i])

    for i in range(heads):
        tab_copy(i).start()
    for z in range(pat):
        wofp[z, 0:HD, :] = jnp.zeros((HD, width), BF)
        wofp[z, HD + heads * HD : 2 * HD + heads * HD, :] = jnp.zeros((HD, width), BF)
    wofp[p.z, HD : HD + heads * HD, :] = wout[...]
    for b in range(batches):
        xb = nn(perm[...], x_ref[b])
        xp[b] = xb.astype(BF)
        mean = jnp.mean(xb, -1, keepdims=True)
        cen = xb - mean
        var = jnp.mean(cen * cen, -1, keepdims=True)
        n1[b] = (cen * lax.rsqrt(var + EPS) * gain[...] + shift[...]).astype(BF)

    shares = [
        Shares(
            p,
            shard,
            True,
            lambda slot, b=b: kvd.at[pl.ds(heads * b, heads), rows_of(slot * shard, shard), :],
            lambda dev, b=b: kvt.at[pl.ds(heads * b, heads), rows_of(dev * half, half), :],
            [ds0.at[b], ds1.at[b]],
            [ts0.at[b], ts1.at[b], ts2.at[b], ts3.at[b]],
        )
        for b in range(batches)
    ]
    parity = [lax.rem(heads * p.z + i, 2) for i in range(heads)]
    for b in range(batches):
        q = ((nn(n1[b], wq[...]) + bq[...]).astype(BF)) * jnp.asarray(HD**-0.5, BF)
        kv = (nn(n1[b], wkv[...]) + bkv[...]).astype(BF)
        for i in range(heads):
            qp[heads * b + i] = q[:, i * 128 : (i + 1) * 128]
            kvd[heads * b + i, rows_of(p.pos * shard, shard), :] = kv[:, i * 128 : (i + 1) * 128]
        for i in range(heads):
            kvt[heads * b + i, rows_of(p.s * half, half), :] = kvd[
                heads * b + i, rows_of(p.pos * shard + parity[i] * half, half), :
            ]
        if b == 0:
            pl.semaphore_wait(bar, greeted)
        shares[b].start()
    w_spread = Spread(p, w_send, w_recv)

    def w_slot(z):
        return wofp.at[z, HD : HD + heads * HD, :]

    for k in range(1, pat):
        w_spread.copy_to(k, w_slot(p.z), w_slot(p.z)).start()
    for i in range(heads):
        tab_copy(i).wait()

    def attend(qx, kv, ext, bias):
        s = nt(qx, jnp.concatenate([kv, ext], 1))
        if bias is not None:
            s = s + bias
        return nn(jnp.exp(s).astype(BF), kv * high + low)

    own = rows_of(p.pos * shard, shard)
    qi = lax.broadcasted_iota(jnp.int32, (shard, shard), 0)
    ki = lax.broadcasted_iota(jnp.int32, (shard, shard), 1)
    qt, kt = token_of(qi, shard), token_of(ki, shard)
    for b in range(batches):
        live = jnp.logical_or(
            jnp.logical_and(kt < qt, kt + p.s * shard < lens[b]), kt == qt
        )
        bias = jnp.where(live, 0.0, NEG)
        for i in range(heads):
            u = heads * b + i
            qx = jnp.concatenate([qp[u], qext[...]], 1)
            acc[u] = attend(qx, kvd[u, own, :], tab[i, 0], bias)

    att_spread = [Spread(p, a_send.at[t], a_recv.at[t]) for t in range(units // 2)]
    lane = lax.broadcasted_iota(jnp.int32, (shard, 128), 1)
    for b in range(batches):
        shares[b].pass_on()
        shares[b].arrive()

        def dense(j, carry, b=b):
            lenl = length_lane(dense_positions(p.seg * SPAN1 + j, shard), lens[b], shard)
            for i in range(heads):
                u = heads * b + i
                qx = jnp.concatenate([qp[u], qext[...]], 1)
                kv = kvd[u, rows_of(j * shard, shard), :]
                acc[u] += attend(qx, kv, tab[i, 0] + lenl, None)
            return carry

        lax.fori_loop(0, p.pos, dense, 0)

        def thin(sg, carry, b=b):
            level = level_of(sg, p.seg, levels)
            for i in range(heads):
                u = heads * b + i
                mine = rows_of(parity[i] * half, half)
                places = thin_positions(sg * SPAN1, parity[i], shard, SPAN1)
                lenl = length_lane(places, lens[b], SPAN1 * half)
                ext = jnp.concatenate([tab[i, level, mine, :]] * SPAN1, 0) + lenl
                qx = jnp.concatenate([qp[u, mine, :], qext[mine, :]], 1)
                kv = kvt[u, rows_of(sg * SPAN1 * half, SPAN1 * half), :]
                acc[u, mine, :] += attend(qx, kv, ext, None)
            return carry

        lax.fori_loop(0, p.seg, thin, 0)
        for t in range(units // 2):
            if (2 * t + 1) // heads != b:
                continue
            even, odd = acc[2 * t], acc[2 * t + 1]
            num = jnp.where(lane < HD, pltpu.roll(even, HD, 1), odd)
            dn = jnp.where(lane < HD, even, pltpu.roll(odd, HD, 1))
            wide = num / dn
            den[t] = dn
            attw[t] = wide
            attf[p.z, t] = wide.astype(BF)
            for k in range(1, pat):
                att_spread[t].copy_to(k, attf.at[p.z, t], attf.at[p.z, t]).start()
    for k in range(1, pat):
        frm = lax.rem(p.z + pat - k, pat)
        w_spread.copy_to(k, w_slot(p.z), w_slot(p.z)).wait_send()
        w_spread.copy_to(k, w_slot(frm), w_slot(frm)).wait_recv()
        for t in range(units // 2):
            att_spread[t].copy_to(k, attf.at[p.z, t], attf.at[p.z, t]).wait_send()
            att_spread[t].copy_to(k, attf.at[frm, t], attf.at[frm, t]).wait_recv()
    for b in range(batches):
        shares[b].finish()


def middle_kernel(
    n,
    pat,
    xp,
    attf,
    wofp,
    bout,
    gain,
    shift,
    wup,
    bup,
    wdown,
    dout,
    perm,
    gud,
    fd,
    dsf,
    dst,
    sto,
    vecs,
    state,
    n2,
    act,
    dop,
    dh,
    dns,
    dno,
    dnr,
    r_send,
    r_recv,
    g_send,
    g_recv,
):
    batches, shard, width = xp.shape
    quarter = shard // pat
    p = Place(n, pat)
    bar, greeted = p.greet(True, False)
    rs = [Spread(p, r_send.at[b], r_recv.at[b]) for b in range(batches)]
    ag = [Spread(p, g_send.at[b], g_recv.at[b]) for b in range(batches)]
    bup_sum = jnp.zeros((1, width), F32)
    bdown_sum = jnp.zeros((1, width), F32)
    for b in range(batches):
        mixed = jnp.zeros((shard, width), F32)
        for z in range(pat):
            pair = jnp.concatenate([attf[z, b], attf[z, b + 1]], 1)
            weight = wofp[z, HD : HD + 256, :] if b == 0 else wofp[z, 0:256, :]
            mixed = mixed + nn(pair, weight)
        st = xp[b].astype(F32) + mixed + bout[...]
        state[b] = st
        mean = jnp.mean(st, -1, keepdims=True)
        cen = st - mean
        var = jnp.mean(cen * cen, -1, keepdims=True)
        norm = (cen * lax.rsqrt(var + EPS) * gain[...] + shift[...]).astype(BF)
        n2[b] = norm
        dob = nn(perm[...], dout[b])
        dop[b] = dob.astype(BF)
        bdown_sum = bdown_sum + jnp.sum(dob, 0, keepdims=True)
        hid = nn(norm, wup[...]) + bup[...]
        cube = hid * hid * hid
        th = jnp.tanh(ROOT * (hid + 0.044715 * cube))
        act[b] = (0.5 * hid * (1.0 + th)).astype(BF)
        slope = 0.5 * (1.0 + th) + 0.5 * hid * (1.0 - th * th) * (
            ROOT * (1.0 + 3.0 * 0.044715 * hid * hid)
        )
        dhid = (nt(dop[b], wdown[...]) * slope).astype(BF)
        dh[b] = dhid
        bup_sum = bup_sum + jnp.sum(dhid.astype(F32), 0, keepdims=True)
        dn = nt(dhid, wup[...])
        for z in range(pat):
            dns[b, z] = dn[z * quarter : (z + 1) * quarter].astype(BF)
        if b == 0:
            pl.semaphore_wait(bar, greeted)
        for k in range(1, pat):
            rs[b].copy_to(k, dns.at[b, p.other_z(k)], dnr.at[b, k - 1]).start()
    vecs[...] = jnp.zeros(vecs.shape, F32)
    for b in range(batches):
        fd[b] = nn(act[b], wdown[...]).astype(BF)
    bout_sum = jnp.zeros((1, width), F32)
    gain_sum = jnp.zeros((1, width), F32)
    shift_sum = jnp.zeros((1, width), F32)
    mine = rows_of(p.z * quarter, quarter)
    for b in range(batches):
        total = dns[b, p.z].astype(F32)
        for k in range(1, pat):
            rs[b].copy_to(k, dns.at[b, p.other_z(k)], dnr.at[b, k - 1]).wait_recv()
            total = total + dnr[b, k - 1].astype(F32)
        st = state[b, mine, :]
        sto[b] = st
        mean = jnp.mean(st, -1, keepdims=True)
        cen = st - mean
        inv = lax.rsqrt(jnp.mean(cen * cen, -1, keepdims=True) + EPS)
        hat = cen * inv
        gain_sum = gain_sum + jnp.sum(total * hat, 0, keepdims=True)
        shift_sum = shift_sum + jnp.sum(total, 0, keepdims=True)
        dhat = total * gain[...]
        back = inv * (
            dhat
            - jnp.mean(dhat, -1, keepdims=True)
            - hat * jnp.mean(dhat * hat, -1, keepdims=True)
        )
        ds = dop[b, mine, :].astype(F32) + back
        dst[b] = ds
        bout_sum = bout_sum + jnp.sum(ds, 0, keepdims=True)
        dsf[b, mine, :] = ds.astype(BF)
        for k in range(1, pat):
            ag[b].copy_to(k, dsf.at[b, mine, :], dsf.at[b, mine, :]).start()
    vecs[2:3, :] = bout_sum
    vecs[3:4, :] = gain_sum
    vecs[4:5, :] = shift_sum
    vecs[5:6, :] = bup_sum
    vecs[6:7, :] = bdown_sum
    up = tn(n2[0], dh[0])
    for b in range(1, batches):
        up = up + tn(n2[b], dh[b])
    gud[0:width, :] = up.astype(BF)
    down = tn(act[0], dop[0])
    for b in range(1, batches):
        down = down + tn(act[b], dop[b])
    gud[width : 2 * width, :] = down.astype(BF)
    for b in range(batches):
        for k in range(1, pat):
            frm = lax.rem(p.z + pat - k, pat)
            theirs = dsf.at[b, rows_of(frm * quarter, quarter), :]
            rs[b].copy_to(k, dns.at[b, p.other_z(k)], dnr.at[b, k - 1]).wait_send()
            ag[b].copy_to(k, dsf.at[b, mine, :], dsf.at[b, mine, :]).wait_send()
            ag[b].copy_to(k, theirs, theirs).wait_recv()


def backward_kernel(
    n,
    pat,
    levels,
    lens,
    dsf,
    wofp,
    attf,
    attw,
    den,
    qp,
    kvd,
    kvt,
    tab,
    qext,
    fd,
    sto,
    bdown,
    permt,
    dq,
    dkv,
    gout,
    outp,
    qud,
    qut,
    crd,
    crt,
    uext,
    acq,
    ack,
    fdr,
    outf,
    f_send,
    f_recv,
    o_send,
    o_recv,
    ds0,
    ds1,
    ts0,
    ts1,
    ts2,
    ts3,
    cd0,
    cd1,
    ct0,
    ct1,
    ct2,
    ct3,
):
    batches, shard, width = dsf.shape
    half = shard // 2
    quarter = shard // pat
    units = qp.shape[0]
    heads = units // batches
    p = Place(n, pat)
    bar, greeted = p.greet(True, True)
    low, high = lane_masks()
    parity = [lax.rem(heads * p.z + i, 2) for i in range(heads)]
    own = rows_of(p.pos * shard, shard)
    lane = lax.broadcasted_iota(jnp.int32, (shard, 128), 1)
    row8 = lax.broadcasted_iota(jnp.int32, (8, 128), 0)
    lane8 = lax.broadcasted_iota(jnp.int32, (8, 128), 1)
    pick = jnp.where(row8 == lax.div(lane8, HD), 1.0, 0.0).astype(F32)
    ri = lax.broadcasted_iota(jnp.int32, (128, 128), 0)
    ci = lax.broadcasted_iota(jnp.int32, (128, 128), 1)
    same = jnp.where(lax.div(ri, HD) == lax.div(ci, HD), 1.0, 0.0).astype(F32)

    wide = [
        nt(dsf[b], wofp[p.z, HD : HD + 256, :] if b == 0 else wofp[p.z, 0:256, :])
        for b in range(batches)
    ]
    tiles = [wide[0][:, 0:128], wide[0][:, 128:256] + wide[1][:, 0:128], wide[1][:, 128:256]]
    crd[p.pos] = jnp.zeros(crd.shape[1:], F32)
    crt[p.s] = jnp.zeros(crt.shape[1:], F32)
    for t in range(units // 2):
        dn = den[t]
        up = tiles[t] / dn
        prod = tiles[t] * attw[t] / dn
        cor = exact_nn(prod, same)
        cor_rows = exact_nt(pick, prod)
        for e in range(2):
            u = 2 * t + e
            i = u % heads
            part = up if e == 1 else pltpu.roll(up, HD, 1)
            mixed = jnp.where(lane < HD, qp[u].astype(F32), part).astype(BF)
            qud[u, own, :] = mixed
            qut[u, rows_of(p.s * half, half), :] = qud[
                u, rows_of(p.pos * shard + parity[i] * half, half), :
            ]
            crd[p.pos, u : u + 1, :] = cor_rows[e : e + 1, :]
            col = -cor[:, e * HD : e * HD + 1]
            first = col.astype(BF).astype(F32)
            ue = jnp.where(lane == COR_LANE, first, 0.0) + jnp.where(
                lane == COR_LANE + 1, col - first, 0.0
            )
            uext[u] = ue.astype(BF)
            thin_cor = jnp.where(parity[i] == 0, cor_rows[e : e + 1, 0:half], cor_rows[e : e + 1, half:shard])
            crt[p.s, u : u + 1, :] = thin_cor
    pl.semaphore_wait(bar, greeted)
    cors = Shares(
        p,
        shard,
        False,
        lambda slot: crd.at[slot],
        lambda dev: crt.at[dev],
        [cd0, cd1],
        [ct0, ct1, ct2, ct3],
    )
    shares = [
        Shares(
            p,
            shard,
            False,
            lambda slot, b=b: qud.at[pl.ds(heads * b, heads), rows_of(slot * shard, shard), :],
            lambda dev, b=b: qut.at[pl.ds(heads * b, heads), rows_of(dev * half, half), :],
            [ds0.at[b], ds1.at[b]],
            [ts0.at[b], ts1.at[b], ts2.at[b], ts3.at[b]],
        )
        for b in range(batches)
    ]
    cors.start()
    for b in range(batches):
        shares[b].start()
    fs = [Spread(p, f_send.at[b], f_recv.at[b]) for b in range(batches)]
    og = [Spread(p, o_send.at[b], o_recv.at[b]) for b in range(batches)]

    def fd_src(b, k):
        return fd.at[b, rows_of(p.other_z(k) * quarter, quarter), :]

    for b in range(batches):
        for k in range(1, pat):
            fs[b].copy_to(k, fd_src(b, k), fdr.at[b, k - 1]).start()

    def query_side(qu, qe, ue, kv, ext, bias):
        kvx = jnp.concatenate([kv, ext], 1)
        s = nt(jnp.concatenate([qu * low, qe], 1), kvx)
        if bias is not None:
            s = s + bias
        dp = nt(jnp.concatenate([qu * high, ue], 1), kvx)
        return nn((jnp.exp(s) * dp).astype(BF), kv)

    def key_side(qu, qe, cor, kv, ext, bias):
        s = nt(jnp.concatenate([kv, ext], 1), jnp.concatenate([qu * low, qe], 1))
        if bias is not None:
            s = s + bias
        w = jnp.exp(s)
        dp = nt(kv, qu * high) - cor
        return nn((w * dp).astype(BF), qu * low) + nn(w.astype(BF), qu * high)

    qi = lax.broadcasted_iota(jnp.int32, (shard, shard), 0)
    ki = lax.broadcasted_iota(jnp.int32, (shard, shard), 1)
    ti, tj = token_of(qi, shard), token_of(ki, shard)
    for b in range(batches):
        bias = jnp.where(
            jnp.logical_or(jnp.logical_and(tj < ti, tj + p.s * shard < lens[b]), tj == ti), 0.0, NEG
        )
        biast = jnp.where(
            jnp.logical_or(jnp.logical_and(ti < tj, ti + p.s * shard < lens[b]), tj == ti), 0.0, NEG
        )
        for i in range(heads):
            u = heads * b + i
            kv = kvd[u, own, :]
            qu = qud[u, own, :]
            acq[u] = query_side(qu, qext[...], uext[u], kv, tab[i, 0], bias)
            ack[u] = key_side(qu, qext[...], crd[p.pos, u : u + 1, :], kv, tab[i, 0], biast)

    for b in range(batches):

        def dense_q(j, carry, b=b):
            lenl = length_lane(dense_positions(p.seg * SPAN1 + j, shard), lens[b], shard)
            for i in range(heads):
                u = heads * b + i
                kv = kvd[u, rows_of(j * shard, shard), :]
                acq[u] += query_side(
                    qud[u, own, :], qext[...], uext[u], kv, tab[i, 0] + lenl, None
                )
            return carry

        lax.fori_loop(0, p.pos, dense_q, 0)

        def thin_q(sg, carry, b=b):
            level = level_of(sg, p.seg, levels)
            for i in range(heads):
                u = heads * b + i
                mine = rows_of(parity[i] * half, half)
                places = thin_positions(sg * SPAN1, parity[i], shard, SPAN1)
                lenl = length_lane(places, lens[b], SPAN1 * half)
                ext = jnp.concatenate([tab[i, level, mine, :]] * SPAN1, 0) + lenl
                kv = kvt[u, rows_of(sg * SPAN1 * half, SPAN1 * half), :]
                qu = qut[u, rows_of(p.s * half, half), :]
                acq[u, mine, :] += query_side(
                    qu, qext[mine, :], uext[u, mine, :], kv, ext, None
                )
            return carry

        lax.fori_loop(0, p.seg, thin_q, 0)

    zrows = rows_of(p.z * quarter, quarter)
    for b in range(batches):
        total = fd[b, zrows, :].astype(F32)
        for k in range(1, pat):
            fs[b].copy_to(k, fd_src(b, k), fdr.at[b, k - 1]).wait_recv()
            total = total + fdr[b, k - 1].astype(F32)
        outf[b, zrows, :] = (sto[b] + total + bdown[...]).astype(BF)
        for k in range(1, pat):
            og[b].copy_to(k, outf.at[b, zrows, :], outf.at[b, zrows, :]).start()
    left = tn(jnp.concatenate([attf[p.z, 0], attf[p.z, 1]], 1), dsf[0])
    right = tn(jnp.concatenate([attf[p.z, 1], attf[p.z, 2]], 1), dsf[1])
    gout[...] = (left[0 : heads * HD] + right[HD : HD + heads * HD]).astype(BF)

    cors.pass_on()
    cors.arrive()
    for b in range(batches):
        shares[b].pass_on()
        shares[b].arrive()
        lenl = length_lane(dense_positions(p.s, shard), lens[b], shard)

        def dense_k(j, carry, b=b, lenl=lenl):
            for i in range(heads):
                u = heads * b + i
                qu = qud[u, rows_of(j * shard, shard), :]
                ack[u] += key_side(
                    qu, qext[...], crd[j, u : u + 1, :], kvd[u, own, :], tab[i, 0] + lenl, None
                )
            return carry

        lax.fori_loop(p.pos + 1, SPAN1, dense_k, 0)

        def thin_k(dev, carry, b=b):
            level = level_of(lax.div(dev, SPAN1), p.seg, levels)
            for i in range(heads):
                u = heads * b + i
                mine = rows_of(parity[i] * half, half)
                ext = tab[i, level, mine, :] + length_lane(
                    thin_positions(p.s, parity[i], shard, 1), lens[b], half
                )
                kv = kvt[u, rows_of(p.s * half, half), :]
                qu = qut[u, rows_of(dev * half, half), :]
                ack[u, mine, :] += key_side(
                    qu, qext[mine, :], crt[dev, u : u + 1, :], kv, ext, None
                )
            return carry

        lax.fori_loop(SPAN1 * (p.seg + 1), n, thin_k, 0)
        for i in range(heads):
            u = heads * b + i
            lanes = slice(i * 128, (i + 1) * 128)
            dq[b, :, lanes] = (acq[u] * HD**-0.5).astype(BF)
            dkv[b, :, lanes] = ack[u].astype(BF)

    for b in range(batches):
        for k in range(1, pat):
            frm = lax.rem(p.z + pat - k, pat)
            theirs = outf.at[b, rows_of(frm * quarter, quarter), :]
            og[b].copy_to(k, theirs, theirs).wait_recv()
            og[b].copy_to(k, outf.at[b, zrows, :], outf.at[b, zrows, :]).wait_send()
            fs[b].copy_to(k, fd_src(b, k), fdr.at[b, k - 1]).wait_send()
        outp[b] = nn(permt[...], outf[b]).astype(BF)
    cors.finish()
    for b in range(batches):
        shares[b].finish()


def tail_kernel(
    n,
    pat,
    xp,
    n1,
    dq,
    dkv,
    wq,
    wkv,
    gain,
    dst,
    vecs,
    gud,
    gout,
    permt,
    ginp,
    vout,
    gup,
    gdown,
    goutf,
    gq,
    gk,
    gv,
    dns,
    dnr,
    gif,
    grad,
    gsum,
    r1,
    r2,
    r3,
    v0,
    vz,
    vs,
    r_send,
    r_recv,
    g_send,
    g_recv,
    s_send,
    s_recv,
    z_send,
    z_recv,
    v_send,
    v_recv,
):
    batches, shard, width = xp.shape
    quarter = shard // pat
    cols = gout.shape[0]
    heads = cols // HD
    p = Place(n, pat)
    bar, greeted = p.greet(True, False, True)
    rs = [Spread(p, r_send.at[b], r_recv.at[b]) for b in range(batches)]
    ag = [Spread(p, g_send.at[b], g_recv.at[b]) for b in range(batches)]
    for b in range(batches):
        part = nt(dq[b], wq[...]) + nt(dkv[b], wkv[...])
        for z in range(pat):
            dns[b, z] = part[z * quarter : (z + 1) * quarter].astype(BF)
        if b == 0:
            pl.semaphore_wait(bar, greeted)
        for k in range(1, pat):
            rs[b].copy_to(k, dns.at[b, p.other_z(k)], dnr.at[b, k - 1]).start()
    qsum = jnp.zeros((1, heads * 128), F32)
    vsum = jnp.zeros((1, heads * 128), F32)
    for b in range(batches):
        qsum = qsum + jnp.sum(dq[b].astype(F32), 0, keepdims=True)
        vsum = vsum + jnp.sum(dkv[b].astype(F32), 0, keepdims=True)
    grad[0 : 2 * width, :] = gud[...]
    base = 2 * width
    for i in range(heads):
        lanes = slice(i * 128, (i + 1) * 128)
        a = tn(dq[0, :, lanes], n1[0])
        c = tn(dkv[0, :, lanes], n1[0])
        for b in range(1, batches):
            a = a + tn(dq[b, :, lanes], n1[b])
            c = c + tn(dkv[b, :, lanes], n1[b])
        grad[base + i * HD : base + (i + 1) * HD, :] = a[0:HD].astype(BF)
        grad[base + cols + i * HD : base + cols + (i + 1) * HD, :] = c[0:HD].astype(BF)
        grad[base + 2 * cols + i * HD : base + 2 * cols + (i + 1) * HD, :] = c[HD:].astype(BF)
    grad[base + 3 * cols : base + 4 * cols, :] = gout[...]

    size = grad.shape[0]
    bit_x = lax.rem(lax.div(p.s, 2), 2)
    bit_y = lax.div(p.s, 4)
    to_x = p.s + 2 - 4 * bit_x
    to_y = p.s + 4 - 8 * bit_y
    first = p.core == 0
    stages = [
        (p.core, p.sib, r1),
        (jnp.where(first, bit_x, bit_y), jnp.where(first, to_x, to_y), r2),
        (jnp.where(first, bit_y, bit_x), jnp.where(first, to_y, to_x), r3),
    ]
    offs = [jnp.int32(0)]
    sizes = [size]

    def red_copy(d):
        bit, to, buf = stages[d]
        h = sizes[d] // 2
        src = grad.at[rows_of(offs[d] + (1 - bit) * h, h), :]
        return remote(src, buf, s_send.at[d], s_recv.at[d], (p.z, to))

    def back_copy(d, got):
        bit, to, _ = stages[d]
        h = sizes[d] // 2
        rows = rows_of(offs[d] + ((1 - bit) if got else bit) * h, h)
        return remote(
            gsum.at[rows, :], gsum.at[rows, :], s_send.at[3 + d], s_recv.at[3 + d], (p.z, to)
        )

    for d in range(3):
        bit, _, buf = stages[d]
        h = sizes[d] // 2
        offs.append(offs[d] + bit * h)
        sizes.append(h)

    red_copy(0).start()

    def norm_back(b, gain_sum, shift_sum):
        zrows = rows_of(p.z * quarter, quarter)
        total = dns[b, p.z].astype(F32)
        for k in range(1, pat):
            rs[b].copy_to(k, dns.at[b, p.other_z(k)], dnr.at[b, k - 1]).wait_recv()
            total = total + dnr[b, k - 1].astype(F32)
        st = xp[b, zrows, :].astype(F32)
        mean = jnp.mean(st, -1, keepdims=True)
        cen = st - mean
        inv = lax.rsqrt(jnp.mean(cen * cen, -1, keepdims=True) + EPS)
        hat = cen * inv
        gain_sum = gain_sum + jnp.sum(total * hat, 0, keepdims=True)
        shift_sum = shift_sum + jnp.sum(total, 0, keepdims=True)
        dhat = total * gain[...]
        back = inv * (
            dhat
            - jnp.mean(dhat, -1, keepdims=True)
            - hat * jnp.mean(dhat * hat, -1, keepdims=True)
        )
        gif[b, zrows, :] = (dst[b] + back).astype(BF)
        for k in range(1, pat):
            ag[b].copy_to(k, gif.at[b, zrows, :], gif.at[b, zrows, :]).start()
        return gain_sum, shift_sum

    def reduce_stage(d):
        rows = rows_of(offs[d + 1], sizes[d + 1])
        red_copy(d).wait_recv()
        total = grad[rows, :].astype(F32) + stages[d][2][...].astype(F32)
        return rows, total.astype(BF)

    rows, total = reduce_stage(0)
    grad[rows, :] = total
    red_copy(1).start()
    zero = jnp.zeros((1, width), F32)
    gain_sum, shift_sum = norm_back(0, zero, zero)
    rows, total = reduce_stage(1)
    grad[rows, :] = total
    red_copy(2).start()
    for b in range(1, batches):
        gain_sum, shift_sum = norm_back(b, gain_sum, shift_sum)
    v0[...] = vecs[...]
    v0[0:1, :] = gain_sum
    v0[1:2, :] = shift_sum
    zsp = Spread(p, z_send, z_recv)
    for k in range(1, pat):
        zsp.copy_to(k, v0, vz.at[k - 1]).start()
    rows, total = reduce_stage(2)
    gsum[rows, :] = total
    back_copy(2, False).start()
    for k in range(1, pat):
        zsp.copy_to(k, v0, vz.at[k - 1]).wait_recv()
    row = lax.broadcasted_iota(jnp.int32, (8, width), 0)
    extra = vz[0]
    for k in range(2, pat):
        extra = extra + vz[k - 1]
    vs[0, 0:8, :] = v0[...] + jnp.where(row < 5, extra, 0.0)
    vs[0, 8:16, :] = jnp.zeros((8, width), F32)
    vs[0, 8:9, 0 : heads * 128] = qsum
    vs[0, 9:10, 0 : heads * 128] = vsum

    def vec_copy(k):
        to = lax.rem(p.s + k, n)
        return remote(vs.at[0], vs.at[k], v_send.at[k - 1], v_recv.at[k - 1], (p.z, to))

    for k in range(1, n):
        vec_copy(k).start()
    back_copy(2, True).wait_recv()
    back_copy(1, False).start()
    for k in range(1, n):
        vec_copy(k).wait_recv()
    allv = vs[0]
    for k in range(1, n):
        allv = allv + vs[k]
    vout[...] = allv
    back_copy(1, True).wait_recv()
    back_copy(0, False).start()
    for b in range(batches):
        for k in range(1, pat):
            frm = lax.rem(p.z + pat - k, pat)
            theirs = gif.at[b, rows_of(frm * quarter, quarter), :]
            ag[b].copy_to(k, theirs, theirs).wait_recv()
        ginp[b] = nn(permt[...], gif[b]).astype(BF)
    back_copy(0, True).wait_recv()
    gup[...] = gsum[0:width, :].astype(F32)
    gdown[...] = gsum[width : 2 * width, :].astype(F32)
    gq[...] = jnp.transpose(gsum[base : base + cols, :].astype(F32))
    gk[...] = jnp.transpose(gsum[base + cols : base + 2 * cols, :].astype(F32))
    gv[...] = jnp.transpose(gsum[base + 2 * cols : base + 3 * cols, :].astype(F32))
    goutf[...] = gsum[base + 3 * cols : base + 4 * cols, :].astype(F32)
    zrows = rows_of(p.z * quarter, quarter)
    for b in range(batches):
        for k in range(1, pat):
            rs[b].copy_to(k, dns.at[b, p.other_z(k)], dnr.at[b, k - 1]).wait_send()
            ag[b].copy_to(k, gif.at[b, zrows, :], gif.at[b, zrows, :]).wait_send()
    for d in range(3):
        red_copy(d).wait_send()
        back_copy(d, False).wait_send()
    for k in range(1, pat):
        zsp.copy_to(k, v0, vz.at[k - 1]).wait_send()
    for k in range(1, n):
        vec_copy(k).wait_send()


def call(kernel, name, outs, scratch, specs, number):
    return pl.pallas_call(
        kernel,
        name=name,
        out_shape=[jax.ShapeDtypeStruct(s, d) for s, d in outs],
        in_specs=[pl.BlockSpec(memory_space=m) for m in specs],
        out_specs=[pl.BlockSpec(memory_space=pltpu.VMEM)] * len(outs),
        scratch_shapes=scratch,
        compiler_params=pltpu.CompilerParams(
            collective_id=number, has_side_effects=True, vmem_limit_bytes=62 << 20
        ),
    )


def shards(
    n,
    pat,
    inputs,
    lengths,
    gain_one,
    shift_one,
    w_query,
    b_query,
    w_key,
    w_value,
    b_value,
    w_out,
    b_out,
    gain_two,
    shift_two,
    w_up,
    b_up,
    w_down,
    b_down,
    d_output,
):
    batches, shard, width = inputs.shape
    cols = w_query.shape[1]
    heads = cols // HD
    units = batches * heads
    chips = n // 2
    half = shard // 2
    quarter = shard // pat
    levels = 1
    while SPAN1 << (levels - 1) < n:
        levels += 1
    perm = jnp.asarray(perm_matrix(shard), BF)
    permt = jnp.asarray(perm_matrix(shard).T, BF)
    qext = jnp.asarray(query_ext(shard), BF)
    ktab = jnp.asarray(key_tables(shard, heads * pat, levels))
    row = lambda v: v.reshape(1, -1)
    by_head = lambda w: w.reshape(w.shape[0], heads, HD)
    pack = lambda a, b: jnp.concatenate([by_head(a), by_head(b)], 2).reshape(a.shape[0], 2 * cols)
    wq = pack(w_query, jnp.zeros_like(w_query))
    wkv = pack(w_key, w_value)
    bq = pack(row(b_query), jnp.zeros((1, cols), F32))
    bkv = pack(jnp.zeros((1, cols), F32), row(b_value))
    vm, sm, anyv = pltpu.VMEM, pltpu.SMEM, pl.ANY
    dma = pltpu.SemaphoreType.DMA
    tiles = units // 2

    xp, n1, qp, kvd, kvt, attf, wofp, attw, den, tab = call(
        functools.partial(forward_kernel, n, pat, levels),
        "attention_forward",
        [
            ((batches, shard, width), BF),
            ((batches, shard, width), BF),
            ((units, shard, 128), BF),
            ((units, SPAN1 * shard, 128), BF),
            ((units, n * half, 128), BF),
            ((pat, tiles, shard, 128), BF),
            ((pat, cols + 2 * HD, width), BF),
            ((tiles, shard, 128), F32),
            ((tiles, shard, 128), F32),
            ((heads, levels, shard, 128), BF),
        ],
        [
            pltpu.VMEM((units, shard, 128), F32),
            dma((heads,)),
            dma((pat - 1,)),
            dma((pat - 1,)),
            dma((tiles, pat - 1)),
            dma((tiles, pat - 1)),
        ]
        + dense_sems(batches)
        + thin_sems(batches, chips),
        [sm] + [vm] * 10 + [anyv],
        0,
    )(lengths, inputs, row(gain_one), row(shift_one), wq, bq, wkv, bkv, w_out, perm, qext, ktab)

    gud, fd, dsf, dst, sto, vecs = call(
        functools.partial(middle_kernel, n, pat),
        "feed_forward",
        [
            ((2 * width, width), BF),
            ((batches, shard, width), BF),
            ((batches, shard, width), BF),
            ((batches, quarter, width), F32),
            ((batches, quarter, width), F32),
            ((8, width), F32),
        ],
        [
            pltpu.VMEM((batches, shard, width), F32),
            pltpu.VMEM((batches, shard, width), BF),
            pltpu.VMEM((batches, shard, width), BF),
            pltpu.VMEM((batches, shard, width), BF),
            pltpu.VMEM((batches, shard, width), BF),
            pltpu.VMEM((batches, pat, quarter, width), BF),
            pltpu.VMEM((batches, quarter, width), F32),
            pltpu.VMEM((batches, pat - 1, quarter, width), BF),
        ]
        + [dma((batches, pat - 1))] * 4,
        [vm] * 11,
        1,
    )(
        xp,
        attf,
        wofp,
        row(b_out),
        row(gain_two),
        row(shift_two),
        w_up,
        row(b_up),
        w_down,
        d_output,
        perm,
    )

    dq, dkv, gout, outputs = call(
        functools.partial(backward_kernel, n, pat, levels),
        "attention_backward",
        [
            ((batches, shard, 2 * cols), BF),
            ((batches, shard, 2 * cols), BF),
            ((cols, width), BF),
            ((batches, shard, width), BF),
        ],
        [
            pltpu.VMEM((units, SPAN1 * shard, 128), BF),
            pltpu.VMEM((units, n * half, 128), BF),
            pltpu.VMEM((SPAN1, 8, shard), F32),
            pltpu.VMEM((n, 8, half), F32),
            pltpu.VMEM((units, shard, 128), BF),
            pltpu.VMEM((units, shard, 128), F32),
            pltpu.VMEM((units, shard, 128), F32),
            pltpu.VMEM((batches, pat - 1, quarter, width), BF),
            pltpu.VMEM((batches, shard, width), BF),
        ]
        + [dma((batches, pat - 1))] * 4
        + dense_sems(batches)
        + thin_sems(batches, chips)
        + [dma((3,))] * 2
        + [dma((chips,))] * 4,
        [sm] + [vm] * 14,
        2,
    )(lengths, dsf, wofp, attf, attw, den, qp, kvd, kvt, tab, qext, fd, sto, row(b_down), permt)

    rows = 2 * width + 4 * cols
    grad_inputs, vout, g_up, g_down, g_out, g_q, g_k, g_v = call(
        functools.partial(tail_kernel, n, pat),
        "gradient_sums",
        [
            ((batches, shard, width), BF),
            ((16, width), F32),
            ((width, width), F32),
            ((width, width), F32),
            ((cols, width), F32),
            ((width, cols), F32),
            ((width, cols), F32),
            ((width, cols), F32),
        ],
        [
            pltpu.VMEM((batches, pat, quarter, width), BF),
            pltpu.VMEM((batches, pat - 1, quarter, width), BF),
            pltpu.VMEM((batches, shard, width), BF),
            pltpu.VMEM((rows, width), BF),
            pltpu.VMEM((rows, width), BF),
            pltpu.VMEM((rows // 2, width), BF),
            pltpu.VMEM((rows // 4, width), BF),
            pltpu.VMEM((rows // 8, width), BF),
            pltpu.VMEM((8, width), F32),
            pltpu.VMEM((pat - 1, 8, width), F32),
            pltpu.VMEM((n, 16, width), F32),
        ]
        + [dma((batches, pat - 1))] * 4
        + [dma((6,))] * 2
        + [dma((pat - 1,))] * 2
        + [dma((n - 1,))] * 2,
        [vm] * 12,
        3,
    )(xp, n1, dq, dkv, wq, wkv, row(gain_one), dst, vecs, gud, gout, permt)
    q_row = vout[8, : 2 * cols].reshape(heads, 2, HD)
    v_row = vout[9, : 2 * cols].reshape(heads, 2, HD)
    return (
        outputs,
        grad_inputs,
        vout[0],
        vout[1],
        g_q,
        q_row[:, 0].reshape(cols),
        g_k,
        g_v,
        v_row[:, 1].reshape(cols),
        g_out,
        vout[2],
        vout[3],
        vout[4],
        g_up,
        vout[5],
        g_down,
        vout[6],
    )


class LineGather:
    def __init__(self, place, block, send, recv):
        self.p, self.block, self.send, self.recv = place, block, send, recv

    def copy(self, frm, up):
        p = self.p
        to = jnp.clip(p.z + (1 if up else -1), 0, p.pat - 1)
        return remote(
            self.block(frm, p.z),
            self.block(frm, to),
            self.send.at[0 if up else 1, frm],
            self.recv.at[frm],
            (to, p.s),
        )

    def got(self, frm):
        p = self.p
        here = self.block(frm, p.z)
        return remote(
            here, here, self.send.at[0, 0], self.recv.at[frm], (lax.rem(p.z + 1, p.pat), p.s)
        )

    def start(self):
        p = self.p
        when(p.z < p.pat - 1, lambda: self.copy(p.z, True).start())
        when(p.z > 0, lambda: self.copy(p.z, False).start())

    def inner(self, hop):
        for z in range(1, self.p.pat - 1):
            if z - hop >= 0:
                yield z, z - hop, True
            if z + hop < self.p.pat:
                yield z, z + hop, False

    def forward(self, hop):
        for z, frm, up in self.inner(hop):

            def hand(frm=frm, up=up):
                self.got(frm).wait_recv()
                self.copy(frm, up).start()

            when(self.p.z == z, hand)

    def arrive(self):
        for frm in range(self.p.pat):
            if frm > 0:
                when(self.p.z == 0, lambda frm=frm: self.got(frm).wait_recv())
            if frm < self.p.pat - 1:
                when(self.p.z == self.p.pat - 1, lambda frm=frm: self.got(frm).wait_recv())

    def finish(self):
        p = self.p
        when(p.z < p.pat - 1, lambda: self.copy(p.z, True).wait_send())
        when(p.z > 0, lambda: self.copy(p.z, False).wait_send())
        for hop in range(1, p.pat - 1):
            for z, frm, up in self.inner(hop):
                when(p.z == z, lambda frm=frm, up=up: self.copy(frm, up).wait_send())


class LineSum:
    def __init__(self, place, part, buf, send, recv):
        self.p, self.part, self.buf, self.send, self.recv = place, part, buf, send, recv

    def copy(self, z, t):
        to = z + 1 if t > z else z - 1
        at = t if (t > z or t < to) else self.p.pat
        return remote(
            self.part(t), self.buf.at[at], self.send.at[t], self.recv.at[at], (to, self.p.s)
        )

    def got(self, at):
        here = self.buf.at[at]
        to = lax.rem(self.p.z + 1, self.p.pat)
        return remote(here, here, self.send.at[0], self.recv.at[at], (to, self.p.s))

    def start(self):
        last = self.p.pat - 1

        def up():
            for t in range(last, 0, -1):
                self.copy(0, t).start()

        def down():
            for t in range(last):
                self.copy(last, t).start()

        when(self.p.z == 0, up)
        when(self.p.z == last, down)

    def inner(self, hop):
        last = self.p.pat - 1
        for z in range(1, last):
            if z == hop:
                for t in range(last, z, -1):
                    yield z, t
            if last - z == hop:
                for t in range(z):
                    yield z, t

    def forward(self, hop):
        for z, t in self.inner(hop):

            def add(z=z, t=t):
                self.got(t).wait_recv()
                part = self.part(t)
                part[...] = (part[...].astype(F32) + self.buf[t].astype(F32)).astype(BF)
                self.copy(z, t).start()

            when(self.p.z == z, add)

    def total(self, out):
        p = self.p
        out[...] = self.part(p.z)[...].astype(F32)

        def below():
            self.got(p.z).wait_recv()
            out[...] += self.buf[p.z].astype(F32)

        def above():
            self.got(p.pat).wait_recv()
            out[...] += self.buf[p.pat].astype(F32)

        when(p.z > 0, below)
        when(p.z < p.pat - 1, above)

    def finish(self):
        last = self.p.pat - 1
        for t in range(last, 0, -1):
            when(self.p.z == 0, lambda t=t: self.copy(0, t).wait_send())
        for t in range(last):
            when(self.p.z == last, lambda t=t: self.copy(last, t).wait_send())
        for hop in range(1, last):
            for z, t in self.inner(hop):
                when(self.p.z == z, lambda z=z, t=t: self.copy(z, t).wait_send())


class PlaneGather:
    def __init__(self, place, piece, sems):
        self.p, self.piece, self.sems = place, piece, sems
        self.chips = place.n // 2

    def direct(self, k, owner):
        p, sems = self.p, self.sems
        to = lax.rem(p.s + 2 * k, p.n)
        return remote(
            self.piece(owner), self.piece(owner), sems[0].at[k - 1], sems[1].at[k - 1], (p.z, to)
        )

    def hand(self, k, owner):
        p, sems = self.p, self.sems
        return remote(
            self.piece(owner), self.piece(owner), sems[2].at[k], sems[3].at[k], (p.z, p.sib)
        )

    def source(self, base, k):
        return lax.rem(base + self.p.n - 2 * k, self.p.n)

    def start(self):
        for k in range(1, self.chips):
            self.direct(k, self.p.s).start()
        self.hand(0, self.p.s).start()

    def pass_on(self):
        for k in range(1, self.chips):
            owner = self.source(self.p.s, k)
            self.direct(k, owner).wait_recv()
            self.hand(k, owner).start()

    def arrive(self):
        for k in range(self.chips):
            self.hand(k, self.source(self.p.sib, k)).wait_recv()

    def finish(self):
        for k in range(1, self.chips):
            self.direct(k, self.p.s).wait_send()
        for k in range(self.chips):
            self.hand(k, self.source(self.p.s, k)).wait_send()


def line_sems(pat):
    return [pltpu.SemaphoreType.DMA((2, pat)), pltpu.SemaphoreType.DMA((pat,))]


def sum_sems(pat):
    return [pltpu.SemaphoreType.DMA((pat,)), pltpu.SemaphoreType.DMA((pat + 1,))]


def plane_sems(chips):
    return [pltpu.SemaphoreType.DMA((chips - 1,))] * 2 + [pltpu.SemaphoreType.DMA((chips,))] * 2


def vec_row(ref):
    return ref[...].reshape(1, -1)


def norm_rows(values, gain, shift):
    mean = jnp.mean(values, -1, keepdims=True)
    cen = values - mean
    var = jnp.mean(cen * cen, -1, keepdims=True)
    return cen * lax.rsqrt(var + EPS) * gain + shift


def norm_back(values, grad, gain):
    mean = jnp.mean(values, -1, keepdims=True)
    cen = values - mean
    inv = lax.rsqrt(jnp.mean(cen * cen, -1, keepdims=True) + EPS)
    hat = cen * inv
    dhat = grad * gain
    back = inv * (
        dhat - jnp.mean(dhat, -1, keepdims=True) - hat * jnp.mean(dhat * hat, -1, keepdims=True)
    )
    return (
        back,
        jnp.sum(grad * hat, 0, keepdims=True),
        jnp.sum(grad, 0, keepdims=True),
    )


def live_bias(first, second, base, length, shard):
    ok = jnp.logical_or(
        jnp.logical_and(second < first, second + base < length), second == first
    )
    return jnp.where(ok, 0.0, NEG)


def first_half(
    n,
    pat,
    levels,
    lens,
    x_ref,
    gain1,
    shift1,
    wp,
    bp,
    wout,
    bout,
    gain2,
    shift2,
    bup,
    perm,
    qext,
    ktab,
    wup_hbm,
    wdown_hbm,
    dout_hbm,
    xp,
    n1,
    qp,
    kvd,
    kvt,
    tab,
    atto,
    attw,
    den,
    wop,
    dsl,
    dst,
    sto,
    fd,
    gud,
    vecs,
    wup,
    wdown,
    dout,
    acc,
    attf,
    wor,
    dact,
    state,
    n2,
    act,
    dop,
    dh,
    dns,
    dnr,
    tot,
    *sems,
):
    batches, shard, width = x_ref.shape
    half = shard // 2
    quarter = shard // pat
    cols = wout.shape[0]
    heads = cols // HD
    units = batches * heads
    tiles = units // 2
    sems = list(sems)
    take = lambda count: [sems.pop(0) for _ in range(count)]
    load_sem, tab_sem = take(2)
    ds0, ds1, ts0, ts1, ts2, ts3 = take(6)
    p = Place(n, pat)
    chips = n // 2
    bar, greeted = p.greet(True, True)
    low, high = lane_masks()

    loads = [
        pltpu.make_async_copy(src, dst, load_sem.at[i])
        for i, (src, dst) in enumerate(((wup_hbm, wup), (wdown_hbm, wdown), (dout_hbm, dout)))
    ]
    tabs = [
        pltpu.make_async_copy(ktab.at[heads * p.z + i], tab.at[i], tab_sem.at[i])
        for i in range(heads)
    ]
    for copy in loads + tabs:
        copy.start()

    slot = lambda frm, at: lax.rem(frm - at + 2 * pat - 1, pat)
    out_rows = cols // chips
    out_cols = width // 2

    def out_piece(dev, slots):
        chip, core = lax.div(dev, 2), lax.rem(dev, 2)
        return wor.at[
            slots,
            rows_of(HD + chip * out_rows, out_rows),
            pl.ds(pl.multiple_of(core * out_cols, 128), out_cols),
        ]

    rel = pl.ds(0, pat - 1)
    out_line = LineGather(p, lambda f, t: out_piece(p.s, slot(f, t)), *take(2))
    out_plane = PlaneGather(p, lambda dev: out_piece(dev, rel), take(4))
    att_line = [
        LineGather(p, lambda f, at, t=t: attf.at[f, t], *take(2)) for t in range(tiles)
    ]
    dn_sum = [
        LineSum(p, lambda t, b=b: dns.at[b, t], dnr.at[b], *take(2)) for b in range(batches)
    ]
    ds_line = [
        LineGather(p, lambda f, at, b=b: dsl.at[b, rows_of(f * quarter, quarter), :], *take(2))
        for b in range(batches)
    ]
    own_slot = pat - 1
    for r in range(pat):
        wor[r, 0:HD, :] = jnp.zeros((HD, width), BF)
        wor[r, HD + cols : 2 * HD + cols, :] = jnp.zeros((HD, width), BF)
    wor[own_slot, HD : HD + cols, :] = wout[...]
    wop[...] = wor[own_slot]

    shares = [
        Shares(
            p,
            shard,
            True,
            lambda at, b=b: kvd.at[pl.ds(heads * b, heads), rows_of(at * shard, shard), :],
            lambda dev, b=b: kvt.at[pl.ds(heads * b, heads), rows_of(dev * half, half), :],
            [ds0.at[b], ds1.at[b]],
            [ts0.at[b], ts1.at[b], ts2.at[b], ts3.at[b]],
        )
        for b in range(batches)
    ]
    parity = [lax.rem(heads * p.z + i, 2) for i in range(heads)]
    lane = lax.broadcasted_iota(jnp.int32, (shard, 128), 1)
    for b in range(batches):
        xb = nn(perm[...], x_ref[b])
        xp[b] = xb.astype(BF)
        n1[b] = norm_rows(xb, vec_row(gain1), vec_row(shift1)).astype(BF)
        qkv = nn(n1[b], wp[...]) + bp[...]
        for i in range(heads):
            kv = qkv[:, i * 128 : (i + 1) * 128].astype(BF)
            kvd[heads * b + i, rows_of(p.pos * shard, shard), :] = kv
            t = heads + i // 2
            q = qkv[:, t * 128 : (t + 1) * 128]
            if i % 2 == 1:
                q = pltpu.roll(q, HD, 1)
            q = jnp.where(lane < HD, q, 0.0).astype(BF) * jnp.asarray(HD**-0.5, BF)
            qp[heads * b + i] = q
        for i in range(heads):
            kvt[heads * b + i, rows_of(p.s * half, half), :] = kvd[
                heads * b + i, rows_of(p.pos * shard + parity[i] * half, half), :
            ]
        if b == 0:
            pl.semaphore_wait(bar, greeted)
        shares[b].start()
        if b == 0:
            out_line.start()
    for copy in tabs:
        copy.wait()

    def attend(qx, kv, ext, bias):
        s = nt(qx, jnp.concatenate([kv, ext], 1))
        if bias is not None:
            s = s + bias
        return nn(jnp.exp(s).astype(BF), kv * high + low)

    own = rows_of(p.pos * shard, shard)
    qt = token_of(lax.broadcasted_iota(jnp.int32, (shard, shard), 0), shard)
    kt = token_of(lax.broadcasted_iota(jnp.int32, (shard, shard), 1), shard)
    for b in range(batches):
        bias = live_bias(qt, kt, p.s * shard, lens[b], shard)
        for i in range(heads):
            u = heads * b + i
            qx = jnp.concatenate([qp[u], qext[...]], 1)
            acc[u] = attend(qx, kvd[u, own, :], tab[i, 0], bias)

    def attend_rest(b, which):
        def dense(j, carry):
            lenl = length_lane(dense_positions(p.seg * SPAN1 + j, shard), lens[b], shard)
            for i in which:
                u = heads * b + i
                qx = jnp.concatenate([qp[u], qext[...]], 1)
                kv = kvd[u, rows_of(j * shard, shard), :]
                acc[u] += attend(qx, kv, tab[i, 0] + lenl, None)
            return carry

        lax.fori_loop(0, p.pos, dense, 0)

        def thin(sg, carry):
            level = level_of(sg, p.seg, levels)
            for i in which:
                u = heads * b + i
                mine = rows_of(parity[i] * half, half)
                places = thin_positions(sg * SPAN1, parity[i], shard, SPAN1)
                lenl = length_lane(places, lens[b], SPAN1 * half)
                ext = jnp.concatenate([tab[i, level, mine, :]] * SPAN1, 0) + lenl
                qx = jnp.concatenate([qp[u, mine, :], qext[mine, :]], 1)
                kv = kvt[u, rows_of(sg * SPAN1 * half, SPAN1 * half), :]
                acc[u, mine, :] += attend(qx, kv, ext, None)
            return carry

        lax.fori_loop(0, p.seg, thin, 0)

    def send_tile(t):
        even, odd = acc[2 * t], acc[2 * t + 1]
        num = jnp.where(lane < HD, pltpu.roll(even, HD, 1), odd)
        dn = jnp.where(lane < HD, even, pltpu.roll(odd, HD, 1))
        wide = num / dn
        den[t] = dn
        attw[t] = wide
        attf[p.z, t] = wide.astype(BF)
        atto[t] = wide.astype(BF)
        att_line[t].start()

    for b in range(batches):
        shares[b].pass_on()
        shares[b].arrive()
        if b == 0:
            attend_rest(b, range(heads))
            send_tile(0)
            for hop in range(1, pat - 1):
                out_line.forward(hop)
            out_line.arrive()
            out_plane.start()
        else:
            attend_rest(b, range(0, 1))
            send_tile(1)
            att_line[0].forward(1)
            attend_rest(b, range(1, heads))
            send_tile(2)
    att_line[0].forward(2)
    att_line[1].forward(1)
    out_plane.pass_on()

    bdown_sum = jnp.zeros((1, width), F32)
    for copy in loads:
        copy.wait()
    for b in range(batches):
        dob = nn(perm[...], dout[b])
        dop[b] = dob.astype(BF)
        bdown_sum = bdown_sum + jnp.sum(dob, 0, keepdims=True)
        dact[b] = nt(dop[b], wdown[...])
        if b == 0:
            att_line[1].forward(2)
            att_line[2].forward(1)
    att_line[2].forward(2)
    out_plane.arrive()
    bup_sum = jnp.zeros((1, width), F32)
    for b in range(batches):
        if b == 0:
            att_line[0].arrive()
            att_line[1].arrive()
        else:
            att_line[2].arrive()
        mixed = xp[b].astype(F32) + vec_row(bout)
        for r in range(pat):
            z = lax.rem(p.z + 1 + r, pat)
            pair = jnp.concatenate([attf[z, b], attf[z, b + 1]], 1)
            weight = wor[r, HD : HD + 256, :] if b == 0 else wor[r, 0:256, :]
            mixed = mixed + nn(pair, weight)
        state[b] = mixed
        sto[b] = state[b, rows_of(p.z * quarter, quarter), :]
        norm = norm_rows(mixed, vec_row(gain2), vec_row(shift2)).astype(BF)
        n2[b] = norm
        hid = nn(norm, wup[...]) + vec_row(bup)
        th = jnp.tanh(ROOT * (hid + 0.044715 * (hid * hid * hid)))
        act[b] = (0.5 * hid * (1.0 + th)).astype(BF)
        slope = 0.5 * (1.0 + th) + 0.5 * hid * (1.0 - th * th) * (
            ROOT * (1.0 + 3.0 * 0.044715 * hid * hid)
        )
        dhid = (dact[b] * slope).astype(BF)
        dh[b] = dhid
        dn = nt(dhid, wup[...])
        for t in range(pat):
            dns[b, t] = dn[t * quarter : (t + 1) * quarter].astype(BF)
        dn_sum[b].start()
        bup_sum = bup_sum + jnp.sum(dhid.astype(F32), 0, keepdims=True)
    dn_sum[0].forward(1)
    fd[0] = nn(act[0], wdown[...]).astype(BF)
    dn_sum[0].forward(2)
    fd[1] = nn(act[1], wdown[...]).astype(BF)
    dn_sum[1].forward(1)
    bout_sum = jnp.zeros((1, width), F32)
    gain_sum = jnp.zeros((1, width), F32)
    shift_sum = jnp.zeros((1, width), F32)
    mine = rows_of(p.z * quarter, quarter)
    for b in range(batches):
        dn_sum[b].total(tot)
        back, more_gain, more_shift = norm_back(sto[b], tot[...], vec_row(gain2))
        gain_sum = gain_sum + more_gain
        shift_sum = shift_sum + more_shift
        ds = dop[b, mine, :].astype(F32) + back
        dst[b] = ds
        dsl[b, mine, :] = ds.astype(BF)
        ds_line[b].start()
        bout_sum = bout_sum + jnp.sum(ds, 0, keepdims=True)
        if b == 0:
            dn_sum[1].forward(2)
    up = tn(n2[0], dh[0])
    for b in range(1, batches):
        up = up + tn(n2[b], dh[b])
    gud[0:width, :] = up.astype(BF)
    ds_line[0].forward(1)
    ds_line[1].forward(1)
    down = tn(act[0], dop[0])
    for b in range(1, batches):
        down = down + tn(act[b], dop[b])
    gud[width : 2 * width, :] = down.astype(BF)
    ds_line[0].forward(2)
    ds_line[1].forward(2)
    vecs[...] = jnp.zeros(vecs.shape, F32)
    vecs[2:3, :] = bout_sum
    vecs[3:4, :] = gain_sum
    vecs[4:5, :] = shift_sum
    vecs[5:6, :] = bup_sum
    vecs[6:7, :] = bdown_sum
    for b in range(batches):
        ds_line[b].arrive()
    for item in [*shares, out_line, out_plane, *att_line, *dn_sum, *ds_line]:
        item.finish()


class TreeSum:
    def __init__(self, place, grad, out, bufs, send, recv):
        self.p, self.grad, self.out, self.send, self.recv = place, grad, out, send, recv
        p = place
        bit_x = lax.rem(lax.div(p.s, 2), 2)
        bit_y = lax.div(p.s, 4)
        to_x = p.s + 2 - 4 * bit_x
        to_y = p.s + 4 - 8 * bit_y
        first = p.core == 0
        self.bits = [p.core, jnp.where(first, bit_x, bit_y), jnp.where(first, bit_y, bit_x)]
        self.to = [p.sib, jnp.where(first, to_x, to_y), jnp.where(first, to_y, to_x)]
        self.bufs = bufs
        self.off, self.size = [jnp.int32(0)], [grad.shape[0]]
        for d in range(3):
            h = self.size[d] // 2
            self.off.append(self.off[d] + self.bits[d] * h)
            self.size.append(h)

    def half_of(self, d, bit):
        h = self.size[d] // 2
        return rows_of(self.off[d] + bit * h, h)

    def red(self, d):
        src = self.grad.at[self.half_of(d, 1 - self.bits[d]), :]
        return remote(
            src, self.bufs[d], self.send.at[d], self.recv.at[d], (self.p.z, self.to[d])
        )

    def back(self, d, got):
        rows = self.half_of(d, (1 - self.bits[d]) if got else self.bits[d])
        return remote(
            self.out.at[rows, :],
            self.out.at[rows, :],
            self.send.at[3 + d],
            self.recv.at[3 + d],
            (self.p.z, self.to[d]),
        )

    def step(self, d):
        if d == 0:
            self.red(0).start()
        elif d <= 3:
            self.red(d - 1).wait_recv()
            rows = rows_of(self.off[d], self.size[d])
            total = self.grad[rows, :].astype(F32) + self.bufs[d - 1][...].astype(F32)
            if d < 3:
                self.grad[rows, :] = total.astype(BF)
                self.red(d).start()
            else:
                self.out[rows, :] = total.astype(BF)
                self.back(2, False).start()
        else:
            self.back(6 - d, True).wait_recv()
            if d < 6:
                self.back(5 - d, False).start()

    def finish(self):
        for d in range(3):
            self.red(d).wait_send()
            self.back(d, False).wait_send()


def second_half(
    n,
    pat,
    levels,
    lens,
    dsl,
    dst,
    wop,
    atto,
    attw,
    den,
    qp,
    kvd,
    kvt,
    tab,
    qext,
    fd,
    sto,
    bdown,
    gud,
    vecs,
    n1,
    xp,
    wp,
    gain1,
    outf,
    gif,
    gsum1,
    gsum2,
    vout,
    qud,
    qut,
    crd,
    crt,
    uext,
    acq,
    ack,
    fdo,
    fdr,
    dqk,
    dns,
    dnr,
    tot,
    grad1,
    grad2,
    a1,
    a2,
    a3,
    b1,
    b2,
    b3,
    vz,
    vs,
    *sems,
):
    batches, shard, width = dsl.shape
    half = shard // 2
    quarter = shard // pat
    units = qp.shape[0]
    heads = units // batches
    cols = heads * HD
    tiles = units // 2
    sems = list(sems)
    take = lambda count: [sems.pop(0) for _ in range(count)]
    ds0, ds1, ts0, ts1, ts2, ts3 = take(6)
    cd0, cd1, ct0, ct1, ct2, ct3 = take(6)
    p = Place(n, pat)
    bar, greeted = p.greet(True, False, True)
    low, high = lane_masks()
    parity = [lax.rem(heads * p.z + i, 2) for i in range(heads)]
    own = rows_of(p.pos * shard, shard)
    lane = lax.broadcasted_iota(jnp.int32, (shard, 128), 1)
    row8 = lax.broadcasted_iota(jnp.int32, (8, 128), 0)
    lane8 = lax.broadcasted_iota(jnp.int32, (8, 128), 1)
    pick = jnp.where(row8 == lax.div(lane8, HD), 1.0, 0.0).astype(F32)
    ri = lax.broadcasted_iota(jnp.int32, (128, 128), 0)
    ci = lax.broadcasted_iota(jnp.int32, (128, 128), 1)
    same = jnp.where(lax.div(ri, HD) == lax.div(ci, HD), 1.0, 0.0).astype(F32)
    zrows = rows_of(p.z * quarter, quarter)
    fd_sum = [
        LineSum(
            p, lambda t, b=b: fdo.at[b, rows_of(t * quarter, quarter), :], fdr.at[b], *take(2)
        )
        for b in range(batches)
    ]
    out_line = [
        LineGather(p, lambda f, t, b=b: outf.at[b, rows_of(f * quarter, quarter), :], *take(2))
        for b in range(batches)
    ]
    dn_sum = [
        LineSum(p, lambda t, b=b: dns.at[b, t], dnr.at[b], *take(2)) for b in range(batches)
    ]
    gi_line = [
        LineGather(p, lambda f, t, b=b: gif.at[b, rows_of(f * quarter, quarter), :], *take(2))
        for b in range(batches)
    ]
    sum1 = TreeSum(p, grad1, gsum1, (a1, a2, a3), *take(2))
    sum2 = TreeSum(p, grad2, gsum2, (b1, b2, b3), *take(2))
    z_send, z_recv, v_send, v_recv = take(4)
    cors = Shares(
        p, shard, False, lambda at: crd.at[at], lambda dev: crt.at[dev], [cd0, cd1], [ct0, ct1, ct2, ct3]
    )
    shares = [
        Shares(
            p,
            shard,
            False,
            lambda at, b=b: qud.at[pl.ds(heads * b, heads), rows_of(at * shard, shard), :],
            lambda dev, b=b: qut.at[pl.ds(heads * b, heads), rows_of(dev * half, half), :],
            [ds0.at[b], ds1.at[b]],
            [ts0.at[b], ts1.at[b], ts2.at[b], ts3.at[b]],
        )
        for b in range(batches)
    ]

    wide = [nt(dsl[b], wop[HD : HD + 256, :] if b == 0 else wop[0:256, :]) for b in range(batches)]
    parts = [wide[0][:, 0:128], wide[0][:, 128:256] + wide[1][:, 0:128], wide[1][:, 128:256]]
    crd[p.pos] = jnp.zeros(crd.shape[1:], F32)
    crt[p.s] = jnp.zeros(crt.shape[1:], F32)
    for t in range(tiles):
        dn = den[t]
        up = parts[t] / dn
        prod = parts[t] * attw[t] / dn
        cor = exact_nn(prod, same)
        cor_rows = exact_nt(pick, prod)
        for e in range(2):
            u = 2 * t + e
            i = u % heads
            part = up if e == 1 else pltpu.roll(up, HD, 1)
            mixed = jnp.where(lane < HD, qp[u].astype(F32), part).astype(BF)
            qud[u, own, :] = mixed
            qut[u, rows_of(p.s * half, half), :] = qud[
                u, rows_of(p.pos * shard + parity[i] * half, half), :
            ]
            cor_row = cor_rows[e : e + 1, :]
            crd[p.pos, u : u + 1, :] = cor_row
            col = -cor[:, e * HD : e * HD + 1]
            first = col.astype(BF).astype(F32)
            uext[u] = (
                jnp.where(lane == COR_LANE, first, 0.0)
                + jnp.where(lane == COR_LANE + 1, col - first, 0.0)
            ).astype(BF)
            crt[p.s, u : u + 1, :] = jnp.where(
                parity[i] == 0, cor_row[:, 0:half], cor_row[:, half:shard]
            )
        if t == tiles - 2:
            pl.semaphore_wait(bar, greeted)
            shares[0].start()
    cors.start()
    shares[1].start()
    for b in range(batches):
        fdo[b] = fd[b]
        fd_sum[b].start()
    grad1[...] = gud[...]
    sum1.step(0)

    def query_side(qu, qe, ue, kv, ext, bias):
        kvx = jnp.concatenate([kv, ext], 1)
        s = nt(jnp.concatenate([qu * low, qe], 1), kvx)
        if bias is not None:
            s = s + bias
        dp = nt(jnp.concatenate([qu * high, ue], 1), kvx)
        return nn((jnp.exp(s) * dp).astype(BF), kv)

    def key_side(qu, qe, cor, kv, ext, bias):
        s = nt(jnp.concatenate([kv, ext], 1), jnp.concatenate([qu * low, qe], 1))
        if bias is not None:
            s = s + bias
        w = jnp.exp(s)
        dp = nt(kv, qu * high) - cor
        return nn((w * dp).astype(BF), qu * low) + nn(w.astype(BF), qu * high)

    ti = token_of(lax.broadcasted_iota(jnp.int32, (shard, shard), 0), shard)
    tj = token_of(lax.broadcasted_iota(jnp.int32, (shard, shard), 1), shard)
    for b in range(batches):
        bias = live_bias(ti, tj, p.s * shard, lens[b], shard)
        biast = live_bias(tj, ti, p.s * shard, lens[b], shard)
        for i in range(heads):
            u = heads * b + i
            kv = kvd[u, own, :]
            qu = qud[u, own, :]
            acq[u] = query_side(qu, qext[...], uext[u], kv, tab[i, 0], bias)
            ack[u] = key_side(qu, qext[...], crd[p.pos, u : u + 1, :], kv, tab[i, 0], biast)
    sum1.step(1)

    def query_rest(b):
        def dense(j, carry):
            lenl = length_lane(dense_positions(p.seg * SPAN1 + j, shard), lens[b], shard)
            for i in range(heads):
                u = heads * b + i
                kv = kvd[u, rows_of(j * shard, shard), :]
                acq[u] += query_side(
                    qud[u, own, :], qext[...], uext[u], kv, tab[i, 0] + lenl, None
                )
            return carry

        lax.fori_loop(0, p.pos, dense, 0)

        def thin(sg, carry):
            level = level_of(sg, p.seg, levels)
            for i in range(heads):
                u = heads * b + i
                mine = rows_of(parity[i] * half, half)
                places = thin_positions(sg * SPAN1, parity[i], shard, SPAN1)
                lenl = length_lane(places, lens[b], SPAN1 * half)
                ext = jnp.concatenate([tab[i, level, mine, :]] * SPAN1, 0) + lenl
                kv = kvt[u, rows_of(sg * SPAN1 * half, SPAN1 * half), :]
                qu = qut[u, rows_of(p.s * half, half), :]
                acq[u, mine, :] += query_side(qu, qext[mine, :], uext[u, mine, :], kv, ext, None)
            return carry

        lax.fori_loop(0, p.seg, thin, 0)

    def key_rest(b):
        lenl = length_lane(dense_positions(p.s, shard), lens[b], shard)

        def dense(j, carry):
            for i in range(heads):
                u = heads * b + i
                qu = qud[u, rows_of(j * shard, shard), :]
                ack[u] += key_side(
                    qu, qext[...], crd[j, u : u + 1, :], kvd[u, own, :], tab[i, 0] + lenl, None
                )
            return carry

        lax.fori_loop(p.pos + 1, SPAN1, dense, 0)

        def thin(dev, carry):
            level = level_of(lax.div(dev, SPAN1), p.seg, levels)
            for i in range(heads):
                u = heads * b + i
                mine = rows_of(parity[i] * half, half)
                ext = tab[i, level, mine, :] + length_lane(
                    thin_positions(p.s, parity[i], shard, 1), lens[b], half
                )
                kv = kvt[u, rows_of(p.s * half, half), :]
                qu = qut[u, rows_of(dev * half, half), :]
                ack[u, mine, :] += key_side(qu, qext[mine, :], crt[dev, u : u + 1, :], kv, ext, None)
            return carry

        lax.fori_loop(SPAN1 * (p.seg + 1), n, thin, 0)

    def send_grads(b):
        for i in range(heads):
            dqk[b, :, i * 128 : (i + 1) * 128] = ack[heads * b + i].astype(BF)
        for t in range((heads + 1) // 2):
            tile = acq[heads * b + 2 * t]
            if 2 * t + 1 < heads:
                other = pltpu.roll(acq[heads * b + 2 * t + 1], HD, 1)
            else:
                other = jnp.zeros((shard, 128), F32)
            tile = jnp.where(lane < HD, tile, other) * HD**-0.5
            at = (heads + t) * 128
            dqk[b, :, at : at + 128] = tile.astype(BF)
        dn = nt(dqk[b], wp[...])
        for t in range(pat):
            dns[b, t] = dn[t * quarter : (t + 1) * quarter].astype(BF)
        dn_sum[b].start()

    fd_sum[0].forward(1)
    fd_sum[1].forward(1)
    query_rest(0)
    fd_sum[0].forward(2)
    fd_sum[1].forward(2)
    cors.pass_on()
    shares[0].pass_on()
    query_rest(1)
    shares[1].pass_on()
    for b in range(batches):
        fd_sum[b].total(tot)
        outf[b, zrows, :] = (sto[b] + tot[...] + vec_row(bdown)).astype(BF)
        out_line[b].start()
    cors.arrive()
    shares[0].arrive()
    key_rest(0)
    send_grads(0)
    sum1.step(2)
    for b in range(batches):
        out_line[b].forward(1)
    shares[1].arrive()
    key_rest(1)
    send_grads(1)
    dn_sum[0].forward(1)
    dn_sum[0].forward(2)

    left = tn(jnp.concatenate([atto[0], atto[1]], 1), dsl[0])
    right = tn(jnp.concatenate([atto[1], atto[2]], 1), dsl[1])
    grad2[3 * cols : 4 * cols, :] = (left[0:cols] + right[HD : HD + cols]).astype(BF)
    dn_sum[1].forward(1)
    for b in range(batches):
        out_line[b].forward(2)
    gain_sum = jnp.zeros((1, width), F32)
    shift_sum = jnp.zeros((1, width), F32)

    def close(b, gain_sum, shift_sum):
        dn_sum[b].total(tot)
        back, more_gain, more_shift = norm_back(
            xp[b, zrows, :].astype(F32), tot[...], vec_row(gain1)
        )
        gif[b, zrows, :] = (dst[b] + back).astype(BF)
        gi_line[b].start()
        return gain_sum + more_gain, shift_sum + more_shift

    gain_sum, shift_sum = close(0, gain_sum, shift_sum)
    packed = tn(dqk[0], n1[0])
    for b in range(1, batches):
        packed = packed + tn(dqk[b], n1[b])
    grad2[0 : 3 * cols, :] = packed[0 : 3 * cols].astype(BF)
    sum2.step(0)
    sum1.step(3)
    dn_sum[1].forward(2)
    gi_line[0].forward(1)
    gain_sum, shift_sum = close(1, gain_sum, shift_sum)
    v0 = vs.at[0]
    v0[...] = vecs[...]
    v0[0:1, :] = gain_sum
    v0[1:2, :] = shift_sum
    zsp = Spread(p, z_send, z_recv)
    for k in range(1, pat):
        zsp.copy_to(k, v0, vz.at[k - 1]).start()
    qkv_sum = jnp.zeros((1, wp.shape[1]), F32)
    for b in range(batches):
        qkv_sum = qkv_sum + jnp.sum(dqk[b].astype(F32), 0, keepdims=True)
    sum2.step(1)
    sum1.step(4)
    gi_line[0].forward(2)
    gi_line[1].forward(1)
    sum2.step(2)
    sum1.step(5)
    for k in range(1, pat):
        zsp.copy_to(k, v0, vz.at[k - 1]).wait_recv()
    row = lax.broadcasted_iota(jnp.int32, (8, width), 0)
    extra = vz[0]
    for k in range(2, pat):
        extra = extra + vz[k - 1]
    v1 = vs.at[1]
    v1[...] = v0[...] + jnp.where(row < 5, extra, 0.0)
    v1[7:8, 0 : wp.shape[1]] = qkv_sum

    def vec_copy(k):
        to = lax.rem(p.s + k, n)
        return remote(v1, vs.at[k + 1], v_send.at[k - 1], v_recv.at[k - 1], (p.z, to))

    for k in range(1, n):
        vec_copy(k).start()
    gi_line[1].forward(2)
    sum2.step(3)
    sum1.step(6)
    sum2.step(4)
    sum2.step(5)
    for k in range(1, n):
        vec_copy(k).wait_recv()
    allv = v1[...]
    for k in range(1, n):
        allv = allv + vs[k + 1]
    vout[...] = allv
    sum2.step(6)
    for b in range(batches):
        out_line[b].arrive()
        gi_line[b].arrive()
    for item in [*shares, cors, *fd_sum, *out_line, *dn_sum, *gi_line, sum1, sum2]:
        item.finish()
    for k in range(1, pat):
        zsp.copy_to(k, v0, vz.at[k - 1]).wait_send()
    for k in range(1, n):
        vec_copy(k).wait_send()


def finish_kernel(
    heads,
    outf,
    gif,
    gsum1,
    gsum2,
    vin,
    permt,
    outp,
    ginp,
    gup,
    gdown,
    gout,
    gq,
    gk,
    gv,
    gain1,
    shift1,
    bq,
    bv,
    bout,
    gain2,
    shift2,
    bup,
    bdown,
):
    batches, _, width = outf.shape
    cols = heads * HD
    for b in range(batches):
        outp[b] = nn(permt[...], outf[b]).astype(BF)
        ginp[b] = nn(permt[...], gif[b]).astype(BF)
    gup[...] = gsum1[0:width, :].astype(F32)
    gdown[...] = gsum1[width : 2 * width, :].astype(F32)
    gout[...] = gsum2[3 * cols : 4 * cols, :].astype(F32)
    k_rows = [gsum2[i * 128 : i * 128 + HD, :] for i in range(heads)]
    v_rows = [gsum2[i * 128 + HD : (i + 1) * 128, :] for i in range(heads)]
    gq[...] = jnp.transpose(gsum2[2 * cols : 3 * cols, :].astype(F32))
    gk[...] = jnp.transpose(jnp.concatenate(k_rows, 0).astype(F32))
    gv[...] = jnp.transpose(jnp.concatenate(v_rows, 0).astype(F32))
    for r, ref in enumerate((gain1, shift1, bout, gain2, shift2, bup, bdown)):
        ref[...] = vin[r : r + 1, :].reshape(width)
    bq[...] = vin[7:8, 2 * cols : 3 * cols].reshape(cols)
    bv[...] = jnp.concatenate(
        [vin[7:8, i * 128 + HD : (i + 1) * 128] for i in range(heads)], 1
    ).reshape(cols)


def plane_program(
    n,
    pat,
    inputs,
    lengths,
    gain_one,
    shift_one,
    w_query,
    b_query,
    w_key,
    w_value,
    b_value,
    w_out,
    b_out,
    gain_two,
    shift_two,
    w_up,
    b_up,
    w_down,
    b_down,
    d_output,
):
    batches, shard, width = inputs.shape
    cols = w_query.shape[1]
    heads = cols // HD
    units = batches * heads
    tiles = units // 2
    chips = n // 2
    half = shard // 2
    quarter = shard // pat
    levels = 1
    while SPAN1 << (levels - 1) < n:
        levels += 1
    perm = jnp.asarray(perm_matrix(shard), BF)
    permt = jnp.asarray(perm_matrix(shard).T, BF)
    qext = jnp.asarray(query_ext(shard), BF)
    ktab = jnp.asarray(key_tables(shard, heads * pat, levels))
    head = lambda w, i: w[..., i * HD : (i + 1) * HD]

    def pack(q, k, v):
        parts = []
        for i in range(heads):
            parts += [head(k, i), head(v, i)]
        parts += [q, jnp.zeros(q.shape[:-1] + (HD,), q.dtype)]
        return jnp.concatenate(parts, -1)

    wp = pack(w_query, w_key, w_value)
    bp = pack(b_query, jnp.zeros_like(b_query), b_value).reshape(1, -1)
    wide = wp.shape[1]
    vm, sm, anyv = pltpu.VMEM, pltpu.SMEM, pl.ANY
    dma = pltpu.SemaphoreType.DMA
    S, W, B = shard, width, batches

    xp, n1, qp, kvd, kvt, tab, atto, attw, den, wop, dsl, dst, sto, fd, gud, vecs = call(
        functools.partial(first_half, n, pat, levels),
        "forward_and_feed",
        [
            ((B, S, W), BF),
            ((B, S, W), BF),
            ((units, S, 128), BF),
            ((units, SPAN1 * S, 128), BF),
            ((units, n * half, 128), BF),
            ((heads, levels, S, 128), BF),
            ((tiles, S, 128), BF),
            ((tiles, S, 128), F32),
            ((tiles, S, 128), F32),
            ((cols + 2 * HD, W), BF),
            ((B, S, W), BF),
            ((B, quarter, W), F32),
            ((B, quarter, W), F32),
            ((B, S, W), BF),
            ((2 * W, W), BF),
            ((8, W), F32),
        ],
        [
            pltpu.VMEM(w_up.shape, BF),
            pltpu.VMEM(w_down.shape, BF),
            pltpu.VMEM((B, S, W), BF),
            pltpu.VMEM((units, S, 128), F32),
            pltpu.VMEM((pat, tiles, S, 128), BF),
            pltpu.VMEM((pat, cols + 2 * HD, W), BF),
            pltpu.VMEM((B, S, w_up.shape[1]), F32),
            pltpu.VMEM((B, S, W), F32),
            pltpu.VMEM((B, S, W), BF),
            pltpu.VMEM((B, S, w_up.shape[1]), BF),
            pltpu.VMEM((B, S, W), BF),
            pltpu.VMEM((B, S, w_up.shape[1]), BF),
            pltpu.VMEM((B, pat, quarter, W), BF),
            pltpu.VMEM((B, pat + 1, quarter, W), BF),
            pltpu.VMEM((quarter, W), F32),
            dma((3,)),
            dma((heads,)),
        ]
        + dense_sems(B)
        + thin_sems(B, chips)
        + line_sems(pat)
        + plane_sems(chips)
        + line_sems(pat) * tiles
        + sum_sems(pat) * B
        + line_sems(pat) * B,
        [sm] + [vm] * 12 + [anyv] * 4,
        0,
    )(
        lengths,
        inputs,
        gain_one,
        shift_one,
        wp,
        bp,
        w_out,
        b_out,
        gain_two,
        shift_two,
        b_up,
        perm,
        qext,
        ktab,
        w_up,
        w_down,
        d_output,
    )

    r1, r2 = 2 * W, 4 * cols
    outf, gif, gsum1, gsum2, vout = call(
        functools.partial(second_half, n, pat, levels),
        "backward_and_sums",
        [
            ((B, S, W), BF),
            ((B, S, W), BF),
            ((r1, W), BF),
            ((r2, W), BF),
            ((8, W), F32),
        ],
        [
            pltpu.VMEM((units, SPAN1 * S, 128), BF),
            pltpu.VMEM((units, n * half, 128), BF),
            pltpu.VMEM((SPAN1, 8, S), F32),
            pltpu.VMEM((n, 8, half), F32),
            pltpu.VMEM((units, S, 128), BF),
            pltpu.VMEM((units, S, 128), F32),
            pltpu.VMEM((units, S, 128), F32),
            pltpu.VMEM((B, S, W), BF),
            pltpu.VMEM((B, pat + 1, quarter, W), BF),
            pltpu.VMEM((B, S, wide), BF),
            pltpu.VMEM((B, pat, quarter, W), BF),
            pltpu.VMEM((B, pat + 1, quarter, W), BF),
            pltpu.VMEM((quarter, W), F32),
            pltpu.VMEM((r1, W), BF),
            pltpu.VMEM((r2, W), BF),
        ]
        + [pltpu.VMEM((r1 >> d, W), BF) for d in (1, 2, 3)]
        + [pltpu.VMEM((r2 >> d, W), BF) for d in (1, 2, 3)]
        + [pltpu.VMEM((pat - 1, 8, W), F32), pltpu.VMEM((n + 1, 8, W), F32)]
        + dense_sems(B)
        + thin_sems(B, chips)
        + [dma((3,))] * 2
        + [dma((chips,))] * 4
        + sum_sems(pat) * B
        + line_sems(pat) * B
        + sum_sems(pat) * B
        + line_sems(pat) * B
        + [dma((6,))] * 4
        + [dma((pat - 1,))] * 2
        + [dma((n - 1,))] * 2,
        [sm] + [vm] * 20,
        1,
    )(
        lengths,
        dsl,
        dst,
        wop,
        atto,
        attw,
        den,
        qp,
        kvd,
        kvt,
        tab,
        qext,
        fd,
        sto,
        b_down,
        gud,
        vecs,
        n1,
        xp,
        wp,
        gain_one,
    )

    outs = [((B, S, W), BF)] * 2
    outs += [((W, W), F32)] * 2 + [((cols, W), F32)] + [((W, cols), F32)] * 3
    outs += [((W,), F32)] * 2 + [((cols,), F32)] * 2 + [((W,), F32)] * 5
    res = pl.pallas_call(
        functools.partial(finish_kernel, heads),
        name="results",
        out_shape=[jax.ShapeDtypeStruct(s, d) for s, d in outs],
        compiler_params=pltpu.CompilerParams(vmem_limit_bytes=62 << 20),
    )(outf, gif, gsum1, gsum2, vout, permt)
    outputs, grad_inputs, g_up, g_down, g_out, g_q, g_k, g_v = res[:8]
    gain1, shift1, bq, bv, bout, gain2, shift2, bup, bdown = res[8:]
    return (
        outputs,
        grad_inputs,
        gain1,
        shift1,
        g_q,
        bq,
        g_k,
        g_v,
        bv,
        g_out,
        bout,
        gain2,
        shift2,
        g_up,
        bup,
        g_down,
        bdown,
    )


def solution(mesh):
    token = P(None, "seq", None)
    in_specs = (
        token,
        P(),
        P(),
        P(),
        P(None, "pat"),
        P("pat"),
        P(None, "pat"),
        P(None, "pat"),
        P("pat"),
        P("pat", None),
        P(),
        P(),
        P(),
        P(None, "pat"),
        P("pat"),
        P("pat", None),
        P(),
        token,
    )
    out_specs = (
        token,
        token,
        P(),
        P(),
        P(None, "pat"),
        P("pat"),
        P(None, "pat"),
        P(None, "pat"),
        P("pat"),
        P("pat", None),
        P(),
        P(),
        P(),
        P(None, "pat"),
        P("pat"),
        P("pat", None),
        P(),
    )
    n, pat = mesh.shape["seq"], mesh.shape["pat"]
    body = functools.partial(plane_program if n == 8 else shards, n, pat)
    return jax.shard_map(body, mesh=mesh, in_specs=in_specs, out_specs=out_specs, check_vma=False)
```

```python
import functools

import jax
import jax.numpy as jnp
import numpy as np
from jax import lax
from jax.experimental import pallas as pl
from jax.experimental.pallas import tpu as pltpu
from jax.sharding import PartitionSpec as P

HD = 64
SPAN1 = 4
DILATIONS = (1, 2, 4, 6, 12)
CYCLE = 12
EPS = 1e-05
NEG = -1e30
LEN_LANE = 24
COR_LANE = 25
MESH = pl.DeviceIdType.MESH
BF = jnp.bfloat16
F32 = jnp.float32
ROOT = float(np.sqrt(2.0 / np.pi))


def nn(a, b):
    return lax.dot_general(a, b, (((1,), (0,)), ((), ())), preferred_element_type=F32)


def nt(a, b):
    return lax.dot_general(a, b, (((1,), (1,)), ((), ())), preferred_element_type=F32)


def tn(a, b):
    return lax.dot_general(a, b, (((0,), (0,)), ((), ())), preferred_element_type=F32)


def exact_nt(a, b):
    return lax.dot_general(
        a, b, (((1,), (1,)), ((), ())), preferred_element_type=F32, precision=lax.Precision.HIGHEST
    )


def exact_nn(a, b):
    return lax.dot_general(
        a, b, (((1,), (0,)), ((), ())), preferred_element_type=F32, precision=lax.Precision.HIGHEST
    )


def remote(src, dst, send, recv, device):
    return pltpu.make_async_remote_copy(
        src_ref=src,
        dst_ref=dst,
        send_sem=send,
        recv_sem=recv,
        device_id=device,
        device_id_type=MESH,
    )


def when(cond, fn):
    pl.when(cond)(fn)


def rows_of(start, size):
    return pl.ds(pl.multiple_of(start, 16), size)


def orders(shard):
    p = np.arange(shard)
    return 2 * (p % (shard // 2)) + p // (shard // 2)


def perm_matrix(shard):
    token = orders(shard)
    m = np.zeros((shard, shard), np.float32)
    m[np.arange(shard), token] = 1.0
    return m


def query_ext(shard):
    cls = orders(shard) % CYCLE
    m = np.zeros((shard, 128), np.float32)
    m[np.arange(shard), cls] = 1.0
    m[np.arange(shard), CYCLE + cls] = 1.0
    m[:, LEN_LANE] = 1.0
    return m


def key_tables(shard, heads, levels):
    cls = orders(shard) % CYCLE
    out = np.zeros((heads, levels, shard, 128), np.float32)
    for h in range(heads):
        for level in range(levels):
            count = np.zeros((CYCLE, CYCLE))
            for r in DILATIONS[level:]:
                on = (np.arange(CYCLE) % r == h % r).astype(np.float64)
                count += on[:, None] * on[None, :]
            with np.errstate(divide="ignore"):
                log = np.log(count)
            high = np.where(count > 0, log, NEG).astype(np.float32).astype(jnp.bfloat16)
            low = np.where(count > 0, log - high.astype(np.float64), 0.0)
            out[h, level, :, :CYCLE] = high.astype(np.float32)[:, cls].T
            out[h, level, :, CYCLE : 2 * CYCLE] = low[:, cls].T
            out[h, level, :, COR_LANE] = 1.0
            out[h, level, :, COR_LANE + 1] = 1.0
    return out.astype(jnp.bfloat16)


class Place:
    def __init__(self, n, pat):
        self.n, self.pat = n, pat
        self.z = lax.axis_index("pat")
        self.s = lax.axis_index("seq")
        self.core = lax.rem(self.s, 2)
        self.chip = lax.div(self.s, 2)
        self.seg = lax.div(self.s, SPAN1)
        self.pos = lax.rem(self.s, SPAN1)
        self.sib = self.s + 1 - 2 * self.core
        self.even = lax.rem(self.chip, 2) == 0

    def other_z(self, k):
        return lax.rem(self.z + k, self.pat)

    def greet(self, z_axis, same_core, all_seq=False):
        bar = pltpu.get_barrier_semaphore()
        count = 0
        if z_axis:
            for k in range(1, self.pat):
                pl.semaphore_signal(
                    bar, inc=1, device_id=(self.other_z(k), self.s), device_id_type=MESH
                )
                count += 1
        if all_seq:
            for k in range(1, self.n):
                to = lax.rem(self.s + k, self.n)
                pl.semaphore_signal(bar, inc=1, device_id=(self.z, to), device_id_type=MESH)
                count += 1
        elif same_core:
            pl.semaphore_signal(bar, inc=1, device_id=(self.z, self.sib), device_id_type=MESH)
            count += 1
            for k in range(1, self.n // 2):
                to = lax.rem(self.s + 2 * k, self.n)
                pl.semaphore_signal(bar, inc=1, device_id=(self.z, to), device_id_type=MESH)
                count += 1
        return bar, count


def lane_masks():
    lane = lax.broadcasted_iota(jnp.int32, (1, 128), 1)
    low = jnp.where(lane < HD, 1.0, 0.0)
    return low.astype(BF), (1.0 - low).astype(BF)


def token_of(index, shard):
    half = jnp.where(index >= shard // 2, 1, 0)
    return 2 * (index - half * (shard // 2)) + half


def length_lane(positions, length, rows):
    lane = lax.broadcasted_iota(jnp.int32, (rows, 128), 1)
    hit = jnp.logical_and(lane == LEN_LANE, positions >= length)
    return jnp.where(hit, NEG, 0.0).astype(BF)


def dense_positions(device, shard):
    row = lax.broadcasted_iota(jnp.int32, (shard, 128), 0)
    return device * shard + token_of(row, shard)


def thin_positions(first_device, parity, shard, blocks):
    half = shard // 2
    row = lax.broadcasted_iota(jnp.int32, (blocks * half, 128), 0)
    block = lax.div(row, half)
    return (first_device + block) * shard + 2 * (row - block * half) + parity


def level_of(seg_a, seg_b, levels):
    level = jnp.int32(1)
    size = 2
    for _ in range(2, levels):
        apart = lax.div(seg_a, size) != lax.div(seg_b, size)
        level = level + jnp.where(apart, 1, 0)
        size *= 2
    return level


class Shares:
    def __init__(self, place, shard, forward, dense, thin, dense_sems, thin_sems):
        self.p, self.shard, self.forward = place, shard, forward
        self.dense, self.thin = dense, thin
        self.ds, self.ts = dense_sems, thin_sems
        p = place
        self.chips = p.n // 2
        if forward:
            self.sib_sends, self.sib_gets = p.core == 0, p.core == 1
            self.x_sends, self.x_gets = p.even, jnp.logical_not(p.even)
            self.x_to, self.x_slot = p.s + 2, p.pos - 2
        else:
            self.sib_sends, self.sib_gets = p.core == 1, p.core == 0
            self.x_sends, self.x_gets = jnp.logical_not(p.even), p.even
            self.x_to, self.x_slot = p.s - 2, p.pos + 2
        self.sib_pos = p.pos + 1 - 2 * p.core
        self.x_sib_slot = self.x_slot + 1 - 2 * p.core

    def sib_copy(self, slot):
        p = self.p
        return remote(
            self.dense(slot), self.dense(slot), self.ds[0].at[0], self.ds[1].at[0], (p.z, p.sib)
        )

    def x_copy(self, slot):
        p = self.p
        to = jnp.where(self.x_sends, self.x_to, p.sib)
        return remote(
            self.dense(slot), self.dense(slot), self.ds[0].at[1], self.ds[1].at[1], (p.z, to)
        )

    def hand_copy(self, slot):
        p = self.p
        return remote(
            self.dense(slot), self.dense(slot), self.ds[0].at[2], self.ds[1].at[2], (p.z, p.sib)
        )

    def thin_to(self, chip):
        seg = chip // 2
        return (seg > self.p.seg) if self.forward else (seg < self.p.seg)

    def thin_from(self, chip):
        seg = chip // 2
        return (seg < self.p.seg) if self.forward else (seg > self.p.seg)

    def thin_copy(self, chip):
        p = self.p
        return remote(
            self.thin(p.s),
            self.thin(p.s),
            self.ts[0].at[chip],
            self.ts[1].at[p.chip],
            (p.z, 2 * chip + p.core),
        )

    def thin_got(self, chip):
        p = self.p
        slot = 2 * chip + p.core
        return remote(
            self.thin(slot), self.thin(slot), self.ts[0].at[chip], self.ts[1].at[chip], (p.z, p.sib)
        )

    def thin_hand(self, chip, mine):
        p = self.p
        slot = 2 * chip + (p.core if mine else 1 - p.core)
        return remote(
            self.thin(slot), self.thin(slot), self.ts[2].at[chip], self.ts[3].at[chip], (p.z, p.sib)
        )

    def start(self):
        p = self.p
        when(self.x_sends, lambda: self.x_copy(p.pos).start())
        for chip in range(self.chips):
            when(self.thin_to(chip), lambda chip=chip: self.thin_copy(chip).start())
        when(self.sib_sends, lambda: self.sib_copy(p.pos).start())

    def pass_on(self):
        def dense_part():
            self.x_copy(self.x_slot).wait_recv()
            self.hand_copy(self.x_slot).start()

        when(self.x_gets, dense_part)
        for chip in range(self.chips):

            def thin_part(chip=chip):
                self.thin_got(chip).wait_recv()
                self.thin_hand(chip, True).start()

            when(self.thin_from(chip), thin_part)

    def arrive(self):
        when(self.sib_gets, lambda: self.sib_copy(self.sib_pos).wait_recv())
        when(self.x_gets, lambda: self.hand_copy(self.x_sib_slot).wait_recv())
        for chip in range(self.chips):
            when(
                self.thin_from(chip),
                lambda chip=chip: self.thin_hand(chip, False).wait_recv(),
            )

    def finish(self):
        p = self.p
        when(self.x_sends, lambda: self.x_copy(p.pos).wait_send())
        when(self.sib_sends, lambda: self.sib_copy(p.pos).wait_send())
        when(self.x_gets, lambda: self.hand_copy(self.x_slot).wait_send())
        for chip in range(self.chips):
            when(self.thin_to(chip), lambda chip=chip: self.thin_copy(chip).wait_send())
            when(self.thin_from(chip), lambda chip=chip: self.thin_hand(chip, True).wait_send())


def dense_sems(batches):
    return [pltpu.SemaphoreType.DMA((batches, 3))] * 2


def thin_sems(batches, chips):
    return [pltpu.SemaphoreType.DMA((batches, chips))] * 4


class Spread:
    def __init__(self, place, send, recv):
        self.p, self.send, self.recv = place, send, recv

    def copy_to(self, k, src, dst):
        p = self.p
        return remote(src, dst, self.send.at[k - 1], self.recv.at[k - 1], (p.other_z(k), p.s))


def forward_kernel(
    n,
    pat,
    levels,
    lens,
    x_ref,
    gain,
    shift,
    wq,
    bq,
    wkv,
    bkv,
    wout,
    perm,
    qext,
    ktab,
    xp,
    n1,
    qp,
    kvd,
    kvt,
    attf,
    wofp,
    attw,
    den,
    tab,
    acc,
    tab_sem,
    w_send,
    w_recv,
    a_send,
    a_recv,
    ds0,
    ds1,
    ts0,
    ts1,
    ts2,
    ts3,
):
    batches, shard, width = x_ref.shape
    half = shard // 2
    heads = wout.shape[0] // HD
    units = batches * heads
    p = Place(n, pat)
    bar, greeted = p.greet(True, True)
    low, high = lane_masks()

    def tab_copy(i):
        return pltpu.make_async_copy(ktab.at[heads * p.z + i], tab.at[i], tab_sem.at[i])

    for i in range(heads):
        tab_copy(i).start()
    for z in range(pat):
        wofp[z, 0:HD, :] = jnp.zeros((HD, width), BF)
        wofp[z, HD + heads * HD : 2 * HD + heads * HD, :] = jnp.zeros((HD, width), BF)
    wofp[p.z, HD : HD + heads * HD, :] = wout[...]
    for b in range(batches):
        xb = nn(perm[...], x_ref[b])
        xp[b] = xb.astype(BF)
        mean = jnp.mean(xb, -1, keepdims=True)
        cen = xb - mean
        var = jnp.mean(cen * cen, -1, keepdims=True)
        n1[b] = (cen * lax.rsqrt(var + EPS) * gain[...] + shift[...]).astype(BF)

    shares = [
        Shares(
            p,
            shard,
            True,
            lambda slot, b=b: kvd.at[pl.ds(heads * b, heads), rows_of(slot * shard, shard), :],
            lambda dev, b=b: kvt.at[pl.ds(heads * b, heads), rows_of(dev * half, half), :],
            [ds0.at[b], ds1.at[b]],
            [ts0.at[b], ts1.at[b], ts2.at[b], ts3.at[b]],
        )
        for b in range(batches)
    ]
    parity = [lax.rem(heads * p.z + i, 2) for i in range(heads)]
    for b in range(batches):
        q = ((nn(n1[b], wq[...]) + bq[...]).astype(BF)) * jnp.asarray(HD**-0.5, BF)
        kv = (nn(n1[b], wkv[...]) + bkv[...]).astype(BF)
        for i in range(heads):
            qp[heads * b + i] = q[:, i * 128 : (i + 1) * 128]
            kvd[heads * b + i, rows_of(p.pos * shard, shard), :] = kv[:, i * 128 : (i + 1) * 128]
        for i in range(heads):
            kvt[heads * b + i, rows_of(p.s * half, half), :] = kvd[
                heads * b + i, rows_of(p.pos * shard + parity[i] * half, half), :
            ]
        if b == 0:
            pl.semaphore_wait(bar, greeted)
        shares[b].start()
    w_spread = Spread(p, w_send, w_recv)

    def w_slot(z):
        return wofp.at[z, HD : HD + heads * HD, :]

    for k in range(1, pat):
        w_spread.copy_to(k, w_slot(p.z), w_slot(p.z)).start()
    for i in range(heads):
        tab_copy(i).wait()

    def attend(qx, kv, ext, bias):
        s = nt(qx, jnp.concatenate([kv, ext], 1))
        if bias is not None:
            s = s + bias
        return nn(jnp.exp(s).astype(BF), kv * high + low)

    own = rows_of(p.pos * shard, shard)
    qi = lax.broadcasted_iota(jnp.int32, (shard, shard), 0)
    ki = lax.broadcasted_iota(jnp.int32, (shard, shard), 1)
    qt, kt = token_of(qi, shard), token_of(ki, shard)
    for b in range(batches):
        live = jnp.logical_or(
            jnp.logical_and(kt < qt, kt + p.s * shard < lens[b]), kt == qt
        )
        bias = jnp.where(live, 0.0, NEG)
        for i in range(heads):
            u = heads * b + i
            qx = jnp.concatenate([qp[u], qext[...]], 1)
            acc[u] = attend(qx, kvd[u, own, :], tab[i, 0], bias)

    att_spread = [Spread(p, a_send.at[t], a_recv.at[t]) for t in range(units // 2)]
    lane = lax.broadcasted_iota(jnp.int32, (shard, 128), 1)
    for b in range(batches):
        shares[b].pass_on()
        shares[b].arrive()

        def dense(j, carry, b=b):
            lenl = length_lane(dense_positions(p.seg * SPAN1 + j, shard), lens[b], shard)
            for i in range(heads):
                u = heads * b + i
                qx = jnp.concatenate([qp[u], qext[...]], 1)
                kv = kvd[u, rows_of(j * shard, shard), :]
                acc[u] += attend(qx, kv, tab[i, 0] + lenl, None)
            return carry

        lax.fori_loop(0, p.pos, dense, 0)

        def thin(sg, carry, b=b):
            level = level_of(sg, p.seg, levels)
            for i in range(heads):
                u = heads * b + i
                mine = rows_of(parity[i] * half, half)
                places = thin_positions(sg * SPAN1, parity[i], shard, SPAN1)
                lenl = length_lane(places, lens[b], SPAN1 * half)
                ext = jnp.concatenate([tab[i, level, mine, :]] * SPAN1, 0) + lenl
                qx = jnp.concatenate([qp[u, mine, :], qext[mine, :]], 1)
                kv = kvt[u, rows_of(sg * SPAN1 * half, SPAN1 * half), :]
                acc[u, mine, :] += attend(qx, kv, ext, None)
            return carry

        lax.fori_loop(0, p.seg, thin, 0)
        for t in range(units // 2):
            if (2 * t + 1) // heads != b:
                continue
            even, odd = acc[2 * t], acc[2 * t + 1]
            num = jnp.where(lane < HD, pltpu.roll(even, HD, 1), odd)
            dn = jnp.where(lane < HD, even, pltpu.roll(odd, HD, 1))
            wide = num / dn
            den[t] = dn
            attw[t] = wide
            attf[p.z, t] = wide.astype(BF)
            for k in range(1, pat):
                att_spread[t].copy_to(k, attf.at[p.z, t], attf.at[p.z, t]).start()
    for k in range(1, pat):
        frm = lax.rem(p.z + pat - k, pat)
        w_spread.copy_to(k, w_slot(p.z), w_slot(p.z)).wait_send()
        w_spread.copy_to(k, w_slot(frm), w_slot(frm)).wait_recv()
        for t in range(units // 2):
            att_spread[t].copy_to(k, attf.at[p.z, t], attf.at[p.z, t]).wait_send()
            att_spread[t].copy_to(k, attf.at[frm, t], attf.at[frm, t]).wait_recv()
    for b in range(batches):
        shares[b].finish()


def middle_kernel(
    n,
    pat,
    xp,
    attf,
    wofp,
    bout,
    gain,
    shift,
    wup,
    bup,
    wdown,
    dout,
    perm,
    gud,
    fd,
    dsf,
    dst,
    sto,
    vecs,
    state,
    n2,
    act,
    dop,
    dh,
    dns,
    dno,
    dnr,
    r_send,
    r_recv,
    g_send,
    g_recv,
):
    batches, shard, width = xp.shape
    quarter = shard // pat
    p = Place(n, pat)
    bar, greeted = p.greet(True, False)
    rs = [Spread(p, r_send.at[b], r_recv.at[b]) for b in range(batches)]
    ag = [Spread(p, g_send.at[b], g_recv.at[b]) for b in range(batches)]
    bup_sum = jnp.zeros((1, width), F32)
    bdown_sum = jnp.zeros((1, width), F32)
    for b in range(batches):
        mixed = jnp.zeros((shard, width), F32)
        for z in range(pat):
            pair = jnp.concatenate([attf[z, b], attf[z, b + 1]], 1)
            weight = wofp[z, HD : HD + 256, :] if b == 0 else wofp[z, 0:256, :]
            mixed = mixed + nn(pair, weight)
        st = xp[b].astype(F32) + mixed + bout[...]
        state[b] = st
        mean = jnp.mean(st, -1, keepdims=True)
        cen = st - mean
        var = jnp.mean(cen * cen, -1, keepdims=True)
        norm = (cen * lax.rsqrt(var + EPS) * gain[...] + shift[...]).astype(BF)
        n2[b] = norm
        dob = nn(perm[...], dout[b])
        dop[b] = dob.astype(BF)
        bdown_sum = bdown_sum + jnp.sum(dob, 0, keepdims=True)
        hid = nn(norm, wup[...]) + bup[...]
        cube = hid * hid * hid
        th = jnp.tanh(ROOT * (hid + 0.044715 * cube))
        act[b] = (0.5 * hid * (1.0 + th)).astype(BF)
        slope = 0.5 * (1.0 + th) + 0.5 * hid * (1.0 - th * th) * (
            ROOT * (1.0 + 3.0 * 0.044715 * hid * hid)
        )
        dhid = (nt(dop[b], wdown[...]) * slope).astype(BF)
        dh[b] = dhid
        bup_sum = bup_sum + jnp.sum(dhid.astype(F32), 0, keepdims=True)
        dn = nt(dhid, wup[...])
        for z in range(pat):
            dns[b, z] = dn[z * quarter : (z + 1) * quarter].astype(BF)
        if b == 0:
            pl.semaphore_wait(bar, greeted)
        for k in range(1, pat):
            rs[b].copy_to(k, dns.at[b, p.other_z(k)], dnr.at[b, k - 1]).start()
    vecs[...] = jnp.zeros(vecs.shape, F32)
    for b in range(batches):
        fd[b] = nn(act[b], wdown[...]).astype(BF)
    bout_sum = jnp.zeros((1, width), F32)
    gain_sum = jnp.zeros((1, width), F32)
    shift_sum = jnp.zeros((1, width), F32)
    mine = rows_of(p.z * quarter, quarter)
    for b in range(batches):
        total = dns[b, p.z].astype(F32)
        for k in range(1, pat):
            rs[b].copy_to(k, dns.at[b, p.other_z(k)], dnr.at[b, k - 1]).wait_recv()
            total = total + dnr[b, k - 1].astype(F32)
        st = state[b, mine, :]
        sto[b] = st
        mean = jnp.mean(st, -1, keepdims=True)
        cen = st - mean
        inv = lax.rsqrt(jnp.mean(cen * cen, -1, keepdims=True) + EPS)
        hat = cen * inv
        gain_sum = gain_sum + jnp.sum(total * hat, 0, keepdims=True)
        shift_sum = shift_sum + jnp.sum(total, 0, keepdims=True)
        dhat = total * gain[...]
        back = inv * (
            dhat
            - jnp.mean(dhat, -1, keepdims=True)
            - hat * jnp.mean(dhat * hat, -1, keepdims=True)
        )
        ds = dop[b, mine, :].astype(F32) + back
        dst[b] = ds
        bout_sum = bout_sum + jnp.sum(ds, 0, keepdims=True)
        dsf[b, mine, :] = ds.astype(BF)
        for k in range(1, pat):
            ag[b].copy_to(k, dsf.at[b, mine, :], dsf.at[b, mine, :]).start()
    vecs[2:3, :] = bout_sum
    vecs[3:4, :] = gain_sum
    vecs[4:5, :] = shift_sum
    vecs[5:6, :] = bup_sum
    vecs[6:7, :] = bdown_sum
    up = tn(n2[0], dh[0])
    for b in range(1, batches):
        up = up + tn(n2[b], dh[b])
    gud[0:width, :] = up.astype(BF)
    down = tn(act[0], dop[0])
    for b in range(1, batches):
        down = down + tn(act[b], dop[b])
    gud[width : 2 * width, :] = down.astype(BF)
    for b in range(batches):
        for k in range(1, pat):
            frm = lax.rem(p.z + pat - k, pat)
            theirs = dsf.at[b, rows_of(frm * quarter, quarter), :]
            rs[b].copy_to(k, dns.at[b, p.other_z(k)], dnr.at[b, k - 1]).wait_send()
            ag[b].copy_to(k, dsf.at[b, mine, :], dsf.at[b, mine, :]).wait_send()
            ag[b].copy_to(k, theirs, theirs).wait_recv()


def backward_kernel(
    n,
    pat,
    levels,
    lens,
    dsf,
    wofp,
    attf,
    attw,
    den,
    qp,
    kvd,
    kvt,
    tab,
    qext,
    fd,
    sto,
    bdown,
    permt,
    dq,
    dkv,
    gout,
    outp,
    qud,
    qut,
    crd,
    crt,
    uext,
    acq,
    ack,
    fdr,
    outf,
    f_send,
    f_recv,
    o_send,
    o_recv,
    ds0,
    ds1,
    ts0,
    ts1,
    ts2,
    ts3,
    cd0,
    cd1,
    ct0,
    ct1,
    ct2,
    ct3,
):
    batches, shard, width = dsf.shape
    half = shard // 2
    quarter = shard // pat
    units = qp.shape[0]
    heads = units // batches
    p = Place(n, pat)
    bar, greeted = p.greet(True, True)
    low, high = lane_masks()
    parity = [lax.rem(heads * p.z + i, 2) for i in range(heads)]
    own = rows_of(p.pos * shard, shard)
    lane = lax.broadcasted_iota(jnp.int32, (shard, 128), 1)
    row8 = lax.broadcasted_iota(jnp.int32, (8, 128), 0)
    lane8 = lax.broadcasted_iota(jnp.int32, (8, 128), 1)
    pick = jnp.where(row8 == lax.div(lane8, HD), 1.0, 0.0).astype(F32)
    ri = lax.broadcasted_iota(jnp.int32, (128, 128), 0)
    ci = lax.broadcasted_iota(jnp.int32, (128, 128), 1)
    same = jnp.where(lax.div(ri, HD) == lax.div(ci, HD), 1.0, 0.0).astype(F32)

    wide = [
        nt(dsf[b], wofp[p.z, HD : HD + 256, :] if b == 0 else wofp[p.z, 0:256, :])
        for b in range(batches)
    ]
    tiles = [wide[0][:, 0:128], wide[0][:, 128:256] + wide[1][:, 0:128], wide[1][:, 128:256]]
    crd[p.pos] = jnp.zeros(crd.shape[1:], F32)
    crt[p.s] = jnp.zeros(crt.shape[1:], F32)
    for t in range(units // 2):
        dn = den[t]
        up = tiles[t] / dn
        prod = tiles[t] * attw[t] / dn
        cor = exact_nn(prod, same)
        cor_rows = exact_nt(pick, prod)
        for e in range(2):
            u = 2 * t + e
            i = u % heads
            part = up if e == 1 else pltpu.roll(up, HD, 1)
            mixed = jnp.where(lane < HD, qp[u].astype(F32), part).astype(BF)
            qud[u, own, :] = mixed
            qut[u, rows_of(p.s * half, half), :] = qud[
                u, rows_of(p.pos * shard + parity[i] * half, half), :
            ]
            crd[p.pos, u : u + 1, :] = cor_rows[e : e + 1, :]
            col = -cor[:, e * HD : e * HD + 1]
            first = col.astype(BF).astype(F32)
            ue = jnp.where(lane == COR_LANE, first, 0.0) + jnp.where(
                lane == COR_LANE + 1, col - first, 0.0
            )
            uext[u] = ue.astype(BF)
            thin_cor = jnp.where(parity[i] == 0, cor_rows[e : e + 1, 0:half], cor_rows[e : e + 1, half:shard])
            crt[p.s, u : u + 1, :] = thin_cor
    pl.semaphore_wait(bar, greeted)
    cors = Shares(
        p,
        shard,
        False,
        lambda slot: crd.at[slot],
        lambda dev: crt.at[dev],
        [cd0, cd1],
        [ct0, ct1, ct2, ct3],
    )
    shares = [
        Shares(
            p,
            shard,
            False,
            lambda slot, b=b: qud.at[pl.ds(heads * b, heads), rows_of(slot * shard, shard), :],
            lambda dev, b=b: qut.at[pl.ds(heads * b, heads), rows_of(dev * half, half), :],
            [ds0.at[b], ds1.at[b]],
            [ts0.at[b], ts1.at[b], ts2.at[b], ts3.at[b]],
        )
        for b in range(batches)
    ]
    cors.start()
    for b in range(batches):
        shares[b].start()
    fs = [Spread(p, f_send.at[b], f_recv.at[b]) for b in range(batches)]
    og = [Spread(p, o_send.at[b], o_recv.at[b]) for b in range(batches)]

    def fd_src(b, k):
        return fd.at[b, rows_of(p.other_z(k) * quarter, quarter), :]

    for b in range(batches):
        for k in range(1, pat):
            fs[b].copy_to(k, fd_src(b, k), fdr.at[b, k - 1]).start()

    def query_side(qu, qe, ue, kv, ext, bias):
        kvx = jnp.concatenate([kv, ext], 1)
        s = nt(jnp.concatenate([qu * low, qe], 1), kvx)
        if bias is not None:
            s = s + bias
        dp = nt(jnp.concatenate([qu * high, ue], 1), kvx)
        return nn((jnp.exp(s) * dp).astype(BF), kv)

    def key_side(qu, qe, cor, kv, ext, bias):
        s = nt(jnp.concatenate([kv, ext], 1), jnp.concatenate([qu * low, qe], 1))
        if bias is not None:
            s = s + bias
        w = jnp.exp(s)
        dp = nt(kv, qu * high) - cor
        return nn((w * dp).astype(BF), qu * low) + nn(w.astype(BF), qu * high)

    qi = lax.broadcasted_iota(jnp.int32, (shard, shard), 0)
    ki = lax.broadcasted_iota(jnp.int32, (shard, shard), 1)
    ti, tj = token_of(qi, shard), token_of(ki, shard)
    for b in range(batches):
        bias = jnp.where(
            jnp.logical_or(jnp.logical_and(tj < ti, tj + p.s * shard < lens[b]), tj == ti), 0.0, NEG
        )
        biast = jnp.where(
            jnp.logical_or(jnp.logical_and(ti < tj, ti + p.s * shard < lens[b]), tj == ti), 0.0, NEG
        )
        for i in range(heads):
            u = heads * b + i
            kv = kvd[u, own, :]
            qu = qud[u, own, :]
            acq[u] = query_side(qu, qext[...], uext[u], kv, tab[i, 0], bias)
            ack[u] = key_side(qu, qext[...], crd[p.pos, u : u + 1, :], kv, tab[i, 0], biast)

    for b in range(batches):

        def dense_q(j, carry, b=b):
            lenl = length_lane(dense_positions(p.seg * SPAN1 + j, shard), lens[b], shard)
            for i in range(heads):
                u = heads * b + i
                kv = kvd[u, rows_of(j * shard, shard), :]
                acq[u] += query_side(
                    qud[u, own, :], qext[...], uext[u], kv, tab[i, 0] + lenl, None
                )
            return carry

        lax.fori_loop(0, p.pos, dense_q, 0)

        def thin_q(sg, carry, b=b):
            level = level_of(sg, p.seg, levels)
            for i in range(heads):
                u = heads * b + i
                mine = rows_of(parity[i] * half, half)
                places = thin_positions(sg * SPAN1, parity[i], shard, SPAN1)
                lenl = length_lane(places, lens[b], SPAN1 * half)
                ext = jnp.concatenate([tab[i, level, mine, :]] * SPAN1, 0) + lenl
                kv = kvt[u, rows_of(sg * SPAN1 * half, SPAN1 * half), :]
                qu = qut[u, rows_of(p.s * half, half), :]
                acq[u, mine, :] += query_side(
                    qu, qext[mine, :], uext[u, mine, :], kv, ext, None
                )
            return carry

        lax.fori_loop(0, p.seg, thin_q, 0)

    zrows = rows_of(p.z * quarter, quarter)
    for b in range(batches):
        total = fd[b, zrows, :].astype(F32)
        for k in range(1, pat):
            fs[b].copy_to(k, fd_src(b, k), fdr.at[b, k - 1]).wait_recv()
            total = total + fdr[b, k - 1].astype(F32)
        outf[b, zrows, :] = (sto[b] + total + bdown[...]).astype(BF)
        for k in range(1, pat):
            og[b].copy_to(k, outf.at[b, zrows, :], outf.at[b, zrows, :]).start()
    left = tn(jnp.concatenate([attf[p.z, 0], attf[p.z, 1]], 1), dsf[0])
    right = tn(jnp.concatenate([attf[p.z, 1], attf[p.z, 2]], 1), dsf[1])
    gout[...] = (left[0 : heads * HD] + right[HD : HD + heads * HD]).astype(BF)

    cors.pass_on()
    cors.arrive()
    for b in range(batches):
        shares[b].pass_on()
        shares[b].arrive()
        lenl = length_lane(dense_positions(p.s, shard), lens[b], shard)

        def dense_k(j, carry, b=b, lenl=lenl):
            for i in range(heads):
                u = heads * b + i
                qu = qud[u, rows_of(j * shard, shard), :]
                ack[u] += key_side(
                    qu, qext[...], crd[j, u : u + 1, :], kvd[u, own, :], tab[i, 0] + lenl, None
                )
            return carry

        lax.fori_loop(p.pos + 1, SPAN1, dense_k, 0)

        def thin_k(dev, carry, b=b):
            level = level_of(lax.div(dev, SPAN1), p.seg, levels)
            for i in range(heads):
                u = heads * b + i
                mine = rows_of(parity[i] * half, half)
                ext = tab[i, level, mine, :] + length_lane(
                    thin_positions(p.s, parity[i], shard, 1), lens[b], half
                )
                kv = kvt[u, rows_of(p.s * half, half), :]
                qu = qut[u, rows_of(dev * half, half), :]
                ack[u, mine, :] += key_side(
                    qu, qext[mine, :], crt[dev, u : u + 1, :], kv, ext, None
                )
            return carry

        lax.fori_loop(SPAN1 * (p.seg + 1), n, thin_k, 0)
        for i in range(heads):
            u = heads * b + i
            lanes = slice(i * 128, (i + 1) * 128)
            dq[b, :, lanes] = (acq[u] * HD**-0.5).astype(BF)
            dkv[b, :, lanes] = ack[u].astype(BF)

    for b in range(batches):
        for k in range(1, pat):
            frm = lax.rem(p.z + pat - k, pat)
            theirs = outf.at[b, rows_of(frm * quarter, quarter), :]
            og[b].copy_to(k, theirs, theirs).wait_recv()
            og[b].copy_to(k, outf.at[b, zrows, :], outf.at[b, zrows, :]).wait_send()
            fs[b].copy_to(k, fd_src(b, k), fdr.at[b, k - 1]).wait_send()
        outp[b] = nn(permt[...], outf[b]).astype(BF)
    cors.finish()
    for b in range(batches):
        shares[b].finish()


def tail_kernel(
    n,
    pat,
    xp,
    n1,
    dq,
    dkv,
    wq,
    wkv,
    gain,
    dst,
    vecs,
    gud,
    gout,
    permt,
    ginp,
    vout,
    grad,
    dns,
    dnr,
    gif,
    v0,
    vz,
    r_send,
    r_recv,
    g_send,
    g_recv,
    z_send,
    z_recv,
):
    batches, shard, width = xp.shape
    quarter = shard // pat
    cols = gout.shape[0]
    heads = cols // HD
    p = Place(n, pat)
    bar, greeted = p.greet(True, False)
    rs = [Spread(p, r_send.at[b], r_recv.at[b]) for b in range(batches)]
    ag = [Spread(p, g_send.at[b], g_recv.at[b]) for b in range(batches)]
    for b in range(batches):
        part = nt(dq[b], wq[...]) + nt(dkv[b], wkv[...])
        for z in range(pat):
            dns[b, z] = part[z * quarter : (z + 1) * quarter].astype(BF)
        if b == 0:
            pl.semaphore_wait(bar, greeted)
        for k in range(1, pat):
            rs[b].copy_to(k, dns.at[b, p.other_z(k)], dnr.at[b, k - 1]).start()
    qsum = jnp.zeros((1, heads * 128), F32)
    vsum = jnp.zeros((1, heads * 128), F32)
    for b in range(batches):
        qsum = qsum + jnp.sum(dq[b].astype(F32), 0, keepdims=True)
        vsum = vsum + jnp.sum(dkv[b].astype(F32), 0, keepdims=True)
    grad[0 : 2 * width, :] = gud[...].astype(F32)
    base = 2 * width
    for i in range(heads):
        lanes = slice(i * 128, (i + 1) * 128)
        a = tn(dq[0, :, lanes], n1[0])
        c = tn(dkv[0, :, lanes], n1[0])
        for b in range(1, batches):
            a = a + tn(dq[b, :, lanes], n1[b])
            c = c + tn(dkv[b, :, lanes], n1[b])
        grad[base + i * HD : base + (i + 1) * HD, :] = a[0:HD]
        grad[base + cols + i * HD : base + cols + (i + 1) * HD, :] = c[0:HD]
        grad[base + 2 * cols + i * HD : base + 2 * cols + (i + 1) * HD, :] = c[HD:]
    grad[base + 3 * cols : base + 4 * cols, :] = gout[...].astype(F32)
    zrows = rows_of(p.z * quarter, quarter)
    gain_sum = jnp.zeros((1, width), F32)
    shift_sum = jnp.zeros((1, width), F32)
    for b in range(batches):
        total = dns[b, p.z].astype(F32)
        for k in range(1, pat):
            rs[b].copy_to(k, dns.at[b, p.other_z(k)], dnr.at[b, k - 1]).wait_recv()
            total = total + dnr[b, k - 1].astype(F32)
        back, more_gain, more_shift = norm_back(xp[b, zrows, :].astype(F32), total, gain[...])
        gain_sum = gain_sum + more_gain
        shift_sum = shift_sum + more_shift
        gif[b, zrows, :] = (dst[b] + back).astype(BF)
        for k in range(1, pat):
            ag[b].copy_to(k, gif.at[b, zrows, :], gif.at[b, zrows, :]).start()
    v0[...] = vecs[...]
    v0[0:1, :] = gain_sum
    v0[1:2, :] = shift_sum
    zsp = Spread(p, z_send, z_recv)
    for k in range(1, pat):
        zsp.copy_to(k, v0, vz.at[k - 1]).start()
    for k in range(1, pat):
        zsp.copy_to(k, v0, vz.at[k - 1]).wait_recv()
    row = lax.broadcasted_iota(jnp.int32, (8, width), 0)
    extra = vz[0]
    for k in range(2, pat):
        extra = extra + vz[k - 1]
    vout[0:8, :] = v0[...] + jnp.where(row < 5, extra, 0.0)
    vout[8:16, :] = jnp.zeros((8, width), F32)
    vout[8:9, 0 : heads * 128] = qsum
    vout[9:10, 0 : heads * 128] = vsum
    for b in range(batches):
        for k in range(1, pat):
            frm = lax.rem(p.z + pat - k, pat)
            theirs = gif.at[b, rows_of(frm * quarter, quarter), :]
            ag[b].copy_to(k, theirs, theirs).wait_recv()
        ginp[b] = nn(permt[...], gif[b]).astype(BF)
    for b in range(batches):
        for k in range(1, pat):
            rs[b].copy_to(k, dns.at[b, p.other_z(k)], dnr.at[b, k - 1]).wait_send()
            ag[b].copy_to(k, gif.at[b, zrows, :], gif.at[b, zrows, :]).wait_send()
    for k in range(1, pat):
        zsp.copy_to(k, v0, vz.at[k - 1]).wait_send()


def call(kernel, name, outs, scratch, specs, number):
    return pl.pallas_call(
        kernel,
        name=name,
        out_shape=[jax.ShapeDtypeStruct(s, d) for s, d in outs],
        in_specs=[pl.BlockSpec(memory_space=m) for m in specs],
        out_specs=[pl.BlockSpec(memory_space=pltpu.VMEM)] * len(outs),
        scratch_shapes=scratch,
        compiler_params=pltpu.CompilerParams(
            collective_id=number, has_side_effects=True, vmem_limit_bytes=62 << 20
        ),
    )


def shards(
    n,
    pat,
    inputs,
    lengths,
    gain_one,
    shift_one,
    w_query,
    b_query,
    w_key,
    w_value,
    b_value,
    w_out,
    b_out,
    gain_two,
    shift_two,
    w_up,
    b_up,
    w_down,
    b_down,
    d_output,
):
    batches, shard, width = inputs.shape
    cols = w_query.shape[1]
    heads = cols // HD
    units = batches * heads
    chips = n // 2
    half = shard // 2
    quarter = shard // pat
    levels = 1
    while SPAN1 << (levels - 1) < n:
        levels += 1
    perm = jnp.asarray(perm_matrix(shard), BF)
    permt = jnp.asarray(perm_matrix(shard).T, BF)
    qext = jnp.asarray(query_ext(shard), BF)
    ktab = jnp.asarray(key_tables(shard, heads * pat, levels))
    row = lambda v: v.reshape(1, -1)
    by_head = lambda w: w.reshape(w.shape[0], heads, HD)
    pack = lambda a, b: jnp.concatenate([by_head(a), by_head(b)], 2).reshape(a.shape[0], 2 * cols)
    wq = pack(w_query, jnp.zeros_like(w_query))
    wkv = pack(w_key, w_value)
    bq = pack(row(b_query), jnp.zeros((1, cols), F32))
    bkv = pack(jnp.zeros((1, cols), F32), row(b_value))
    vm, sm, anyv = pltpu.VMEM, pltpu.SMEM, pl.ANY
    dma = pltpu.SemaphoreType.DMA
    tiles = units // 2

    xp, n1, qp, kvd, kvt, attf, wofp, attw, den, tab = call(
        functools.partial(forward_kernel, n, pat, levels),
        "attention_forward",
        [
            ((batches, shard, width), BF),
            ((batches, shard, width), BF),
            ((units, shard, 128), BF),
            ((units, SPAN1 * shard, 128), BF),
            ((units, n * half, 128), BF),
            ((pat, tiles, shard, 128), BF),
            ((pat, cols + 2 * HD, width), BF),
            ((tiles, shard, 128), F32),
            ((tiles, shard, 128), F32),
            ((heads, levels, shard, 128), BF),
        ],
        [
            pltpu.VMEM((units, shard, 128), F32),
            dma((heads,)),
            dma((pat - 1,)),
            dma((pat - 1,)),
            dma((tiles, pat - 1)),
            dma((tiles, pat - 1)),
        ]
        + dense_sems(batches)
        + thin_sems(batches, chips),
        [sm] + [vm] * 10 + [anyv],
        0,
    )(lengths, inputs, row(gain_one), row(shift_one), wq, bq, wkv, bkv, w_out, perm, qext, ktab)

    gud, fd, dsf, dst, sto, vecs = call(
        functools.partial(middle_kernel, n, pat),
        "feed_forward",
        [
            ((2 * width, width), BF),
            ((batches, shard, width), BF),
            ((batches, shard, width), BF),
            ((batches, quarter, width), F32),
            ((batches, quarter, width), F32),
            ((8, width), F32),
        ],
        [
            pltpu.VMEM((batches, shard, width), F32),
            pltpu.VMEM((batches, shard, width), BF),
            pltpu.VMEM((batches, shard, width), BF),
            pltpu.VMEM((batches, shard, width), BF),
            pltpu.VMEM((batches, shard, width), BF),
            pltpu.VMEM((batches, pat, quarter, width), BF),
            pltpu.VMEM((batches, quarter, width), F32),
            pltpu.VMEM((batches, pat - 1, quarter, width), BF),
        ]
        + [dma((batches, pat - 1))] * 4,
        [vm] * 11,
        1,
    )(
        xp,
        attf,
        wofp,
        row(b_out),
        row(gain_two),
        row(shift_two),
        w_up,
        row(b_up),
        w_down,
        d_output,
        perm,
    )

    dq, dkv, gout, outputs = call(
        functools.partial(backward_kernel, n, pat, levels),
        "attention_backward",
        [
            ((batches, shard, 2 * cols), BF),
            ((batches, shard, 2 * cols), BF),
            ((cols, width), BF),
            ((batches, shard, width), BF),
        ],
        [
            pltpu.VMEM((units, SPAN1 * shard, 128), BF),
            pltpu.VMEM((units, n * half, 128), BF),
            pltpu.VMEM((SPAN1, 8, shard), F32),
            pltpu.VMEM((n, 8, half), F32),
            pltpu.VMEM((units, shard, 128), BF),
            pltpu.VMEM((units, shard, 128), F32),
            pltpu.VMEM((units, shard, 128), F32),
            pltpu.VMEM((batches, pat - 1, quarter, width), BF),
            pltpu.VMEM((batches, shard, width), BF),
        ]
        + [dma((batches, pat - 1))] * 4
        + dense_sems(batches)
        + thin_sems(batches, chips)
        + [dma((3,))] * 2
        + [dma((chips,))] * 4,
        [sm] + [vm] * 14,
        2,
    )(lengths, dsf, wofp, attf, attw, den, qp, kvd, kvt, tab, qext, fd, sto, row(b_down), permt)

    rows = 2 * width + 4 * cols
    grad_inputs, vout, grads = call(
        functools.partial(tail_kernel, n, pat),
        "input_gradient",
        [
            ((batches, shard, width), BF),
            ((16, width), F32),
            ((rows, width), F32),
        ],
        [
            pltpu.VMEM((batches, pat, quarter, width), BF),
            pltpu.VMEM((batches, pat - 1, quarter, width), BF),
            pltpu.VMEM((batches, shard, width), BF),
            pltpu.VMEM((8, width), F32),
            pltpu.VMEM((pat - 1, 8, width), F32),
        ]
        + [dma((batches, pat - 1))] * 4
        + [dma((pat - 1,))] * 2,
        [vm] * 12,
        3,
    )(xp, n1, dq, dkv, wq, wkv, row(gain_one), dst, vecs, gud, gout, permt)
    vout, grads = lax.psum((vout, grads), "seq")
    base = 2 * width
    g_q, g_k, g_v, g_out = [grads[base + i * cols : base + (i + 1) * cols] for i in range(4)]
    q_row = vout[8, : 2 * cols].reshape(heads, 2, HD)
    v_row = vout[9, : 2 * cols].reshape(heads, 2, HD)
    return (
        outputs,
        grad_inputs,
        vout[0],
        vout[1],
        g_q.T,
        q_row[:, 0].reshape(cols),
        g_k.T,
        g_v.T,
        v_row[:, 1].reshape(cols),
        g_out,
        vout[2],
        vout[3],
        vout[4],
        grads[:width],
        vout[5],
        grads[width:base],
        vout[6],
    )


class LineGather:
    def __init__(self, place, block, send, recv):
        self.p, self.block, self.send, self.recv = place, block, send, recv

    def copy(self, frm, up):
        p = self.p
        to = jnp.clip(p.z + (1 if up else -1), 0, p.pat - 1)
        return remote(
            self.block(frm, p.z),
            self.block(frm, to),
            self.send.at[0 if up else 1, frm],
            self.recv.at[frm],
            (to, p.s),
        )

    def got(self, frm):
        p = self.p
        here = self.block(frm, p.z)
        return remote(
            here, here, self.send.at[0, 0], self.recv.at[frm], (lax.rem(p.z + 1, p.pat), p.s)
        )

    def start(self):
        p = self.p
        when(p.z < p.pat - 1, lambda: self.copy(p.z, True).start())
        when(p.z > 0, lambda: self.copy(p.z, False).start())

    def inner(self, hop):
        for z in range(1, self.p.pat - 1):
            if z - hop >= 0:
                yield z, z - hop, True
            if z + hop < self.p.pat:
                yield z, z + hop, False

    def forward(self, hop):
        for z, frm, up in self.inner(hop):

            def hand(frm=frm, up=up):
                self.got(frm).wait_recv()
                self.copy(frm, up).start()

            when(self.p.z == z, hand)

    def arrive(self):
        for frm in range(self.p.pat):
            if frm > 0:
                when(self.p.z == 0, lambda frm=frm: self.got(frm).wait_recv())
            if frm < self.p.pat - 1:
                when(self.p.z == self.p.pat - 1, lambda frm=frm: self.got(frm).wait_recv())

    def finish(self):
        p = self.p
        when(p.z < p.pat - 1, lambda: self.copy(p.z, True).wait_send())
        when(p.z > 0, lambda: self.copy(p.z, False).wait_send())
        for hop in range(1, p.pat - 1):
            for z, frm, up in self.inner(hop):
                when(p.z == z, lambda frm=frm, up=up: self.copy(frm, up).wait_send())


class LineSum:
    def __init__(self, place, part, buf, send, recv):
        self.p, self.part, self.buf, self.send, self.recv = place, part, buf, send, recv

    def copy(self, z, t):
        to = z + 1 if t > z else z - 1
        at = t if (t > z or t < to) else self.p.pat
        return remote(
            self.part(t), self.buf.at[at], self.send.at[t], self.recv.at[at], (to, self.p.s)
        )

    def got(self, at):
        here = self.buf.at[at]
        to = lax.rem(self.p.z + 1, self.p.pat)
        return remote(here, here, self.send.at[0], self.recv.at[at], (to, self.p.s))

    def start(self):
        last = self.p.pat - 1

        def up():
            for t in range(last, 0, -1):
                self.copy(0, t).start()

        def down():
            for t in range(last):
                self.copy(last, t).start()

        when(self.p.z == 0, up)
        when(self.p.z == last, down)

    def inner(self, hop):
        last = self.p.pat - 1
        for z in range(1, last):
            if z == hop:
                for t in range(last, z, -1):
                    yield z, t
            if last - z == hop:
                for t in range(z):
                    yield z, t

    def forward(self, hop):
        for z, t in self.inner(hop):

            def add(z=z, t=t):
                self.got(t).wait_recv()
                part = self.part(t)
                part[...] = (part[...].astype(F32) + self.buf[t].astype(F32)).astype(BF)
                self.copy(z, t).start()

            when(self.p.z == z, add)

    def total(self, out):
        p = self.p
        out[...] = self.part(p.z)[...].astype(F32)

        def below():
            self.got(p.z).wait_recv()
            out[...] += self.buf[p.z].astype(F32)

        def above():
            self.got(p.pat).wait_recv()
            out[...] += self.buf[p.pat].astype(F32)

        when(p.z > 0, below)
        when(p.z < p.pat - 1, above)

    def finish(self):
        last = self.p.pat - 1
        for t in range(last, 0, -1):
            when(self.p.z == 0, lambda t=t: self.copy(0, t).wait_send())
        for t in range(last):
            when(self.p.z == last, lambda t=t: self.copy(last, t).wait_send())
        for hop in range(1, last):
            for z, t in self.inner(hop):
                when(self.p.z == z, lambda z=z, t=t: self.copy(z, t).wait_send())


class PlaneGather:
    def __init__(self, place, piece, sems):
        self.p, self.piece, self.sems = place, piece, sems
        self.chips = place.n // 2

    def direct(self, k, owner):
        p, sems = self.p, self.sems
        to = lax.rem(p.s + 2 * k, p.n)
        return remote(
            self.piece(owner), self.piece(owner), sems[0].at[k - 1], sems[1].at[k - 1], (p.z, to)
        )

    def hand(self, k, owner):
        p, sems = self.p, self.sems
        return remote(
            self.piece(owner), self.piece(owner), sems[2].at[k], sems[3].at[k], (p.z, p.sib)
        )

    def source(self, base, k):
        return lax.rem(base + self.p.n - 2 * k, self.p.n)

    def start(self):
        for k in range(1, self.chips):
            self.direct(k, self.p.s).start()
        self.hand(0, self.p.s).start()

    def pass_on(self):
        for k in range(1, self.chips):
            owner = self.source(self.p.s, k)
            self.direct(k, owner).wait_recv()
            self.hand(k, owner).start()

    def arrive(self):
        for k in range(self.chips):
            self.hand(k, self.source(self.p.sib, k)).wait_recv()

    def finish(self):
        for k in range(1, self.chips):
            self.direct(k, self.p.s).wait_send()
        for k in range(self.chips):
            self.hand(k, self.source(self.p.s, k)).wait_send()


def line_sems(pat):
    return [pltpu.SemaphoreType.DMA((2, pat)), pltpu.SemaphoreType.DMA((pat,))]


def sum_sems(pat):
    return [pltpu.SemaphoreType.DMA((pat,)), pltpu.SemaphoreType.DMA((pat + 1,))]


def plane_sems(chips):
    return [pltpu.SemaphoreType.DMA((chips - 1,))] * 2 + [pltpu.SemaphoreType.DMA((chips,))] * 2


def vec_row(ref):
    return ref[...].reshape(1, -1)


def norm_rows(values, gain, shift):
    mean = jnp.mean(values, -1, keepdims=True)
    cen = values - mean
    var = jnp.mean(cen * cen, -1, keepdims=True)
    return cen * lax.rsqrt(var + EPS) * gain + shift


def norm_back(values, grad, gain):
    mean = jnp.mean(values, -1, keepdims=True)
    cen = values - mean
    inv = lax.rsqrt(jnp.mean(cen * cen, -1, keepdims=True) + EPS)
    hat = cen * inv
    dhat = grad * gain
    back = inv * (
        dhat - jnp.mean(dhat, -1, keepdims=True) - hat * jnp.mean(dhat * hat, -1, keepdims=True)
    )
    return (
        back,
        jnp.sum(grad * hat, 0, keepdims=True),
        jnp.sum(grad, 0, keepdims=True),
    )


def live_bias(first, second, base, length, shard):
    ok = jnp.logical_or(
        jnp.logical_and(second < first, second + base < length), second == first
    )
    return jnp.where(ok, 0.0, NEG)


class TreeSum:
    def __init__(self, place, grad, out, bufs, send, recv):
        self.p, self.grad, self.out, self.send, self.recv = place, grad, out, send, recv
        p = place
        bit_x = lax.rem(lax.div(p.s, 2), 2)
        bit_y = lax.div(p.s, 4)
        to_x = p.s + 2 - 4 * bit_x
        to_y = p.s + 4 - 8 * bit_y
        first = p.core == 0
        self.bits = [p.core, jnp.where(first, bit_x, bit_y), jnp.where(first, bit_y, bit_x)]
        self.to = [p.sib, jnp.where(first, to_x, to_y), jnp.where(first, to_y, to_x)]
        self.bufs = bufs
        self.off, self.size = [jnp.int32(0)], [grad.shape[0]]
        for d in range(3):
            h = self.size[d] // 2
            self.off.append(self.off[d] + self.bits[d] * h)
            self.size.append(h)

    def half_of(self, d, bit):
        h = self.size[d] // 2
        return rows_of(self.off[d] + bit * h, h)

    def red(self, d):
        src = self.grad.at[self.half_of(d, 1 - self.bits[d]), :]
        return remote(
            src, self.bufs[d], self.send.at[d], self.recv.at[d], (self.p.z, self.to[d])
        )

    def back(self, d, got):
        rows = self.half_of(d, (1 - self.bits[d]) if got else self.bits[d])
        return remote(
            self.out.at[rows, :],
            self.out.at[rows, :],
            self.send.at[3 + d],
            self.recv.at[3 + d],
            (self.p.z, self.to[d]),
        )

    def step(self, d):
        if d == 0:
            self.red(0).start()
        elif d <= 3:
            self.red(d - 1).wait_recv()
            rows = rows_of(self.off[d], self.size[d])
            total = self.grad[rows, :].astype(F32) + self.bufs[d - 1][...].astype(F32)
            if d < 3:
                self.grad[rows, :] = total.astype(BF)
                self.red(d).start()
            else:
                self.out[rows, :] = total.astype(BF)
                self.back(2, False).start()
        else:
            self.back(6 - d, True).wait_recv()
            if d < 6:
                self.back(5 - d, False).start()

    def finish(self):
        for d in range(3):
            self.red(d).wait_send()
            self.back(d, False).wait_send()


def layer_kernel(
    n,
    pat,
    levels,
    lens,
    gain1,
    shift1,
    wq,
    wk,
    wv,
    bq,
    bv,
    wout,
    bout,
    gain2,
    shift2,
    bup,
    bdown,
    perm,
    qext,
    ktab,
    x_hbm,
    wup_hbm,
    wdown_hbm,
    dout_hbm,
    outf,
    gif,
    gsum1,
    gsum2,
    vout,
    grad1,
    grad2,
    xp,
    n1,
    wp,
    qp,
    kvd,
    kvt,
    tab,
    acc,
    ack,
    attf,
    attw,
    den,
    wor,
    wup,
    wdown,
    state,
    sto,
    n2,
    act,
    dop,
    dh,
    dns,
    dnr,
    tot,
    dsl,
    dst,
    fd,
    fdr,
    qud,
    qut,
    crd,
    crt,
    uext,
    dqk,
    dms,
    dmr,
    a1,
    a2,
    a3,
    b1,
    b2,
    b3,
    vecs,
    vz,
    vs,
    *sems,
):
    batches, shard, width = xp.shape
    half = shard // 2
    quarter = shard // pat
    cols = wout.shape[0]
    heads = cols // HD
    units = batches * heads
    tiles = units // 2
    chips = n // 2
    sems = list(sems)
    take = lambda count: [sems.pop(0) for _ in range(count)]
    p = Place(n, pat)
    bar, greeted = p.greet(True, False, True)
    low, high = lane_masks()

    x_sem, load_sem, tab_sem = take(3)
    x_loads = [
        pltpu.make_async_copy(x_hbm.at[b], xp.at[b], x_sem.at[b]) for b in range(batches)
    ]
    loads = [
        pltpu.make_async_copy(src, dst, load_sem.at[i])
        for i, (src, dst) in enumerate(((dout_hbm, dop), (wup_hbm, wup), (wdown_hbm, wdown)))
    ]
    tabs = [
        pltpu.make_async_copy(ktab.at[heads * p.z + i], tab.at[i], tab_sem.at[i])
        for i in range(heads)
    ]
    for copy in x_loads + tabs + loads:
        copy.start()

    slot = lambda frm, at: lax.rem(frm - at + 2 * pat - 1, pat)
    own_slot = pat - 1
    out_rows, out_cols = cols // chips, width // 2

    def out_piece(dev, slots):
        chip, core = lax.div(dev, 2), lax.rem(dev, 2)
        return wor.at[
            slots,
            rows_of(HD + chip * out_rows, out_rows),
            pl.ds(pl.multiple_of(core * out_cols, 128), out_cols),
        ]

    def quarters(ref, b):
        return lambda f, *_: ref.at[b, rows_of(f * quarter, quarter), :]

    def share_pair(forward, dense, thin):
        out = []
        sems = take(6)
        for b in range(batches):
            out.append(
                Shares(
                    p,
                    shard,
                    forward,
                    lambda at, b=b: dense.at[
                        pl.ds(heads * b, heads), rows_of(at * shard, shard), :
                    ],
                    lambda dev, b=b: thin.at[pl.ds(heads * b, heads), rows_of(dev * half, half), :],
                    [sem.at[b] for sem in sems[:2]],
                    [sem.at[b] for sem in sems[2:]],
                )
            )
        return out

    rows = range(batches)
    kv_shares = share_pair(True, kvd, kvt)
    qu_shares = share_pair(False, qud, qut)
    cor_sems = take(6)
    cors = [
        Shares(
            p,
            shard,
            False,
            lambda at, b=b: crd.at[b, at],
            lambda dev, b=b: crt.at[b, dev],
            [sem.at[b] for sem in cor_sems[:2]],
            [sem.at[b] for sem in cor_sems[2:]],
        )
        for b in rows
    ]
    wo_line = LineGather(p, lambda f, t: out_piece(p.s, slot(f, t)), *take(2))
    wo_plane = PlaneGather(p, lambda dev: out_piece(dev, pl.ds(0, pat - 1)), take(4))
    att_line = [
        LineGather(p, lambda f, at, t=t: attf.at[f, t], *take(2)) for t in range(tiles)
    ]
    dn_sum = [LineSum(p, lambda t, b=b: dns.at[b, t], dnr.at[b], *take(2)) for b in rows]
    ds_line = [LineGather(p, quarters(dsl, b), *take(2)) for b in rows]
    fd_sum = [LineSum(p, quarters(fd, b), fdr.at[b], *take(2)) for b in rows]
    out_line = [LineGather(p, quarters(outf, b), *take(2)) for b in rows]
    dm_sum = [LineSum(p, lambda t, b=b: dms.at[b, t], dmr.at[b], *take(2)) for b in rows]
    gi_line = [LineGather(p, quarters(gif, b), *take(2)) for b in rows]
    sum1 = TreeSum(p, grad1, gsum1, (a1, a2, a3), *take(2))
    sum2 = TreeSum(p, grad2, gsum2, (b1, b2, b3), *take(2))
    z_send, z_recv, v_send, v_recv = take(4)
    zsp = Spread(p, z_send, z_recv)

    for r in range(pat):
        wor[r, 0:HD, :] = jnp.zeros((HD, width), BF)
        wor[r, HD + cols : 2 * HD + cols, :] = jnp.zeros((HD, width), BF)
    wor[own_slot, HD : HD + cols, :] = wout[...]
    zero_bias = jnp.zeros((1, HD), F32)
    bias_v, bias_q = vec_row(bv), vec_row(bq)
    bias = []
    for i in range(heads):
        wp[i * 128 : i * 128 + HD, :] = wk[i * HD : (i + 1) * HD, :]
        wp[i * 128 + HD : (i + 1) * 128, :] = wv[i * HD : (i + 1) * HD, :]
        bias += [zero_bias, bias_v[:, i * HD : (i + 1) * HD]]
    wp[2 * cols : 3 * cols, :] = wq[...]
    wp[3 * cols :, :] = jnp.zeros((wp.shape[0] - 3 * cols, width), BF)
    bias = jnp.concatenate(bias + [bias_q, zero_bias], 1)

    parity = [lax.rem(heads * p.z + i, 2) for i in range(heads)]
    own = rows_of(p.pos * shard, shard)
    zrows = rows_of(p.z * quarter, quarter)
    lane = lax.broadcasted_iota(jnp.int32, (shard, 128), 1)
    for b in rows:
        x_loads[b].wait()
        xb = nn(perm[...], xp[b])
        xp[b] = xb.astype(BF)
        n1[b] = norm_rows(xb, vec_row(gain1), vec_row(shift1)).astype(BF)
        qkv = nt(n1[b], wp[...]) + bias
        for i in range(heads):
            kv = qkv[:, i * 128 : (i + 1) * 128].astype(BF)
            kvd[heads * b + i, own, :] = kv
            t = heads + i // 2
            q = qkv[:, t * 128 : (t + 1) * 128]
            if i % 2 == 1:
                q = pltpu.roll(q, HD, 1)
            q = jnp.where(lane < HD, q, 0.0).astype(BF) * jnp.asarray(HD**-0.5, BF)
            qp[heads * b + i] = q
        for i in range(heads):
            kvt[heads * b + i, rows_of(p.s * half, half), :] = kvd[
                heads * b + i, rows_of(p.pos * shard + parity[i] * half, half), :
            ]
        if b == 0:
            pl.semaphore_wait(bar, greeted)
        kv_shares[b].start()
        if b == 0:
            wo_line.start()
    for copy in tabs:
        copy.wait()

    def attend(qx, kv, ext, bias):
        s = nt(qx, jnp.concatenate([kv, ext], 1))
        if bias is not None:
            s = s + bias
        return nn(jnp.exp(s).astype(BF), kv * high + low)

    first = token_of(lax.broadcasted_iota(jnp.int32, (shard, shard), 0), shard)
    second = token_of(lax.broadcasted_iota(jnp.int32, (shard, shard), 1), shard)

    def attend_own(b):
        bias = live_bias(first, second, p.s * shard, lens[b], shard)
        for i in range(heads):
            u = heads * b + i
            qx = jnp.concatenate([qp[u], qext[...]], 1)
            acc[u] = attend(qx, kvd[u, own, :], tab[i, 0], bias)

    def thin_keys(b, i, sg):
        level = level_of(sg, p.seg, levels)
        places = thin_positions(sg * SPAN1, parity[i], shard, SPAN1)
        lenl = length_lane(places, lens[b], SPAN1 * half)
        part = tab[i, level, rows_of(parity[i] * half, half), :]
        ext = jnp.concatenate([part] * SPAN1, 0) + lenl
        return kvt[heads * b + i, rows_of(sg * SPAN1 * half, SPAN1 * half), :], ext

    def attend_rest(b, which):
        def dense(j, carry):
            lenl = length_lane(dense_positions(p.seg * SPAN1 + j, shard), lens[b], shard)
            for i in which:
                u = heads * b + i
                qx = jnp.concatenate([qp[u], qext[...]], 1)
                kv = kvd[u, rows_of(j * shard, shard), :]
                acc[u] += attend(qx, kv, tab[i, 0] + lenl, None)
            return carry

        lax.fori_loop(0, p.pos, dense, 0)

        def thin(sg, carry):
            for i in which:
                u = heads * b + i
                mine = rows_of(parity[i] * half, half)
                kv, ext = thin_keys(b, i, sg)
                qx = jnp.concatenate([qp[u, mine, :], qext[mine, :]], 1)
                acc[u, mine, :] += attend(qx, kv, ext, None)
            return carry

        lax.fori_loop(0, p.seg, thin, 0)

    def send_tile(t):
        even, odd = acc[2 * t], acc[2 * t + 1]
        num = jnp.where(lane < HD, pltpu.roll(even, HD, 1), odd)
        dn = jnp.where(lane < HD, even, pltpu.roll(odd, HD, 1))
        wide = num / dn
        den[t] = dn
        attw[t] = wide
        attf[p.z, t] = wide.astype(BF)
        att_line[t].start()

    attend_own(0)
    wo_line.forward(1)
    attend_own(1)
    wo_line.forward(2)
    wo_line.arrive()
    bdown_sum = jnp.zeros((1, width), F32)
    loads[0].wait()
    for b in rows:
        dob = nn(perm[...], dop[b])
        dop[b] = dob.astype(BF)
        bdown_sum = bdown_sum + jnp.sum(dob, 0, keepdims=True)
    kv_shares[0].pass_on()
    kv_shares[0].arrive()
    attend_rest(0, range(heads))
    send_tile(0)
    kv_shares[1].pass_on()
    wo_plane.start()
    kv_shares[1].arrive()
    attend_rest(1, range(0, 1))
    send_tile(1)
    att_line[0].forward(1)
    attend_rest(1, range(1, heads))
    send_tile(2)
    att_line[0].forward(2)
    att_line[1].forward(1)
    wo_plane.pass_on()
    for copy in loads[1:]:
        copy.wait()
    wo_plane.arrive()
    att_line[1].forward(2)
    att_line[2].forward(1)

    def feed_in(b):
        mixed = xp[b].astype(F32) + vec_row(bout)
        for r in range(pat):
            z = lax.rem(p.z + 1 + r, pat)
            pair = jnp.concatenate([attf[z, b], attf[z, b + 1]], 1)
            weight = wor[r, HD : HD + 256, :] if b == 0 else wor[r, 0:256, :]
            mixed = mixed + nn(pair, weight)
        state[...] = mixed
        sto[b] = state[zrows, :]
        n2[b] = norm_rows(mixed, vec_row(gain2), vec_row(shift2)).astype(BF)

    def feed_out(b):
        hid = nn(n2[b], wup[...]) + vec_row(bup)
        th = jnp.tanh(ROOT * (hid + 0.044715 * (hid * hid * hid)))
        act[b] = (0.5 * hid * (1.0 + th)).astype(BF)
        slope = 0.5 * (1.0 + th) + 0.5 * hid * (1.0 - th * th) * (
            ROOT * (1.0 + 3.0 * 0.044715 * hid * hid)
        )
        dhid = (nt(dop[b], wdown[...]) * slope).astype(BF)
        dh[b] = dhid
        dn = nt(dhid, wup[...])
        for t in range(pat):
            dns[b, t] = dn[t * quarter : (t + 1) * quarter].astype(BF)
        dn_sum[b].start()
        return jnp.sum(dhid.astype(F32), 0, keepdims=True)

    att_line[0].arrive()
    att_line[1].arrive()
    feed_in(0)
    att_line[2].forward(2)
    bup_sum = feed_out(0)
    att_line[2].arrive()
    feed_in(1)
    dn_sum[0].forward(1)
    bup_sum = bup_sum + feed_out(1)
    dn_sum[0].forward(2)
    fd[0] = nn(act[0], wdown[...]).astype(BF)
    dn_sum[1].forward(1)
    bout_sum = jnp.zeros((1, width), F32)
    gain_sum = jnp.zeros((1, width), F32)
    shift_sum = jnp.zeros((1, width), F32)

    def state_grad(b, sums):
        dn_sum[b].total(tot)
        back, more_gain, more_shift = norm_back(sto[b], tot[...], vec_row(gain2))
        ds = dop[b, zrows, :].astype(F32) + back
        dst[b] = ds
        dsl[b, zrows, :] = ds.astype(BF)
        ds_line[b].start()
        return (
            sums[0] + jnp.sum(ds, 0, keepdims=True),
            sums[1] + more_gain,
            sums[2] + more_shift,
        )

    sums = state_grad(0, (bout_sum, gain_sum, shift_sum))
    fd[1] = nn(act[1], wdown[...]).astype(BF)
    dn_sum[1].forward(2)
    ds_line[0].forward(1)
    sums = state_grad(1, sums)
    up = tn(n2[0], dh[0])
    for b in range(1, batches):
        up = up + tn(n2[b], dh[b])
    grad1[0:width, :] = up.astype(BF)
    ds_line[0].forward(2)
    ds_line[1].forward(1)
    for b in rows:
        fd_sum[b].start()
    vecs[...] = jnp.zeros(vecs.shape, F32)
    for r, value in ((2, sums[0]), (3, sums[1]), (4, sums[2]), (5, bup_sum), (6, bdown_sum)):
        vecs[r : r + 1, :] = value

    row8 = lax.broadcasted_iota(jnp.int32, (8, 128), 0)
    lane8 = lax.broadcasted_iota(jnp.int32, (8, 128), 1)
    pick = jnp.where(row8 == lax.div(lane8, HD), 1.0, 0.0).astype(F32)
    ri = lax.broadcasted_iota(jnp.int32, (128, 128), 0)
    ci = lax.broadcasted_iota(jnp.int32, (128, 128), 1)
    same = jnp.where(lax.div(ri, HD) == lax.div(ci, HD), 1.0, 0.0).astype(F32)
    wo = wor.at[own_slot]

    def upstream(b):
        wide = nt(dsl[b], wo[HD : HD + 256, :] if b == 0 else wo[0:256, :])
        crd[b, p.pos] = jnp.zeros(crd.shape[2:], F32)
        crt[b, p.s] = jnp.zeros(crt.shape[2:], F32)
        for side in range(2):
            t = b + side
            datt = wide[:, side * 128 : (side + 1) * 128]
            dn = den[t]
            up = datt / dn
            prod = datt * attw[t] / dn
            cor = exact_nn(prod, same)
            cor_rows = exact_nt(pick, prod)
            for e in range(2):
                u = 2 * t + e
                if u // heads != b:
                    continue
                i = u % heads
                part = up if e == 1 else pltpu.roll(up, HD, 1)
                qud[u, own, :] = jnp.where(lane < HD, qp[u].astype(F32), part).astype(BF)
                qut[u, rows_of(p.s * half, half), :] = qud[
                    u, rows_of(p.pos * shard + parity[i] * half, half), :
                ]
                cor_row = cor_rows[e : e + 1, :]
                crd[b, p.pos, i : i + 1, :] = cor_row
                col = -cor[:, e * HD : e * HD + 1]
                lead = col.astype(BF).astype(F32)
                uext[u] = (
                    jnp.where(lane == COR_LANE, lead, 0.0)
                    + jnp.where(lane == COR_LANE + 1, col - lead, 0.0)
                ).astype(BF)
                crt[b, p.s, i : i + 1, :] = jnp.where(
                    parity[i] == 0, cor_row[:, 0:half], cor_row[:, half:shard]
                )
        qu_shares[b].start()
        cors[b].start()

    def query_side(qu, qe, ue, kv, ext, bias):
        kvx = jnp.concatenate([kv, ext], 1)
        s = nt(jnp.concatenate([qu * low, qe], 1), kvx)
        if bias is not None:
            s = s + bias
        dp = nt(jnp.concatenate([qu * high, ue], 1), kvx)
        return nn((jnp.exp(s) * dp).astype(BF), kv)

    def key_side(qu, qe, cor, kv, ext, bias):
        s = nt(jnp.concatenate([kv, ext], 1), jnp.concatenate([qu * low, qe], 1))
        if bias is not None:
            s = s + bias
        w = jnp.exp(s)
        dp = nt(kv, qu * high) - cor
        return nn((w * dp).astype(BF), qu * low) + nn(w.astype(BF), qu * high)

    def grads_own(b):
        bias = live_bias(first, second, p.s * shard, lens[b], shard)
        biast = live_bias(second, first, p.s * shard, lens[b], shard)
        for i in range(heads):
            u = heads * b + i
            kv, qu = kvd[u, own, :], qud[u, own, :]
            acc[u] = query_side(qu, qext[...], uext[u], kv, tab[i, 0], bias)
            ack[u] = key_side(qu, qext[...], crd[b, p.pos, i : i + 1, :], kv, tab[i, 0], biast)

    def query_rest(b):
        def dense(j, carry):
            lenl = length_lane(dense_positions(p.seg * SPAN1 + j, shard), lens[b], shard)
            for i in range(heads):
                u = heads * b + i
                kv = kvd[u, rows_of(j * shard, shard), :]
                acc[u] += query_side(
                    qud[u, own, :], qext[...], uext[u], kv, tab[i, 0] + lenl, None
                )
            return carry

        lax.fori_loop(0, p.pos, dense, 0)

        def thin(sg, carry):
            for i in range(heads):
                u = heads * b + i
                mine = rows_of(parity[i] * half, half)
                kv, ext = thin_keys(b, i, sg)
                qu = qut[u, rows_of(p.s * half, half), :]
                acc[u, mine, :] += query_side(qu, qext[mine, :], uext[u, mine, :], kv, ext, None)
            return carry

        lax.fori_loop(0, p.seg, thin, 0)

    def key_rest(b):
        lenl = length_lane(dense_positions(p.s, shard), lens[b], shard)

        def dense(j, carry):
            for i in range(heads):
                u = heads * b + i
                qu = qud[u, rows_of(j * shard, shard), :]
                ack[u] += key_side(
                    qu, qext[...], crd[b, j, i : i + 1, :], kvd[u, own, :], tab[i, 0] + lenl, None
                )
            return carry

        lax.fori_loop(p.pos + 1, SPAN1, dense, 0)

        def thin(dev, carry):
            level = level_of(lax.div(dev, SPAN1), p.seg, levels)
            for i in range(heads):
                u = heads * b + i
                mine = rows_of(parity[i] * half, half)
                ext = tab[i, level, mine, :] + length_lane(
                    thin_positions(p.s, parity[i], shard, 1), lens[b], half
                )
                kv = kvt[u, rows_of(p.s * half, half), :]
                qu = qut[u, rows_of(dev * half, half), :]
                ack[u, mine, :] += key_side(
                    qu, qext[mine, :], crt[b, dev, i : i + 1, :], kv, ext, None
                )
            return carry

        lax.fori_loop(SPAN1 * (p.seg + 1), n, thin, 0)

    def send_grads(b):
        for i in range(heads):
            dqk[b, :, i * 128 : (i + 1) * 128] = ack[heads * b + i].astype(BF)
        for t in range((heads + 1) // 2):
            tile = acc[heads * b + 2 * t]
            if 2 * t + 1 < heads:
                other = pltpu.roll(acc[heads * b + 2 * t + 1], HD, 1)
            else:
                other = jnp.zeros((shard, 128), F32)
            tile = jnp.where(lane < HD, tile, other) * HD**-0.5
            at = (heads + t) * 128
            dqk[b, :, at : at + 128] = tile.astype(BF)
        dm = nn(dqk[b], wp[...])
        for t in range(pat):
            dms[b, t] = dm[t * quarter : (t + 1) * quarter].astype(BF)
        dm_sum[b].start()

    ds_line[0].arrive()
    upstream(0)
    ds_line[1].forward(2)
    down = tn(act[0], dop[0])
    for b in range(1, batches):
        down = down + tn(act[b], dop[b])
    grad1[width : 2 * width, :] = down.astype(BF)
    sum1.step(0)
    ds_line[1].arrive()
    upstream(1)
    sum1.step(1)
    grads_own(0)
    for b in rows:
        fd_sum[b].forward(1)
    grads_own(1)
    for b in rows:
        fd_sum[b].forward(2)
    query_rest(0)
    cors[0].pass_on()
    qu_shares[0].pass_on()
    query_rest(1)
    cors[1].pass_on()
    qu_shares[1].pass_on()
    for b in rows:
        fd_sum[b].total(tot)
        outf[b, zrows, :] = (sto[b] + tot[...] + vec_row(bdown)).astype(BF)
        out_line[b].start()
    cors[0].arrive()
    qu_shares[0].arrive()
    key_rest(0)
    send_grads(0)
    sum1.step(2)
    for b in rows:
        out_line[b].forward(1)
    cors[1].arrive()
    qu_shares[1].arrive()
    key_rest(1)
    send_grads(1)

    dm_sum[0].forward(1)
    sum1.step(3)
    dm_sum[0].forward(2)
    left = tn(jnp.concatenate([attf[p.z, 0], attf[p.z, 1]], 1), dsl[0])
    right = tn(jnp.concatenate([attf[p.z, 1], attf[p.z, 2]], 1), dsl[1])
    grad2[3 * cols : 4 * cols, :] = (left[0:cols] + right[HD : HD + cols]).astype(BF)
    dm_sum[1].forward(1)
    packed = tn(dqk[0], n1[0])
    for b in range(1, batches):
        packed = packed + tn(dqk[b], n1[b])
    grad2[0 : 3 * cols, :] = packed[0 : 3 * cols].astype(BF)
    sum2.step(0)
    sum1.step(4)
    for b in rows:
        out_line[b].forward(2)

    def close(b, sums):
        dm_sum[b].total(tot)
        back, more_gain, more_shift = norm_back(
            xp[b, zrows, :].astype(F32), tot[...], vec_row(gain1)
        )
        gif[b, zrows, :] = (dst[b] + back).astype(BF)
        gi_line[b].start()
        return sums[0] + more_gain, sums[1] + more_shift

    zero = jnp.zeros((1, width), F32)
    sums = close(0, (zero, zero))
    dm_sum[1].forward(2)
    sum2.step(1)
    sum1.step(5)
    gi_line[0].forward(1)
    sums = close(1, sums)
    v0, v1 = vs.at[0], vs.at[1]
    v0[...] = vecs[...]
    v0[0:1, :] = sums[0]
    v0[1:2, :] = sums[1]
    for k in range(1, pat):
        zsp.copy_to(k, v0, vz.at[k - 1]).start()
    qkv_sum = jnp.zeros((1, wp.shape[0]), F32)
    for b in rows:
        qkv_sum = qkv_sum + jnp.sum(dqk[b].astype(F32), 0, keepdims=True)
    sum2.step(2)
    gi_line[0].forward(2)
    gi_line[1].forward(1)
    for k in range(1, pat):
        zsp.copy_to(k, v0, vz.at[k - 1]).wait_recv()
    row = lax.broadcasted_iota(jnp.int32, (8, width), 0)
    extra = vz[0]
    for k in range(2, pat):
        extra = extra + vz[k - 1]
    v1[...] = v0[...] + jnp.where(row < 5, extra, 0.0)
    v1[7:8, 0 : wp.shape[0]] = qkv_sum

    def vec_copy(k):
        to = lax.rem(p.s + k, n)
        return remote(v1, vs.at[k + 1], v_send.at[k - 1], v_recv.at[k - 1], (p.z, to))

    for k in range(1, n):
        vec_copy(k).start()
    sum2.step(3)
    gi_line[1].forward(2)
    sum1.step(6)
    sum2.step(4)
    sum2.step(5)
    for k in range(1, n):
        vec_copy(k).wait_recv()
    allv = v1[...]
    for k in range(1, n):
        allv = allv + vs[k + 1]
    vout[...] = allv
    sum2.step(6)
    for b in rows:
        out_line[b].arrive()
        gi_line[b].arrive()
    for item in [*kv_shares, *qu_shares, *cors, wo_line, wo_plane, *att_line, *dn_sum, *ds_line]:
        item.finish()
    for item in [*fd_sum, *out_line, *dm_sum, *gi_line, sum1, sum2]:
        item.finish()
    for k in range(1, pat):
        zsp.copy_to(k, v0, vz.at[k - 1]).wait_send()
    for k in range(1, n):
        vec_copy(k).wait_send()


def finish_kernel(
    heads,
    outf,
    gif,
    gsum1,
    gsum2,
    vin,
    permt,
    outp,
    ginp,
    gup,
    gdown,
    gout,
    gq,
    gk,
    gv,
    gain1,
    shift1,
    bq,
    bv,
    bout,
    gain2,
    shift2,
    bup,
    bdown,
):
    batches, _, width = outf.shape
    cols = heads * HD
    for b in range(batches):
        outp[b] = nn(permt[...], outf[b]).astype(BF)
        ginp[b] = nn(permt[...], gif[b]).astype(BF)
    gup[...] = gsum1[0:width, :].astype(F32)
    gdown[...] = gsum1[width : 2 * width, :].astype(F32)
    gout[...] = gsum2[3 * cols : 4 * cols, :].astype(F32)
    k_rows = [gsum2[i * 128 : i * 128 + HD, :] for i in range(heads)]
    v_rows = [gsum2[i * 128 + HD : (i + 1) * 128, :] for i in range(heads)]
    gq[...] = gsum2[2 * cols : 3 * cols, :].astype(F32)
    gk[...] = jnp.concatenate(k_rows, 0).astype(F32)
    gv[...] = jnp.concatenate(v_rows, 0).astype(F32)
    for r, ref in enumerate((gain1, shift1, bout, gain2, shift2, bup, bdown)):
        ref[...] = vin[r : r + 1, :].reshape(width)
    bq[...] = vin[7:8, 2 * cols : 3 * cols].reshape(cols)
    bv[...] = jnp.concatenate(
        [vin[7:8, i * 128 + HD : (i + 1) * 128] for i in range(heads)], 1
    ).reshape(cols)


def plane_program(
    n,
    pat,
    inputs,
    lengths,
    gain_one,
    shift_one,
    w_query,
    b_query,
    w_key,
    w_value,
    b_value,
    w_out,
    b_out,
    gain_two,
    shift_two,
    w_up,
    b_up,
    w_down,
    b_down,
    d_output,
):
    B, S, W = inputs.shape
    cols = w_query.shape[1]
    hidden = w_up.shape[1]
    heads = cols // HD
    units = B * heads
    tiles = units // 2
    chips = n // 2
    half = S // 2
    quarter = S // pat
    levels = 1
    while SPAN1 << (levels - 1) < n:
        levels += 1
    perm = jnp.asarray(perm_matrix(S), BF)
    permt = jnp.asarray(perm_matrix(S).T, BF)
    qext = jnp.asarray(query_ext(S), BF)
    ktab = jnp.asarray(key_tables(S, heads * pat, levels))
    wide = 3 * cols + (-3 * cols) % 128
    r1, r2 = 2 * W, 4 * cols
    vm, sm, anyv = pltpu.VMEM, pltpu.SMEM, pl.ANY
    dma = pltpu.SemaphoreType.DMA

    outf, gif, gsum1, gsum2, vout = call(
        functools.partial(layer_kernel, n, pat, levels),
        "layer",
        [((B, S, W), BF), ((B, S, W), BF), ((r1, W), BF), ((r2, W), BF), ((8, W), F32)],
        [
            vm((r1, W), BF),
            vm((r2, W), BF),
            vm((B, S, W), BF),
            vm((B, S, W), BF),
            vm((wide, W), BF),
            vm((units, S, 128), BF),
            vm((units, SPAN1 * S, 128), BF),
            vm((units, n * half, 128), BF),
            vm((heads, levels, S, 128), BF),
            vm((units, S, 128), F32),
            vm((units, S, 128), F32),
            vm((pat, tiles, S, 128), BF),
            vm((tiles, S, 128), F32),
            vm((tiles, S, 128), F32),
            vm((pat, cols + 2 * HD, W), BF),
            vm(w_up.shape, BF),
            vm(w_down.shape, BF),
            vm((S, W), F32),
            vm((B, quarter, W), F32),
            vm((B, S, W), BF),
            vm((B, S, hidden), BF),
            vm((B, S, W), BF),
            vm((B, S, hidden), BF),
            vm((B, pat, quarter, W), BF),
            vm((B, pat + 1, quarter, W), BF),
            vm((quarter, W), F32),
            vm((B, S, W), BF),
            vm((B, quarter, W), F32),
            vm((B, S, W), BF),
            vm((B, pat + 1, quarter, W), BF),
            vm((units, SPAN1 * S, 128), BF),
            vm((units, n * half, 128), BF),
            vm((B, SPAN1, 8, S), F32),
            vm((B, n, 8, half), F32),
            vm((units, S, 128), BF),
            vm((B, S, wide), BF),
            vm((B, pat, quarter, W), BF),
            vm((B, pat + 1, quarter, W), BF),
        ]
        + [vm((r1 >> d, W), BF) for d in (1, 2, 3)]
        + [vm((r2 >> d, W), BF) for d in (1, 2, 3)]
        + [vm((8, W), F32), vm((pat - 1, 8, W), F32), vm((n + 1, 8, W), F32)]
        + [dma((B,)), dma((3,)), dma((heads,))]
        + (dense_sems(B) + thin_sems(B, chips)) * 3
        + line_sems(pat)
        + plane_sems(chips)
        + line_sems(pat) * tiles
        + (sum_sems(pat) * B + line_sems(pat) * B) * 3
        + [dma((6,))] * 4
        + [dma((pat - 1,))] * 2
        + [dma((n - 1,))] * 2,
        [sm] + [vm] * 15 + [anyv] * 5,
        0,
    )(
        lengths,
        gain_one,
        shift_one,
        w_query.T,
        w_key.T,
        w_value.T,
        b_query,
        b_value,
        w_out,
        b_out,
        gain_two,
        shift_two,
        b_up,
        b_down,
        perm,
        qext,
        ktab,
        inputs,
        w_up,
        w_down,
        d_output,
    )

    outs = [((B, S, W), BF)] * 2
    outs += [((W, W), F32)] * 2 + [((cols, W), F32)] * 4
    outs += [((W,), F32)] * 2 + [((cols,), F32)] * 2 + [((W,), F32)] * 5
    res = pl.pallas_call(
        functools.partial(finish_kernel, heads),
        name="results",
        out_shape=[jax.ShapeDtypeStruct(s, d) for s, d in outs],
        compiler_params=pltpu.CompilerParams(vmem_limit_bytes=62 << 20),
    )(outf, gif, gsum1, gsum2, vout, permt)
    outputs, grad_inputs, g_up, g_down, g_out, g_q, g_k, g_v = res[:8]
    gain1, shift1, bq, bv, bout, gain2, shift2, bup, bdown = res[8:]
    return (
        outputs,
        grad_inputs,
        gain1,
        shift1,
        g_q.T,
        bq,
        g_k.T,
        g_v.T,
        bv,
        g_out,
        bout,
        gain2,
        shift2,
        g_up,
        bup,
        g_down,
        bdown,
    )


def solution(mesh):
    token = P(None, "seq", None)
    in_specs = (
        token,
        P(),
        P(),
        P(),
        P(None, "pat"),
        P("pat"),
        P(None, "pat"),
        P(None, "pat"),
        P("pat"),
        P("pat", None),
        P(),
        P(),
        P(),
        P(None, "pat"),
        P("pat"),
        P("pat", None),
        P(),
        token,
    )
    out_specs = (
        token,
        token,
        P(),
        P(),
        P(None, "pat"),
        P("pat"),
        P(None, "pat"),
        P(None, "pat"),
        P("pat"),
        P("pat", None),
        P(),
        P(),
        P(),
        P(None, "pat"),
        P("pat"),
        P("pat", None),
        P(),
    )
    n, pat = mesh.shape["seq"], mesh.shape["pat"]
    body = functools.partial(plane_program if n == 8 else shards, n, pat)
    return jax.shard_map(body, mesh=mesh, in_specs=in_specs, out_specs=out_specs, check_vma=False)
```

```python
import functools

import jax
import jax.numpy as jnp
import numpy as np
from jax import lax
from jax.experimental import pallas as pl
from jax.experimental.pallas import tpu as pltpu
from jax.sharding import PartitionSpec as P

HD = 64
SPAN1 = 4
DILATIONS = (1, 2, 4, 6, 12)
CYCLE = 12
EPS = 1e-05
NEG = -1e30
LEN_LANE = 24
COR_LANE = 25
MESH = pl.DeviceIdType.MESH
BF = jnp.bfloat16
F32 = jnp.float32
ROOT = float(np.sqrt(2.0 / np.pi))


def nn(a, b):
    return lax.dot_general(a, b, (((1,), (0,)), ((), ())), preferred_element_type=F32)


def nt(a, b):
    return lax.dot_general(a, b, (((1,), (1,)), ((), ())), preferred_element_type=F32)


def tn(a, b):
    return lax.dot_general(a, b, (((0,), (0,)), ((), ())), preferred_element_type=F32)


def exact_nt(a, b):
    return lax.dot_general(
        a, b, (((1,), (1,)), ((), ())), preferred_element_type=F32, precision=lax.Precision.HIGHEST
    )


def exact_nn(a, b):
    return lax.dot_general(
        a, b, (((1,), (0,)), ((), ())), preferred_element_type=F32, precision=lax.Precision.HIGHEST
    )


def remote(src, dst, send, recv, device):
    return pltpu.make_async_remote_copy(
        src_ref=src,
        dst_ref=dst,
        send_sem=send,
        recv_sem=recv,
        device_id=device,
        device_id_type=MESH,
    )


def when(cond, fn):
    pl.when(cond)(fn)


def rows_of(start, size):
    return pl.ds(pl.multiple_of(start, 16), size)


def orders(shard):
    p = np.arange(shard)
    return 2 * (p % (shard // 2)) + p // (shard // 2)


def perm_matrix(shard):
    token = orders(shard)
    m = np.zeros((shard, shard), np.float32)
    m[np.arange(shard), token] = 1.0
    return m


def query_ext(shard):
    cls = orders(shard) % CYCLE
    m = np.zeros((shard, 128), np.float32)
    m[np.arange(shard), cls] = 1.0
    m[np.arange(shard), CYCLE + cls] = 1.0
    m[:, LEN_LANE] = 1.0
    return m


def key_tables(shard, heads, levels):
    cls = orders(shard) % CYCLE
    out = np.zeros((heads, levels, shard, 128), np.float32)
    for h in range(heads):
        for level in range(levels):
            count = np.zeros((CYCLE, CYCLE))
            for r in DILATIONS[level:]:
                on = (np.arange(CYCLE) % r == h % r).astype(np.float64)
                count += on[:, None] * on[None, :]
            with np.errstate(divide="ignore"):
                log = np.log(count)
            high = np.where(count > 0, log, NEG).astype(np.float32).astype(jnp.bfloat16)
            low = np.where(count > 0, log - high.astype(np.float64), 0.0)
            out[h, level, :, :CYCLE] = high.astype(np.float32)[:, cls].T
            out[h, level, :, CYCLE : 2 * CYCLE] = low[:, cls].T
            out[h, level, :, COR_LANE] = 1.0
            out[h, level, :, COR_LANE + 1] = 1.0
    return out.astype(jnp.bfloat16)


class Place:
    def __init__(self, n, pat):
        self.n, self.pat = n, pat
        self.z = lax.axis_index("pat")
        self.s = lax.axis_index("seq")
        self.core = lax.rem(self.s, 2)
        self.chip = lax.div(self.s, 2)
        self.seg = lax.div(self.s, SPAN1)
        self.pos = lax.rem(self.s, SPAN1)
        self.sib = self.s + 1 - 2 * self.core
        self.even = lax.rem(self.chip, 2) == 0

    def other_z(self, k):
        return lax.rem(self.z + k, self.pat)

    def greet(self, z_axis, same_core, all_seq=False):
        bar = pltpu.get_barrier_semaphore()
        count = 0
        if z_axis:
            for k in range(1, self.pat):
                pl.semaphore_signal(
                    bar, inc=1, device_id=(self.other_z(k), self.s), device_id_type=MESH
                )
                count += 1
        if all_seq:
            for k in range(1, self.n):
                to = lax.rem(self.s + k, self.n)
                pl.semaphore_signal(bar, inc=1, device_id=(self.z, to), device_id_type=MESH)
                count += 1
        elif same_core:
            pl.semaphore_signal(bar, inc=1, device_id=(self.z, self.sib), device_id_type=MESH)
            count += 1
            for k in range(1, self.n // 2):
                to = lax.rem(self.s + 2 * k, self.n)
                pl.semaphore_signal(bar, inc=1, device_id=(self.z, to), device_id_type=MESH)
                count += 1
        return bar, count


def lane_masks():
    lane = lax.broadcasted_iota(jnp.int32, (1, 128), 1)
    low = jnp.where(lane < HD, 1.0, 0.0)
    return low.astype(BF), (1.0 - low).astype(BF)


def token_of(index, shard):
    half = jnp.where(index >= shard // 2, 1, 0)
    return 2 * (index - half * (shard // 2)) + half


def length_lane(positions, length, rows):
    lane = lax.broadcasted_iota(jnp.int32, (rows, 128), 1)
    hit = jnp.logical_and(lane == LEN_LANE, positions >= length)
    return jnp.where(hit, NEG, 0.0).astype(BF)


def dense_positions(device, shard):
    row = lax.broadcasted_iota(jnp.int32, (shard, 128), 0)
    return device * shard + token_of(row, shard)


def thin_positions(first_device, parity, shard, blocks):
    half = shard // 2
    row = lax.broadcasted_iota(jnp.int32, (blocks * half, 128), 0)
    block = lax.div(row, half)
    return (first_device + block) * shard + 2 * (row - block * half) + parity


def level_of(seg_a, seg_b, levels):
    level = jnp.int32(1)
    size = 2
    for _ in range(2, levels):
        apart = lax.div(seg_a, size) != lax.div(seg_b, size)
        level = level + jnp.where(apart, 1, 0)
        size *= 2
    return level


class Shares:
    def __init__(self, place, shard, forward, dense, thin, dense_sems, thin_sems):
        self.p, self.shard, self.forward = place, shard, forward
        self.dense, self.thin = dense, thin
        self.ds, self.ts = dense_sems, thin_sems
        p = place
        self.chips = p.n // 2
        if forward:
            self.sib_sends, self.sib_gets = p.core == 0, p.core == 1
            self.x_sends, self.x_gets = p.even, jnp.logical_not(p.even)
            self.x_to, self.x_slot = p.s + 2, p.pos - 2
        else:
            self.sib_sends, self.sib_gets = p.core == 1, p.core == 0
            self.x_sends, self.x_gets = jnp.logical_not(p.even), p.even
            self.x_to, self.x_slot = p.s - 2, p.pos + 2
        self.sib_pos = p.pos + 1 - 2 * p.core
        self.x_sib_slot = self.x_slot + 1 - 2 * p.core

    def sib_copy(self, slot):
        p = self.p
        return remote(
            self.dense(slot), self.dense(slot), self.ds[0].at[0], self.ds[1].at[0], (p.z, p.sib)
        )

    def x_copy(self, slot):
        p = self.p
        to = jnp.where(self.x_sends, self.x_to, p.sib)
        return remote(
            self.dense(slot), self.dense(slot), self.ds[0].at[1], self.ds[1].at[1], (p.z, to)
        )

    def hand_copy(self, slot):
        p = self.p
        return remote(
            self.dense(slot), self.dense(slot), self.ds[0].at[2], self.ds[1].at[2], (p.z, p.sib)
        )

    def thin_to(self, chip):
        seg = chip // 2
        return (seg > self.p.seg) if self.forward else (seg < self.p.seg)

    def thin_from(self, chip):
        seg = chip // 2
        return (seg < self.p.seg) if self.forward else (seg > self.p.seg)

    def thin_copy(self, chip):
        p = self.p
        return remote(
            self.thin(p.s),
            self.thin(p.s),
            self.ts[0].at[chip],
            self.ts[1].at[p.chip],
            (p.z, 2 * chip + p.core),
        )

    def thin_got(self, chip):
        p = self.p
        slot = 2 * chip + p.core
        return remote(
            self.thin(slot), self.thin(slot), self.ts[0].at[chip], self.ts[1].at[chip], (p.z, p.sib)
        )

    def thin_hand(self, chip, mine):
        p = self.p
        slot = 2 * chip + (p.core if mine else 1 - p.core)
        return remote(
            self.thin(slot), self.thin(slot), self.ts[2].at[chip], self.ts[3].at[chip], (p.z, p.sib)
        )

    def start(self):
        p = self.p
        for chip in range(self.chips - 1, -1, -1) if self.forward else range(self.chips):
            when(self.thin_to(chip), lambda chip=chip: self.thin_copy(chip).start())
        when(self.x_sends, lambda: self.x_copy(p.pos).start())
        when(self.sib_sends, lambda: self.sib_copy(p.pos).start())

    def pass_on(self):
        def dense_part():
            self.x_copy(self.x_slot).wait_recv()
            self.hand_copy(self.x_slot).start()

        when(self.x_gets, dense_part)
        for chip in range(self.chips):

            def thin_part(chip=chip):
                self.thin_got(chip).wait_recv()
                self.thin_hand(chip, True).start()

            when(self.thin_from(chip), thin_part)

    def arrive(self):
        when(self.sib_gets, lambda: self.sib_copy(self.sib_pos).wait_recv())
        when(self.x_gets, lambda: self.hand_copy(self.x_sib_slot).wait_recv())
        for chip in range(self.chips):
            when(
                self.thin_from(chip),
                lambda chip=chip: self.thin_hand(chip, False).wait_recv(),
            )

    def finish(self):
        p = self.p
        when(self.x_sends, lambda: self.x_copy(p.pos).wait_send())
        when(self.sib_sends, lambda: self.sib_copy(p.pos).wait_send())
        when(self.x_gets, lambda: self.hand_copy(self.x_slot).wait_send())
        for chip in range(self.chips):
            when(self.thin_to(chip), lambda chip=chip: self.thin_copy(chip).wait_send())
            when(self.thin_from(chip), lambda chip=chip: self.thin_hand(chip, True).wait_send())


def dense_sems(batches):
    return [pltpu.SemaphoreType.DMA((batches, 3))] * 2


def thin_sems(batches, chips):
    return [pltpu.SemaphoreType.DMA((batches, chips))] * 4


class Spread:
    def __init__(self, place, send, recv):
        self.p, self.send, self.recv = place, send, recv

    def copy_to(self, k, src, dst):
        p = self.p
        return remote(src, dst, self.send.at[k - 1], self.recv.at[k - 1], (p.other_z(k), p.s))


def forward_kernel(
    n,
    pat,
    levels,
    lens,
    x_ref,
    gain,
    shift,
    wq,
    bq,
    wkv,
    bkv,
    wout,
    perm,
    qext,
    ktab,
    xp,
    n1,
    qp,
    kvd,
    kvt,
    attf,
    wofp,
    attw,
    den,
    tab,
    acc,
    tab_sem,
    w_send,
    w_recv,
    a_send,
    a_recv,
    ds0,
    ds1,
    ts0,
    ts1,
    ts2,
    ts3,
):
    batches, shard, width = x_ref.shape
    half = shard // 2
    heads = wout.shape[0] // HD
    units = batches * heads
    p = Place(n, pat)
    bar, greeted = p.greet(True, True)
    low, high = lane_masks()

    def tab_copy(i):
        return pltpu.make_async_copy(ktab.at[heads * p.z + i], tab.at[i], tab_sem.at[i])

    for i in range(heads):
        tab_copy(i).start()
    for z in range(pat):
        wofp[z, 0:HD, :] = jnp.zeros((HD, width), BF)
        wofp[z, HD + heads * HD : 2 * HD + heads * HD, :] = jnp.zeros((HD, width), BF)
    wofp[p.z, HD : HD + heads * HD, :] = wout[...]
    for b in range(batches):
        xb = nn(perm[...], x_ref[b])
        xp[b] = xb.astype(BF)
        mean = jnp.mean(xb, -1, keepdims=True)
        cen = xb - mean
        var = jnp.mean(cen * cen, -1, keepdims=True)
        n1[b] = (cen * lax.rsqrt(var + EPS) * gain[...] + shift[...]).astype(BF)

    shares = [
        Shares(
            p,
            shard,
            True,
            lambda slot, b=b: kvd.at[pl.ds(heads * b, heads), rows_of(slot * shard, shard), :],
            lambda dev, b=b: kvt.at[pl.ds(heads * b, heads), rows_of(dev * half, half), :],
            [ds0.at[b], ds1.at[b]],
            [ts0.at[b], ts1.at[b], ts2.at[b], ts3.at[b]],
        )
        for b in range(batches)
    ]
    parity = [lax.rem(heads * p.z + i, 2) for i in range(heads)]
    for b in range(batches):
        q = ((nn(n1[b], wq[...]) + bq[...]).astype(BF)) * jnp.asarray(HD**-0.5, BF)
        kv = (nn(n1[b], wkv[...]) + bkv[...]).astype(BF)
        for i in range(heads):
            qp[heads * b + i] = q[:, i * 128 : (i + 1) * 128]
            kvd[heads * b + i, rows_of(p.pos * shard, shard), :] = kv[:, i * 128 : (i + 1) * 128]
        for i in range(heads):
            kvt[heads * b + i, rows_of(p.s * half, half), :] = kvd[
                heads * b + i, rows_of(p.pos * shard + parity[i] * half, half), :
            ]
        if b == 0:
            pl.semaphore_wait(bar, greeted)
        shares[b].start()
    w_spread = Spread(p, w_send, w_recv)

    def w_slot(z):
        return wofp.at[z, HD : HD + heads * HD, :]

    for k in range(1, pat):
        w_spread.copy_to(k, w_slot(p.z), w_slot(p.z)).start()
    for i in range(heads):
        tab_copy(i).wait()

    def attend(qx, kv, ext, bias):
        s = nt(qx, jnp.concatenate([kv, ext], 1))
        if bias is not None:
            s = s + bias
        return nn(jnp.exp(s).astype(BF), kv * high + low)

    own = rows_of(p.pos * shard, shard)
    qi = lax.broadcasted_iota(jnp.int32, (shard, shard), 0)
    ki = lax.broadcasted_iota(jnp.int32, (shard, shard), 1)
    qt, kt = token_of(qi, shard), token_of(ki, shard)
    for b in range(batches):
        live = jnp.logical_or(
            jnp.logical_and(kt < qt, kt + p.s * shard < lens[b]), kt == qt
        )
        bias = jnp.where(live, 0.0, NEG)
        for i in range(heads):
            u = heads * b + i
            qx = jnp.concatenate([qp[u], qext[...]], 1)
            acc[u] = attend(qx, kvd[u, own, :], tab[i, 0], bias)

    att_spread = [Spread(p, a_send.at[t], a_recv.at[t]) for t in range(units // 2)]
    lane = lax.broadcasted_iota(jnp.int32, (shard, 128), 1)
    for b in range(batches):
        shares[b].pass_on()
        shares[b].arrive()

        def dense(j, carry, b=b):
            lenl = length_lane(dense_positions(p.seg * SPAN1 + j, shard), lens[b], shard)
            for i in range(heads):
                u = heads * b + i
                qx = jnp.concatenate([qp[u], qext[...]], 1)
                kv = kvd[u, rows_of(j * shard, shard), :]
                acc[u] += attend(qx, kv, tab[i, 0] + lenl, None)
            return carry

        lax.fori_loop(0, p.pos, dense, 0)

        def thin(sg, carry, b=b):
            level = level_of(sg, p.seg, levels)
            for i in range(heads):
                u = heads * b + i
                mine = rows_of(parity[i] * half, half)
                places = thin_positions(sg * SPAN1, parity[i], shard, SPAN1)
                lenl = length_lane(places, lens[b], SPAN1 * half)
                ext = jnp.concatenate([tab[i, level, mine, :]] * SPAN1, 0) + lenl
                qx = jnp.concatenate([qp[u, mine, :], qext[mine, :]], 1)
                kv = kvt[u, rows_of(sg * SPAN1 * half, SPAN1 * half), :]
                acc[u, mine, :] += attend(qx, kv, ext, None)
            return carry

        lax.fori_loop(0, p.seg, thin, 0)
        for t in range(units // 2):
            if (2 * t + 1) // heads != b:
                continue
            even, odd = acc[2 * t], acc[2 * t + 1]
            num = jnp.where(lane < HD, pltpu.roll(even, HD, 1), odd)
            dn = jnp.where(lane < HD, even, pltpu.roll(odd, HD, 1))
            wide = num / dn
            den[t] = dn
            attw[t] = wide
            attf[p.z, t] = wide.astype(BF)
            for k in range(1, pat):
                att_spread[t].copy_to(k, attf.at[p.z, t], attf.at[p.z, t]).start()
    for k in range(1, pat):
        frm = lax.rem(p.z + pat - k, pat)
        w_spread.copy_to(k, w_slot(p.z), w_slot(p.z)).wait_send()
        w_spread.copy_to(k, w_slot(frm), w_slot(frm)).wait_recv()
        for t in range(units // 2):
            att_spread[t].copy_to(k, attf.at[p.z, t], attf.at[p.z, t]).wait_send()
            att_spread[t].copy_to(k, attf.at[frm, t], attf.at[frm, t]).wait_recv()
    for b in range(batches):
        shares[b].finish()


def middle_kernel(
    n,
    pat,
    xp,
    attf,
    wofp,
    bout,
    gain,
    shift,
    wup,
    bup,
    wdown,
    dout,
    perm,
    gud,
    fd,
    dsf,
    dst,
    sto,
    vecs,
    state,
    n2,
    act,
    dop,
    dh,
    dns,
    dno,
    dnr,
    r_send,
    r_recv,
    g_send,
    g_recv,
):
    batches, shard, width = xp.shape
    quarter = shard // pat
    p = Place(n, pat)
    bar, greeted = p.greet(True, False)
    rs = [Spread(p, r_send.at[b], r_recv.at[b]) for b in range(batches)]
    ag = [Spread(p, g_send.at[b], g_recv.at[b]) for b in range(batches)]
    bup_sum = jnp.zeros((1, width), F32)
    bdown_sum = jnp.zeros((1, width), F32)
    for b in range(batches):
        mixed = jnp.zeros((shard, width), F32)
        for z in range(pat):
            pair = jnp.concatenate([attf[z, b], attf[z, b + 1]], 1)
            weight = wofp[z, HD : HD + 256, :] if b == 0 else wofp[z, 0:256, :]
            mixed = mixed + nn(pair, weight)
        st = xp[b].astype(F32) + mixed + bout[...]
        state[b] = st
        mean = jnp.mean(st, -1, keepdims=True)
        cen = st - mean
        var = jnp.mean(cen * cen, -1, keepdims=True)
        norm = (cen * lax.rsqrt(var + EPS) * gain[...] + shift[...]).astype(BF)
        n2[b] = norm
        dob = nn(perm[...], dout[b])
        dop[b] = dob.astype(BF)
        bdown_sum = bdown_sum + jnp.sum(dob, 0, keepdims=True)
        hid = nn(norm, wup[...]) + bup[...]
        cube = hid * hid * hid
        th = jnp.tanh(ROOT * (hid + 0.044715 * cube))
        act[b] = (0.5 * hid * (1.0 + th)).astype(BF)
        slope = 0.5 * (1.0 + th) + 0.5 * hid * (1.0 - th * th) * (
            ROOT * (1.0 + 3.0 * 0.044715 * hid * hid)
        )
        dhid = (nt(dop[b], wdown[...]) * slope).astype(BF)
        dh[b] = dhid
        bup_sum = bup_sum + jnp.sum(dhid.astype(F32), 0, keepdims=True)
        dn = nt(dhid, wup[...])
        for z in range(pat):
            dns[b, z] = dn[z * quarter : (z + 1) * quarter].astype(BF)
        if b == 0:
            pl.semaphore_wait(bar, greeted)
        for k in range(1, pat):
            rs[b].copy_to(k, dns.at[b, p.other_z(k)], dnr.at[b, k - 1]).start()
    vecs[...] = jnp.zeros(vecs.shape, F32)
    for b in range(batches):
        fd[b] = nn(act[b], wdown[...]).astype(BF)
    bout_sum = jnp.zeros((1, width), F32)
    gain_sum = jnp.zeros((1, width), F32)
    shift_sum = jnp.zeros((1, width), F32)
    mine = rows_of(p.z * quarter, quarter)
    for b in range(batches):
        total = dns[b, p.z].astype(F32)
        for k in range(1, pat):
            rs[b].copy_to(k, dns.at[b, p.other_z(k)], dnr.at[b, k - 1]).wait_recv()
            total = total + dnr[b, k - 1].astype(F32)
        st = state[b, mine, :]
        sto[b] = st
        mean = jnp.mean(st, -1, keepdims=True)
        cen = st - mean
        inv = lax.rsqrt(jnp.mean(cen * cen, -1, keepdims=True) + EPS)
        hat = cen * inv
        gain_sum = gain_sum + jnp.sum(total * hat, 0, keepdims=True)
        shift_sum = shift_sum + jnp.sum(total, 0, keepdims=True)
        dhat = total * gain[...]
        back = inv * (
            dhat
            - jnp.mean(dhat, -1, keepdims=True)
            - hat * jnp.mean(dhat * hat, -1, keepdims=True)
        )
        ds = dop[b, mine, :].astype(F32) + back
        dst[b] = ds
        bout_sum = bout_sum + jnp.sum(ds, 0, keepdims=True)
        dsf[b, mine, :] = ds.astype(BF)
        for k in range(1, pat):
            ag[b].copy_to(k, dsf.at[b, mine, :], dsf.at[b, mine, :]).start()
    vecs[2:3, :] = bout_sum
    vecs[3:4, :] = gain_sum
    vecs[4:5, :] = shift_sum
    vecs[5:6, :] = bup_sum
    vecs[6:7, :] = bdown_sum
    up = tn(n2[0], dh[0])
    for b in range(1, batches):
        up = up + tn(n2[b], dh[b])
    gud[0:width, :] = up.astype(BF)
    down = tn(act[0], dop[0])
    for b in range(1, batches):
        down = down + tn(act[b], dop[b])
    gud[width : 2 * width, :] = down.astype(BF)
    for b in range(batches):
        for k in range(1, pat):
            frm = lax.rem(p.z + pat - k, pat)
            theirs = dsf.at[b, rows_of(frm * quarter, quarter), :]
            rs[b].copy_to(k, dns.at[b, p.other_z(k)], dnr.at[b, k - 1]).wait_send()
            ag[b].copy_to(k, dsf.at[b, mine, :], dsf.at[b, mine, :]).wait_send()
            ag[b].copy_to(k, theirs, theirs).wait_recv()


def backward_kernel(
    n,
    pat,
    levels,
    lens,
    dsf,
    wofp,
    attf,
    attw,
    den,
    qp,
    kvd,
    kvt,
    tab,
    qext,
    fd,
    sto,
    bdown,
    permt,
    dq,
    dkv,
    gout,
    outp,
    qud,
    qut,
    crd,
    crt,
    uext,
    acq,
    ack,
    fdr,
    outf,
    f_send,
    f_recv,
    o_send,
    o_recv,
    ds0,
    ds1,
    ts0,
    ts1,
    ts2,
    ts3,
    cd0,
    cd1,
    ct0,
    ct1,
    ct2,
    ct3,
):
    batches, shard, width = dsf.shape
    half = shard // 2
    quarter = shard // pat
    units = qp.shape[0]
    heads = units // batches
    p = Place(n, pat)
    bar, greeted = p.greet(True, True)
    low, high = lane_masks()
    parity = [lax.rem(heads * p.z + i, 2) for i in range(heads)]
    own = rows_of(p.pos * shard, shard)
    lane = lax.broadcasted_iota(jnp.int32, (shard, 128), 1)
    row8 = lax.broadcasted_iota(jnp.int32, (8, 128), 0)
    lane8 = lax.broadcasted_iota(jnp.int32, (8, 128), 1)
    pick = jnp.where(row8 == lax.div(lane8, HD), 1.0, 0.0).astype(F32)
    ri = lax.broadcasted_iota(jnp.int32, (128, 128), 0)
    ci = lax.broadcasted_iota(jnp.int32, (128, 128), 1)
    same = jnp.where(lax.div(ri, HD) == lax.div(ci, HD), 1.0, 0.0).astype(F32)

    wide = [
        nt(dsf[b], wofp[p.z, HD : HD + 256, :] if b == 0 else wofp[p.z, 0:256, :])
        for b in range(batches)
    ]
    tiles = [wide[0][:, 0:128], wide[0][:, 128:256] + wide[1][:, 0:128], wide[1][:, 128:256]]
    crd[p.pos] = jnp.zeros(crd.shape[1:], F32)
    crt[p.s] = jnp.zeros(crt.shape[1:], F32)
    for t in range(units // 2):
        dn = den[t]
        up = tiles[t] / dn
        prod = tiles[t] * attw[t] / dn
        cor = exact_nn(prod, same)
        cor_rows = exact_nt(pick, prod)
        for e in range(2):
            u = 2 * t + e
            i = u % heads
            part = up if e == 1 else pltpu.roll(up, HD, 1)
            mixed = jnp.where(lane < HD, qp[u].astype(F32), part).astype(BF)
            qud[u, own, :] = mixed
            qut[u, rows_of(p.s * half, half), :] = qud[
                u, rows_of(p.pos * shard + parity[i] * half, half), :
            ]
            crd[p.pos, u : u + 1, :] = cor_rows[e : e + 1, :]
            col = -cor[:, e * HD : e * HD + 1]
            first = col.astype(BF).astype(F32)
            ue = jnp.where(lane == COR_LANE, first, 0.0) + jnp.where(
                lane == COR_LANE + 1, col - first, 0.0
            )
            uext[u] = ue.astype(BF)
            thin_cor = jnp.where(parity[i] == 0, cor_rows[e : e + 1, 0:half], cor_rows[e : e + 1, half:shard])
            crt[p.s, u : u + 1, :] = thin_cor
    pl.semaphore_wait(bar, greeted)
    cors = Shares(
        p,
        shard,
        False,
        lambda slot: crd.at[slot],
        lambda dev: crt.at[dev],
        [cd0, cd1],
        [ct0, ct1, ct2, ct3],
    )
    shares = [
        Shares(
            p,
            shard,
            False,
            lambda slot, b=b: qud.at[pl.ds(heads * b, heads), rows_of(slot * shard, shard), :],
            lambda dev, b=b: qut.at[pl.ds(heads * b, heads), rows_of(dev * half, half), :],
            [ds0.at[b], ds1.at[b]],
            [ts0.at[b], ts1.at[b], ts2.at[b], ts3.at[b]],
        )
        for b in range(batches)
    ]
    cors.start()
    for b in range(batches):
        shares[b].start()
    fs = [Spread(p, f_send.at[b], f_recv.at[b]) for b in range(batches)]
    og = [Spread(p, o_send.at[b], o_recv.at[b]) for b in range(batches)]

    def fd_src(b, k):
        return fd.at[b, rows_of(p.other_z(k) * quarter, quarter), :]

    for b in range(batches):
        for k in range(1, pat):
            fs[b].copy_to(k, fd_src(b, k), fdr.at[b, k - 1]).start()

    def query_side(qu, qe, ue, kv, ext, bias):
        kvx = jnp.concatenate([kv, ext], 1)
        s = nt(jnp.concatenate([qu * low, qe], 1), kvx)
        if bias is not None:
            s = s + bias
        dp = nt(jnp.concatenate([qu * high, ue], 1), kvx)
        return nn((jnp.exp(s) * dp).astype(BF), kv)

    def key_side(qu, qe, cor, kv, ext, bias):
        s = nt(jnp.concatenate([kv, ext], 1), jnp.concatenate([qu * low, qe], 1))
        if bias is not None:
            s = s + bias
        w = jnp.exp(s)
        dp = nt(kv, qu * high) - cor
        return nn((w * dp).astype(BF), qu * low) + nn(w.astype(BF), qu * high)

    qi = lax.broadcasted_iota(jnp.int32, (shard, shard), 0)
    ki = lax.broadcasted_iota(jnp.int32, (shard, shard), 1)
    ti, tj = token_of(qi, shard), token_of(ki, shard)
    for b in range(batches):
        bias = jnp.where(
            jnp.logical_or(jnp.logical_and(tj < ti, tj + p.s * shard < lens[b]), tj == ti), 0.0, NEG
        )
        biast = jnp.where(
            jnp.logical_or(jnp.logical_and(ti < tj, ti + p.s * shard < lens[b]), tj == ti), 0.0, NEG
        )
        for i in range(heads):
            u = heads * b + i
            kv = kvd[u, own, :]
            qu = qud[u, own, :]
            acq[u] = query_side(qu, qext[...], uext[u], kv, tab[i, 0], bias)
            ack[u] = key_side(qu, qext[...], crd[p.pos, u : u + 1, :], kv, tab[i, 0], biast)

    for b in range(batches):

        def dense_q(j, carry, b=b):
            lenl = length_lane(dense_positions(p.seg * SPAN1 + j, shard), lens[b], shard)
            for i in range(heads):
                u = heads * b + i
                kv = kvd[u, rows_of(j * shard, shard), :]
                acq[u] += query_side(
                    qud[u, own, :], qext[...], uext[u], kv, tab[i, 0] + lenl, None
                )
            return carry

        lax.fori_loop(0, p.pos, dense_q, 0)

        def thin_q(sg, carry, b=b):
            level = level_of(sg, p.seg, levels)
            for i in range(heads):
                u = heads * b + i
                mine = rows_of(parity[i] * half, half)
                places = thin_positions(sg * SPAN1, parity[i], shard, SPAN1)
                lenl = length_lane(places, lens[b], SPAN1 * half)
                ext = jnp.concatenate([tab[i, level, mine, :]] * SPAN1, 0) + lenl
                kv = kvt[u, rows_of(sg * SPAN1 * half, SPAN1 * half), :]
                qu = qut[u, rows_of(p.s * half, half), :]
                acq[u, mine, :] += query_side(
                    qu, qext[mine, :], uext[u, mine, :], kv, ext, None
                )
            return carry

        lax.fori_loop(0, p.seg, thin_q, 0)

    zrows = rows_of(p.z * quarter, quarter)
    for b in range(batches):
        total = fd[b, zrows, :].astype(F32)
        for k in range(1, pat):
            fs[b].copy_to(k, fd_src(b, k), fdr.at[b, k - 1]).wait_recv()
            total = total + fdr[b, k - 1].astype(F32)
        outf[b, zrows, :] = (sto[b] + total + bdown[...]).astype(BF)
        for k in range(1, pat):
            og[b].copy_to(k, outf.at[b, zrows, :], outf.at[b, zrows, :]).start()
    left = tn(jnp.concatenate([attf[p.z, 0], attf[p.z, 1]], 1), dsf[0])
    right = tn(jnp.concatenate([attf[p.z, 1], attf[p.z, 2]], 1), dsf[1])
    gout[...] = (left[0 : heads * HD] + right[HD : HD + heads * HD]).astype(BF)

    cors.pass_on()
    cors.arrive()
    for b in range(batches):
        shares[b].pass_on()
        shares[b].arrive()
        lenl = length_lane(dense_positions(p.s, shard), lens[b], shard)

        def dense_k(j, carry, b=b, lenl=lenl):
            for i in range(heads):
                u = heads * b + i
                qu = qud[u, rows_of(j * shard, shard), :]
                ack[u] += key_side(
                    qu, qext[...], crd[j, u : u + 1, :], kvd[u, own, :], tab[i, 0] + lenl, None
                )
            return carry

        lax.fori_loop(p.pos + 1, SPAN1, dense_k, 0)

        def thin_k(dev, carry, b=b):
            level = level_of(lax.div(dev, SPAN1), p.seg, levels)
            for i in range(heads):
                u = heads * b + i
                mine = rows_of(parity[i] * half, half)
                ext = tab[i, level, mine, :] + length_lane(
                    thin_positions(p.s, parity[i], shard, 1), lens[b], half
                )
                kv = kvt[u, rows_of(p.s * half, half), :]
                qu = qut[u, rows_of(dev * half, half), :]
                ack[u, mine, :] += key_side(
                    qu, qext[mine, :], crt[dev, u : u + 1, :], kv, ext, None
                )
            return carry

        lax.fori_loop(SPAN1 * (p.seg + 1), n, thin_k, 0)
        for i in range(heads):
            u = heads * b + i
            lanes = slice(i * 128, (i + 1) * 128)
            dq[b, :, lanes] = (acq[u] * HD**-0.5).astype(BF)
            dkv[b, :, lanes] = ack[u].astype(BF)

    for b in range(batches):
        for k in range(1, pat):
            frm = lax.rem(p.z + pat - k, pat)
            theirs = outf.at[b, rows_of(frm * quarter, quarter), :]
            og[b].copy_to(k, theirs, theirs).wait_recv()
            og[b].copy_to(k, outf.at[b, zrows, :], outf.at[b, zrows, :]).wait_send()
            fs[b].copy_to(k, fd_src(b, k), fdr.at[b, k - 1]).wait_send()
        outp[b] = nn(permt[...], outf[b]).astype(BF)
    cors.finish()
    for b in range(batches):
        shares[b].finish()


def tail_kernel(
    n,
    pat,
    xp,
    n1,
    dq,
    dkv,
    wq,
    wkv,
    gain,
    dst,
    vecs,
    gud,
    gout,
    permt,
    ginp,
    vout,
    grad,
    dns,
    dnr,
    gif,
    v0,
    vz,
    r_send,
    r_recv,
    g_send,
    g_recv,
    z_send,
    z_recv,
):
    batches, shard, width = xp.shape
    quarter = shard // pat
    cols = gout.shape[0]
    heads = cols // HD
    p = Place(n, pat)
    bar, greeted = p.greet(True, False)
    rs = [Spread(p, r_send.at[b], r_recv.at[b]) for b in range(batches)]
    ag = [Spread(p, g_send.at[b], g_recv.at[b]) for b in range(batches)]
    for b in range(batches):
        part = nt(dq[b], wq[...]) + nt(dkv[b], wkv[...])
        for z in range(pat):
            dns[b, z] = part[z * quarter : (z + 1) * quarter].astype(BF)
        if b == 0:
            pl.semaphore_wait(bar, greeted)
        for k in range(1, pat):
            rs[b].copy_to(k, dns.at[b, p.other_z(k)], dnr.at[b, k - 1]).start()
    qsum = jnp.zeros((1, heads * 128), F32)
    vsum = jnp.zeros((1, heads * 128), F32)
    for b in range(batches):
        qsum = qsum + jnp.sum(dq[b].astype(F32), 0, keepdims=True)
        vsum = vsum + jnp.sum(dkv[b].astype(F32), 0, keepdims=True)
    grad[0 : 2 * width, :] = gud[...].astype(F32)
    base = 2 * width
    for i in range(heads):
        lanes = slice(i * 128, (i + 1) * 128)
        a = tn(dq[0, :, lanes], n1[0])
        c = tn(dkv[0, :, lanes], n1[0])
        for b in range(1, batches):
            a = a + tn(dq[b, :, lanes], n1[b])
            c = c + tn(dkv[b, :, lanes], n1[b])
        grad[base + i * HD : base + (i + 1) * HD, :] = a[0:HD]
        grad[base + cols + i * HD : base + cols + (i + 1) * HD, :] = c[0:HD]
        grad[base + 2 * cols + i * HD : base + 2 * cols + (i + 1) * HD, :] = c[HD:]
    grad[base + 3 * cols : base + 4 * cols, :] = gout[...].astype(F32)
    zrows = rows_of(p.z * quarter, quarter)
    gain_sum = jnp.zeros((1, width), F32)
    shift_sum = jnp.zeros((1, width), F32)
    for b in range(batches):
        total = dns[b, p.z].astype(F32)
        for k in range(1, pat):
            rs[b].copy_to(k, dns.at[b, p.other_z(k)], dnr.at[b, k - 1]).wait_recv()
            total = total + dnr[b, k - 1].astype(F32)
        back, more_gain, more_shift = norm_back(xp[b, zrows, :].astype(F32), total, gain[...])
        gain_sum = gain_sum + more_gain
        shift_sum = shift_sum + more_shift
        gif[b, zrows, :] = (dst[b] + back).astype(BF)
        for k in range(1, pat):
            ag[b].copy_to(k, gif.at[b, zrows, :], gif.at[b, zrows, :]).start()
    v0[...] = vecs[...]
    v0[0:1, :] = gain_sum
    v0[1:2, :] = shift_sum
    zsp = Spread(p, z_send, z_recv)
    for k in range(1, pat):
        zsp.copy_to(k, v0, vz.at[k - 1]).start()
    for k in range(1, pat):
        zsp.copy_to(k, v0, vz.at[k - 1]).wait_recv()
    row = lax.broadcasted_iota(jnp.int32, (8, width), 0)
    extra = vz[0]
    for k in range(2, pat):
        extra = extra + vz[k - 1]
    vout[0:8, :] = v0[...] + jnp.where(row < 5, extra, 0.0)
    vout[8:16, :] = jnp.zeros((8, width), F32)
    vout[8:9, 0 : heads * 128] = qsum
    vout[9:10, 0 : heads * 128] = vsum
    for b in range(batches):
        for k in range(1, pat):
            frm = lax.rem(p.z + pat - k, pat)
            theirs = gif.at[b, rows_of(frm * quarter, quarter), :]
            ag[b].copy_to(k, theirs, theirs).wait_recv()
        ginp[b] = nn(permt[...], gif[b]).astype(BF)
    for b in range(batches):
        for k in range(1, pat):
            rs[b].copy_to(k, dns.at[b, p.other_z(k)], dnr.at[b, k - 1]).wait_send()
            ag[b].copy_to(k, gif.at[b, zrows, :], gif.at[b, zrows, :]).wait_send()
    for k in range(1, pat):
        zsp.copy_to(k, v0, vz.at[k - 1]).wait_send()


def call(kernel, name, outs, scratch, specs, number, places=None):
    return pl.pallas_call(
        kernel,
        name=name,
        out_shape=[jax.ShapeDtypeStruct(s, d) for s, d in outs],
        in_specs=[pl.BlockSpec(memory_space=m) for m in specs],
        out_specs=[
            pl.BlockSpec(memory_space=m) for m in places or [pltpu.VMEM] * len(outs)
        ],
        scratch_shapes=scratch,
        compiler_params=pltpu.CompilerParams(
            collective_id=number, has_side_effects=True, vmem_limit_bytes=62 << 20
        ),
    )


def shards(
    n,
    pat,
    inputs,
    lengths,
    gain_one,
    shift_one,
    w_query,
    b_query,
    w_key,
    w_value,
    b_value,
    w_out,
    b_out,
    gain_two,
    shift_two,
    w_up,
    b_up,
    w_down,
    b_down,
    d_output,
):
    batches, shard, width = inputs.shape
    cols = w_query.shape[1]
    heads = cols // HD
    units = batches * heads
    chips = n // 2
    half = shard // 2
    quarter = shard // pat
    levels = 1
    while SPAN1 << (levels - 1) < n:
        levels += 1
    perm = jnp.asarray(perm_matrix(shard), BF)
    permt = jnp.asarray(perm_matrix(shard).T, BF)
    qext = jnp.asarray(query_ext(shard), BF)
    ktab = jnp.asarray(key_tables(shard, heads * pat, levels))
    row = lambda v: v.reshape(1, -1)
    by_head = lambda w: w.reshape(w.shape[0], heads, HD)
    pack = lambda a, b: jnp.concatenate([by_head(a), by_head(b)], 2).reshape(a.shape[0], 2 * cols)
    wq = pack(w_query, jnp.zeros_like(w_query))
    wkv = pack(w_key, w_value)
    bq = pack(row(b_query), jnp.zeros((1, cols), F32))
    bkv = pack(jnp.zeros((1, cols), F32), row(b_value))
    vm, sm, anyv = pltpu.VMEM, pltpu.SMEM, pl.ANY
    dma = pltpu.SemaphoreType.DMA
    tiles = units // 2

    xp, n1, qp, kvd, kvt, attf, wofp, attw, den, tab = call(
        functools.partial(forward_kernel, n, pat, levels),
        "attention_forward",
        [
            ((batches, shard, width), BF),
            ((batches, shard, width), BF),
            ((units, shard, 128), BF),
            ((units, SPAN1 * shard, 128), BF),
            ((units, n * half, 128), BF),
            ((pat, tiles, shard, 128), BF),
            ((pat, cols + 2 * HD, width), BF),
            ((tiles, shard, 128), F32),
            ((tiles, shard, 128), F32),
            ((heads, levels, shard, 128), BF),
        ],
        [
            pltpu.VMEM((units, shard, 128), F32),
            dma((heads,)),
            dma((pat - 1,)),
            dma((pat - 1,)),
            dma((tiles, pat - 1)),
            dma((tiles, pat - 1)),
        ]
        + dense_sems(batches)
        + thin_sems(batches, chips),
        [sm] + [vm] * 10 + [anyv],
        0,
    )(lengths, inputs, row(gain_one), row(shift_one), wq, bq, wkv, bkv, w_out, perm, qext, ktab)

    gud, fd, dsf, dst, sto, vecs = call(
        functools.partial(middle_kernel, n, pat),
        "feed_forward",
        [
            ((2 * width, width), BF),
            ((batches, shard, width), BF),
            ((batches, shard, width), BF),
            ((batches, quarter, width), F32),
            ((batches, quarter, width), F32),
            ((8, width), F32),
        ],
        [
            pltpu.VMEM((batches, shard, width), F32),
            pltpu.VMEM((batches, shard, width), BF),
            pltpu.VMEM((batches, shard, width), BF),
            pltpu.VMEM((batches, shard, width), BF),
            pltpu.VMEM((batches, shard, width), BF),
            pltpu.VMEM((batches, pat, quarter, width), BF),
            pltpu.VMEM((batches, quarter, width), F32),
            pltpu.VMEM((batches, pat - 1, quarter, width), BF),
        ]
        + [dma((batches, pat - 1))] * 4,
        [vm] * 11,
        1,
    )(
        xp,
        attf,
        wofp,
        row(b_out),
        row(gain_two),
        row(shift_two),
        w_up,
        row(b_up),
        w_down,
        d_output,
        perm,
    )

    dq, dkv, gout, outputs = call(
        functools.partial(backward_kernel, n, pat, levels),
        "attention_backward",
        [
            ((batches, shard, 2 * cols), BF),
            ((batches, shard, 2 * cols), BF),
            ((cols, width), BF),
            ((batches, shard, width), BF),
        ],
        [
            pltpu.VMEM((units, SPAN1 * shard, 128), BF),
            pltpu.VMEM((units, n * half, 128), BF),
            pltpu.VMEM((SPAN1, 8, shard), F32),
            pltpu.VMEM((n, 8, half), F32),
            pltpu.VMEM((units, shard, 128), BF),
            pltpu.VMEM((units, shard, 128), F32),
            pltpu.VMEM((units, shard, 128), F32),
            pltpu.VMEM((batches, pat - 1, quarter, width), BF),
            pltpu.VMEM((batches, shard, width), BF),
        ]
        + [dma((batches, pat - 1))] * 4
        + dense_sems(batches)
        + thin_sems(batches, chips)
        + [dma((3,))] * 2
        + [dma((chips,))] * 4,
        [sm] + [vm] * 14,
        2,
    )(lengths, dsf, wofp, attf, attw, den, qp, kvd, kvt, tab, qext, fd, sto, row(b_down), permt)

    rows = 2 * width + 4 * cols
    grad_inputs, vout, grads = call(
        functools.partial(tail_kernel, n, pat),
        "input_gradient",
        [
            ((batches, shard, width), BF),
            ((16, width), F32),
            ((rows, width), F32),
        ],
        [
            pltpu.VMEM((batches, pat, quarter, width), BF),
            pltpu.VMEM((batches, pat - 1, quarter, width), BF),
            pltpu.VMEM((batches, shard, width), BF),
            pltpu.VMEM((8, width), F32),
            pltpu.VMEM((pat - 1, 8, width), F32),
        ]
        + [dma((batches, pat - 1))] * 4
        + [dma((pat - 1,))] * 2,
        [vm] * 12,
        3,
    )(xp, n1, dq, dkv, wq, wkv, row(gain_one), dst, vecs, gud, gout, permt)
    vout, grads = lax.psum((vout, grads), "seq")
    base = 2 * width
    g_q, g_k, g_v, g_out = [grads[base + i * cols : base + (i + 1) * cols] for i in range(4)]
    q_row = vout[8, : 2 * cols].reshape(heads, 2, HD)
    v_row = vout[9, : 2 * cols].reshape(heads, 2, HD)
    return (
        outputs,
        grad_inputs,
        vout[0],
        vout[1],
        g_q.T,
        q_row[:, 0].reshape(cols),
        g_k.T,
        g_v.T,
        v_row[:, 1].reshape(cols),
        g_out,
        vout[2],
        vout[3],
        vout[4],
        grads[:width],
        vout[5],
        grads[width:base],
        vout[6],
    )


class LineGather:
    def __init__(self, place, block, send, recv):
        self.p, self.block, self.send, self.recv = place, block, send, recv

    def copy(self, frm, to, sem):
        return remote(
            self.block(frm, self.p.z),
            self.block(frm, to),
            self.send.at[sem],
            self.recv.at[frm],
            (to, self.p.s),
        )

    def got(self, frm):
        here = self.block(frm, self.p.z)
        to = lax.rem(self.p.z + 1, self.p.pat)
        return remote(here, here, self.send.at[0], self.recv.at[frm], (to, self.p.s))

    def direct(self, fn):
        last = self.p.pat - 1
        for z in range(self.p.pat):

            def own(z=z):
                for to in sorted(range(last + 1), key=lambda t: -abs(t - z)):
                    if 0 < abs(to - z) < last:
                        fn(self.copy(z, to, to))

            when(self.p.z == z, own)

    def handed(self, fn):
        last = self.p.pat - 1
        when(self.p.z == last - 1, lambda: fn(0, self.copy(0, last, last + 1)))
        when(self.p.z == 1, lambda: fn(last, self.copy(last, 0, last + 1)))

    def start(self):
        self.direct(lambda copy: copy.start())

    def forward(self):
        def hand(frm, copy):
            self.got(frm).wait_recv()
            copy.start()

        self.handed(hand)

    def arrive(self):
        last = self.p.pat - 1
        for z in range(last + 1):

            def rest(z=z):
                for frm in range(last + 1):
                    if frm != z and (z, frm) not in ((1, last), (last - 1, 0)):
                        self.got(frm).wait_recv()

            when(self.p.z == z, rest)

    def finish(self):
        self.direct(lambda copy: copy.wait_send())
        self.handed(lambda frm, copy: copy.wait_send())


class LineChain:
    def __init__(self, place, block, send, recv):
        self.p, self.block, self.send, self.recv = place, block, send, recv

    def copy(self, frm, up):
        p = self.p
        to = jnp.clip(p.z + (1 if up else -1), 0, p.pat - 1)
        return remote(
            self.block(frm),
            self.block(frm),
            self.send.at[0 if up else 1, frm],
            self.recv.at[frm],
            (to, p.s),
        )

    def start(self):
        p = self.p
        when(p.z < p.pat - 1, lambda: self.copy(p.z, True).start())
        when(p.z > 0, lambda: self.copy(p.z, False).start())

    def inner(self, hop):
        for z in range(1, self.p.pat - 1):
            if z - hop >= 0:
                yield z, z - hop, True
            if z + hop < self.p.pat:
                yield z, z + hop, False

    def got(self, frm):
        p = self.p
        here = self.block(frm)
        to = lax.rem(p.z + 1, p.pat)
        return remote(here, here, self.send.at[0, 0], self.recv.at[frm], (to, p.s))

    def forward(self, hop):
        for z, frm, up in self.inner(hop):

            def hand(frm=frm, up=up):
                self.got(frm).wait_recv()
                self.copy(frm, up).start()

            when(self.p.z == z, hand)

    def arrive(self):
        last = self.p.pat - 1
        for frm in range(self.p.pat):
            if frm > 0:
                when(self.p.z == 0, lambda frm=frm: self.got(frm).wait_recv())
            if frm < last:
                when(self.p.z == last, lambda frm=frm: self.got(frm).wait_recv())

    def finish(self):
        p = self.p
        when(p.z < p.pat - 1, lambda: self.copy(p.z, True).wait_send())
        when(p.z > 0, lambda: self.copy(p.z, False).wait_send())
        for hop in range(1, p.pat - 1):
            for z, frm, up in self.inner(hop):
                when(p.z == z, lambda frm=frm, up=up: self.copy(frm, up).wait_send())


class LineSum:
    def __init__(self, place, part, buf, send, recv):
        self.p, self.part, self.buf, self.send, self.recv = place, part, buf, send, recv

    def copy(self, z, t):
        to = z + 1 if t > z else z - 1
        at = t if (t > z or t < to) else self.p.pat
        return remote(
            self.part(t), self.buf.at[at], self.send.at[t], self.recv.at[at], (to, self.p.s)
        )

    def got(self, at):
        here = self.buf.at[at]
        to = lax.rem(self.p.z + 1, self.p.pat)
        return remote(here, here, self.send.at[0], self.recv.at[at], (to, self.p.s))

    def start(self):
        last = self.p.pat - 1

        def up():
            for t in range(last, 0, -1):
                self.copy(0, t).start()

        def down():
            for t in range(last):
                self.copy(last, t).start()

        when(self.p.z == 0, up)
        when(self.p.z == last, down)

    def inner(self, hop):
        last = self.p.pat - 1
        for z in range(1, last):
            if z == hop:
                for t in range(last, z, -1):
                    yield z, t
            if last - z == hop:
                for t in range(z):
                    yield z, t

    def forward(self, hop):
        for z, t in self.inner(hop):

            def add(z=z, t=t):
                self.got(t).wait_recv()
                part = self.part(t)
                part[...] = (part[...].astype(F32) + self.buf[t].astype(F32)).astype(BF)
                self.copy(z, t).start()

            when(self.p.z == z, add)

    def total(self, out):
        p = self.p
        out[...] = self.part(p.z)[...].astype(F32)

        def below():
            self.got(p.z).wait_recv()
            out[...] += self.buf[p.z].astype(F32)

        def above():
            self.got(p.pat).wait_recv()
            out[...] += self.buf[p.pat].astype(F32)

        when(p.z > 0, below)
        when(p.z < p.pat - 1, above)

    def finish(self):
        last = self.p.pat - 1
        for t in range(last, 0, -1):
            when(self.p.z == 0, lambda t=t: self.copy(0, t).wait_send())
        for t in range(last):
            when(self.p.z == last, lambda t=t: self.copy(last, t).wait_send())
        for hop in range(1, last):
            for z, t in self.inner(hop):
                when(self.p.z == z, lambda z=z, t=t: self.copy(z, t).wait_send())


class PlaneGather:
    def __init__(self, place, piece, sems):
        self.p, self.piece, self.sems = place, piece, sems
        self.chips = place.n // 2

    def direct(self, k, owner):
        p, sems = self.p, self.sems
        to = lax.rem(p.s + 2 * k, p.n)
        return remote(
            self.piece(owner), self.piece(owner), sems[0].at[k - 1], sems[1].at[k - 1], (p.z, to)
        )

    def hand(self, k, owner):
        p, sems = self.p, self.sems
        return remote(
            self.piece(owner), self.piece(owner), sems[2].at[k], sems[3].at[k], (p.z, p.sib)
        )

    def source(self, base, k):
        return lax.rem(base + self.p.n - 2 * k, self.p.n)

    def start(self):
        for k in range(1, self.chips):
            self.direct(k, self.p.s).start()
        self.hand(0, self.p.s).start()

    def pass_on(self):
        for k in range(1, self.chips):
            owner = self.source(self.p.s, k)
            self.direct(k, owner).wait_recv()
            self.hand(k, owner).start()

    def arrive(self):
        for k in range(self.chips):
            self.hand(k, self.source(self.p.sib, k)).wait_recv()

    def finish(self):
        for k in range(1, self.chips):
            self.direct(k, self.p.s).wait_send()
        for k in range(self.chips):
            self.hand(k, self.source(self.p.s, k)).wait_send()


def line_sems(pat):
    return [pltpu.SemaphoreType.DMA((pat + 1,)), pltpu.SemaphoreType.DMA((pat,))]


def chain_sems(pat):
    return [pltpu.SemaphoreType.DMA((2, pat)), pltpu.SemaphoreType.DMA((pat,))]


def sum_sems(pat):
    return [pltpu.SemaphoreType.DMA((pat,)), pltpu.SemaphoreType.DMA((pat + 1,))]


def plane_sems(chips):
    return [pltpu.SemaphoreType.DMA((chips - 1,))] * 2 + [pltpu.SemaphoreType.DMA((chips,))] * 2


def vec_row(ref):
    return ref[...].reshape(1, -1)


def norm_rows(values, gain, shift):
    mean = jnp.mean(values, -1, keepdims=True)
    cen = values - mean
    var = jnp.mean(cen * cen, -1, keepdims=True)
    return cen * lax.rsqrt(var + EPS) * gain + shift


def norm_back(values, grad, gain):
    mean = jnp.mean(values, -1, keepdims=True)
    cen = values - mean
    inv = lax.rsqrt(jnp.mean(cen * cen, -1, keepdims=True) + EPS)
    hat = cen * inv
    dhat = grad * gain
    back = inv * (
        dhat - jnp.mean(dhat, -1, keepdims=True) - hat * jnp.mean(dhat * hat, -1, keepdims=True)
    )
    return (
        back,
        jnp.sum(grad * hat, 0, keepdims=True),
        jnp.sum(grad, 0, keepdims=True),
    )


def live_bias(first, second, base, length, shard):
    ok = jnp.logical_or(
        jnp.logical_and(second < first, second + base < length), second == first
    )
    return jnp.where(ok, 0.0, NEG)


class TreeSum:
    def __init__(self, place, grad, out, bufs, send, recv, keep=False):
        self.p, self.grad, self.out, self.send, self.recv = place, grad, out, send, recv
        self.keep = keep
        p = place
        bit_x = lax.rem(lax.div(p.s, 2), 2)
        bit_y = lax.div(p.s, 4)
        to_x = p.s + 2 - 4 * bit_x
        to_y = p.s + 4 - 8 * bit_y
        first = p.core == 0
        self.bits = [p.core, jnp.where(first, bit_x, bit_y), jnp.where(first, bit_y, bit_x)]
        self.to = [p.sib, jnp.where(first, to_x, to_y), jnp.where(first, to_y, to_x)]
        self.bufs = bufs
        self.off, self.size = [jnp.int32(0)], [grad.shape[0]]
        for d in range(3):
            h = self.size[d] // 2
            self.off.append(self.off[d] + self.bits[d] * h)
            self.size.append(h)

    def half_of(self, d, bit):
        h = self.size[d] // 2
        return rows_of(self.off[d] + bit * h, h)

    def red(self, d):
        src = self.grad.at[self.half_of(d, 1 - self.bits[d]), :]
        return remote(
            src, self.bufs[d], self.send.at[d], self.recv.at[d], (self.p.z, self.to[d])
        )

    def back(self, d, got):
        rows = self.half_of(d, (1 - self.bits[d]) if got else self.bits[d])
        return remote(
            self.out.at[rows, :],
            self.out.at[rows, :],
            self.send.at[3 + d],
            self.recv.at[3 + d],
            (self.p.z, self.to[d]),
        )

    def step(self, d):
        if d == 0:
            self.red(0).start()
        elif d <= 3:
            self.red(d - 1).wait_recv()
            rows = rows_of(self.off[d], self.size[d])
            total = self.grad[rows, :].astype(F32) + self.bufs[d - 1][...].astype(F32)
            if d < 3:
                self.grad[rows, :] = total.astype(BF)
                self.red(d).start()
            elif self.keep:
                self.out[...] = total.astype(BF)
            else:
                self.out[rows, :] = total.astype(BF)
                self.back(2, False).start()
        else:
            self.back(6 - d, True).wait_recv()
            if d < 6:
                self.back(5 - d, False).start()

    def finish(self):
        for d in range(3):
            self.red(d).wait_send()
            if not self.keep:
                self.back(d, False).wait_send()


def layer_kernel(
    n,
    pat,
    levels,
    lens,
    gain1,
    shift1,
    bq,
    bv,
    bout,
    gain2,
    shift2,
    bup,
    bdown,
    wq_hbm,
    wk_hbm,
    wv_hbm,
    wout_hbm,
    perm_hbm,
    qext_hbm,
    ktab,
    x_hbm,
    wup_hbm,
    wdown_hbm,
    dout_hbm,
    outf_hbm,
    gif_hbm,
    gsum1_hbm,
    gsum2_hbm,
    vout,
    perm,
    qext,
    outf,
    gif,
    gsum1,
    gsum2,
    grad1,
    grad2,
    xp,
    n1,
    wp,
    qp,
    kvd,
    kvt,
    tab,
    acc,
    ack,
    attf,
    attu,
    attw,
    den,
    wor,
    wup,
    wdown,
    state,
    sto,
    n2,
    act,
    dop,
    dh,
    dns,
    dnr,
    tot,
    dsl,
    dst,
    dab,
    dat,
    fd,
    fdr,
    qud,
    qut,
    crd,
    crt,
    uext,
    dmr,
    a1,
    a2,
    a3,
    b1,
    b2,
    b3,
    grad3,
    c1,
    c2,
    c3,
    pz,
    pr,
    vecs,
    vz,
    vs,
    *sems,
):
    batches, shard, width = xp.shape
    half = shard // 2
    quarter = shard // pat
    cols = wout_hbm.shape[0]
    heads = cols // HD
    units = batches * heads
    tiles = units // 2
    chips = n // 2
    sems = list(sems)
    take = lambda count: [sems.pop(0) for _ in range(count)]
    p = Place(n, pat)
    bar, greeted = p.greet(True, False, True)
    low, high = lane_masks()

    own_slot = pat - 1
    pairs = [(perm_hbm, perm), (x_hbm.at[0], xp.at[0])]
    for i in range(heads):
        for off, src in ((0, wk_hbm), (HD, wv_hbm)):
            pairs.append((src.at[i * HD : (i + 1) * HD, :], wp.at[pl.ds(i * 128 + off, HD), :]))
    pairs.append((wq_hbm, wp.at[pl.ds(2 * cols, cols), :]))
    at_x = len(pairs)
    pairs += [(x_hbm.at[b], xp.at[b]) for b in range(1, batches)]
    at_out = len(pairs)
    pairs += [(wout_hbm, wor.at[own_slot, pl.ds(HD, cols), :])]
    at_tab = len(pairs)
    pairs += [(ktab.at[heads * p.z + i], tab.at[i]) for i in range(heads)] + [(qext_hbm, qext)]
    at_late = len(pairs)
    pairs += [(dout_hbm, dop), (wup_hbm, wup), (wdown_hbm, wdown)]
    load_sem, save_sem = take(2)
    loads = [
        pltpu.make_async_copy(src, dst, load_sem.at[i]) for i, (src, dst) in enumerate(pairs)
    ]
    for copy in loads:
        copy.start()
    saves = [
        pltpu.make_async_copy(src, dst, save_sem.at[i])
        for i, (src, dst) in enumerate(
            ((gsum1, gsum1_hbm), (outf, outf_hbm), (gsum2, gsum2_hbm), (gif, gif_hbm))
        )
    ]

    slot = lambda frm, at: lax.rem(frm - at + 2 * pat - 1, pat)
    out_rows, out_cols = cols // chips, width // 2

    def out_piece(dev, slots):
        chip, core = lax.div(dev, 2), lax.rem(dev, 2)
        return wor.at[
            slots,
            rows_of(HD + chip * out_rows, out_rows),
            pl.ds(pl.multiple_of(core * out_cols, 128), out_cols),
        ]

    def quarters(ref, b):
        return lambda f, *_: ref.at[b, rows_of(f * quarter, quarter), :]

    parity = [lax.rem(heads * p.z + i, 2) for i in range(heads)]

    def share_pair(forward, dense, thin):
        out = []
        sems = take(6)
        for b in range(batches):
            out.append(
                Shares(
                    p,
                    shard,
                    forward,
                    lambda at, b=b: dense.at[
                        pl.ds(heads * b, heads), rows_of(at * shard, shard), :
                    ],
                    lambda dev, b=b: thin.at[pl.ds(heads * b, heads), rows_of(dev * half, half), :],
                    [sem.at[b] for sem in sems[:2]],
                    [sem.at[b] for sem in sems[2:]],
                )
            )
        return out

    rows = range(batches)
    kv_shares = share_pair(True, kvd, kvt)
    qu_shares = share_pair(False, qud, qut)
    cor_sems = take(6)
    cors = [
        Shares(
            p,
            shard,
            False,
            lambda at, b=b: crd.at[b, at],
            lambda dev, b=b: crt.at[b, dev],
            [sem.at[b] for sem in cor_sems[:2]],
            [sem.at[b] for sem in cor_sems[2:]],
        )
        for b in rows
    ]
    wo_line = LineGather(p, lambda f, t: out_piece(p.s, slot(f, t)), *take(2))
    wo_plane = PlaneGather(p, lambda dev: out_piece(dev, pl.ds(0, pat - 1)), take(4))
    att_line = [LineGather(p, lambda f, at, b=b: attf.at[f, b], *take(2)) for b in rows]
    dn_sum = [LineSum(p, lambda t, b=b: dns.at[b, t], dnr.at[b], *take(2)) for b in rows]
    da_send, da_recv = take(2)
    da_spread = [Spread(p, da_send.at[b], da_recv.at[b]) for b in rows]
    fd_sum = [LineSum(p, quarters(fd, b), fdr.at[b], *take(2)) for b in rows]
    out_line = [LineChain(p, quarters(outf, b), *take(2)) for b in rows]
    dm_sum = [LineSum(p, lambda t, b=b: dns.at[b, t], dmr.at[b], *take(2)) for b in rows]
    dqk = dh
    gi_line = [LineGather(p, quarters(gif, b), *take(2)) for b in rows]
    sum1 = TreeSum(p, grad1, gsum1, (a1, a2, a3), *take(2))
    sum2 = TreeSum(p, grad2, gsum2, (b1, b2, b3), *take(2))
    sum3 = TreeSum(p, grad3, pz, (c1, c2, c3), *take(2), keep=True)
    p_send, p_recv = take(2)
    z_send, z_recv, v_send, v_recv = take(4)
    zsp = Spread(p, z_send, z_recv)

    for r in range(pat):
        wor[r, 0:HD, :] = jnp.zeros((HD, width), BF)
        wor[r, HD + cols : 2 * HD + cols, :] = jnp.zeros((HD, width), BF)
    wp[3 * cols :, :] = jnp.zeros((wp.shape[0] - 3 * cols, width), BF)
    zero_bias = jnp.zeros((1, HD), F32)
    bias_v, bias_q = vec_row(bv), vec_row(bq)
    bias = []
    for i in range(heads):
        bias += [zero_bias, bias_v[:, i * HD : (i + 1) * HD]]
    bias = jnp.concatenate(bias + [bias_q, zero_bias], 1)

    own = rows_of(p.pos * shard, shard)
    zrows = rows_of(p.z * quarter, quarter)
    lane = lax.broadcasted_iota(jnp.int32, (shard, 128), 1)
    for b in rows:
        if b == 0:
            for copy in loads[:at_x]:
                copy.wait()
        else:
            loads[at_x + b - 1].wait()
        xb = nn(perm[...], xp[b])
        xp[b] = xb.astype(BF)
        n1[b] = norm_rows(xb, vec_row(gain1), vec_row(shift1)).astype(BF)
        qkv = nt(n1[b], wp[...]) + bias
        for i in range(heads):
            kv = qkv[:, i * 128 : (i + 1) * 128].astype(BF)
            kvd[heads * b + i, own, :] = kv
            t = heads + i // 2
            q = qkv[:, t * 128 : (t + 1) * 128]
            if i % 2 == 1:
                q = pltpu.roll(q, HD, 1)
            q = jnp.where(lane < HD, q, 0.0).astype(BF) * jnp.asarray(HD**-0.5, BF)
            qp[heads * b + i] = q
        for i in range(heads):
            kvt[heads * b + i, rows_of(p.s * half, half), :] = kvd[
                heads * b + i, rows_of(p.pos * shard + parity[i] * half, half), :
            ]
        if b == 0:
            pl.semaphore_wait(bar, greeted)
        if b == 0:
            kv_shares[b].start()
            loads[at_out].wait()
            wo_line.start()
    for copy in loads[at_tab:at_late]:
        copy.wait()

    def attend(qx, kv, ext, bias):
        s = nt(qx, jnp.concatenate([kv, ext], 1))
        if bias is not None:
            s = s + bias
        return nn(jnp.exp(s).astype(BF), kv * high + low)

    first = token_of(lax.broadcasted_iota(jnp.int32, (shard, shard), 0), shard)
    second = token_of(lax.broadcasted_iota(jnp.int32, (shard, shard), 1), shard)

    def attend_own(b):
        bias = live_bias(first, second, p.s * shard, lens[b], shard)
        for i in range(heads):
            u = heads * b + i
            qx = jnp.concatenate([qp[u], qext[...]], 1)
            acc[u] = attend(qx, kvd[u, own, :], tab[i, 0], bias)

    def thin_keys(b, i, sg):
        level = level_of(sg, p.seg, levels)
        places = thin_positions(sg * SPAN1, parity[i], shard, SPAN1)
        lenl = length_lane(places, lens[b], SPAN1 * half)
        part = tab[i, level, rows_of(parity[i] * half, half), :]
        ext = jnp.concatenate([part] * SPAN1, 0) + lenl
        return kvt[heads * b + i, rows_of(sg * SPAN1 * half, SPAN1 * half), :], ext

    def attend_rest(b, which):
        def dense(j, carry):
            lenl = length_lane(dense_positions(p.seg * SPAN1 + j, shard), lens[b], shard)
            for i in which:
                u = heads * b + i
                qx = jnp.concatenate([qp[u], qext[...]], 1)
                kv = kvd[u, rows_of(j * shard, shard), :]
                acc[u] += attend(qx, kv, tab[i, 0] + lenl, None)
            return carry

        lax.fori_loop(0, p.pos, dense, 0)

        def thin(sg, carry):
            for i in which:
                u = heads * b + i
                mine = rows_of(parity[i] * half, half)
                kv, ext = thin_keys(b, i, sg)
                qx = jnp.concatenate([qp[u, mine, :], qext[mine, :]], 1)
                acc[u, mine, :] += attend(qx, kv, ext, None)
            return carry

        lax.fori_loop(0, p.seg, thin, 0)

    def send_att(b):
        first_unit = heads * b
        zero, one, two = acc[first_unit], acc[first_unit + 1], acc[first_unit + 2]
        num = jnp.where(lane < HD, pltpu.roll(zero, HD, 1), one)
        dn = jnp.where(lane < HD, zero, pltpu.roll(one, HD, 1))
        wide = num / dn
        den[b, 0] = dn
        attw[b, 0] = wide
        attf[p.z, b, 0:shard, :] = wide.astype(BF)
        dn = jnp.where(lane < HD, two, 1.0)
        wide = jnp.where(lane < HD, pltpu.roll(two, HD, 1), 0.0) / dn
        den[b, 1] = dn
        attw[b, 1] = wide
        packed = wide[0:half] + pltpu.roll(wide[half:shard], HD, 1)
        attf[p.z, b, shard : shard + half, :] = packed.astype(BF)
        att_line[b].start()

    attend_own(0)
    kv_shares[1].start()
    attend_own(1)
    wo_line.forward()
    bdown_sum = jnp.zeros((1, width), F32)
    loads[at_late].wait()
    for b in rows:
        dob = nn(perm[...], dop[b])
        dop[b] = dob.astype(BF)
        bdown_sum = bdown_sum + jnp.sum(dob, 0, keepdims=True)
    kv_shares[0].pass_on()
    wo_line.arrive()
    wo_plane.start()
    kv_shares[0].arrive()
    attend_rest(0, range(heads))
    send_att(0)
    kv_shares[1].pass_on()
    kv_shares[1].arrive()
    attend_rest(1, range(0, 1))
    att_line[0].forward()
    attend_rest(1, range(1, heads))
    send_att(1)
    wo_plane.pass_on()
    for copy in loads[at_late + 1 :]:
        copy.wait()
    wo_plane.arrive()

    def feed_in(b):
        mixed = xp[b].astype(F32) + vec_row(bout)
        for r in range(pat):
            z = lax.rem(p.z + 1 + r, pat)
            packed = attf[z, b, shard : shard + half, :]
            attu[z, b, 0:half, :] = packed
            attu[z, b, half:shard, :] = pltpu.roll(packed.astype(F32), HD, 1).astype(BF)
            pair = jnp.concatenate([attf[z, b, 0:shard, :], attu[z, b]], 1)
            mixed = mixed + nn(pair, wor[r, HD : HD + 256, :])
        state[...] = mixed
        sto[b] = state[zrows, :]
        n2[b] = norm_rows(mixed, vec_row(gain2), vec_row(shift2)).astype(BF)

    def feed_out(b):
        hid = nn(n2[b], wup[...]) + vec_row(bup)
        th = jnp.tanh(ROOT * (hid + 0.044715 * (hid * hid * hid)))
        act[b] = (0.5 * hid * (1.0 + th)).astype(BF)
        slope = 0.5 * (1.0 + th) + 0.5 * hid * (1.0 - th * th) * (
            ROOT * (1.0 + 3.0 * 0.044715 * hid * hid)
        )
        dhid = (nt(dop[b], wdown[...]) * slope).astype(BF)
        dh[b] = dhid
        dn = nt(dhid, wup[...])
        for t in range(pat):
            dns[b, t] = dn[t * quarter : (t + 1) * quarter].astype(BF)
        dn_sum[b].start()
        return jnp.sum(dhid.astype(F32), 0, keepdims=True)

    att_line[0].arrive()
    feed_in(0)
    bup_sum = feed_out(0)
    att_line[1].forward()
    att_line[1].arrive()
    feed_in(1)
    dn_sum[0].forward(1)
    bup_sum = bup_sum + feed_out(1)
    fd[0] = nn(act[0], wdown[...]).astype(BF)
    dn_sum[0].forward(2)
    up = tn(n2[0], dh[0])
    for b in range(1, batches):
        up = up + tn(n2[b], dh[b])
    grad1[0:width, :] = up.astype(BF)
    dn_sum[1].forward(1)
    down = tn(act[0], dop[0])
    for b in range(1, batches):
        down = down + tn(act[b], dop[b])
    grad1[width : 2 * width, :] = down.astype(BF)
    sum1.step(0)
    bout_sum = jnp.zeros((1, width), F32)
    gain_sum = jnp.zeros((1, width), F32)
    shift_sum = jnp.zeros((1, width), F32)

    def head_grads(b, r):
        wide = nt(dsl[b], wor[r, HD : HD + 256, :]).astype(BF)
        return jnp.stack([wide[:, 0:128], wide[:, 128:256]])

    def da_copy(b, k, frm=None):
        at = p.z if frm is None else frm
        return da_spread[b].copy_to(
            k, dab.at[b, k - 1], dat.at[b, :, rows_of(at * quarter, quarter), :]
        )

    def da_arrive(b):
        for k in range(1, pat):
            da_copy(b, k, lax.rem(p.z + pat - k, pat)).wait_recv()

    def state_grad(b, sums):
        dn_sum[b].total(tot)
        back, more_gain, more_shift = norm_back(sto[b], tot[...], vec_row(gain2))
        ds = dop[b, zrows, :].astype(F32) + back
        dst[b] = ds
        dsl[b] = ds.astype(BF)
        for k in range(1, pat):
            dab[b, k - 1] = head_grads(b, k - 1)
            da_copy(b, k).start()
        dat[b, :, zrows, :] = head_grads(b, own_slot)
        return (
            sums[0] + jnp.sum(ds, 0, keepdims=True),
            sums[1] + more_gain,
            sums[2] + more_shift,
        )

    sums = state_grad(0, (bout_sum, gain_sum, shift_sum))
    fd_sum[0].start()
    fd[1] = nn(act[1], wdown[...]).astype(BF)
    dn_sum[1].forward(2)
    sum1.step(1)
    sums = state_grad(1, sums)
    fd_sum[1].start()
    fd_sum[0].forward(1)
    vecs[...] = jnp.zeros(vecs.shape, F32)
    for r, value in ((2, sums[0]), (3, sums[1]), (4, sums[2]), (5, bup_sum), (6, bdown_sum)):
        vecs[r : r + 1, :] = value

    row8 = lax.broadcasted_iota(jnp.int32, (8, 128), 0)
    lane8 = lax.broadcasted_iota(jnp.int32, (8, 128), 1)
    pick = jnp.where(row8 == lax.div(lane8, HD), 1.0, 0.0).astype(F32)
    ri = lax.broadcasted_iota(jnp.int32, (128, 128), 0)
    ci = lax.broadcasted_iota(jnp.int32, (128, 128), 1)
    same = jnp.where(lax.div(ri, HD) == lax.div(ci, HD), 1.0, 0.0).astype(F32)

    def upstream(b):
        crd[b, p.pos] = jnp.zeros(crd.shape[2:], F32)
        crt[b, p.s] = jnp.zeros(crt.shape[2:], F32)
        for side in range(2):
            datt = dat[b, side].astype(F32)
            dn = den[b, side]
            up = datt / dn
            prod = datt * attw[b, side] / dn
            cor = exact_nn(prod, same)
            cor_rows = exact_nt(pick, prod)
            for e in range(2):
                i = 2 * side + e
                if i >= heads:
                    continue
                u = heads * b + i
                part = up if e == 1 else pltpu.roll(up, HD, 1)
                qud[u, own, :] = jnp.where(lane < HD, qp[u].astype(F32), part).astype(BF)
                qut[u, rows_of(p.s * half, half), :] = qud[
                    u, rows_of(p.pos * shard + parity[i] * half, half), :
                ]
                cor_row = cor_rows[e : e + 1, :]
                crd[b, p.pos, i : i + 1, :] = cor_row
                col = -cor[:, e * HD : e * HD + 1]
                lead = col.astype(BF).astype(F32)
                uext[u] = (
                    jnp.where(lane == COR_LANE, lead, 0.0)
                    + jnp.where(lane == COR_LANE + 1, col - lead, 0.0)
                ).astype(BF)
                crt[b, p.s, i : i + 1, :] = jnp.where(
                    parity[i] == 0, cor_row[:, 0:half], cor_row[:, half:shard]
                )
        qu_shares[b].start()
        cors[b].start()

    def query_side(qu, qe, ue, kv, ext, bias):
        kvx = jnp.concatenate([kv, ext], 1)
        s = nt(jnp.concatenate([qu * low, qe], 1), kvx)
        if bias is not None:
            s = s + bias
        dp = nt(jnp.concatenate([qu * high, ue], 1), kvx)
        return nn((jnp.exp(s) * dp).astype(BF), kv)

    def key_side(qu, qe, cor, kv, ext, bias):
        s = nt(jnp.concatenate([kv, ext], 1), jnp.concatenate([qu * low, qe], 1))
        if bias is not None:
            s = s + bias
        w = jnp.exp(s)
        dp = nt(kv, qu * high) - cor
        return nn((w * dp).astype(BF), qu * low) + nn(w.astype(BF), qu * high)

    def grads_own(b):
        bias = live_bias(first, second, p.s * shard, lens[b], shard)
        biast = live_bias(second, first, p.s * shard, lens[b], shard)
        for i in range(heads):
            u = heads * b + i
            kv, qu = kvd[u, own, :], qud[u, own, :]
            acc[u] = query_side(qu, qext[...], uext[u], kv, tab[i, 0], bias)
            ack[u] = key_side(qu, qext[...], crd[b, p.pos, i : i + 1, :], kv, tab[i, 0], biast)

    def query_rest(b):
        def dense(j, carry):
            lenl = length_lane(dense_positions(p.seg * SPAN1 + j, shard), lens[b], shard)
            for i in range(heads):
                u = heads * b + i
                kv = kvd[u, rows_of(j * shard, shard), :]
                acc[u] += query_side(
                    qud[u, own, :], qext[...], uext[u], kv, tab[i, 0] + lenl, None
                )
            return carry

        lax.fori_loop(0, p.pos, dense, 0)

        def thin(sg, carry):
            for i in range(heads):
                u = heads * b + i
                mine = rows_of(parity[i] * half, half)
                kv, ext = thin_keys(b, i, sg)
                qu = qut[u, rows_of(p.s * half, half), :]
                acc[u, mine, :] += query_side(qu, qext[mine, :], uext[u, mine, :], kv, ext, None)
            return carry

        lax.fori_loop(0, p.seg, thin, 0)

    def key_rest(b):
        lenl = length_lane(dense_positions(p.s, shard), lens[b], shard)

        def dense(j, carry):
            for i in range(heads):
                u = heads * b + i
                qu = qud[u, rows_of(j * shard, shard), :]
                ack[u] += key_side(
                    qu, qext[...], crd[b, j, i : i + 1, :], kvd[u, own, :], tab[i, 0] + lenl, None
                )
            return carry

        lax.fori_loop(p.pos + 1, SPAN1, dense, 0)

        def thin(sg, carry):
            level = level_of(sg, p.seg, levels)
            for i in range(heads):
                u = heads * b + i
                mine = rows_of(parity[i] * half, half)
                ext = tab[i, level, mine, :] + length_lane(
                    thin_positions(p.s, parity[i], shard, 1), lens[b], half
                )
                kv = kvt[u, rows_of(p.s * half, half), :]
                qu = qut[u, rows_of(sg * SPAN1 * half, SPAN1 * half), :]
                qe = jnp.concatenate([qext[mine, :]] * SPAN1, 0)
                cor = jnp.concatenate(
                    [crt[b, sg * SPAN1 + d, i : i + 1, :] for d in range(SPAN1)], 1
                )
                ack[u, mine, :] += key_side(qu, qe, cor, kv, ext, None)
            return carry

        lax.fori_loop(p.seg + 1, n // SPAN1, thin, 0)

    def send_grads(b):
        dn_sum[b].finish()
        for i in range(heads):
            dqk[b, :, i * 128 : (i + 1) * 128] = ack[heads * b + i].astype(BF)
        for t in range((heads + 1) // 2):
            tile = acc[heads * b + 2 * t]
            if 2 * t + 1 < heads:
                other = pltpu.roll(acc[heads * b + 2 * t + 1], HD, 1)
            else:
                other = jnp.zeros((shard, 128), F32)
            tile = jnp.where(lane < HD, tile, other) * HD**-0.5
            at = (heads + t) * 128
            dqk[b, :, at : at + 128] = tile.astype(BF)
        dm = nn(dqk[b, :, 0 : wp.shape[0]], wp[...])
        for t in range(pat):
            dns[b, t] = dm[t * quarter : (t + 1) * quarter].astype(BF)
        dm_sum[b].start()

    def output(b):
        fd_sum[b].total(tot)
        outf[b, zrows, :] = (sto[b] + tot[...] + vec_row(bdown)).astype(BF)
        out_line[b].start()

    da_arrive(0)
    upstream(0)
    for z in range(pat):
        part = jnp.zeros((256, width), F32)
        for b in rows:
            pair = jnp.concatenate([attf[z, b, zrows, :], attu[z, b, zrows, :]], 1)
            part = part + tn(pair, dsl[b])
        grad3[z * cols : (z + 1) * cols, :] = part[0:cols].astype(BF)
    sum3.step(0)
    da_arrive(1)
    upstream(1)
    fd_sum[0].forward(2)
    grads_own(0)
    sum3.step(1)
    fd_sum[1].forward(1)
    output(0)
    grads_own(1)
    sum1.step(2)
    fd_sum[1].forward(2)
    cors[0].pass_on()
    qu_shares[0].pass_on()
    out_line[0].forward(1)
    query_rest(0)
    output(1)
    cors[0].arrive()
    qu_shares[0].arrive()
    key_rest(0)
    send_grads(0)
    out_line[0].forward(2)
    cors[1].pass_on()
    qu_shares[1].pass_on()
    query_rest(1)
    out_line[1].forward(1)
    cors[1].arrive()
    qu_shares[1].arrive()
    key_rest(1)
    send_grads(1)
    dm_sum[0].forward(1)
    out_line[1].forward(2)
    sum3.step(2)
    sum1.step(3)
    dm_sum[0].forward(2)
    sum3.step(3)
    owner = 2 * p.core + sum3.bits[1]
    ahead = lax.rem(owner - p.z + pat, pat)

    def piece_copy(at):
        return remote(pz, pr.at[at], p_send.at[0], p_recv.at[at], (owner, p.s))

    def piece_got(at):
        return remote(
            pr.at[at], pr.at[at], p_send.at[0], p_recv.at[at], (p.other_z(1), p.s)
        )

    when(ahead != 0, lambda: piece_copy(jnp.maximum(ahead - 1, 0)).start())

    packed = tn(dqk[0, :, 0 : 3 * cols], n1[0])
    for b in range(1, batches):
        packed = packed + tn(dqk[b, :, 0 : 3 * cols], n1[b])
    for i in range(heads):
        at = i * 128
        grad2[i * HD : (i + 1) * HD, :] = packed[at : at + HD].astype(BF)
        grad2[cols + i * HD : cols + (i + 1) * HD, :] = packed[at + HD : at + 128].astype(BF)
    grad2[2 * cols : 3 * cols, :] = packed[2 * cols : 3 * cols].astype(BF)
    grad2[3 * cols : 4 * cols, :] = jnp.zeros((cols, width), BF)

    def own_piece():
        total = pz[...].astype(F32)
        for at in range(pat - 1):
            piece_got(at).wait_recv()
            total = total + pr[at].astype(F32)
        at = rows_of(3 * cols + sum3.bits[2] * (cols // 2), cols // 2)
        grad2[at, :] = total.astype(BF)

    dm_sum[1].forward(1)

    def close(b, sums):
        dm_sum[b].total(tot)
        back, more_gain, more_shift = norm_back(
            xp[b, zrows, :].astype(F32), tot[...], vec_row(gain1)
        )
        gif[b, zrows, :] = (dst[b] + back).astype(BF)
        return sums[0] + more_gain, sums[1] + more_shift

    zero = jnp.zeros((1, width), F32)
    sums = close(0, (zero, zero))
    gi_line[0].start()
    dm_sum[1].forward(2)
    when(ahead == 0, own_piece)
    sum2.step(0)
    sum1.step(4)
    sum2.step(1)
    qkv_sum = jnp.zeros((1, 3 * cols), F32)
    for b in rows:
        qkv_sum = qkv_sum + jnp.sum(dqk[b, :, 0 : 3 * cols].astype(F32), 0, keepdims=True)
    sums = close(1, sums)
    v0, v1 = vs.at[0], vs.at[1]
    v0[...] = vecs[...]
    v0[0:1, :] = sums[0]
    v0[1:2, :] = sums[1]
    for k in range(1, pat):
        zsp.copy_to(k, v0, vz.at[k - 1]).start()
    gi_line[1].start()
    gi_line[0].forward()
    sum2.step(2)
    gi_line[1].forward()
    sum2.step(3)
    for k in range(1, pat):
        zsp.copy_to(k, v0, vz.at[k - 1]).wait_recv()
    row = lax.broadcasted_iota(jnp.int32, (8, width), 0)
    extra = vz[0]
    for k in range(2, pat):
        extra = extra + vz[k - 1]
    v1[...] = v0[...] + jnp.where(row < 5, extra, 0.0)
    v1[7:8, 0 : 3 * cols] = qkv_sum

    def vec_copy(k):
        to = lax.rem(p.s + k, n)
        return remote(v1, vs.at[k + 1], v_send.at[k - 1], v_recv.at[k - 1], (p.z, to))

    for k in range(1, n):
        vec_copy(k).start()
    sum2.step(4)
    sum1.step(5)
    sum2.step(5)
    sum1.step(6)
    saves[0].start()
    for k in range(1, n):
        vec_copy(k).wait_recv()
    allv = v1[...]
    for k in range(1, n):
        allv = allv + vs[k + 1]
    vout[...] = allv
    for b in rows:
        out_line[b].arrive()
    saves[1].start()
    sum2.step(6)
    saves[2].start()
    for b in rows:
        gi_line[b].arrive()
    saves[3].start()
    for copy in saves:
        copy.wait()
    when(ahead != 0, lambda: piece_copy(jnp.maximum(ahead - 1, 0)).wait_send())
    for b in rows:
        for k in range(1, pat):
            da_copy(b, k).wait_send()
    sum3.finish()
    for item in [*kv_shares, *qu_shares, *cors, wo_line, wo_plane, *att_line]:
        item.finish()
    for item in [*fd_sum, *out_line, *dm_sum, *gi_line, sum1, sum2]:
        item.finish()
    for k in range(1, pat):
        zsp.copy_to(k, v0, vz.at[k - 1]).wait_send()
    for k in range(1, n):
        vec_copy(k).wait_send()


def finish_kernel(
    outf,
    gif,
    gsum1,
    gsum2,
    vin,
    permt,
    outp,
    ginp,
    gup,
    gdown,
    gk,
    gv,
    gq,
    gout,
    gain1,
    shift1,
    bq,
    bv,
    bout,
    gain2,
    shift2,
    bup,
    bdown,
):
    step = pl.program_id(0)
    batches = gsum1.shape[0]
    cols, width = gsum2.shape
    heads = cols // HD

    def first():
        outp[0] = nn(permt[...], outf[0]).astype(BF)
        gup[...] = gsum1[...].astype(F32)

    def second():
        ginp[0] = nn(permt[...], gif[0]).astype(BF)
        gdown[...] = gsum1[...].astype(F32)

    def vectors():
        for r, ref in enumerate((gain1, shift1, bout, gain2, shift2, bup, bdown)):
            ref[...] = vin[r : r + 1, :].reshape(width)
        bq[...] = vin[7:8, 2 * cols : 3 * cols].reshape(cols)
        bv[...] = jnp.concatenate(
            [vin[7:8, i * 128 + HD : (i + 1) * 128] for i in range(heads)], 1
        ).reshape(cols)

    when(step < 2, first)
    when(step >= 2, second)
    when(step == 0, vectors)
    for at, ref in enumerate((gk, gv, gq, gout)):

        def widen(ref=ref):
            ref[...] = gsum2[...].astype(F32)

        when(step == at, widen)


def plane_program(
    n,
    pat,
    inputs,
    lengths,
    gain_one,
    shift_one,
    w_query,
    b_query,
    w_key,
    w_value,
    b_value,
    w_out,
    b_out,
    gain_two,
    shift_two,
    w_up,
    b_up,
    w_down,
    b_down,
    d_output,
):
    B, S, W = inputs.shape
    cols = w_query.shape[1]
    hidden = w_up.shape[1]
    heads = cols // HD
    units = B * heads
    tiles = units // 2
    chips = n // 2
    half = S // 2
    quarter = S // pat
    levels = 1
    while SPAN1 << (levels - 1) < n:
        levels += 1
    perm = jnp.asarray(perm_matrix(S), BF)
    permt = jnp.asarray(perm_matrix(S).T, BF)
    qext = jnp.asarray(query_ext(S), BF)
    ktab = jnp.asarray(key_tables(S, heads * pat, levels))
    wide = 3 * cols + (-3 * cols) % 128
    r1, r2 = 2 * W, 4 * cols
    vm, sm, anyv = pltpu.VMEM, pltpu.SMEM, pl.ANY
    dma = pltpu.SemaphoreType.DMA

    outf, gif, gsum1, gsum2, vout = call(
        functools.partial(layer_kernel, n, pat, levels),
        "layer",
        [((B, S, W), BF), ((B, S, W), BF), ((r1, W), BF), ((r2, W), BF), ((8, W), F32)],
        [
            vm((S, S), BF),
            vm((S, 128), BF),
            vm((B, S, W), BF),
            vm((B, S, W), BF),
            vm((r1, W), BF),
            vm((r2, W), BF),
            vm((r1, W), BF),
            vm((r2, W), BF),
            vm((B, S, W), BF),
            vm((B, S, W), BF),
            vm((wide, W), BF),
            vm((units, S, 128), BF),
            vm((units, SPAN1 * S, 128), BF),
            vm((units, n * half, 128), BF),
            vm((heads, levels, S, 128), BF),
            vm((units, S, 128), F32),
            vm((units, S, 128), F32),
            vm((pat, B, S + half, 128), BF),
            vm((pat, B, S, 128), BF),
            vm((B, 2, S, 128), F32),
            vm((B, 2, S, 128), F32),
            vm((pat, cols + 2 * HD, W), BF),
            vm(w_up.shape, BF),
            vm(w_down.shape, BF),
            vm((S, W), F32),
            vm((B, quarter, W), F32),
            vm((B, S, W), BF),
            vm((B, S, hidden), BF),
            vm((B, S, W), BF),
            vm((B, S, hidden), BF),
            vm((B, pat, quarter, W), BF),
            vm((B, pat + 1, quarter, W), BF),
            vm((quarter, W), F32),
            vm((B, quarter, W), BF),
            vm((B, quarter, W), F32),
            vm((B, pat - 1, 2, quarter, 128), BF),
            vm((B, 2, S, 128), BF),
            vm((B, S, W), BF),
            vm((B, pat + 1, quarter, W), BF),
            vm((units, SPAN1 * S, 128), BF),
            vm((units, n * half, 128), BF),
            vm((B, SPAN1, 8, S), F32),
            vm((B, n, 8, half), F32),
            vm((units, S, 128), BF),
            vm((B, pat + 1, quarter, W), BF),
        ]
        + [vm((r1 >> d, W), BF) for d in (1, 2, 3)]
        + [vm((r2 >> d, W), BF) for d in (1, 2, 3)]
        + [vm((pat * cols, W), BF)]
        + [vm((pat * cols >> d, W), BF) for d in (1, 2, 3)]
        + [vm((cols // 2, W), BF), vm((pat - 1, cols // 2, W), BF)]
        + [vm((8, W), F32), vm((pat - 1, 8, W), F32), vm((n + 1, 8, W), F32)]
        + [dma((3 * heads + B + 7,)), dma((4,))]
        + (dense_sems(B) + thin_sems(B, chips)) * 3
        + line_sems(pat)
        + plane_sems(chips)
        + line_sems(pat) * B
        + sum_sems(pat) * B
        + [dma((B, pat - 1))] * 2
        + sum_sems(pat) * B
        + chain_sems(pat) * B
        + sum_sems(pat) * B
        + line_sems(pat) * B
        + [dma((6,))] * 6
        + [dma((1,)), dma((pat - 1,))]
        + [dma((pat - 1,))] * 2
        + [dma((n - 1,))] * 2,
        [sm] + [vm] * 9 + [anyv] * 11,
        0,
        [anyv] * 4 + [vm],
    )(
        lengths,
        gain_one,
        shift_one,
        b_query,
        b_value,
        b_out,
        gain_two,
        shift_two,
        b_up,
        b_down,
        w_query.T,
        w_key.T,
        w_value.T,
        w_out,
        perm,
        qext,
        ktab,
        inputs,
        w_up,
        w_down,
        d_output,
    )

    row_spec = lambda rows: pl.BlockSpec((rows, W), lambda i: (i, 0))
    whole = lambda shape: pl.BlockSpec(shape, lambda i: (0,) * len(shape))
    early = pl.BlockSpec((1, S, W), lambda i: (jnp.minimum(i, 1), 0, 0))
    late = pl.BlockSpec((1, S, W), lambda i: (jnp.maximum(i - 2, 0), 0, 0))
    early_rows = pl.BlockSpec((W // 2, W), lambda i: (jnp.minimum(i, 1), 0))
    late_rows = pl.BlockSpec((W // 2, W), lambda i: (jnp.maximum(i - 2, 0), 0))
    outs = [((B, S, W), BF, early), ((B, S, W), BF, late)]
    outs += [((W, W), F32, early_rows), ((W, W), F32, late_rows)]
    outs += [((cols, W), F32, whole((cols, W)))] * 4
    for size in (W, W, cols, cols, W, W, W, W, W):
        outs.append(((size,), F32, whole((size,))))
    res = pl.pallas_call(
        finish_kernel,
        name="results",
        grid=(4,),
        in_specs=[early, late, row_spec(W // 2), row_spec(cols), whole((8, W)), whole((S, S))],
        out_specs=[spec for _, _, spec in outs],
        out_shape=[jax.ShapeDtypeStruct(s, d) for s, d, _ in outs],
        compiler_params=pltpu.CompilerParams(vmem_limit_bytes=62 << 20),
    )(outf, gif, gsum1, gsum2, vout, permt)
    outputs, grad_inputs, g_up, g_down, g_k, g_v, g_q, g_out = res[:8]
    gain1, shift1, bq, bv, bout, gain2, shift2, bup, bdown = res[8:]
    return (
        outputs,
        grad_inputs,
        gain1,
        shift1,
        g_q.T,
        bq,
        g_k.T,
        g_v.T,
        bv,
        g_out,
        bout,
        gain2,
        shift2,
        g_up,
        bup,
        g_down,
        bdown,
    )


def solution(mesh):
    token = P(None, "seq", None)
    in_specs = (
        token,
        P(),
        P(),
        P(),
        P(None, "pat"),
        P("pat"),
        P(None, "pat"),
        P(None, "pat"),
        P("pat"),
        P("pat", None),
        P(),
        P(),
        P(),
        P(None, "pat"),
        P("pat"),
        P("pat", None),
        P(),
        token,
    )
    out_specs = (
        token,
        token,
        P(),
        P(),
        P(None, "pat"),
        P("pat"),
        P(None, "pat"),
        P(None, "pat"),
        P("pat"),
        P("pat", None),
        P(),
        P(),
        P(),
        P(None, "pat"),
        P("pat"),
        P("pat", None),
        P(),
    )
    n, pat = mesh.shape["seq"], mesh.shape["pat"]
    body = functools.partial(plane_program if n == 8 else shards, n, pat)
    return jax.shard_map(body, mesh=mesh, in_specs=in_specs, out_specs=out_specs, check_vma=False)
```

```python
import functools

import jax
import jax.numpy as jnp
import numpy as np
from jax import lax
from jax.experimental import pallas as pl
from jax.experimental.pallas import tpu as pltpu
from jax.sharding import PartitionSpec as P

HD = 64
SPAN1 = 4
DILATIONS = (1, 2, 4, 6, 12)
CYCLE = 12
EPS = 1e-05
NEG = -1e30
LEN_LANE = 24
COR_LANE = 25
MESH = pl.DeviceIdType.MESH
BF = jnp.bfloat16
F32 = jnp.float32
ROOT = float(np.sqrt(2.0 / np.pi))


def nn(a, b):
    return lax.dot_general(a, b, (((1,), (0,)), ((), ())), preferred_element_type=F32)


def nt(a, b):
    return lax.dot_general(a, b, (((1,), (1,)), ((), ())), preferred_element_type=F32)


def tn(a, b):
    return lax.dot_general(a, b, (((0,), (0,)), ((), ())), preferred_element_type=F32)


def exact_nt(a, b):
    return lax.dot_general(
        a, b, (((1,), (1,)), ((), ())), preferred_element_type=F32, precision=lax.Precision.HIGHEST
    )


def exact_nn(a, b):
    return lax.dot_general(
        a, b, (((1,), (0,)), ((), ())), preferred_element_type=F32, precision=lax.Precision.HIGHEST
    )


def remote(src, dst, send, recv, device):
    return pltpu.make_async_remote_copy(
        src_ref=src,
        dst_ref=dst,
        send_sem=send,
        recv_sem=recv,
        device_id=device,
        device_id_type=MESH,
    )


def when(cond, fn):
    pl.when(cond)(fn)


def rows_of(start, size):
    return pl.ds(pl.multiple_of(start, 16), size)


def orders(shard):
    p = np.arange(shard)
    return 2 * (p % (shard // 2)) + p // (shard // 2)


def perm_matrix(shard):
    token = orders(shard)
    m = np.zeros((shard, shard), np.float32)
    m[np.arange(shard), token] = 1.0
    return m


def query_ext(shard):
    cls = orders(shard) % CYCLE
    m = np.zeros((shard, 128), np.float32)
    m[np.arange(shard), cls] = 1.0
    m[np.arange(shard), CYCLE + cls] = 1.0
    m[:, LEN_LANE] = 1.0
    return m


def key_tables(shard, heads, levels):
    cls = orders(shard) % CYCLE
    out = np.zeros((heads, levels, shard, 128), np.float32)
    for h in range(heads):
        for level in range(levels):
            count = np.zeros((CYCLE, CYCLE))
            for r in DILATIONS[level:]:
                on = (np.arange(CYCLE) % r == h % r).astype(np.float64)
                count += on[:, None] * on[None, :]
            with np.errstate(divide="ignore"):
                log = np.log(count)
            high = np.where(count > 0, log, NEG).astype(np.float32).astype(jnp.bfloat16)
            low = np.where(count > 0, log - high.astype(np.float64), 0.0)
            out[h, level, :, :CYCLE] = high.astype(np.float32)[:, cls].T
            out[h, level, :, CYCLE : 2 * CYCLE] = low[:, cls].T
            out[h, level, :, COR_LANE] = 1.0
            out[h, level, :, COR_LANE + 1] = 1.0
    return out.astype(jnp.bfloat16)


class Place:
    def __init__(self, n, pat):
        self.n, self.pat = n, pat
        self.z = lax.axis_index("pat")
        self.s = lax.axis_index("seq")
        self.core = lax.rem(self.s, 2)
        self.chip = lax.div(self.s, 2)
        self.seg = lax.div(self.s, SPAN1)
        self.pos = lax.rem(self.s, SPAN1)
        self.sib = self.s + 1 - 2 * self.core
        self.even = lax.rem(self.chip, 2) == 0

    def other_z(self, k):
        return lax.rem(self.z + k, self.pat)

    def greet(self, z_axis, same_core, all_seq=False):
        bar = pltpu.get_barrier_semaphore()
        count = 0
        if z_axis:
            for k in range(1, self.pat):
                pl.semaphore_signal(
                    bar, inc=1, device_id=(self.other_z(k), self.s), device_id_type=MESH
                )
                count += 1
        if all_seq:
            for k in range(1, self.n):
                to = lax.rem(self.s + k, self.n)
                pl.semaphore_signal(bar, inc=1, device_id=(self.z, to), device_id_type=MESH)
                count += 1
        elif same_core:
            pl.semaphore_signal(bar, inc=1, device_id=(self.z, self.sib), device_id_type=MESH)
            count += 1
            for k in range(1, self.n // 2):
                to = lax.rem(self.s + 2 * k, self.n)
                pl.semaphore_signal(bar, inc=1, device_id=(self.z, to), device_id_type=MESH)
                count += 1
        return bar, count


def lane_masks():
    lane = lax.broadcasted_iota(jnp.int32, (1, 128), 1)
    low = jnp.where(lane < HD, 1.0, 0.0)
    return low.astype(BF), (1.0 - low).astype(BF)


def token_of(index, shard):
    half = jnp.where(index >= shard // 2, 1, 0)
    return 2 * (index - half * (shard // 2)) + half


def length_lane(positions, length, rows):
    lane = lax.broadcasted_iota(jnp.int32, (rows, 128), 1)
    hit = jnp.logical_and(lane == LEN_LANE, positions >= length)
    return jnp.where(hit, NEG, 0.0).astype(BF)


def dense_positions(device, shard):
    row = lax.broadcasted_iota(jnp.int32, (shard, 128), 0)
    return device * shard + token_of(row, shard)


def thin_positions(first_device, parity, shard, blocks):
    half = shard // 2
    row = lax.broadcasted_iota(jnp.int32, (blocks * half, 128), 0)
    block = lax.div(row, half)
    return (first_device + block) * shard + 2 * (row - block * half) + parity


def level_of(seg_a, seg_b, levels):
    level = jnp.int32(1)
    size = 2
    for _ in range(2, levels):
        apart = lax.div(seg_a, size) != lax.div(seg_b, size)
        level = level + jnp.where(apart, 1, 0)
        size *= 2
    return level


class Shares:
    def __init__(self, place, shard, forward, dense, thin, dense_sems, thin_sems):
        self.p, self.shard, self.forward = place, shard, forward
        self.dense, self.thin = dense, thin
        self.ds, self.ts = dense_sems, thin_sems
        p = place
        self.chips = p.n // 2
        if forward:
            self.sib_sends, self.sib_gets = p.core == 0, p.core == 1
            self.x_sends, self.x_gets = p.even, jnp.logical_not(p.even)
            self.x_to, self.x_slot = p.s + 2, p.pos - 2
        else:
            self.sib_sends, self.sib_gets = p.core == 1, p.core == 0
            self.x_sends, self.x_gets = jnp.logical_not(p.even), p.even
            self.x_to, self.x_slot = p.s - 2, p.pos + 2
        self.sib_pos = p.pos + 1 - 2 * p.core
        self.x_sib_slot = self.x_slot + 1 - 2 * p.core

    def sib_copy(self, slot):
        p = self.p
        return remote(
            self.dense(slot), self.dense(slot), self.ds[0].at[0], self.ds[1].at[0], (p.z, p.sib)
        )

    def x_copy(self, slot):
        p = self.p
        to = jnp.where(self.x_sends, self.x_to, p.sib)
        return remote(
            self.dense(slot), self.dense(slot), self.ds[0].at[1], self.ds[1].at[1], (p.z, to)
        )

    def hand_copy(self, slot):
        p = self.p
        return remote(
            self.dense(slot), self.dense(slot), self.ds[0].at[2], self.ds[1].at[2], (p.z, p.sib)
        )

    def thin_to(self, chip):
        seg = chip // 2
        return (seg > self.p.seg) if self.forward else (seg < self.p.seg)

    def thin_from(self, chip):
        seg = chip // 2
        return (seg < self.p.seg) if self.forward else (seg > self.p.seg)

    def thin_copy(self, chip):
        p = self.p
        return remote(
            self.thin(p.s),
            self.thin(p.s),
            self.ts[0].at[chip],
            self.ts[1].at[p.chip],
            (p.z, 2 * chip + p.core),
        )

    def thin_got(self, chip):
        p = self.p
        slot = 2 * chip + p.core
        return remote(
            self.thin(slot), self.thin(slot), self.ts[0].at[chip], self.ts[1].at[chip], (p.z, p.sib)
        )

    def thin_hand(self, chip, mine):
        p = self.p
        slot = 2 * chip + (p.core if mine else 1 - p.core)
        return remote(
            self.thin(slot), self.thin(slot), self.ts[2].at[chip], self.ts[3].at[chip], (p.z, p.sib)
        )

    def start(self):
        p = self.p
        for chip in range(self.chips - 1, -1, -1) if self.forward else range(self.chips):
            when(self.thin_to(chip), lambda chip=chip: self.thin_copy(chip).start())
        when(self.x_sends, lambda: self.x_copy(p.pos).start())
        when(self.sib_sends, lambda: self.sib_copy(p.pos).start())

    def pass_on(self):
        def dense_part():
            self.x_copy(self.x_slot).wait_recv()
            self.hand_copy(self.x_slot).start()

        when(self.x_gets, dense_part)
        for chip in range(self.chips):

            def thin_part(chip=chip):
                self.thin_got(chip).wait_recv()
                self.thin_hand(chip, True).start()

            when(self.thin_from(chip), thin_part)

    def arrive(self):
        when(self.sib_gets, lambda: self.sib_copy(self.sib_pos).wait_recv())
        when(self.x_gets, lambda: self.hand_copy(self.x_sib_slot).wait_recv())
        for chip in range(self.chips):
            when(
                self.thin_from(chip),
                lambda chip=chip: self.thin_hand(chip, False).wait_recv(),
            )

    def finish(self):
        p = self.p
        when(self.x_sends, lambda: self.x_copy(p.pos).wait_send())
        when(self.sib_sends, lambda: self.sib_copy(p.pos).wait_send())
        when(self.x_gets, lambda: self.hand_copy(self.x_slot).wait_send())
        for chip in range(self.chips):
            when(self.thin_to(chip), lambda chip=chip: self.thin_copy(chip).wait_send())
            when(self.thin_from(chip), lambda chip=chip: self.thin_hand(chip, True).wait_send())


def dense_sems(batches):
    return [pltpu.SemaphoreType.DMA((batches, 3))] * 2


def thin_sems(batches, chips):
    return [pltpu.SemaphoreType.DMA((batches, chips))] * 4


class Spread:
    def __init__(self, place, send, recv):
        self.p, self.send, self.recv = place, send, recv

    def copy_to(self, k, src, dst):
        p = self.p
        return remote(src, dst, self.send.at[k - 1], self.recv.at[k - 1], (p.other_z(k), p.s))


def forward_kernel(
    n,
    pat,
    levels,
    lens,
    x_ref,
    gain,
    shift,
    wq,
    bq,
    wkv,
    bkv,
    wout,
    perm,
    qext,
    ktab,
    xp,
    n1,
    qp,
    kvd,
    kvt,
    attf,
    wofp,
    attw,
    den,
    tab,
    acc,
    tab_sem,
    w_send,
    w_recv,
    a_send,
    a_recv,
    ds0,
    ds1,
    ts0,
    ts1,
    ts2,
    ts3,
):
    batches, shard, width = x_ref.shape
    half = shard // 2
    heads = wout.shape[0] // HD
    units = batches * heads
    p = Place(n, pat)
    bar, greeted = p.greet(True, True)
    low, high = lane_masks()

    def tab_copy(i):
        return pltpu.make_async_copy(ktab.at[heads * p.z + i], tab.at[i], tab_sem.at[i])

    for i in range(heads):
        tab_copy(i).start()
    for z in range(pat):
        wofp[z, 0:HD, :] = jnp.zeros((HD, width), BF)
        wofp[z, HD + heads * HD : 2 * HD + heads * HD, :] = jnp.zeros((HD, width), BF)
    wofp[p.z, HD : HD + heads * HD, :] = wout[...]
    for b in range(batches):
        xb = nn(perm[...], x_ref[b])
        xp[b] = xb.astype(BF)
        mean = jnp.mean(xb, -1, keepdims=True)
        cen = xb - mean
        var = jnp.mean(cen * cen, -1, keepdims=True)
        n1[b] = (cen * lax.rsqrt(var + EPS) * gain[...] + shift[...]).astype(BF)

    shares = [
        Shares(
            p,
            shard,
            True,
            lambda slot, b=b: kvd.at[pl.ds(heads * b, heads), rows_of(slot * shard, shard), :],
            lambda dev, b=b: kvt.at[pl.ds(heads * b, heads), rows_of(dev * half, half), :],
            [ds0.at[b], ds1.at[b]],
            [ts0.at[b], ts1.at[b], ts2.at[b], ts3.at[b]],
        )
        for b in range(batches)
    ]
    parity = [lax.rem(heads * p.z + i, 2) for i in range(heads)]
    for b in range(batches):
        q = ((nn(n1[b], wq[...]) + bq[...]).astype(BF)) * jnp.asarray(HD**-0.5, BF)
        kv = (nn(n1[b], wkv[...]) + bkv[...]).astype(BF)
        for i in range(heads):
            qp[heads * b + i] = q[:, i * 128 : (i + 1) * 128]
            kvd[heads * b + i, rows_of(p.pos * shard, shard), :] = kv[:, i * 128 : (i + 1) * 128]
        for i in range(heads):
            kvt[heads * b + i, rows_of(p.s * half, half), :] = kvd[
                heads * b + i, rows_of(p.pos * shard + parity[i] * half, half), :
            ]
        if b == 0:
            pl.semaphore_wait(bar, greeted)
        shares[b].start()
    w_spread = Spread(p, w_send, w_recv)

    def w_slot(z):
        return wofp.at[z, HD : HD + heads * HD, :]

    for k in range(1, pat):
        w_spread.copy_to(k, w_slot(p.z), w_slot(p.z)).start()
    for i in range(heads):
        tab_copy(i).wait()

    def attend(qx, kv, ext, bias):
        s = nt(qx, jnp.concatenate([kv, ext], 1))
        if bias is not None:
            s = s + bias
        return nn(jnp.exp(s).astype(BF), kv * high + low)

    own = rows_of(p.pos * shard, shard)
    qi = lax.broadcasted_iota(jnp.int32, (shard, shard), 0)
    ki = lax.broadcasted_iota(jnp.int32, (shard, shard), 1)
    qt, kt = token_of(qi, shard), token_of(ki, shard)
    for b in range(batches):
        live = jnp.logical_or(
            jnp.logical_and(kt < qt, kt + p.s * shard < lens[b]), kt == qt
        )
        bias = jnp.where(live, 0.0, NEG)
        for i in range(heads):
            u = heads * b + i
            qx = jnp.concatenate([qp[u], qext[...]], 1)
            acc[u] = attend(qx, kvd[u, own, :], tab[i, 0], bias)

    att_spread = [Spread(p, a_send.at[t], a_recv.at[t]) for t in range(units // 2)]
    lane = lax.broadcasted_iota(jnp.int32, (shard, 128), 1)
    for b in range(batches):
        shares[b].pass_on()
        shares[b].arrive()

        def dense(j, carry, b=b):
            lenl = length_lane(dense_positions(p.seg * SPAN1 + j, shard), lens[b], shard)
            for i in range(heads):
                u = heads * b + i
                qx = jnp.concatenate([qp[u], qext[...]], 1)
                kv = kvd[u, rows_of(j * shard, shard), :]
                acc[u] += attend(qx, kv, tab[i, 0] + lenl, None)
            return carry

        lax.fori_loop(0, p.pos, dense, 0)

        def thin(sg, carry, b=b):
            level = level_of(sg, p.seg, levels)
            for i in range(heads):
                u = heads * b + i
                mine = rows_of(parity[i] * half, half)
                places = thin_positions(sg * SPAN1, parity[i], shard, SPAN1)
                lenl = length_lane(places, lens[b], SPAN1 * half)
                ext = jnp.concatenate([tab[i, level, mine, :]] * SPAN1, 0) + lenl
                qx = jnp.concatenate([qp[u, mine, :], qext[mine, :]], 1)
                kv = kvt[u, rows_of(sg * SPAN1 * half, SPAN1 * half), :]
                acc[u, mine, :] += attend(qx, kv, ext, None)
            return carry

        lax.fori_loop(0, p.seg, thin, 0)
        for t in range(units // 2):
            if (2 * t + 1) // heads != b:
                continue
            even, odd = acc[2 * t], acc[2 * t + 1]
            num = jnp.where(lane < HD, pltpu.roll(even, HD, 1), odd)
            dn = jnp.where(lane < HD, even, pltpu.roll(odd, HD, 1))
            wide = num / dn
            den[t] = dn
            attw[t] = wide
            attf[p.z, t] = wide.astype(BF)
            for k in range(1, pat):
                att_spread[t].copy_to(k, attf.at[p.z, t], attf.at[p.z, t]).start()
    for k in range(1, pat):
        frm = lax.rem(p.z + pat - k, pat)
        w_spread.copy_to(k, w_slot(p.z), w_slot(p.z)).wait_send()
        w_spread.copy_to(k, w_slot(frm), w_slot(frm)).wait_recv()
        for t in range(units // 2):
            att_spread[t].copy_to(k, attf.at[p.z, t], attf.at[p.z, t]).wait_send()
            att_spread[t].copy_to(k, attf.at[frm, t], attf.at[frm, t]).wait_recv()
    for b in range(batches):
        shares[b].finish()


def middle_kernel(
    n,
    pat,
    xp,
    attf,
    wofp,
    bout,
    gain,
    shift,
    wup,
    bup,
    wdown,
    dout,
    perm,
    gud,
    fd,
    dsf,
    dst,
    sto,
    vecs,
    state,
    n2,
    act,
    dop,
    dh,
    dns,
    dno,
    dnr,
    r_send,
    r_recv,
    g_send,
    g_recv,
):
    batches, shard, width = xp.shape
    quarter = shard // pat
    p = Place(n, pat)
    bar, greeted = p.greet(True, False)
    rs = [Spread(p, r_send.at[b], r_recv.at[b]) for b in range(batches)]
    ag = [Spread(p, g_send.at[b], g_recv.at[b]) for b in range(batches)]
    bup_sum = jnp.zeros((1, width), F32)
    bdown_sum = jnp.zeros((1, width), F32)
    for b in range(batches):
        mixed = jnp.zeros((shard, width), F32)
        for z in range(pat):
            pair = jnp.concatenate([attf[z, b], attf[z, b + 1]], 1)
            weight = wofp[z, HD : HD + 256, :] if b == 0 else wofp[z, 0:256, :]
            mixed = mixed + nn(pair, weight)
        st = xp[b].astype(F32) + mixed + bout[...]
        state[b] = st
        mean = jnp.mean(st, -1, keepdims=True)
        cen = st - mean
        var = jnp.mean(cen * cen, -1, keepdims=True)
        norm = (cen * lax.rsqrt(var + EPS) * gain[...] + shift[...]).astype(BF)
        n2[b] = norm
        dob = nn(perm[...], dout[b])
        dop[b] = dob.astype(BF)
        bdown_sum = bdown_sum + jnp.sum(dob, 0, keepdims=True)
        hid = nn(norm, wup[...]) + bup[...]
        cube = hid * hid * hid
        th = jnp.tanh(ROOT * (hid + 0.044715 * cube))
        act[b] = (0.5 * hid * (1.0 + th)).astype(BF)
        slope = 0.5 * (1.0 + th) + 0.5 * hid * (1.0 - th * th) * (
            ROOT * (1.0 + 3.0 * 0.044715 * hid * hid)
        )
        dhid = (nt(dop[b], wdown[...]) * slope).astype(BF)
        dh[b] = dhid
        bup_sum = bup_sum + jnp.sum(dhid.astype(F32), 0, keepdims=True)
        dn = nt(dhid, wup[...])
        for z in range(pat):
            dns[b, z] = dn[z * quarter : (z + 1) * quarter].astype(BF)
        if b == 0:
            pl.semaphore_wait(bar, greeted)
        for k in range(1, pat):
            rs[b].copy_to(k, dns.at[b, p.other_z(k)], dnr.at[b, k - 1]).start()
    vecs[...] = jnp.zeros(vecs.shape, F32)
    for b in range(batches):
        fd[b] = nn(act[b], wdown[...]).astype(BF)
    bout_sum = jnp.zeros((1, width), F32)
    gain_sum = jnp.zeros((1, width), F32)
    shift_sum = jnp.zeros((1, width), F32)
    mine = rows_of(p.z * quarter, quarter)
    for b in range(batches):
        total = dns[b, p.z].astype(F32)
        for k in range(1, pat):
            rs[b].copy_to(k, dns.at[b, p.other_z(k)], dnr.at[b, k - 1]).wait_recv()
            total = total + dnr[b, k - 1].astype(F32)
        st = state[b, mine, :]
        sto[b] = st
        mean = jnp.mean(st, -1, keepdims=True)
        cen = st - mean
        inv = lax.rsqrt(jnp.mean(cen * cen, -1, keepdims=True) + EPS)
        hat = cen * inv
        gain_sum = gain_sum + jnp.sum(total * hat, 0, keepdims=True)
        shift_sum = shift_sum + jnp.sum(total, 0, keepdims=True)
        dhat = total * gain[...]
        back = inv * (
            dhat
            - jnp.mean(dhat, -1, keepdims=True)
            - hat * jnp.mean(dhat * hat, -1, keepdims=True)
        )
        ds = dop[b, mine, :].astype(F32) + back
        dst[b] = ds
        bout_sum = bout_sum + jnp.sum(ds, 0, keepdims=True)
        dsf[b, mine, :] = ds.astype(BF)
        for k in range(1, pat):
            ag[b].copy_to(k, dsf.at[b, mine, :], dsf.at[b, mine, :]).start()
    vecs[2:3, :] = bout_sum
    vecs[3:4, :] = gain_sum
    vecs[4:5, :] = shift_sum
    vecs[5:6, :] = bup_sum
    vecs[6:7, :] = bdown_sum
    up = tn(n2[0], dh[0])
    for b in range(1, batches):
        up = up + tn(n2[b], dh[b])
    gud[0:width, :] = up.astype(BF)
    down = tn(act[0], dop[0])
    for b in range(1, batches):
        down = down + tn(act[b], dop[b])
    gud[width : 2 * width, :] = down.astype(BF)
    for b in range(batches):
        for k in range(1, pat):
            frm = lax.rem(p.z + pat - k, pat)
            theirs = dsf.at[b, rows_of(frm * quarter, quarter), :]
            rs[b].copy_to(k, dns.at[b, p.other_z(k)], dnr.at[b, k - 1]).wait_send()
            ag[b].copy_to(k, dsf.at[b, mine, :], dsf.at[b, mine, :]).wait_send()
            ag[b].copy_to(k, theirs, theirs).wait_recv()


def backward_kernel(
    n,
    pat,
    levels,
    lens,
    dsf,
    wofp,
    attf,
    attw,
    den,
    qp,
    kvd,
    kvt,
    tab,
    qext,
    fd,
    sto,
    bdown,
    permt,
    dq,
    dkv,
    gout,
    outp,
    qud,
    qut,
    crd,
    crt,
    uext,
    acq,
    ack,
    fdr,
    outf,
    f_send,
    f_recv,
    o_send,
    o_recv,
    ds0,
    ds1,
    ts0,
    ts1,
    ts2,
    ts3,
    cd0,
    cd1,
    ct0,
    ct1,
    ct2,
    ct3,
):
    batches, shard, width = dsf.shape
    half = shard // 2
    quarter = shard // pat
    units = qp.shape[0]
    heads = units // batches
    p = Place(n, pat)
    bar, greeted = p.greet(True, True)
    low, high = lane_masks()
    parity = [lax.rem(heads * p.z + i, 2) for i in range(heads)]
    own = rows_of(p.pos * shard, shard)
    lane = lax.broadcasted_iota(jnp.int32, (shard, 128), 1)
    row8 = lax.broadcasted_iota(jnp.int32, (8, 128), 0)
    lane8 = lax.broadcasted_iota(jnp.int32, (8, 128), 1)
    pick = jnp.where(row8 == lax.div(lane8, HD), 1.0, 0.0).astype(F32)
    ri = lax.broadcasted_iota(jnp.int32, (128, 128), 0)
    ci = lax.broadcasted_iota(jnp.int32, (128, 128), 1)
    same = jnp.where(lax.div(ri, HD) == lax.div(ci, HD), 1.0, 0.0).astype(F32)

    wide = [
        nt(dsf[b], wofp[p.z, HD : HD + 256, :] if b == 0 else wofp[p.z, 0:256, :])
        for b in range(batches)
    ]
    tiles = [wide[0][:, 0:128], wide[0][:, 128:256] + wide[1][:, 0:128], wide[1][:, 128:256]]
    crd[p.pos] = jnp.zeros(crd.shape[1:], F32)
    crt[p.s] = jnp.zeros(crt.shape[1:], F32)
    for t in range(units // 2):
        dn = den[t]
        up = tiles[t] / dn
        prod = tiles[t] * attw[t] / dn
        cor = exact_nn(prod, same)
        cor_rows = exact_nt(pick, prod)
        for e in range(2):
            u = 2 * t + e
            i = u % heads
            part = up if e == 1 else pltpu.roll(up, HD, 1)
            mixed = jnp.where(lane < HD, qp[u].astype(F32), part).astype(BF)
            qud[u, own, :] = mixed
            qut[u, rows_of(p.s * half, half), :] = qud[
                u, rows_of(p.pos * shard + parity[i] * half, half), :
            ]
            crd[p.pos, u : u + 1, :] = cor_rows[e : e + 1, :]
            col = -cor[:, e * HD : e * HD + 1]
            first = col.astype(BF).astype(F32)
            ue = jnp.where(lane == COR_LANE, first, 0.0) + jnp.where(
                lane == COR_LANE + 1, col - first, 0.0
            )
            uext[u] = ue.astype(BF)
            thin_cor = jnp.where(parity[i] == 0, cor_rows[e : e + 1, 0:half], cor_rows[e : e + 1, half:shard])
            crt[p.s, u : u + 1, :] = thin_cor
    pl.semaphore_wait(bar, greeted)
    cors = Shares(
        p,
        shard,
        False,
        lambda slot: crd.at[slot],
        lambda dev: crt.at[dev],
        [cd0, cd1],
        [ct0, ct1, ct2, ct3],
    )
    shares = [
        Shares(
            p,
            shard,
            False,
            lambda slot, b=b: qud.at[pl.ds(heads * b, heads), rows_of(slot * shard, shard), :],
            lambda dev, b=b: qut.at[pl.ds(heads * b, heads), rows_of(dev * half, half), :],
            [ds0.at[b], ds1.at[b]],
            [ts0.at[b], ts1.at[b], ts2.at[b], ts3.at[b]],
        )
        for b in range(batches)
    ]
    cors.start()
    for b in range(batches):
        shares[b].start()
    fs = [Spread(p, f_send.at[b], f_recv.at[b]) for b in range(batches)]
    og = [Spread(p, o_send.at[b], o_recv.at[b]) for b in range(batches)]

    def fd_src(b, k):
        return fd.at[b, rows_of(p.other_z(k) * quarter, quarter), :]

    for b in range(batches):
        for k in range(1, pat):
            fs[b].copy_to(k, fd_src(b, k), fdr.at[b, k - 1]).start()

    def query_side(qu, qe, ue, kv, ext, bias):
        kvx = jnp.concatenate([kv, ext], 1)
        s = nt(jnp.concatenate([qu * low, qe], 1), kvx)
        if bias is not None:
            s = s + bias
        dp = nt(jnp.concatenate([qu * high, ue], 1), kvx)
        return nn((jnp.exp(s) * dp).astype(BF), kv)

    def key_side(qu, qe, cor, kv, ext, bias):
        s = nt(jnp.concatenate([kv, ext], 1), jnp.concatenate([qu * low, qe], 1))
        if bias is not None:
            s = s + bias
        w = jnp.exp(s)
        dp = nt(kv, qu * high) - cor
        return nn((w * dp).astype(BF), qu * low) + nn(w.astype(BF), qu * high)

    qi = lax.broadcasted_iota(jnp.int32, (shard, shard), 0)
    ki = lax.broadcasted_iota(jnp.int32, (shard, shard), 1)
    ti, tj = token_of(qi, shard), token_of(ki, shard)
    for b in range(batches):
        bias = jnp.where(
            jnp.logical_or(jnp.logical_and(tj < ti, tj + p.s * shard < lens[b]), tj == ti), 0.0, NEG
        )
        biast = jnp.where(
            jnp.logical_or(jnp.logical_and(ti < tj, ti + p.s * shard < lens[b]), tj == ti), 0.0, NEG
        )
        for i in range(heads):
            u = heads * b + i
            kv = kvd[u, own, :]
            qu = qud[u, own, :]
            acq[u] = query_side(qu, qext[...], uext[u], kv, tab[i, 0], bias)
            ack[u] = key_side(qu, qext[...], crd[p.pos, u : u + 1, :], kv, tab[i, 0], biast)

    for b in range(batches):

        def dense_q(j, carry, b=b):
            lenl = length_lane(dense_positions(p.seg * SPAN1 + j, shard), lens[b], shard)
            for i in range(heads):
                u = heads * b + i
                kv = kvd[u, rows_of(j * shard, shard), :]
                acq[u] += query_side(
                    qud[u, own, :], qext[...], uext[u], kv, tab[i, 0] + lenl, None
                )
            return carry

        lax.fori_loop(0, p.pos, dense_q, 0)

        def thin_q(sg, carry, b=b):
            level = level_of(sg, p.seg, levels)
            for i in range(heads):
                u = heads * b + i
                mine = rows_of(parity[i] * half, half)
                places = thin_positions(sg * SPAN1, parity[i], shard, SPAN1)
                lenl = length_lane(places, lens[b], SPAN1 * half)
                ext = jnp.concatenate([tab[i, level, mine, :]] * SPAN1, 0) + lenl
                kv = kvt[u, rows_of(sg * SPAN1 * half, SPAN1 * half), :]
                qu = qut[u, rows_of(p.s * half, half), :]
                acq[u, mine, :] += query_side(
                    qu, qext[mine, :], uext[u, mine, :], kv, ext, None
                )
            return carry

        lax.fori_loop(0, p.seg, thin_q, 0)

    zrows = rows_of(p.z * quarter, quarter)
    for b in range(batches):
        total = fd[b, zrows, :].astype(F32)
        for k in range(1, pat):
            fs[b].copy_to(k, fd_src(b, k), fdr.at[b, k - 1]).wait_recv()
            total = total + fdr[b, k - 1].astype(F32)
        outf[b, zrows, :] = (sto[b] + total + bdown[...]).astype(BF)
        for k in range(1, pat):
            og[b].copy_to(k, outf.at[b, zrows, :], outf.at[b, zrows, :]).start()
    left = tn(jnp.concatenate([attf[p.z, 0], attf[p.z, 1]], 1), dsf[0])
    right = tn(jnp.concatenate([attf[p.z, 1], attf[p.z, 2]], 1), dsf[1])
    gout[...] = (left[0 : heads * HD] + right[HD : HD + heads * HD]).astype(BF)

    cors.pass_on()
    cors.arrive()
    for b in range(batches):
        shares[b].pass_on()
        shares[b].arrive()
        lenl = length_lane(dense_positions(p.s, shard), lens[b], shard)

        def dense_k(j, carry, b=b, lenl=lenl):
            for i in range(heads):
                u = heads * b + i
                qu = qud[u, rows_of(j * shard, shard), :]
                ack[u] += key_side(
                    qu, qext[...], crd[j, u : u + 1, :], kvd[u, own, :], tab[i, 0] + lenl, None
                )
            return carry

        lax.fori_loop(p.pos + 1, SPAN1, dense_k, 0)

        def thin_k(dev, carry, b=b):
            level = level_of(lax.div(dev, SPAN1), p.seg, levels)
            for i in range(heads):
                u = heads * b + i
                mine = rows_of(parity[i] * half, half)
                ext = tab[i, level, mine, :] + length_lane(
                    thin_positions(p.s, parity[i], shard, 1), lens[b], half
                )
                kv = kvt[u, rows_of(p.s * half, half), :]
                qu = qut[u, rows_of(dev * half, half), :]
                ack[u, mine, :] += key_side(
                    qu, qext[mine, :], crt[dev, u : u + 1, :], kv, ext, None
                )
            return carry

        lax.fori_loop(SPAN1 * (p.seg + 1), n, thin_k, 0)
        for i in range(heads):
            u = heads * b + i
            lanes = slice(i * 128, (i + 1) * 128)
            dq[b, :, lanes] = (acq[u] * HD**-0.5).astype(BF)
            dkv[b, :, lanes] = ack[u].astype(BF)

    for b in range(batches):
        for k in range(1, pat):
            frm = lax.rem(p.z + pat - k, pat)
            theirs = outf.at[b, rows_of(frm * quarter, quarter), :]
            og[b].copy_to(k, theirs, theirs).wait_recv()
            og[b].copy_to(k, outf.at[b, zrows, :], outf.at[b, zrows, :]).wait_send()
            fs[b].copy_to(k, fd_src(b, k), fdr.at[b, k - 1]).wait_send()
        outp[b] = nn(permt[...], outf[b]).astype(BF)
    cors.finish()
    for b in range(batches):
        shares[b].finish()


def tail_kernel(
    n,
    pat,
    xp,
    n1,
    dq,
    dkv,
    wq,
    wkv,
    gain,
    dst,
    vecs,
    gud,
    gout,
    permt,
    ginp,
    vout,
    grad,
    dns,
    dnr,
    gif,
    v0,
    vz,
    r_send,
    r_recv,
    g_send,
    g_recv,
    z_send,
    z_recv,
):
    batches, shard, width = xp.shape
    quarter = shard // pat
    cols = gout.shape[0]
    heads = cols // HD
    p = Place(n, pat)
    bar, greeted = p.greet(True, False)
    rs = [Spread(p, r_send.at[b], r_recv.at[b]) for b in range(batches)]
    ag = [Spread(p, g_send.at[b], g_recv.at[b]) for b in range(batches)]
    for b in range(batches):
        part = nt(dq[b], wq[...]) + nt(dkv[b], wkv[...])
        for z in range(pat):
            dns[b, z] = part[z * quarter : (z + 1) * quarter].astype(BF)
        if b == 0:
            pl.semaphore_wait(bar, greeted)
        for k in range(1, pat):
            rs[b].copy_to(k, dns.at[b, p.other_z(k)], dnr.at[b, k - 1]).start()
    qsum = jnp.zeros((1, heads * 128), F32)
    vsum = jnp.zeros((1, heads * 128), F32)
    for b in range(batches):
        qsum = qsum + jnp.sum(dq[b].astype(F32), 0, keepdims=True)
        vsum = vsum + jnp.sum(dkv[b].astype(F32), 0, keepdims=True)
    grad[0 : 2 * width, :] = gud[...].astype(F32)
    base = 2 * width
    for i in range(heads):
        lanes = slice(i * 128, (i + 1) * 128)
        a = tn(dq[0, :, lanes], n1[0])
        c = tn(dkv[0, :, lanes], n1[0])
        for b in range(1, batches):
            a = a + tn(dq[b, :, lanes], n1[b])
            c = c + tn(dkv[b, :, lanes], n1[b])
        grad[base + i * HD : base + (i + 1) * HD, :] = a[0:HD]
        grad[base + cols + i * HD : base + cols + (i + 1) * HD, :] = c[0:HD]
        grad[base + 2 * cols + i * HD : base + 2 * cols + (i + 1) * HD, :] = c[HD:]
    grad[base + 3 * cols : base + 4 * cols, :] = gout[...].astype(F32)
    zrows = rows_of(p.z * quarter, quarter)
    gain_sum = jnp.zeros((1, width), F32)
    shift_sum = jnp.zeros((1, width), F32)
    for b in range(batches):
        total = dns[b, p.z].astype(F32)
        for k in range(1, pat):
            rs[b].copy_to(k, dns.at[b, p.other_z(k)], dnr.at[b, k - 1]).wait_recv()
            total = total + dnr[b, k - 1].astype(F32)
        back, more_gain, more_shift = norm_back(xp[b, zrows, :].astype(F32), total, gain[...])
        gain_sum = gain_sum + more_gain
        shift_sum = shift_sum + more_shift
        gif[b, zrows, :] = (dst[b] + back).astype(BF)
        for k in range(1, pat):
            ag[b].copy_to(k, gif.at[b, zrows, :], gif.at[b, zrows, :]).start()
    v0[...] = vecs[...]
    v0[0:1, :] = gain_sum
    v0[1:2, :] = shift_sum
    zsp = Spread(p, z_send, z_recv)
    for k in range(1, pat):
        zsp.copy_to(k, v0, vz.at[k - 1]).start()
    for k in range(1, pat):
        zsp.copy_to(k, v0, vz.at[k - 1]).wait_recv()
    row = lax.broadcasted_iota(jnp.int32, (8, width), 0)
    extra = vz[0]
    for k in range(2, pat):
        extra = extra + vz[k - 1]
    vout[0:8, :] = v0[...] + jnp.where(row < 5, extra, 0.0)
    vout[8:16, :] = jnp.zeros((8, width), F32)
    vout[8:9, 0 : heads * 128] = qsum
    vout[9:10, 0 : heads * 128] = vsum
    for b in range(batches):
        for k in range(1, pat):
            frm = lax.rem(p.z + pat - k, pat)
            theirs = gif.at[b, rows_of(frm * quarter, quarter), :]
            ag[b].copy_to(k, theirs, theirs).wait_recv()
        ginp[b] = nn(permt[...], gif[b]).astype(BF)
    for b in range(batches):
        for k in range(1, pat):
            rs[b].copy_to(k, dns.at[b, p.other_z(k)], dnr.at[b, k - 1]).wait_send()
            ag[b].copy_to(k, gif.at[b, zrows, :], gif.at[b, zrows, :]).wait_send()
    for k in range(1, pat):
        zsp.copy_to(k, v0, vz.at[k - 1]).wait_send()


def call(kernel, name, outs, scratch, specs, number, places=None):
    return pl.pallas_call(
        kernel,
        name=name,
        out_shape=[jax.ShapeDtypeStruct(s, d) for s, d in outs],
        in_specs=[pl.BlockSpec(memory_space=m) for m in specs],
        out_specs=[
            pl.BlockSpec(memory_space=m) for m in places or [pltpu.VMEM] * len(outs)
        ],
        scratch_shapes=scratch,
        compiler_params=pltpu.CompilerParams(
            collective_id=number, has_side_effects=True, vmem_limit_bytes=62 << 20
        ),
    )


def shards(
    n,
    pat,
    inputs,
    lengths,
    gain_one,
    shift_one,
    w_query,
    b_query,
    w_key,
    w_value,
    b_value,
    w_out,
    b_out,
    gain_two,
    shift_two,
    w_up,
    b_up,
    w_down,
    b_down,
    d_output,
):
    batches, shard, width = inputs.shape
    cols = w_query.shape[1]
    heads = cols // HD
    units = batches * heads
    chips = n // 2
    half = shard // 2
    quarter = shard // pat
    levels = 1
    while SPAN1 << (levels - 1) < n:
        levels += 1
    perm = jnp.asarray(perm_matrix(shard), BF)
    permt = jnp.asarray(perm_matrix(shard).T, BF)
    qext = jnp.asarray(query_ext(shard), BF)
    ktab = jnp.asarray(key_tables(shard, heads * pat, levels))
    row = lambda v: v.reshape(1, -1)
    by_head = lambda w: w.reshape(w.shape[0], heads, HD)
    pack = lambda a, b: jnp.concatenate([by_head(a), by_head(b)], 2).reshape(a.shape[0], 2 * cols)
    wq = pack(w_query, jnp.zeros_like(w_query))
    wkv = pack(w_key, w_value)
    bq = pack(row(b_query), jnp.zeros((1, cols), F32))
    bkv = pack(jnp.zeros((1, cols), F32), row(b_value))
    vm, sm, anyv = pltpu.VMEM, pltpu.SMEM, pl.ANY
    dma = pltpu.SemaphoreType.DMA
    tiles = units // 2

    xp, n1, qp, kvd, kvt, attf, wofp, attw, den, tab = call(
        functools.partial(forward_kernel, n, pat, levels),
        "attention_forward",
        [
            ((batches, shard, width), BF),
            ((batches, shard, width), BF),
            ((units, shard, 128), BF),
            ((units, SPAN1 * shard, 128), BF),
            ((units, n * half, 128), BF),
            ((pat, tiles, shard, 128), BF),
            ((pat, cols + 2 * HD, width), BF),
            ((tiles, shard, 128), F32),
            ((tiles, shard, 128), F32),
            ((heads, levels, shard, 128), BF),
        ],
        [
            pltpu.VMEM((units, shard, 128), F32),
            dma((heads,)),
            dma((pat - 1,)),
            dma((pat - 1,)),
            dma((tiles, pat - 1)),
            dma((tiles, pat - 1)),
        ]
        + dense_sems(batches)
        + thin_sems(batches, chips),
        [sm] + [vm] * 10 + [anyv],
        0,
    )(lengths, inputs, row(gain_one), row(shift_one), wq, bq, wkv, bkv, w_out, perm, qext, ktab)

    gud, fd, dsf, dst, sto, vecs = call(
        functools.partial(middle_kernel, n, pat),
        "feed_forward",
        [
            ((2 * width, width), BF),
            ((batches, shard, width), BF),
            ((batches, shard, width), BF),
            ((batches, quarter, width), F32),
            ((batches, quarter, width), F32),
            ((8, width), F32),
        ],
        [
            pltpu.VMEM((batches, shard, width), F32),
            pltpu.VMEM((batches, shard, width), BF),
            pltpu.VMEM((batches, shard, width), BF),
            pltpu.VMEM((batches, shard, width), BF),
            pltpu.VMEM((batches, shard, width), BF),
            pltpu.VMEM((batches, pat, quarter, width), BF),
            pltpu.VMEM((batches, quarter, width), F32),
            pltpu.VMEM((batches, pat - 1, quarter, width), BF),
        ]
        + [dma((batches, pat - 1))] * 4,
        [vm] * 11,
        1,
    )(
        xp,
        attf,
        wofp,
        row(b_out),
        row(gain_two),
        row(shift_two),
        w_up,
        row(b_up),
        w_down,
        d_output,
        perm,
    )

    dq, dkv, gout, outputs = call(
        functools.partial(backward_kernel, n, pat, levels),
        "attention_backward",
        [
            ((batches, shard, 2 * cols), BF),
            ((batches, shard, 2 * cols), BF),
            ((cols, width), BF),
            ((batches, shard, width), BF),
        ],
        [
            pltpu.VMEM((units, SPAN1 * shard, 128), BF),
            pltpu.VMEM((units, n * half, 128), BF),
            pltpu.VMEM((SPAN1, 8, shard), F32),
            pltpu.VMEM((n, 8, half), F32),
            pltpu.VMEM((units, shard, 128), BF),
            pltpu.VMEM((units, shard, 128), F32),
            pltpu.VMEM((units, shard, 128), F32),
            pltpu.VMEM((batches, pat - 1, quarter, width), BF),
            pltpu.VMEM((batches, shard, width), BF),
        ]
        + [dma((batches, pat - 1))] * 4
        + dense_sems(batches)
        + thin_sems(batches, chips)
        + [dma((3,))] * 2
        + [dma((chips,))] * 4,
        [sm] + [vm] * 14,
        2,
    )(lengths, dsf, wofp, attf, attw, den, qp, kvd, kvt, tab, qext, fd, sto, row(b_down), permt)

    rows = 2 * width + 4 * cols
    grad_inputs, vout, grads = call(
        functools.partial(tail_kernel, n, pat),
        "input_gradient",
        [
            ((batches, shard, width), BF),
            ((16, width), F32),
            ((rows, width), F32),
        ],
        [
            pltpu.VMEM((batches, pat, quarter, width), BF),
            pltpu.VMEM((batches, pat - 1, quarter, width), BF),
            pltpu.VMEM((batches, shard, width), BF),
            pltpu.VMEM((8, width), F32),
            pltpu.VMEM((pat - 1, 8, width), F32),
        ]
        + [dma((batches, pat - 1))] * 4
        + [dma((pat - 1,))] * 2,
        [vm] * 12,
        3,
    )(xp, n1, dq, dkv, wq, wkv, row(gain_one), dst, vecs, gud, gout, permt)
    vout, grads = lax.psum((vout, grads), "seq")
    base = 2 * width
    g_q, g_k, g_v, g_out = [grads[base + i * cols : base + (i + 1) * cols] for i in range(4)]
    q_row = vout[8, : 2 * cols].reshape(heads, 2, HD)
    v_row = vout[9, : 2 * cols].reshape(heads, 2, HD)
    return (
        outputs,
        grad_inputs,
        vout[0],
        vout[1],
        g_q.T,
        q_row[:, 0].reshape(cols),
        g_k.T,
        g_v.T,
        v_row[:, 1].reshape(cols),
        g_out,
        vout[2],
        vout[3],
        vout[4],
        grads[:width],
        vout[5],
        grads[width:base],
        vout[6],
    )


class LineGather:
    def __init__(self, place, block, send, recv):
        self.p, self.block, self.send, self.recv = place, block, send, recv

    def copy(self, frm, to, sem):
        return remote(
            self.block(frm, self.p.z),
            self.block(frm, to),
            self.send.at[sem],
            self.recv.at[frm],
            (to, self.p.s),
        )

    def got(self, frm):
        here = self.block(frm, self.p.z)
        to = lax.rem(self.p.z + 1, self.p.pat)
        return remote(here, here, self.send.at[0], self.recv.at[frm], (to, self.p.s))

    def direct(self, fn):
        last = self.p.pat - 1
        for z in range(self.p.pat):

            def own(z=z):
                for to in sorted(range(last + 1), key=lambda t: -abs(t - z)):
                    if 0 < abs(to - z) < last:
                        fn(self.copy(z, to, to))

            when(self.p.z == z, own)

    def handed(self, fn):
        last = self.p.pat - 1
        when(self.p.z == last - 1, lambda: fn(0, self.copy(0, last, last + 1)))
        when(self.p.z == 1, lambda: fn(last, self.copy(last, 0, last + 1)))

    def start(self):
        self.direct(lambda copy: copy.start())

    def forward(self):
        def hand(frm, copy):
            self.got(frm).wait_recv()
            copy.start()

        self.handed(hand)

    def arrive(self):
        last = self.p.pat - 1
        for z in range(last + 1):

            def rest(z=z):
                for frm in range(last + 1):
                    if frm != z and (z, frm) not in ((1, last), (last - 1, 0)):
                        self.got(frm).wait_recv()

            when(self.p.z == z, rest)

    def finish(self):
        self.direct(lambda copy: copy.wait_send())
        self.handed(lambda frm, copy: copy.wait_send())


class LineChain:
    def __init__(self, place, block, send, recv):
        self.p, self.block, self.send, self.recv = place, block, send, recv

    def copy(self, frm, up):
        p = self.p
        to = jnp.clip(p.z + (1 if up else -1), 0, p.pat - 1)
        return remote(
            self.block(frm),
            self.block(frm),
            self.send.at[0 if up else 1, frm],
            self.recv.at[frm],
            (to, p.s),
        )

    def start(self):
        p = self.p
        when(p.z < p.pat - 1, lambda: self.copy(p.z, True).start())
        when(p.z > 0, lambda: self.copy(p.z, False).start())

    def inner(self, hop):
        for z in range(1, self.p.pat - 1):
            if z - hop >= 0:
                yield z, z - hop, True
            if z + hop < self.p.pat:
                yield z, z + hop, False

    def got(self, frm):
        p = self.p
        here = self.block(frm)
        to = lax.rem(p.z + 1, p.pat)
        return remote(here, here, self.send.at[0, 0], self.recv.at[frm], (to, p.s))

    def forward(self, hop):
        for z, frm, up in self.inner(hop):

            def hand(frm=frm, up=up):
                self.got(frm).wait_recv()
                self.copy(frm, up).start()

            when(self.p.z == z, hand)

    def arrive(self):
        last = self.p.pat - 1
        for frm in range(self.p.pat):
            if frm > 0:
                when(self.p.z == 0, lambda frm=frm: self.got(frm).wait_recv())
            if frm < last:
                when(self.p.z == last, lambda frm=frm: self.got(frm).wait_recv())

    def finish(self):
        p = self.p
        when(p.z < p.pat - 1, lambda: self.copy(p.z, True).wait_send())
        when(p.z > 0, lambda: self.copy(p.z, False).wait_send())
        for hop in range(1, p.pat - 1):
            for z, frm, up in self.inner(hop):
                when(p.z == z, lambda frm=frm, up=up: self.copy(frm, up).wait_send())


class LineSum:
    def __init__(self, place, part, buf, send, recv):
        self.p, self.part, self.buf, self.send, self.recv = place, part, buf, send, recv

    def copy(self, z, t):
        to = z + 1 if t > z else z - 1
        at = t if (t > z or t < to) else self.p.pat
        return remote(
            self.part(t), self.buf.at[at], self.send.at[t], self.recv.at[at], (to, self.p.s)
        )

    def got(self, at):
        here = self.buf.at[at]
        to = lax.rem(self.p.z + 1, self.p.pat)
        return remote(here, here, self.send.at[0], self.recv.at[at], (to, self.p.s))

    def start(self):
        last = self.p.pat - 1

        def up():
            for t in range(last, 0, -1):
                self.copy(0, t).start()

        def down():
            for t in range(last):
                self.copy(last, t).start()

        when(self.p.z == 0, up)
        when(self.p.z == last, down)

    def inner(self, hop):
        last = self.p.pat - 1
        for z in range(1, last):
            if z == hop:
                for t in range(last, z, -1):
                    yield z, t
            if last - z == hop:
                for t in range(z):
                    yield z, t

    def forward(self, hop):
        for z, t in self.inner(hop):

            def add(z=z, t=t):
                self.got(t).wait_recv()
                part = self.part(t)
                part[...] = (part[...].astype(F32) + self.buf[t].astype(F32)).astype(BF)
                self.copy(z, t).start()

            when(self.p.z == z, add)

    def total(self, out):
        p = self.p
        out[...] = self.part(p.z)[...].astype(F32)

        def below():
            self.got(p.z).wait_recv()
            out[...] += self.buf[p.z].astype(F32)

        def above():
            self.got(p.pat).wait_recv()
            out[...] += self.buf[p.pat].astype(F32)

        when(p.z > 0, below)
        when(p.z < p.pat - 1, above)

    def finish(self):
        last = self.p.pat - 1
        for t in range(last, 0, -1):
            when(self.p.z == 0, lambda t=t: self.copy(0, t).wait_send())
        for t in range(last):
            when(self.p.z == last, lambda t=t: self.copy(last, t).wait_send())
        for hop in range(1, last):
            for z, t in self.inner(hop):
                when(self.p.z == z, lambda z=z, t=t: self.copy(z, t).wait_send())


class PlaneGather:
    def __init__(self, place, piece, sems):
        self.p, self.piece, self.sems = place, piece, sems
        self.chips = place.n // 2

    def direct(self, k, owner):
        p, sems = self.p, self.sems
        to = lax.rem(p.s + 2 * k, p.n)
        return remote(
            self.piece(owner), self.piece(owner), sems[0].at[k - 1], sems[1].at[k - 1], (p.z, to)
        )

    def hand(self, k, owner):
        p, sems = self.p, self.sems
        return remote(
            self.piece(owner), self.piece(owner), sems[2].at[k], sems[3].at[k], (p.z, p.sib)
        )

    def source(self, base, k):
        return lax.rem(base + self.p.n - 2 * k, self.p.n)

    def start(self):
        for k in range(1, self.chips):
            self.direct(k, self.p.s).start()
        self.hand(0, self.p.s).start()

    def pass_on(self):
        for k in range(1, self.chips):
            owner = self.source(self.p.s, k)
            self.direct(k, owner).wait_recv()
            self.hand(k, owner).start()

    def arrive(self):
        for k in range(self.chips):
            self.hand(k, self.source(self.p.sib, k)).wait_recv()

    def finish(self):
        for k in range(1, self.chips):
            self.direct(k, self.p.s).wait_send()
        for k in range(self.chips):
            self.hand(k, self.source(self.p.s, k)).wait_send()


def line_sems(pat):
    return [pltpu.SemaphoreType.DMA((pat + 1,)), pltpu.SemaphoreType.DMA((pat,))]


def chain_sems(pat):
    return [pltpu.SemaphoreType.DMA((2, pat)), pltpu.SemaphoreType.DMA((pat,))]


def sum_sems(pat):
    return [pltpu.SemaphoreType.DMA((pat,)), pltpu.SemaphoreType.DMA((pat + 1,))]


def plane_sems(chips):
    return [pltpu.SemaphoreType.DMA((chips - 1,))] * 2 + [pltpu.SemaphoreType.DMA((chips,))] * 2


def vec_row(ref):
    return ref[...].reshape(1, -1)


def norm_rows(values, gain, shift):
    mean = jnp.mean(values, -1, keepdims=True)
    cen = values - mean
    var = jnp.mean(cen * cen, -1, keepdims=True)
    return cen * lax.rsqrt(var + EPS) * gain + shift


def norm_back(values, grad, gain):
    mean = jnp.mean(values, -1, keepdims=True)
    cen = values - mean
    inv = lax.rsqrt(jnp.mean(cen * cen, -1, keepdims=True) + EPS)
    hat = cen * inv
    dhat = grad * gain
    back = inv * (
        dhat - jnp.mean(dhat, -1, keepdims=True) - hat * jnp.mean(dhat * hat, -1, keepdims=True)
    )
    return (
        back,
        jnp.sum(grad * hat, 0, keepdims=True),
        jnp.sum(grad, 0, keepdims=True),
    )


def live_bias(first, second, base, length, shard):
    ok = jnp.logical_or(
        jnp.logical_and(second < first, second + base < length), second == first
    )
    return jnp.where(ok, 0.0, NEG)


class TreeSum:
    def __init__(self, place, grad, out, bufs, send, recv, keep=False):
        self.p, self.grad, self.out, self.send, self.recv = place, grad, out, send, recv
        self.keep = keep
        p = place
        bit_x = lax.rem(lax.div(p.s, 2), 2)
        bit_y = lax.div(p.s, 4)
        to_x = p.s + 2 - 4 * bit_x
        to_y = p.s + 4 - 8 * bit_y
        first = p.core == 0
        self.bits = [p.core, jnp.where(first, bit_x, bit_y), jnp.where(first, bit_y, bit_x)]
        self.to = [p.sib, jnp.where(first, to_x, to_y), jnp.where(first, to_y, to_x)]
        self.bufs = bufs
        self.off, self.size = [jnp.int32(0)], [grad.shape[0]]
        for d in range(3):
            h = self.size[d] // 2
            self.off.append(self.off[d] + self.bits[d] * h)
            self.size.append(h)

    def half_of(self, d, bit):
        h = self.size[d] // 2
        return rows_of(self.off[d] + bit * h, h)

    def red(self, d):
        src = self.grad.at[self.half_of(d, 1 - self.bits[d]), :]
        return remote(
            src, self.bufs[d], self.send.at[d], self.recv.at[d], (self.p.z, self.to[d])
        )

    def back(self, d, got):
        rows = self.half_of(d, (1 - self.bits[d]) if got else self.bits[d])
        return remote(
            self.out.at[rows, :],
            self.out.at[rows, :],
            self.send.at[3 + d],
            self.recv.at[3 + d],
            (self.p.z, self.to[d]),
        )

    def step(self, d):
        if d == 0:
            self.red(0).start()
        elif d <= 3:
            self.red(d - 1).wait_recv()
            rows = rows_of(self.off[d], self.size[d])
            total = self.grad[rows, :].astype(F32) + self.bufs[d - 1][...].astype(F32)
            if d < 3:
                self.grad[rows, :] = total.astype(BF)
                self.red(d).start()
            elif self.keep:
                self.out[...] = total.astype(BF)
            else:
                self.out[rows, :] = total.astype(BF)
                self.back(2, False).start()
        else:
            self.back(6 - d, True).wait_recv()
            if d < 6:
                self.back(5 - d, False).start()

    def finish(self):
        for d in range(3):
            self.red(d).wait_send()
            if not self.keep:
                self.back(d, False).wait_send()


def layer_kernel(
    n,
    pat,
    levels,
    lens,
    gain1,
    shift1,
    bq,
    bv,
    bout,
    gain2,
    shift2,
    bup,
    bdown,
    wq_hbm,
    wk_hbm,
    wv_hbm,
    wout_hbm,
    perm_hbm,
    qext_hbm,
    ktab,
    x_hbm,
    wup_hbm,
    wdown_hbm,
    dout_hbm,
    outf_hbm,
    gif_hbm,
    gsum1_hbm,
    gsum2_hbm,
    gout_hbm,
    vout,
    perm,
    qext,
    outf,
    gif,
    gsum1,
    gsum2,
    gout,
    grad1,
    grad2,
    xp,
    n1,
    wp,
    qp,
    kvd,
    kvt,
    tab,
    acc,
    ack,
    attf,
    attu,
    attw,
    den,
    wor,
    wup,
    wdown,
    state,
    sto,
    n2,
    act,
    dop,
    dh,
    dns,
    dnr,
    tot,
    dsl,
    dst,
    dab,
    dat,
    fd,
    fdr,
    qud,
    qut,
    crd,
    crt,
    uext,
    dmr,
    a1,
    a2,
    a3,
    b1,
    b2,
    b3,
    grad3,
    c1,
    c2,
    c3,
    pz,
    pr,
    vecs,
    vz,
    vs,
    *sems,
):
    batches, shard, width = xp.shape
    half = shard // 2
    quarter = shard // pat
    cols = wout_hbm.shape[0]
    heads = cols // HD
    units = batches * heads
    tiles = units // 2
    chips = n // 2
    sems = list(sems)
    take = lambda count: [sems.pop(0) for _ in range(count)]
    p = Place(n, pat)
    bar, greeted = p.greet(True, False, True)
    low, high = lane_masks()

    own_slot = pat - 1
    pairs = [(perm_hbm, perm), (x_hbm.at[0], xp.at[0])]
    for i in range(heads):
        for off, src in ((0, wk_hbm), (HD, wv_hbm)):
            pairs.append((src.at[i * HD : (i + 1) * HD, :], wp.at[pl.ds(i * 128 + off, HD), :]))
    pairs.append((wq_hbm, wp.at[pl.ds(2 * cols, cols), :]))
    at_x = len(pairs)
    pairs += [(x_hbm.at[b], xp.at[b]) for b in range(1, batches)]
    at_out = len(pairs)
    pairs += [(wout_hbm, wor.at[own_slot, pl.ds(HD, cols), :])]
    at_tab = len(pairs)
    pairs += [(ktab.at[heads * p.z + i], tab.at[i]) for i in range(heads)] + [(qext_hbm, qext)]
    at_late = len(pairs)
    pairs += [(dout_hbm, dop), (wup_hbm, wup), (wdown_hbm, wdown)]
    load_sem, save_sem = take(2)
    loads = [
        pltpu.make_async_copy(src, dst, load_sem.at[i]) for i, (src, dst) in enumerate(pairs)
    ]
    for copy in loads:
        copy.start()
    saves = [
        pltpu.make_async_copy(src, dst, save_sem.at[i])
        for i, (src, dst) in enumerate(
            (
                (gsum1, gsum1_hbm),
                (outf, outf_hbm),
                (gsum2, gsum2_hbm),
                (gif, gif_hbm),
                (gout, gout_hbm),
            )
        )
    ]

    slot = lambda frm, at: lax.rem(frm - at + 2 * pat - 1, pat)
    out_rows, out_cols = cols // chips, width // 2

    def out_piece(dev, slots):
        chip, core = lax.div(dev, 2), lax.rem(dev, 2)
        return wor.at[
            slots,
            rows_of(HD + chip * out_rows, out_rows),
            pl.ds(pl.multiple_of(core * out_cols, 128), out_cols),
        ]

    def quarters(ref, b):
        return lambda f, *_: ref.at[b, rows_of(f * quarter, quarter), :]

    parity = [lax.rem(heads * p.z + i, 2) for i in range(heads)]

    def share_pair(forward, dense, thin):
        out = []
        sems = take(6)
        for b in range(batches):
            out.append(
                Shares(
                    p,
                    shard,
                    forward,
                    lambda at, b=b: dense.at[
                        pl.ds(heads * b, heads), rows_of(at * shard, shard), :
                    ],
                    lambda dev, b=b: thin.at[pl.ds(heads * b, heads), rows_of(dev * half, half), :],
                    [sem.at[b] for sem in sems[:2]],
                    [sem.at[b] for sem in sems[2:]],
                )
            )
        return out

    rows = range(batches)
    kv_shares = share_pair(True, kvd, kvt)
    qu_shares = share_pair(False, qud, qut)
    cor_sems = take(6)
    cors = [
        Shares(
            p,
            shard,
            False,
            lambda at, b=b: crd.at[b, at],
            lambda dev, b=b: crt.at[b, dev],
            [sem.at[b] for sem in cor_sems[:2]],
            [sem.at[b] for sem in cor_sems[2:]],
        )
        for b in rows
    ]
    wo_line = LineGather(p, lambda f, t: out_piece(p.s, slot(f, t)), *take(2))
    wo_plane = PlaneGather(p, lambda dev: out_piece(dev, pl.ds(0, pat - 1)), take(4))
    att_line = [LineGather(p, lambda f, at, b=b: attf.at[f, b], *take(2)) for b in rows]
    dn_sum = [LineSum(p, lambda t, b=b: dns.at[b, t], dnr.at[b], *take(2)) for b in rows]
    da_send, da_recv = take(2)
    da_spread = [Spread(p, da_send.at[b], da_recv.at[b]) for b in rows]
    fd_sum = [LineSum(p, quarters(fd, b), fdr.at[b], *take(2)) for b in rows]
    out_line = [LineChain(p, quarters(outf, b), *take(2)) for b in rows]
    dm_sum = [LineSum(p, lambda t, b=b: dns.at[b, t], dmr.at[b], *take(2)) for b in rows]
    dqk = dh
    gi_line = [LineChain(p, quarters(gif, b), *take(2)) for b in rows]
    sum1 = TreeSum(p, grad1, gsum1, (a1, a2, a3), *take(2))
    sum2 = TreeSum(p, grad2, gsum2, (b1, b2, b3), *take(2))
    sum3 = TreeSum(p, grad3, pz, (c1, c2, c3), *take(2), keep=True)
    p_send, p_recv, w_send, w_recv = take(4)
    z_send, z_recv, v_send, v_recv = take(4)
    zsp = Spread(p, z_send, z_recv)

    for r in range(pat):
        wor[r, 0:HD, :] = jnp.zeros((HD, width), BF)
        wor[r, HD + cols : 2 * HD + cols, :] = jnp.zeros((HD, width), BF)
    wp[3 * cols :, :] = jnp.zeros((wp.shape[0] - 3 * cols, width), BF)
    zero_bias = jnp.zeros((1, HD), F32)
    bias_v, bias_q = vec_row(bv), vec_row(bq)
    bias = []
    for i in range(heads):
        bias += [zero_bias, bias_v[:, i * HD : (i + 1) * HD]]
    bias = jnp.concatenate(bias + [bias_q, zero_bias], 1)

    own = rows_of(p.pos * shard, shard)
    zrows = rows_of(p.z * quarter, quarter)
    lane = lax.broadcasted_iota(jnp.int32, (shard, 128), 1)
    for b in rows:
        if b == 0:
            for copy in loads[:at_x]:
                copy.wait()
        else:
            loads[at_x + b - 1].wait()
        xb = nn(perm[...], xp[b])
        xp[b] = xb.astype(BF)
        n1[b] = norm_rows(xb, vec_row(gain1), vec_row(shift1)).astype(BF)
        qkv = nt(n1[b], wp[...]) + bias
        for i in range(heads):
            kv = qkv[:, i * 128 : (i + 1) * 128].astype(BF)
            kvd[heads * b + i, own, :] = kv
            t = heads + i // 2
            q = qkv[:, t * 128 : (t + 1) * 128]
            if i % 2 == 1:
                q = pltpu.roll(q, HD, 1)
            q = jnp.where(lane < HD, q, 0.0).astype(BF) * jnp.asarray(HD**-0.5, BF)
            qp[heads * b + i] = q
        for i in range(heads):
            kvt[heads * b + i, rows_of(p.s * half, half), :] = kvd[
                heads * b + i, rows_of(p.pos * shard + parity[i] * half, half), :
            ]
        if b == 0:
            pl.semaphore_wait(bar, greeted)
        if b == 0:
            kv_shares[b].start()
            loads[at_out].wait()
            wo_line.start()
    for copy in loads[at_tab:at_late]:
        copy.wait()

    def attend(qx, kv, ext, bias):
        s = nt(qx, jnp.concatenate([kv, ext], 1))
        if bias is not None:
            s = s + bias
        return nn(jnp.exp(s).astype(BF), kv * high + low)

    first = token_of(lax.broadcasted_iota(jnp.int32, (shard, shard), 0), shard)
    second = token_of(lax.broadcasted_iota(jnp.int32, (shard, shard), 1), shard)

    def attend_own(b):
        bias = live_bias(first, second, p.s * shard, lens[b], shard)
        for i in range(heads):
            u = heads * b + i
            qx = jnp.concatenate([qp[u], qext[...]], 1)
            acc[u] = attend(qx, kvd[u, own, :], tab[i, 0], bias)

    def thin_keys(b, i, sg):
        level = level_of(sg, p.seg, levels)
        places = thin_positions(sg * SPAN1, parity[i], shard, SPAN1)
        lenl = length_lane(places, lens[b], SPAN1 * half)
        part = tab[i, level, rows_of(parity[i] * half, half), :]
        ext = jnp.concatenate([part] * SPAN1, 0) + lenl
        return kvt[heads * b + i, rows_of(sg * SPAN1 * half, SPAN1 * half), :], ext

    def attend_rest(b, which):
        def dense(j, carry):
            lenl = length_lane(dense_positions(p.seg * SPAN1 + j, shard), lens[b], shard)
            for i in which:
                u = heads * b + i
                qx = jnp.concatenate([qp[u], qext[...]], 1)
                kv = kvd[u, rows_of(j * shard, shard), :]
                acc[u] += attend(qx, kv, tab[i, 0] + lenl, None)
            return carry

        lax.fori_loop(0, p.pos, dense, 0)

        def thin(sg, carry):
            for i in which:
                u = heads * b + i
                mine = rows_of(parity[i] * half, half)
                kv, ext = thin_keys(b, i, sg)
                qx = jnp.concatenate([qp[u, mine, :], qext[mine, :]], 1)
                acc[u, mine, :] += attend(qx, kv, ext, None)
            return carry

        lax.fori_loop(0, p.seg, thin, 0)

    def send_att(b):
        first_unit = heads * b
        zero, one, two = acc[first_unit], acc[first_unit + 1], acc[first_unit + 2]
        num = jnp.where(lane < HD, pltpu.roll(zero, HD, 1), one)
        dn = jnp.where(lane < HD, zero, pltpu.roll(one, HD, 1))
        wide = num / dn
        den[b, 0] = dn
        attw[b, 0] = wide
        attf[p.z, b, 0:shard, :] = wide.astype(BF)
        dn = jnp.where(lane < HD, two, 1.0)
        wide = jnp.where(lane < HD, pltpu.roll(two, HD, 1), 0.0) / dn
        den[b, 1] = dn
        attw[b, 1] = wide
        packed = wide[0:half] + pltpu.roll(wide[half:shard], HD, 1)
        attf[p.z, b, shard : shard + half, :] = packed.astype(BF)
        att_line[b].start()

    attend_own(0)
    kv_shares[1].start()
    attend_own(1)
    wo_line.forward()
    bdown_sum = jnp.zeros((1, width), F32)
    loads[at_late].wait()
    for b in rows:
        dob = nn(perm[...], dop[b])
        dop[b] = dob.astype(BF)
        bdown_sum = bdown_sum + jnp.sum(dob, 0, keepdims=True)
    kv_shares[0].pass_on()
    wo_line.arrive()
    wo_plane.start()
    kv_shares[0].arrive()
    attend_rest(0, range(heads))
    send_att(0)
    kv_shares[1].pass_on()
    kv_shares[1].arrive()
    attend_rest(1, range(0, 1))
    att_line[0].forward()
    attend_rest(1, range(1, heads))
    send_att(1)
    wo_plane.pass_on()
    for copy in loads[at_late + 1 :]:
        copy.wait()
    wo_plane.arrive()

    def feed_in(b):
        mixed = xp[b].astype(F32) + vec_row(bout)
        for r in range(pat):
            z = lax.rem(p.z + 1 + r, pat)
            packed = attf[z, b, shard : shard + half, :]
            attu[z, b, 0:half, :] = packed
            attu[z, b, half:shard, :] = pltpu.roll(packed.astype(F32), HD, 1).astype(BF)
            pair = jnp.concatenate([attf[z, b, 0:shard, :], attu[z, b]], 1)
            mixed = mixed + nn(pair, wor[r, HD : HD + 256, :])
        state[...] = mixed
        sto[b] = state[zrows, :]
        n2[b] = norm_rows(mixed, vec_row(gain2), vec_row(shift2)).astype(BF)

    def feed_out(b):
        hid = nn(n2[b], wup[...]) + vec_row(bup)
        th = jnp.tanh(ROOT * (hid + 0.044715 * (hid * hid * hid)))
        act[b] = (0.5 * hid * (1.0 + th)).astype(BF)
        slope = 0.5 * (1.0 + th) + 0.5 * hid * (1.0 - th * th) * (
            ROOT * (1.0 + 3.0 * 0.044715 * hid * hid)
        )
        dhid = (nt(dop[b], wdown[...]) * slope).astype(BF)
        dh[b] = dhid
        dn = nt(dhid, wup[...])
        for t in range(pat):
            dns[b, t] = dn[t * quarter : (t + 1) * quarter].astype(BF)
        dn_sum[b].start()
        return jnp.sum(dhid.astype(F32), 0, keepdims=True)

    att_line[0].arrive()
    feed_in(0)
    bup_sum = feed_out(0)
    att_line[1].forward()
    att_line[1].arrive()
    feed_in(1)
    dn_sum[0].forward(1)
    bup_sum = bup_sum + feed_out(1)
    fd[0] = nn(act[0], wdown[...]).astype(BF)
    dn_sum[0].forward(2)
    up = tn(n2[0], dh[0])
    for b in range(1, batches):
        up = up + tn(n2[b], dh[b])
    grad1[0:width, :] = up.astype(BF)
    dn_sum[1].forward(1)
    down = tn(act[0], dop[0])
    for b in range(1, batches):
        down = down + tn(act[b], dop[b])
    grad1[width : 2 * width, :] = down.astype(BF)
    sum1.step(0)
    bout_sum = jnp.zeros((1, width), F32)
    gain_sum = jnp.zeros((1, width), F32)
    shift_sum = jnp.zeros((1, width), F32)

    def head_grads(b, r):
        wide = nt(dsl[b], wor[r, HD : HD + 256, :]).astype(BF)
        return jnp.stack([wide[:, 0:128], wide[:, 128:256]])

    def da_copy(b, k, frm=None):
        at = p.z if frm is None else frm
        return da_spread[b].copy_to(
            k, dab.at[b, k - 1], dat.at[b, :, rows_of(at * quarter, quarter), :]
        )

    def da_arrive(b):
        for k in range(1, pat):
            da_copy(b, k, lax.rem(p.z + pat - k, pat)).wait_recv()

    def state_grad(b, sums):
        dn_sum[b].total(tot)
        back, more_gain, more_shift = norm_back(sto[b], tot[...], vec_row(gain2))
        ds = dop[b, zrows, :].astype(F32) + back
        dst[b] = ds
        dsl[b] = ds.astype(BF)
        for k in range(1, pat):
            dab[b, k - 1] = head_grads(b, k - 1)
            da_copy(b, k).start()
        dat[b, :, zrows, :] = head_grads(b, own_slot)
        return (
            sums[0] + jnp.sum(ds, 0, keepdims=True),
            sums[1] + more_gain,
            sums[2] + more_shift,
        )

    sums = state_grad(0, (bout_sum, gain_sum, shift_sum))
    fd_sum[0].start()
    fd[1] = nn(act[1], wdown[...]).astype(BF)
    dn_sum[1].forward(2)
    sum1.step(1)
    sums = state_grad(1, sums)
    fd_sum[1].start()
    fd_sum[0].forward(1)
    vecs[...] = jnp.zeros(vecs.shape, F32)
    for r, value in ((2, sums[0]), (3, sums[1]), (4, sums[2]), (5, bup_sum), (6, bdown_sum)):
        vecs[r : r + 1, :] = value

    row8 = lax.broadcasted_iota(jnp.int32, (8, 128), 0)
    lane8 = lax.broadcasted_iota(jnp.int32, (8, 128), 1)
    pick = jnp.where(row8 == lax.div(lane8, HD), 1.0, 0.0).astype(F32)
    ri = lax.broadcasted_iota(jnp.int32, (128, 128), 0)
    ci = lax.broadcasted_iota(jnp.int32, (128, 128), 1)
    same = jnp.where(lax.div(ri, HD) == lax.div(ci, HD), 1.0, 0.0).astype(F32)

    def upstream(b):
        crd[b, p.pos] = jnp.zeros(crd.shape[2:], F32)
        crt[b, p.s] = jnp.zeros(crt.shape[2:], F32)
        for side in range(2):
            datt = dat[b, side].astype(F32)
            dn = den[b, side]
            up = datt / dn
            prod = datt * attw[b, side] / dn
            cor = exact_nn(prod, same)
            cor_rows = exact_nt(pick, prod)
            for e in range(2):
                i = 2 * side + e
                if i >= heads:
                    continue
                u = heads * b + i
                part = up if e == 1 else pltpu.roll(up, HD, 1)
                qud[u, own, :] = jnp.where(lane < HD, qp[u].astype(F32), part).astype(BF)
                qut[u, rows_of(p.s * half, half), :] = qud[
                    u, rows_of(p.pos * shard + parity[i] * half, half), :
                ]
                cor_row = cor_rows[e : e + 1, :]
                crd[b, p.pos, i : i + 1, :] = cor_row
                col = -cor[:, e * HD : e * HD + 1]
                lead = col.astype(BF).astype(F32)
                uext[u] = (
                    jnp.where(lane == COR_LANE, lead, 0.0)
                    + jnp.where(lane == COR_LANE + 1, col - lead, 0.0)
                ).astype(BF)
                crt[b, p.s, i : i + 1, :] = jnp.where(
                    parity[i] == 0, cor_row[:, 0:half], cor_row[:, half:shard]
                )
        qu_shares[b].start()
        cors[b].start()

    def query_side(qu, qe, ue, kv, ext, bias):
        kvx = jnp.concatenate([kv, ext], 1)
        s = nt(jnp.concatenate([qu * low, qe], 1), kvx)
        if bias is not None:
            s = s + bias
        dp = nt(jnp.concatenate([qu * high, ue], 1), kvx)
        return nn((jnp.exp(s) * dp).astype(BF), kv)

    def key_side(qu, qe, cor, kv, ext, bias):
        s = nt(jnp.concatenate([kv, ext], 1), jnp.concatenate([qu * low, qe], 1))
        if bias is not None:
            s = s + bias
        w = jnp.exp(s)
        dp = nt(kv, qu * high) - cor
        return nn((w * dp).astype(BF), qu * low) + nn(w.astype(BF), qu * high)

    def grads_own(b):
        bias = live_bias(first, second, p.s * shard, lens[b], shard)
        biast = live_bias(second, first, p.s * shard, lens[b], shard)
        for i in range(heads):
            u = heads * b + i
            kv, qu = kvd[u, own, :], qud[u, own, :]
            acc[u] = query_side(qu, qext[...], uext[u], kv, tab[i, 0], bias)
            ack[u] = key_side(qu, qext[...], crd[b, p.pos, i : i + 1, :], kv, tab[i, 0], biast)

    def query_rest(b):
        def dense(j, carry):
            lenl = length_lane(dense_positions(p.seg * SPAN1 + j, shard), lens[b], shard)
            for i in range(heads):
                u = heads * b + i
                kv = kvd[u, rows_of(j * shard, shard), :]
                acc[u] += query_side(
                    qud[u, own, :], qext[...], uext[u], kv, tab[i, 0] + lenl, None
                )
            return carry

        lax.fori_loop(0, p.pos, dense, 0)

        def thin(sg, carry):
            for i in range(heads):
                u = heads * b + i
                mine = rows_of(parity[i] * half, half)
                kv, ext = thin_keys(b, i, sg)
                qu = qut[u, rows_of(p.s * half, half), :]
                acc[u, mine, :] += query_side(qu, qext[mine, :], uext[u, mine, :], kv, ext, None)
            return carry

        lax.fori_loop(0, p.seg, thin, 0)

    def key_rest(b):
        lenl = length_lane(dense_positions(p.s, shard), lens[b], shard)

        def dense(j, carry):
            for i in range(heads):
                u = heads * b + i
                qu = qud[u, rows_of(j * shard, shard), :]
                ack[u] += key_side(
                    qu, qext[...], crd[b, j, i : i + 1, :], kvd[u, own, :], tab[i, 0] + lenl, None
                )
            return carry

        lax.fori_loop(p.pos + 1, SPAN1, dense, 0)

        def thin(sg, carry):
            level = level_of(sg, p.seg, levels)
            for i in range(heads):
                u = heads * b + i
                mine = rows_of(parity[i] * half, half)
                ext = tab[i, level, mine, :] + length_lane(
                    thin_positions(p.s, parity[i], shard, 1), lens[b], half
                )
                kv = kvt[u, rows_of(p.s * half, half), :]
                qu = qut[u, rows_of(sg * SPAN1 * half, SPAN1 * half), :]
                qe = jnp.concatenate([qext[mine, :]] * SPAN1, 0)
                cor = jnp.concatenate(
                    [crt[b, sg * SPAN1 + d, i : i + 1, :] for d in range(SPAN1)], 1
                )
                ack[u, mine, :] += key_side(qu, qe, cor, kv, ext, None)
            return carry

        lax.fori_loop(p.seg + 1, n // SPAN1, thin, 0)

    def send_grads(b):
        dn_sum[b].finish()
        for i in range(heads):
            dqk[b, :, i * 128 : (i + 1) * 128] = ack[heads * b + i].astype(BF)
        for t in range((heads + 1) // 2):
            tile = acc[heads * b + 2 * t]
            if 2 * t + 1 < heads:
                other = pltpu.roll(acc[heads * b + 2 * t + 1], HD, 1)
            else:
                other = jnp.zeros((shard, 128), F32)
            tile = jnp.where(lane < HD, tile, other) * HD**-0.5
            at = (heads + t) * 128
            dqk[b, :, at : at + 128] = tile.astype(BF)
        dm = nn(dqk[b, :, 0 : wp.shape[0]], wp[...])
        for t in range(pat):
            dns[b, t] = dm[t * quarter : (t + 1) * quarter].astype(BF)
        dm_sum[b].start()

    def output(b):
        fd_sum[b].total(tot)
        outf[b, zrows, :] = (sto[b] + tot[...] + vec_row(bdown)).astype(BF)
        out_line[b].start()

    da_arrive(0)
    upstream(0)
    for z in range(pat):
        part = jnp.zeros((256, width), F32)
        for b in rows:
            pair = jnp.concatenate([attf[z, b, zrows, :], attu[z, b, zrows, :]], 1)
            part = part + tn(pair, dsl[b])
        grad3[z * cols : (z + 1) * cols, :] = part[0:cols].astype(BF)
    sum3.step(0)
    da_arrive(1)
    upstream(1)
    fd_sum[0].forward(2)
    grads_own(0)
    sum3.step(1)
    fd_sum[1].forward(1)
    output(0)
    grads_own(1)
    sum1.step(2)
    fd_sum[1].forward(2)
    cors[0].pass_on()
    qu_shares[0].pass_on()
    query_rest(0)
    out_line[0].forward(1)
    output(1)
    cors[0].arrive()
    qu_shares[0].arrive()
    key_rest(0)
    send_grads(0)
    out_line[0].forward(2)
    cors[1].pass_on()
    qu_shares[1].pass_on()
    query_rest(1)
    out_line[1].forward(1)
    cors[1].arrive()
    qu_shares[1].arrive()
    key_rest(1)
    send_grads(1)
    dm_sum[0].forward(1)
    out_line[1].forward(2)
    sum3.step(2)
    sum1.step(3)
    dm_sum[0].forward(2)
    sum3.step(3)
    owner = 2 * p.core + sum3.bits[1]
    ahead = lax.rem(owner - p.z + pat, pat)

    def piece_copy(at):
        return remote(pz, pr.at[at], p_send.at[0], p_recv.at[at], (owner, p.s))

    def piece_got(at):
        return remote(
            pr.at[at], pr.at[at], p_send.at[0], p_recv.at[at], (p.other_z(1), p.s)
        )

    when(ahead != 0, lambda: piece_copy(jnp.maximum(ahead - 1, 0)).start())

    packed = tn(dqk[0, :, 0 : 3 * cols], n1[0])
    for b in range(1, batches):
        packed = packed + tn(dqk[b, :, 0 : 3 * cols], n1[b])
    for i in range(heads):
        at = i * 128
        grad2[i * HD : (i + 1) * HD, :] = packed[at : at + HD].astype(BF)
        grad2[cols + i * HD : cols + (i + 1) * HD, :] = packed[at + HD : at + 128].astype(BF)
    grad2[2 * cols : 3 * cols, :] = packed[2 * cols : 3 * cols].astype(BF)
    grad2[3 * cols :, :] = jnp.zeros((grad2.shape[0] - 3 * cols, width), BF)
    sum2.step(0)
    sum1.step(4)

    def piece_rows(at):
        return gout.at[rows_of(at * (cols // 2), cols // 2), :]

    def piece_out(k):
        rows = piece_rows(sum3.bits[2])
        to = lax.rem(p.s + k, n)
        return remote(rows, rows, w_send.at[k - 1], w_recv.at[sum3.bits[2]], (p.z, to))

    def piece_in(at):
        rows = piece_rows(at)
        return remote(rows, rows, w_send.at[0], w_recv.at[at], (p.z, p.sib))

    def own_piece():
        total = pz[...].astype(F32)
        for at in range(pat - 1):
            piece_got(at).wait_recv()
            total = total + pr[at].astype(F32)
        piece_rows(sum3.bits[2])[...] = total.astype(BF)
        for k in range(1, n):
            piece_out(k).start()

    dm_sum[1].forward(1)

    def close(b, sums):
        dm_sum[b].total(tot)
        back, more_gain, more_shift = norm_back(
            xp[b, zrows, :].astype(F32), tot[...], vec_row(gain1)
        )
        gif[b, zrows, :] = (dst[b] + back).astype(BF)
        return sums[0] + more_gain, sums[1] + more_shift

    zero = jnp.zeros((1, width), F32)
    sums = close(0, (zero, zero))
    gi_line[0].start()
    sum2.step(1)
    dm_sum[1].forward(2)
    gi_line[0].forward(1)
    when(ahead == 0, own_piece)
    sum1.step(5)
    qkv_sum = jnp.zeros((1, 3 * cols), F32)
    for b in rows:
        qkv_sum = qkv_sum + jnp.sum(dqk[b, :, 0 : 3 * cols].astype(F32), 0, keepdims=True)
    sums = close(1, sums)
    v0, v1 = vs.at[0], vs.at[1]
    v0[...] = vecs[...]
    v0[0:1, :] = sums[0]
    v0[1:2, :] = sums[1]
    for k in range(1, pat):
        zsp.copy_to(k, v0, vz.at[k - 1]).start()
    gi_line[1].start()
    sum2.step(2)
    gi_line[0].forward(2)
    gi_line[1].forward(1)
    sum2.step(3)
    gi_line[1].forward(2)
    for k in range(1, pat):
        zsp.copy_to(k, v0, vz.at[k - 1]).wait_recv()
    row = lax.broadcasted_iota(jnp.int32, (8, width), 0)
    extra = vz[0]
    for k in range(2, pat):
        extra = extra + vz[k - 1]
    v1[...] = v0[...] + jnp.where(row < 5, extra, 0.0)
    v1[7:8, 0 : 3 * cols] = qkv_sum

    def vec_copy(k):
        to = lax.rem(p.s + k, n)
        return remote(v1, vs.at[k + 1], v_send.at[k - 1], v_recv.at[k - 1], (p.z, to))

    for k in range(1, n):
        vec_copy(k).start()
    sum2.step(4)
    sum1.step(6)
    saves[0].start()
    sum2.step(5)
    for at in range(2):
        mine = jnp.logical_and(ahead == 0, sum3.bits[2] == at)
        when(jnp.logical_not(mine), lambda at=at: piece_in(at).wait_recv())
    saves[4].start()
    for k in range(1, n):
        vec_copy(k).wait_recv()
    allv = v1[...]
    for k in range(1, n):
        allv = allv + vs[k + 1]
    vout[...] = allv
    for b in rows:
        out_line[b].arrive()
    saves[1].start()
    sum2.step(6)
    saves[2].start()
    for b in rows:
        gi_line[b].arrive()
    saves[3].start()
    for copy in saves:
        copy.wait()
    when(ahead != 0, lambda: piece_copy(jnp.maximum(ahead - 1, 0)).wait_send())
    for k in range(1, n):
        when(ahead == 0, lambda k=k: piece_out(k).wait_send())
    for b in rows:
        for k in range(1, pat):
            da_copy(b, k).wait_send()
    sum3.finish()
    for item in [*kv_shares, *qu_shares, *cors, wo_line, wo_plane, *att_line]:
        item.finish()
    for item in [*fd_sum, *out_line, *dm_sum, *gi_line, sum1, sum2]:
        item.finish()
    for k in range(1, pat):
        zsp.copy_to(k, v0, vz.at[k - 1]).wait_send()
    for k in range(1, n):
        vec_copy(k).wait_send()


def finish_kernel(
    vin,
    permt_hbm,
    outf_hbm,
    gif_hbm,
    gsum1_hbm,
    gsum2_hbm,
    gsum3_hbm,
    gain1,
    shift1,
    bq,
    bv,
    bout,
    gain2,
    shift2,
    bup,
    bdown,
    outp_hbm,
    ginp_hbm,
    gup_hbm,
    gdown_hbm,
    gk_hbm,
    gv_hbm,
    gq_hbm,
    gout_hbm,
    permt,
    outf,
    gif,
    gsum1,
    gsum2,
    gsum3,
    outp,
    ginp,
    gup,
    gdown,
    gk,
    gv,
    gq,
    gout,
    load_sem,
    save_sem,
):
    batches = outf.shape[0]
    cols, width = gsum3.shape
    heads = cols // HD
    jobs = []

    def widen(src, dst):
        def run():
            dst[...] = src[...].astype(F32)

        return run

    def turn(src, dst):
        def run():
            dst[...] = nn(permt[...], src[...]).astype(BF)

        return run

    parts = 4
    for src_hbm, src, dst, dst_hbm in (
        (gsum1_hbm.at[0:width], gsum1.at[0:width], gup, gup_hbm),
        (gsum1_hbm.at[width : 2 * width], gsum1.at[width : 2 * width], gdown, gdown_hbm),
    ):
        step = width // parts
        for i in range(parts):
            rows = slice(i * step, (i + 1) * step)
            jobs.append(
                (src_hbm.at[rows], src.at[rows], widen(src.at[rows], dst.at[rows]), dst.at[rows], dst_hbm.at[rows])
            )
    for b in range(batches):
        for src_hbm, src, dst, dst_hbm in (
            (outf_hbm, outf, outp, outp_hbm),
            (gif_hbm, gif, ginp, ginp_hbm),
        ):
            jobs.append((src_hbm.at[b], src.at[b], turn(src.at[b], dst.at[b]), dst.at[b], dst_hbm.at[b]))
    for i, (dst, dst_hbm) in enumerate(((gk, gk_hbm), (gv, gv_hbm), (gq, gq_hbm))):
        rows = slice(i * cols, (i + 1) * cols)
        jobs.append((gsum2_hbm.at[rows], gsum2.at[rows], widen(gsum2.at[rows], dst), dst, dst_hbm))
    jobs.append((gsum3_hbm, gsum3, widen(gsum3, gout), gout, gout_hbm))

    loads = [
        pltpu.make_async_copy(job[0], job[1], load_sem.at[i]) for i, job in enumerate(jobs)
    ]
    perm_load = pltpu.make_async_copy(permt_hbm, permt, load_sem.at[len(jobs)])
    saves = [
        pltpu.make_async_copy(job[3], job[4], save_sem.at[i]) for i, job in enumerate(jobs)
    ]
    for i, copy in enumerate(loads):
        copy.start()
        if i == 0:
            perm_load.start()
    for r, ref in enumerate((gain1, shift1, bout, gain2, shift2, bup, bdown)):
        ref[...] = vin[r : r + 1, :].reshape(width)
    bq[...] = vin[7:8, 2 * cols : 3 * cols].reshape(cols)
    bv[...] = jnp.concatenate(
        [vin[7:8, i * 128 + HD : (i + 1) * 128] for i in range(heads)], 1
    ).reshape(cols)
    perm_load.wait()
    for i, job in enumerate(jobs):
        loads[i].wait()
        job[2]()
        saves[i].start()
    for copy in saves:
        copy.wait()


def plane_program(
    n,
    pat,
    inputs,
    lengths,
    gain_one,
    shift_one,
    w_query,
    b_query,
    w_key,
    w_value,
    b_value,
    w_out,
    b_out,
    gain_two,
    shift_two,
    w_up,
    b_up,
    w_down,
    b_down,
    d_output,
):
    B, S, W = inputs.shape
    cols = w_query.shape[1]
    hidden = w_up.shape[1]
    heads = cols // HD
    units = B * heads
    tiles = units // 2
    chips = n // 2
    half = S // 2
    quarter = S // pat
    levels = 1
    while SPAN1 << (levels - 1) < n:
        levels += 1
    perm = jnp.asarray(perm_matrix(S), BF)
    permt = jnp.asarray(perm_matrix(S).T, BF)
    qext = jnp.asarray(query_ext(S), BF)
    ktab = jnp.asarray(key_tables(S, heads * pat, levels))
    wide = 3 * cols + (-3 * cols) % 128
    r1, r2 = 2 * W, wide
    vm, sm, anyv = pltpu.VMEM, pltpu.SMEM, pl.ANY
    dma = pltpu.SemaphoreType.DMA

    outf, gif, gsum1, gsum2, gout, vout = call(
        functools.partial(layer_kernel, n, pat, levels),
        "layer",
        [
            ((B, S, W), BF),
            ((B, S, W), BF),
            ((r1, W), BF),
            ((r2, W), BF),
            ((cols, W), BF),
            ((8, W), F32),
        ],
        [
            vm((S, S), BF),
            vm((S, 128), BF),
            vm((B, S, W), BF),
            vm((B, S, W), BF),
            vm((r1, W), BF),
            vm((r2, W), BF),
            vm((cols, W), BF),
            vm((r1, W), BF),
            vm((r2, W), BF),
            vm((B, S, W), BF),
            vm((B, S, W), BF),
            vm((wide, W), BF),
            vm((units, S, 128), BF),
            vm((units, SPAN1 * S, 128), BF),
            vm((units, n * half, 128), BF),
            vm((heads, levels, S, 128), BF),
            vm((units, S, 128), F32),
            vm((units, S, 128), F32),
            vm((pat, B, S + half, 128), BF),
            vm((pat, B, S, 128), BF),
            vm((B, 2, S, 128), F32),
            vm((B, 2, S, 128), F32),
            vm((pat, cols + 2 * HD, W), BF),
            vm(w_up.shape, BF),
            vm(w_down.shape, BF),
            vm((S, W), F32),
            vm((B, quarter, W), F32),
            vm((B, S, W), BF),
            vm((B, S, hidden), BF),
            vm((B, S, W), BF),
            vm((B, S, hidden), BF),
            vm((B, pat, quarter, W), BF),
            vm((B, pat + 1, quarter, W), BF),
            vm((quarter, W), F32),
            vm((B, quarter, W), BF),
            vm((B, quarter, W), F32),
            vm((B, pat - 1, 2, quarter, 128), BF),
            vm((B, 2, S, 128), BF),
            vm((B, S, W), BF),
            vm((B, pat + 1, quarter, W), BF),
            vm((units, SPAN1 * S, 128), BF),
            vm((units, n * half, 128), BF),
            vm((B, SPAN1, 8, S), F32),
            vm((B, n, 8, half), F32),
            vm((units, S, 128), BF),
            vm((B, pat + 1, quarter, W), BF),
        ]
        + [vm((r1 >> d, W), BF) for d in (1, 2, 3)]
        + [vm((r2 >> d, W), BF) for d in (1, 2, 3)]
        + [vm((pat * cols, W), BF)]
        + [vm((pat * cols >> d, W), BF) for d in (1, 2, 3)]
        + [vm((cols // 2, W), BF), vm((pat - 1, cols // 2, W), BF)]
        + [vm((8, W), F32), vm((pat - 1, 8, W), F32), vm((n + 1, 8, W), F32)]
        + [dma((3 * heads + B + 7,)), dma((5,))]
        + (dense_sems(B) + thin_sems(B, chips)) * 3
        + line_sems(pat)
        + plane_sems(chips)
        + line_sems(pat) * B
        + sum_sems(pat) * B
        + [dma((B, pat - 1))] * 2
        + sum_sems(pat) * B
        + chain_sems(pat) * B
        + sum_sems(pat) * B
        + chain_sems(pat) * B
        + [dma((6,))] * 6
        + [dma((1,)), dma((pat - 1,)), dma((n - 1,)), dma((2,))]
        + [dma((pat - 1,))] * 2
        + [dma((n - 1,))] * 2,
        [sm] + [vm] * 9 + [anyv] * 11,
        0,
        [anyv] * 5 + [vm],
    )(
        lengths,
        gain_one,
        shift_one,
        b_query,
        b_value,
        b_out,
        gain_two,
        shift_two,
        b_up,
        b_down,
        w_query.T,
        w_key.T,
        w_value.T,
        w_out,
        perm,
        qext,
        ktab,
        inputs,
        w_up,
        w_down,
        d_output,
    )

    small = [((size,), F32) for size in (W, W, cols, cols, W, W, W, W, W)]
    large = [((B, S, W), BF)] * 2 + [((W, W), F32)] * 2 + [((cols, W), F32)] * 4
    jobs = 8 + 2 * B + 4
    res = pl.pallas_call(
        finish_kernel,
        name="results",
        in_specs=[pl.BlockSpec(memory_space=m) for m in [vm] + [anyv] * 6],
        out_specs=[pl.BlockSpec(memory_space=m) for m in [vm] * len(small) + [anyv] * len(large)],
        out_shape=[jax.ShapeDtypeStruct(s, d) for s, d in small + large],
        scratch_shapes=[
            vm((S, S), BF),
            vm((B, S, W), BF),
            vm((B, S, W), BF),
            vm((r1, W), BF),
            vm((r2, W), BF),
            vm((cols, W), BF),
        ]
        + [vm(s, d) for s, d in large]
        + [dma((jobs + 1,)), dma((jobs,))],
        compiler_params=pltpu.CompilerParams(vmem_limit_bytes=62 << 20),
    )(vout, permt, outf, gif, gsum1, gsum2, gout)
    gain1, shift1, bq, bv, bout, gain2, shift2, bup, bdown = res[:9]
    outputs, grad_inputs, g_up, g_down, g_k, g_v, g_q, g_out = res[9:]
    return (
        outputs,
        grad_inputs,
        gain1,
        shift1,
        g_q.T,
        bq,
        g_k.T,
        g_v.T,
        bv,
        g_out,
        bout,
        gain2,
        shift2,
        g_up,
        bup,
        g_down,
        bdown,
    )


def solution(mesh):
    token = P(None, "seq", None)
    in_specs = (
        token,
        P(),
        P(),
        P(),
        P(None, "pat"),
        P("pat"),
        P(None, "pat"),
        P(None, "pat"),
        P("pat"),
        P("pat", None),
        P(),
        P(),
        P(),
        P(None, "pat"),
        P("pat"),
        P("pat", None),
        P(),
        token,
    )
    out_specs = (
        token,
        token,
        P(),
        P(),
        P(None, "pat"),
        P("pat"),
        P(None, "pat"),
        P(None, "pat"),
        P("pat"),
        P("pat", None),
        P(),
        P(),
        P(),
        P(None, "pat"),
        P("pat"),
        P("pat", None),
        P(),
    )
    n, pat = mesh.shape["seq"], mesh.shape["pat"]
    body = functools.partial(plane_program if n == 8 else shards, n, pat)
    return jax.shard_map(body, mesh=mesh, in_specs=in_specs, out_specs=out_specs, check_vma=False)
```

```python
import functools

import jax
import jax.numpy as jnp
import numpy as np
from jax import lax
from jax.experimental import pallas as pl
from jax.experimental.pallas import tpu as pltpu
from jax.sharding import PartitionSpec as P

HD = 64
SPAN1 = 4
DILATIONS = (1, 2, 4, 6, 12)
CYCLE = 12
EPS = 1e-05
NEG = -1e30
LEN_LANE = 24
COR_LANE = 25
MESH = pl.DeviceIdType.MESH
BF = jnp.bfloat16
F32 = jnp.float32
ROOT = float(np.sqrt(2.0 / np.pi))


def nn(a, b):
    return lax.dot_general(a, b, (((1,), (0,)), ((), ())), preferred_element_type=F32)


def nt(a, b):
    return lax.dot_general(a, b, (((1,), (1,)), ((), ())), preferred_element_type=F32)


def tn(a, b):
    return lax.dot_general(a, b, (((0,), (0,)), ((), ())), preferred_element_type=F32)


def exact_nt(a, b):
    return lax.dot_general(
        a, b, (((1,), (1,)), ((), ())), preferred_element_type=F32, precision=lax.Precision.HIGHEST
    )


def exact_nn(a, b):
    return lax.dot_general(
        a, b, (((1,), (0,)), ((), ())), preferred_element_type=F32, precision=lax.Precision.HIGHEST
    )


def remote(src, dst, send, recv, device):
    return pltpu.make_async_remote_copy(
        src_ref=src,
        dst_ref=dst,
        send_sem=send,
        recv_sem=recv,
        device_id=device,
        device_id_type=MESH,
    )


def when(cond, fn):
    pl.when(cond)(fn)


def rows_of(start, size):
    return pl.ds(pl.multiple_of(start, 16), size)


def orders(shard):
    p = np.arange(shard)
    return 2 * (p % (shard // 2)) + p // (shard // 2)


def perm_matrix(shard):
    token = orders(shard)
    m = np.zeros((shard, shard), np.float32)
    m[np.arange(shard), token] = 1.0
    return m


def query_ext(shard):
    cls = orders(shard) % CYCLE
    m = np.zeros((shard, 128), np.float32)
    m[np.arange(shard), cls] = 1.0
    m[np.arange(shard), CYCLE + cls] = 1.0
    m[:, LEN_LANE] = 1.0
    return m


def key_tables(shard, heads, levels):
    cls = orders(shard) % CYCLE
    out = np.zeros((heads, levels, shard, 128), np.float32)
    for h in range(heads):
        for level in range(levels):
            count = np.zeros((CYCLE, CYCLE))
            for r in DILATIONS[level:]:
                on = (np.arange(CYCLE) % r == h % r).astype(np.float64)
                count += on[:, None] * on[None, :]
            with np.errstate(divide="ignore"):
                log = np.log(count)
            high = np.where(count > 0, log, NEG).astype(np.float32).astype(jnp.bfloat16)
            low = np.where(count > 0, log - high.astype(np.float64), 0.0)
            out[h, level, :, :CYCLE] = high.astype(np.float32)[:, cls].T
            out[h, level, :, CYCLE : 2 * CYCLE] = low[:, cls].T
            out[h, level, :, COR_LANE] = 1.0
            out[h, level, :, COR_LANE + 1] = 1.0
    return out.astype(jnp.bfloat16)


class Place:
    def __init__(self, n, pat):
        self.n, self.pat = n, pat
        self.z = lax.axis_index("pat")
        self.s = lax.axis_index("seq")
        self.core = lax.rem(self.s, 2)
        self.chip = lax.div(self.s, 2)
        self.seg = lax.div(self.s, SPAN1)
        self.pos = lax.rem(self.s, SPAN1)
        self.sib = self.s + 1 - 2 * self.core
        self.even = lax.rem(self.chip, 2) == 0

    def other_z(self, k):
        return lax.rem(self.z + k, self.pat)

    def greet(self, z_axis, same_core, all_seq=False):
        bar = pltpu.get_barrier_semaphore()
        count = 0
        if z_axis:
            for k in range(1, self.pat):
                pl.semaphore_signal(
                    bar, inc=1, device_id=(self.other_z(k), self.s), device_id_type=MESH
                )
                count += 1
        if all_seq:
            for k in range(1, self.n):
                to = lax.rem(self.s + k, self.n)
                pl.semaphore_signal(bar, inc=1, device_id=(self.z, to), device_id_type=MESH)
                count += 1
        elif same_core:
            pl.semaphore_signal(bar, inc=1, device_id=(self.z, self.sib), device_id_type=MESH)
            count += 1
            for k in range(1, self.n // 2):
                to = lax.rem(self.s + 2 * k, self.n)
                pl.semaphore_signal(bar, inc=1, device_id=(self.z, to), device_id_type=MESH)
                count += 1
        return bar, count


def lane_masks():
    lane = lax.broadcasted_iota(jnp.int32, (1, 128), 1)
    low = jnp.where(lane < HD, 1.0, 0.0)
    return low.astype(BF), (1.0 - low).astype(BF)


def token_of(index, shard):
    half = jnp.where(index >= shard // 2, 1, 0)
    return 2 * (index - half * (shard // 2)) + half


def length_lane(positions, length, rows):
    lane = lax.broadcasted_iota(jnp.int32, (rows, 128), 1)
    hit = jnp.logical_and(lane == LEN_LANE, positions >= length)
    return jnp.where(hit, NEG, 0.0).astype(BF)


def dense_positions(device, shard):
    row = lax.broadcasted_iota(jnp.int32, (shard, 128), 0)
    return device * shard + token_of(row, shard)


def thin_positions(first_device, parity, shard, blocks):
    half = shard // 2
    row = lax.broadcasted_iota(jnp.int32, (blocks * half, 128), 0)
    block = lax.div(row, half)
    return (first_device + block) * shard + 2 * (row - block * half) + parity


def level_of(seg_a, seg_b, levels):
    level = jnp.int32(1)
    size = 2
    for _ in range(2, levels):
        apart = lax.div(seg_a, size) != lax.div(seg_b, size)
        level = level + jnp.where(apart, 1, 0)
        size *= 2
    return level


class Shares:
    def __init__(self, place, shard, forward, dense, thin, dense_sems, thin_sems):
        self.p, self.shard, self.forward = place, shard, forward
        self.dense, self.thin = dense, thin
        self.ds, self.ts = dense_sems, thin_sems
        p = place
        self.chips = p.n // 2
        if forward:
            self.sib_sends, self.sib_gets = p.core == 0, p.core == 1
            self.x_sends, self.x_gets = p.even, jnp.logical_not(p.even)
            self.x_to, self.x_slot = p.s + 2, p.pos - 2
        else:
            self.sib_sends, self.sib_gets = p.core == 1, p.core == 0
            self.x_sends, self.x_gets = jnp.logical_not(p.even), p.even
            self.x_to, self.x_slot = p.s - 2, p.pos + 2
        self.sib_pos = p.pos + 1 - 2 * p.core
        self.x_sib_slot = self.x_slot + 1 - 2 * p.core

    def sib_copy(self, slot):
        p = self.p
        return remote(
            self.dense(slot), self.dense(slot), self.ds[0].at[0], self.ds[1].at[0], (p.z, p.sib)
        )

    def x_copy(self, slot):
        p = self.p
        to = jnp.where(self.x_sends, self.x_to, p.sib)
        return remote(
            self.dense(slot), self.dense(slot), self.ds[0].at[1], self.ds[1].at[1], (p.z, to)
        )

    def hand_copy(self, slot):
        p = self.p
        return remote(
            self.dense(slot), self.dense(slot), self.ds[0].at[2], self.ds[1].at[2], (p.z, p.sib)
        )

    def thin_to(self, chip):
        seg = chip // 2
        return (seg > self.p.seg) if self.forward else (seg < self.p.seg)

    def thin_from(self, chip):
        seg = chip // 2
        return (seg < self.p.seg) if self.forward else (seg > self.p.seg)

    def thin_copy(self, chip):
        p = self.p
        return remote(
            self.thin(p.s),
            self.thin(p.s),
            self.ts[0].at[chip],
            self.ts[1].at[p.chip],
            (p.z, 2 * chip + p.core),
        )

    def thin_got(self, chip):
        p = self.p
        slot = 2 * chip + p.core
        return remote(
            self.thin(slot), self.thin(slot), self.ts[0].at[chip], self.ts[1].at[chip], (p.z, p.sib)
        )

    def thin_hand(self, chip, mine):
        p = self.p
        slot = 2 * chip + (p.core if mine else 1 - p.core)
        return remote(
            self.thin(slot), self.thin(slot), self.ts[2].at[chip], self.ts[3].at[chip], (p.z, p.sib)
        )

    def start(self):
        p = self.p
        for chip in range(self.chips - 1, -1, -1) if self.forward else range(self.chips):
            when(self.thin_to(chip), lambda chip=chip: self.thin_copy(chip).start())
        when(self.x_sends, lambda: self.x_copy(p.pos).start())
        when(self.sib_sends, lambda: self.sib_copy(p.pos).start())

    def pass_on(self):
        def dense_part():
            self.x_copy(self.x_slot).wait_recv()
            self.hand_copy(self.x_slot).start()

        when(self.x_gets, dense_part)
        for chip in range(self.chips):

            def thin_part(chip=chip):
                self.thin_got(chip).wait_recv()
                self.thin_hand(chip, True).start()

            when(self.thin_from(chip), thin_part)

    def arrive(self):
        when(self.sib_gets, lambda: self.sib_copy(self.sib_pos).wait_recv())
        when(self.x_gets, lambda: self.hand_copy(self.x_sib_slot).wait_recv())
        for chip in range(self.chips):
            when(
                self.thin_from(chip),
                lambda chip=chip: self.thin_hand(chip, False).wait_recv(),
            )

    def finish(self):
        p = self.p
        when(self.x_sends, lambda: self.x_copy(p.pos).wait_send())
        when(self.sib_sends, lambda: self.sib_copy(p.pos).wait_send())
        when(self.x_gets, lambda: self.hand_copy(self.x_slot).wait_send())
        for chip in range(self.chips):
            when(self.thin_to(chip), lambda chip=chip: self.thin_copy(chip).wait_send())
            when(self.thin_from(chip), lambda chip=chip: self.thin_hand(chip, True).wait_send())


def dense_sems(batches):
    return [pltpu.SemaphoreType.DMA((batches, 3))] * 2


def thin_sems(batches, chips):
    return [pltpu.SemaphoreType.DMA((batches, chips))] * 4


class Spread:
    def __init__(self, place, send, recv):
        self.p, self.send, self.recv = place, send, recv

    def copy_to(self, k, src, dst):
        p = self.p
        return remote(src, dst, self.send.at[k - 1], self.recv.at[k - 1], (p.other_z(k), p.s))


def forward_kernel(
    n,
    pat,
    levels,
    lens,
    x_ref,
    gain,
    shift,
    wq,
    bq,
    wkv,
    bkv,
    wout,
    perm,
    qext,
    ktab,
    xp,
    n1,
    qp,
    kvd,
    kvt,
    attf,
    wofp,
    attw,
    den,
    tab,
    acc,
    tab_sem,
    w_send,
    w_recv,
    a_send,
    a_recv,
    ds0,
    ds1,
    ts0,
    ts1,
    ts2,
    ts3,
):
    batches, shard, width = x_ref.shape
    half = shard // 2
    heads = wout.shape[0] // HD
    units = batches * heads
    p = Place(n, pat)
    bar, greeted = p.greet(True, True)
    low, high = lane_masks()

    def tab_copy(i):
        return pltpu.make_async_copy(ktab.at[heads * p.z + i], tab.at[i], tab_sem.at[i])

    for i in range(heads):
        tab_copy(i).start()
    for z in range(pat):
        wofp[z, 0:HD, :] = jnp.zeros((HD, width), BF)
        wofp[z, HD + heads * HD : 2 * HD + heads * HD, :] = jnp.zeros((HD, width), BF)
    wofp[p.z, HD : HD + heads * HD, :] = wout[...]
    for b in range(batches):
        xb = nn(perm[...], x_ref[b])
        xp[b] = xb.astype(BF)
        mean = jnp.mean(xb, -1, keepdims=True)
        cen = xb - mean
        var = jnp.mean(cen * cen, -1, keepdims=True)
        n1[b] = (cen * lax.rsqrt(var + EPS) * gain[...] + shift[...]).astype(BF)

    shares = [
        Shares(
            p,
            shard,
            True,
            lambda slot, b=b: kvd.at[pl.ds(heads * b, heads), rows_of(slot * shard, shard), :],
            lambda dev, b=b: kvt.at[pl.ds(heads * b, heads), rows_of(dev * half, half), :],
            [ds0.at[b], ds1.at[b]],
            [ts0.at[b], ts1.at[b], ts2.at[b], ts3.at[b]],
        )
        for b in range(batches)
    ]
    parity = [lax.rem(heads * p.z + i, 2) for i in range(heads)]
    for b in range(batches):
        q = ((nn(n1[b], wq[...]) + bq[...]).astype(BF)) * jnp.asarray(HD**-0.5, BF)
        kv = (nn(n1[b], wkv[...]) + bkv[...]).astype(BF)
        for i in range(heads):
            qp[heads * b + i] = q[:, i * 128 : (i + 1) * 128]
            kvd[heads * b + i, rows_of(p.pos * shard, shard), :] = kv[:, i * 128 : (i + 1) * 128]
        for i in range(heads):
            kvt[heads * b + i, rows_of(p.s * half, half), :] = kvd[
                heads * b + i, rows_of(p.pos * shard + parity[i] * half, half), :
            ]
        if b == 0:
            pl.semaphore_wait(bar, greeted)
        shares[b].start()
    w_spread = Spread(p, w_send, w_recv)

    def w_slot(z):
        return wofp.at[z, HD : HD + heads * HD, :]

    for k in range(1, pat):
        w_spread.copy_to(k, w_slot(p.z), w_slot(p.z)).start()
    for i in range(heads):
        tab_copy(i).wait()

    def attend(qx, kv, ext, bias):
        s = nt(qx, jnp.concatenate([kv, ext], 1))
        if bias is not None:
            s = s + bias
        return nn(jnp.exp(s).astype(BF), kv * high + low)

    own = rows_of(p.pos * shard, shard)
    qi = lax.broadcasted_iota(jnp.int32, (shard, shard), 0)
    ki = lax.broadcasted_iota(jnp.int32, (shard, shard), 1)
    qt, kt = token_of(qi, shard), token_of(ki, shard)
    for b in range(batches):
        live = jnp.logical_or(
            jnp.logical_and(kt < qt, kt + p.s * shard < lens[b]), kt == qt
        )
        bias = jnp.where(live, 0.0, NEG)
        for i in range(heads):
            u = heads * b + i
            qx = jnp.concatenate([qp[u], qext[...]], 1)
            acc[u] = attend(qx, kvd[u, own, :], tab[i, 0], bias)

    att_spread = [Spread(p, a_send.at[t], a_recv.at[t]) for t in range(units // 2)]
    lane = lax.broadcasted_iota(jnp.int32, (shard, 128), 1)
    for b in range(batches):
        shares[b].pass_on()
        shares[b].arrive()

        def dense(j, carry, b=b):
            lenl = length_lane(dense_positions(p.seg * SPAN1 + j, shard), lens[b], shard)
            for i in range(heads):
                u = heads * b + i
                qx = jnp.concatenate([qp[u], qext[...]], 1)
                kv = kvd[u, rows_of(j * shard, shard), :]
                acc[u] += attend(qx, kv, tab[i, 0] + lenl, None)
            return carry

        lax.fori_loop(0, p.pos, dense, 0)

        def thin(sg, carry, b=b):
            level = level_of(sg, p.seg, levels)
            for i in range(heads):
                u = heads * b + i
                mine = rows_of(parity[i] * half, half)
                places = thin_positions(sg * SPAN1, parity[i], shard, SPAN1)
                lenl = length_lane(places, lens[b], SPAN1 * half)
                ext = jnp.concatenate([tab[i, level, mine, :]] * SPAN1, 0) + lenl
                qx = jnp.concatenate([qp[u, mine, :], qext[mine, :]], 1)
                kv = kvt[u, rows_of(sg * SPAN1 * half, SPAN1 * half), :]
                acc[u, mine, :] += attend(qx, kv, ext, None)
            return carry

        lax.fori_loop(0, p.seg, thin, 0)
        for t in range(units // 2):
            if (2 * t + 1) // heads != b:
                continue
            even, odd = acc[2 * t], acc[2 * t + 1]
            num = jnp.where(lane < HD, pltpu.roll(even, HD, 1), odd)
            dn = jnp.where(lane < HD, even, pltpu.roll(odd, HD, 1))
            wide = num / dn
            den[t] = dn
            attw[t] = wide
            attf[p.z, t] = wide.astype(BF)
            for k in range(1, pat):
                att_spread[t].copy_to(k, attf.at[p.z, t], attf.at[p.z, t]).start()
    for k in range(1, pat):
        frm = lax.rem(p.z + pat - k, pat)
        w_spread.copy_to(k, w_slot(p.z), w_slot(p.z)).wait_send()
        w_spread.copy_to(k, w_slot(frm), w_slot(frm)).wait_recv()
        for t in range(units // 2):
            att_spread[t].copy_to(k, attf.at[p.z, t], attf.at[p.z, t]).wait_send()
            att_spread[t].copy_to(k, attf.at[frm, t], attf.at[frm, t]).wait_recv()
    for b in range(batches):
        shares[b].finish()


def middle_kernel(
    n,
    pat,
    xp,
    attf,
    wofp,
    bout,
    gain,
    shift,
    wup,
    bup,
    wdown,
    dout,
    perm,
    gud,
    fd,
    dsf,
    dst,
    sto,
    vecs,
    state,
    n2,
    act,
    dop,
    dh,
    dns,
    dno,
    dnr,
    r_send,
    r_recv,
    g_send,
    g_recv,
):
    batches, shard, width = xp.shape
    quarter = shard // pat
    p = Place(n, pat)
    bar, greeted = p.greet(True, False)
    rs = [Spread(p, r_send.at[b], r_recv.at[b]) for b in range(batches)]
    ag = [Spread(p, g_send.at[b], g_recv.at[b]) for b in range(batches)]
    bup_sum = jnp.zeros((1, width), F32)
    bdown_sum = jnp.zeros((1, width), F32)
    for b in range(batches):
        mixed = jnp.zeros((shard, width), F32)
        for z in range(pat):
            pair = jnp.concatenate([attf[z, b], attf[z, b + 1]], 1)
            weight = wofp[z, HD : HD + 256, :] if b == 0 else wofp[z, 0:256, :]
            mixed = mixed + nn(pair, weight)
        st = xp[b].astype(F32) + mixed + bout[...]
        state[b] = st
        mean = jnp.mean(st, -1, keepdims=True)
        cen = st - mean
        var = jnp.mean(cen * cen, -1, keepdims=True)
        norm = (cen * lax.rsqrt(var + EPS) * gain[...] + shift[...]).astype(BF)
        n2[b] = norm
        dob = nn(perm[...], dout[b])
        dop[b] = dob.astype(BF)
        bdown_sum = bdown_sum + jnp.sum(dob, 0, keepdims=True)
        hid = nn(norm, wup[...]) + bup[...]
        cube = hid * hid * hid
        th = jnp.tanh(ROOT * (hid + 0.044715 * cube))
        act[b] = (0.5 * hid * (1.0 + th)).astype(BF)
        slope = 0.5 * (1.0 + th) + 0.5 * hid * (1.0 - th * th) * (
            ROOT * (1.0 + 3.0 * 0.044715 * hid * hid)
        )
        dhid = (nt(dop[b], wdown[...]) * slope).astype(BF)
        dh[b] = dhid
        bup_sum = bup_sum + jnp.sum(dhid.astype(F32), 0, keepdims=True)
        dn = nt(dhid, wup[...])
        for z in range(pat):
            dns[b, z] = dn[z * quarter : (z + 1) * quarter].astype(BF)
        if b == 0:
            pl.semaphore_wait(bar, greeted)
        for k in range(1, pat):
            rs[b].copy_to(k, dns.at[b, p.other_z(k)], dnr.at[b, k - 1]).start()
    vecs[...] = jnp.zeros(vecs.shape, F32)
    for b in range(batches):
        fd[b] = nn(act[b], wdown[...]).astype(BF)
    bout_sum = jnp.zeros((1, width), F32)
    gain_sum = jnp.zeros((1, width), F32)
    shift_sum = jnp.zeros((1, width), F32)
    mine = rows_of(p.z * quarter, quarter)
    for b in range(batches):
        total = dns[b, p.z].astype(F32)
        for k in range(1, pat):
            rs[b].copy_to(k, dns.at[b, p.other_z(k)], dnr.at[b, k - 1]).wait_recv()
            total = total + dnr[b, k - 1].astype(F32)
        st = state[b, mine, :]
        sto[b] = st
        mean = jnp.mean(st, -1, keepdims=True)
        cen = st - mean
        inv = lax.rsqrt(jnp.mean(cen * cen, -1, keepdims=True) + EPS)
        hat = cen * inv
        gain_sum = gain_sum + jnp.sum(total * hat, 0, keepdims=True)
        shift_sum = shift_sum + jnp.sum(total, 0, keepdims=True)
        dhat = total * gain[...]
        back = inv * (
            dhat
            - jnp.mean(dhat, -1, keepdims=True)
            - hat * jnp.mean(dhat * hat, -1, keepdims=True)
        )
        ds = dop[b, mine, :].astype(F32) + back
        dst[b] = ds
        bout_sum = bout_sum + jnp.sum(ds, 0, keepdims=True)
        dsf[b, mine, :] = ds.astype(BF)
        for k in range(1, pat):
            ag[b].copy_to(k, dsf.at[b, mine, :], dsf.at[b, mine, :]).start()
    vecs[2:3, :] = bout_sum
    vecs[3:4, :] = gain_sum
    vecs[4:5, :] = shift_sum
    vecs[5:6, :] = bup_sum
    vecs[6:7, :] = bdown_sum
    up = tn(n2[0], dh[0])
    for b in range(1, batches):
        up = up + tn(n2[b], dh[b])
    gud[0:width, :] = up.astype(BF)
    down = tn(act[0], dop[0])
    for b in range(1, batches):
        down = down + tn(act[b], dop[b])
    gud[width : 2 * width, :] = down.astype(BF)
    for b in range(batches):
        for k in range(1, pat):
            frm = lax.rem(p.z + pat - k, pat)
            theirs = dsf.at[b, rows_of(frm * quarter, quarter), :]
            rs[b].copy_to(k, dns.at[b, p.other_z(k)], dnr.at[b, k - 1]).wait_send()
            ag[b].copy_to(k, dsf.at[b, mine, :], dsf.at[b, mine, :]).wait_send()
            ag[b].copy_to(k, theirs, theirs).wait_recv()


def backward_kernel(
    n,
    pat,
    levels,
    lens,
    dsf,
    wofp,
    attf,
    attw,
    den,
    qp,
    kvd,
    kvt,
    tab,
    qext,
    fd,
    sto,
    bdown,
    permt,
    dq,
    dkv,
    gout,
    outp,
    qud,
    qut,
    crd,
    crt,
    uext,
    acq,
    ack,
    fdr,
    outf,
    f_send,
    f_recv,
    o_send,
    o_recv,
    ds0,
    ds1,
    ts0,
    ts1,
    ts2,
    ts3,
    cd0,
    cd1,
    ct0,
    ct1,
    ct2,
    ct3,
):
    batches, shard, width = dsf.shape
    half = shard // 2
    quarter = shard // pat
    units = qp.shape[0]
    heads = units // batches
    p = Place(n, pat)
    bar, greeted = p.greet(True, True)
    low, high = lane_masks()
    parity = [lax.rem(heads * p.z + i, 2) for i in range(heads)]
    own = rows_of(p.pos * shard, shard)
    lane = lax.broadcasted_iota(jnp.int32, (shard, 128), 1)
    row8 = lax.broadcasted_iota(jnp.int32, (8, 128), 0)
    lane8 = lax.broadcasted_iota(jnp.int32, (8, 128), 1)
    pick = jnp.where(row8 == lax.div(lane8, HD), 1.0, 0.0).astype(F32)
    ri = lax.broadcasted_iota(jnp.int32, (128, 128), 0)
    ci = lax.broadcasted_iota(jnp.int32, (128, 128), 1)
    same = jnp.where(lax.div(ri, HD) == lax.div(ci, HD), 1.0, 0.0).astype(F32)

    wide = [
        nt(dsf[b], wofp[p.z, HD : HD + 256, :] if b == 0 else wofp[p.z, 0:256, :])
        for b in range(batches)
    ]
    tiles = [wide[0][:, 0:128], wide[0][:, 128:256] + wide[1][:, 0:128], wide[1][:, 128:256]]
    crd[p.pos] = jnp.zeros(crd.shape[1:], F32)
    crt[p.s] = jnp.zeros(crt.shape[1:], F32)
    for t in range(units // 2):
        dn = den[t]
        up = tiles[t] / dn
        prod = tiles[t] * attw[t] / dn
        cor = exact_nn(prod, same)
        cor_rows = exact_nt(pick, prod)
        for e in range(2):
            u = 2 * t + e
            i = u % heads
            part = up if e == 1 else pltpu.roll(up, HD, 1)
            mixed = jnp.where(lane < HD, qp[u].astype(F32), part).astype(BF)
            qud[u, own, :] = mixed
            qut[u, rows_of(p.s * half, half), :] = qud[
                u, rows_of(p.pos * shard + parity[i] * half, half), :
            ]
            crd[p.pos, u : u + 1, :] = cor_rows[e : e + 1, :]
            col = -cor[:, e * HD : e * HD + 1]
            first = col.astype(BF).astype(F32)
            ue = jnp.where(lane == COR_LANE, first, 0.0) + jnp.where(
                lane == COR_LANE + 1, col - first, 0.0
            )
            uext[u] = ue.astype(BF)
            thin_cor = jnp.where(parity[i] == 0, cor_rows[e : e + 1, 0:half], cor_rows[e : e + 1, half:shard])
            crt[p.s, u : u + 1, :] = thin_cor
    pl.semaphore_wait(bar, greeted)
    cors = Shares(
        p,
        shard,
        False,
        lambda slot: crd.at[slot],
        lambda dev: crt.at[dev],
        [cd0, cd1],
        [ct0, ct1, ct2, ct3],
    )
    shares = [
        Shares(
            p,
            shard,
            False,
            lambda slot, b=b: qud.at[pl.ds(heads * b, heads), rows_of(slot * shard, shard), :],
            lambda dev, b=b: qut.at[pl.ds(heads * b, heads), rows_of(dev * half, half), :],
            [ds0.at[b], ds1.at[b]],
            [ts0.at[b], ts1.at[b], ts2.at[b], ts3.at[b]],
        )
        for b in range(batches)
    ]
    cors.start()
    for b in range(batches):
        shares[b].start()
    fs = [Spread(p, f_send.at[b], f_recv.at[b]) for b in range(batches)]
    og = [Spread(p, o_send.at[b], o_recv.at[b]) for b in range(batches)]

    def fd_src(b, k):
        return fd.at[b, rows_of(p.other_z(k) * quarter, quarter), :]

    for b in range(batches):
        for k in range(1, pat):
            fs[b].copy_to(k, fd_src(b, k), fdr.at[b, k - 1]).start()

    def query_side(qu, qe, ue, kv, ext, bias):
        kvx = jnp.concatenate([kv, ext], 1)
        s = nt(jnp.concatenate([qu * low, qe], 1), kvx)
        if bias is not None:
            s = s + bias
        dp = nt(jnp.concatenate([qu * high, ue], 1), kvx)
        return nn((jnp.exp(s) * dp).astype(BF), kv)

    def key_side(qu, qe, cor, kv, ext, bias):
        s = nt(jnp.concatenate([kv, ext], 1), jnp.concatenate([qu * low, qe], 1))
        if bias is not None:
            s = s + bias
        w = jnp.exp(s)
        dp = nt(kv, qu * high) - cor
        return nn((w * dp).astype(BF), qu * low) + nn(w.astype(BF), qu * high)

    qi = lax.broadcasted_iota(jnp.int32, (shard, shard), 0)
    ki = lax.broadcasted_iota(jnp.int32, (shard, shard), 1)
    ti, tj = token_of(qi, shard), token_of(ki, shard)
    for b in range(batches):
        bias = jnp.where(
            jnp.logical_or(jnp.logical_and(tj < ti, tj + p.s * shard < lens[b]), tj == ti), 0.0, NEG
        )
        biast = jnp.where(
            jnp.logical_or(jnp.logical_and(ti < tj, ti + p.s * shard < lens[b]), tj == ti), 0.0, NEG
        )
        for i in range(heads):
            u = heads * b + i
            kv = kvd[u, own, :]
            qu = qud[u, own, :]
            acq[u] = query_side(qu, qext[...], uext[u], kv, tab[i, 0], bias)
            ack[u] = key_side(qu, qext[...], crd[p.pos, u : u + 1, :], kv, tab[i, 0], biast)

    for b in range(batches):

        def dense_q(j, carry, b=b):
            lenl = length_lane(dense_positions(p.seg * SPAN1 + j, shard), lens[b], shard)
            for i in range(heads):
                u = heads * b + i
                kv = kvd[u, rows_of(j * shard, shard), :]
                acq[u] += query_side(
                    qud[u, own, :], qext[...], uext[u], kv, tab[i, 0] + lenl, None
                )
            return carry

        lax.fori_loop(0, p.pos, dense_q, 0)

        def thin_q(sg, carry, b=b):
            level = level_of(sg, p.seg, levels)
            for i in range(heads):
                u = heads * b + i
                mine = rows_of(parity[i] * half, half)
                places = thin_positions(sg * SPAN1, parity[i], shard, SPAN1)
                lenl = length_lane(places, lens[b], SPAN1 * half)
                ext = jnp.concatenate([tab[i, level, mine, :]] * SPAN1, 0) + lenl
                kv = kvt[u, rows_of(sg * SPAN1 * half, SPAN1 * half), :]
                qu = qut[u, rows_of(p.s * half, half), :]
                acq[u, mine, :] += query_side(
                    qu, qext[mine, :], uext[u, mine, :], kv, ext, None
                )
            return carry

        lax.fori_loop(0, p.seg, thin_q, 0)

    zrows = rows_of(p.z * quarter, quarter)
    for b in range(batches):
        total = fd[b, zrows, :].astype(F32)
        for k in range(1, pat):
            fs[b].copy_to(k, fd_src(b, k), fdr.at[b, k - 1]).wait_recv()
            total = total + fdr[b, k - 1].astype(F32)
        outf[b, zrows, :] = (sto[b] + total + bdown[...]).astype(BF)
        for k in range(1, pat):
            og[b].copy_to(k, outf.at[b, zrows, :], outf.at[b, zrows, :]).start()
    left = tn(jnp.concatenate([attf[p.z, 0], attf[p.z, 1]], 1), dsf[0])
    right = tn(jnp.concatenate([attf[p.z, 1], attf[p.z, 2]], 1), dsf[1])
    gout[...] = (left[0 : heads * HD] + right[HD : HD + heads * HD]).astype(BF)

    cors.pass_on()
    cors.arrive()
    for b in range(batches):
        shares[b].pass_on()
        shares[b].arrive()
        lenl = length_lane(dense_positions(p.s, shard), lens[b], shard)

        def dense_k(j, carry, b=b, lenl=lenl):
            for i in range(heads):
                u = heads * b + i
                qu = qud[u, rows_of(j * shard, shard), :]
                ack[u] += key_side(
                    qu, qext[...], crd[j, u : u + 1, :], kvd[u, own, :], tab[i, 0] + lenl, None
                )
            return carry

        lax.fori_loop(p.pos + 1, SPAN1, dense_k, 0)

        def thin_k(dev, carry, b=b):
            level = level_of(lax.div(dev, SPAN1), p.seg, levels)
            for i in range(heads):
                u = heads * b + i
                mine = rows_of(parity[i] * half, half)
                ext = tab[i, level, mine, :] + length_lane(
                    thin_positions(p.s, parity[i], shard, 1), lens[b], half
                )
                kv = kvt[u, rows_of(p.s * half, half), :]
                qu = qut[u, rows_of(dev * half, half), :]
                ack[u, mine, :] += key_side(
                    qu, qext[mine, :], crt[dev, u : u + 1, :], kv, ext, None
                )
            return carry

        lax.fori_loop(SPAN1 * (p.seg + 1), n, thin_k, 0)
        for i in range(heads):
            u = heads * b + i
            lanes = slice(i * 128, (i + 1) * 128)
            dq[b, :, lanes] = (acq[u] * HD**-0.5).astype(BF)
            dkv[b, :, lanes] = ack[u].astype(BF)

    for b in range(batches):
        for k in range(1, pat):
            frm = lax.rem(p.z + pat - k, pat)
            theirs = outf.at[b, rows_of(frm * quarter, quarter), :]
            og[b].copy_to(k, theirs, theirs).wait_recv()
            og[b].copy_to(k, outf.at[b, zrows, :], outf.at[b, zrows, :]).wait_send()
            fs[b].copy_to(k, fd_src(b, k), fdr.at[b, k - 1]).wait_send()
        outp[b] = nn(permt[...], outf[b]).astype(BF)
    cors.finish()
    for b in range(batches):
        shares[b].finish()


def tail_kernel(
    n,
    pat,
    xp,
    n1,
    dq,
    dkv,
    wq,
    wkv,
    gain,
    dst,
    vecs,
    gud,
    gout,
    permt,
    ginp,
    vout,
    grad,
    dns,
    dnr,
    gif,
    v0,
    vz,
    r_send,
    r_recv,
    g_send,
    g_recv,
    z_send,
    z_recv,
):
    batches, shard, width = xp.shape
    quarter = shard // pat
    cols = gout.shape[0]
    heads = cols // HD
    p = Place(n, pat)
    bar, greeted = p.greet(True, False)
    rs = [Spread(p, r_send.at[b], r_recv.at[b]) for b in range(batches)]
    ag = [Spread(p, g_send.at[b], g_recv.at[b]) for b in range(batches)]
    for b in range(batches):
        part = nt(dq[b], wq[...]) + nt(dkv[b], wkv[...])
        for z in range(pat):
            dns[b, z] = part[z * quarter : (z + 1) * quarter].astype(BF)
        if b == 0:
            pl.semaphore_wait(bar, greeted)
        for k in range(1, pat):
            rs[b].copy_to(k, dns.at[b, p.other_z(k)], dnr.at[b, k - 1]).start()
    qsum = jnp.zeros((1, heads * 128), F32)
    vsum = jnp.zeros((1, heads * 128), F32)
    for b in range(batches):
        qsum = qsum + jnp.sum(dq[b].astype(F32), 0, keepdims=True)
        vsum = vsum + jnp.sum(dkv[b].astype(F32), 0, keepdims=True)
    grad[0 : 2 * width, :] = gud[...].astype(F32)
    base = 2 * width
    for i in range(heads):
        lanes = slice(i * 128, (i + 1) * 128)
        a = tn(dq[0, :, lanes], n1[0])
        c = tn(dkv[0, :, lanes], n1[0])
        for b in range(1, batches):
            a = a + tn(dq[b, :, lanes], n1[b])
            c = c + tn(dkv[b, :, lanes], n1[b])
        grad[base + i * HD : base + (i + 1) * HD, :] = a[0:HD]
        grad[base + cols + i * HD : base + cols + (i + 1) * HD, :] = c[0:HD]
        grad[base + 2 * cols + i * HD : base + 2 * cols + (i + 1) * HD, :] = c[HD:]
    grad[base + 3 * cols : base + 4 * cols, :] = gout[...].astype(F32)
    zrows = rows_of(p.z * quarter, quarter)
    gain_sum = jnp.zeros((1, width), F32)
    shift_sum = jnp.zeros((1, width), F32)
    for b in range(batches):
        total = dns[b, p.z].astype(F32)
        for k in range(1, pat):
            rs[b].copy_to(k, dns.at[b, p.other_z(k)], dnr.at[b, k - 1]).wait_recv()
            total = total + dnr[b, k - 1].astype(F32)
        back, more_gain, more_shift = norm_back(xp[b, zrows, :].astype(F32), total, gain[...])
        gain_sum = gain_sum + more_gain
        shift_sum = shift_sum + more_shift
        gif[b, zrows, :] = (dst[b] + back).astype(BF)
        for k in range(1, pat):
            ag[b].copy_to(k, gif.at[b, zrows, :], gif.at[b, zrows, :]).start()
    v0[...] = vecs[...]
    v0[0:1, :] = gain_sum
    v0[1:2, :] = shift_sum
    zsp = Spread(p, z_send, z_recv)
    for k in range(1, pat):
        zsp.copy_to(k, v0, vz.at[k - 1]).start()
    for k in range(1, pat):
        zsp.copy_to(k, v0, vz.at[k - 1]).wait_recv()
    row = lax.broadcasted_iota(jnp.int32, (8, width), 0)
    extra = vz[0]
    for k in range(2, pat):
        extra = extra + vz[k - 1]
    vout[0:8, :] = v0[...] + jnp.where(row < 5, extra, 0.0)
    vout[8:16, :] = jnp.zeros((8, width), F32)
    vout[8:9, 0 : heads * 128] = qsum
    vout[9:10, 0 : heads * 128] = vsum
    for b in range(batches):
        for k in range(1, pat):
            frm = lax.rem(p.z + pat - k, pat)
            theirs = gif.at[b, rows_of(frm * quarter, quarter), :]
            ag[b].copy_to(k, theirs, theirs).wait_recv()
        ginp[b] = nn(permt[...], gif[b]).astype(BF)
    for b in range(batches):
        for k in range(1, pat):
            rs[b].copy_to(k, dns.at[b, p.other_z(k)], dnr.at[b, k - 1]).wait_send()
            ag[b].copy_to(k, gif.at[b, zrows, :], gif.at[b, zrows, :]).wait_send()
    for k in range(1, pat):
        zsp.copy_to(k, v0, vz.at[k - 1]).wait_send()


def call(kernel, name, outs, scratch, specs, number, places=None):
    return pl.pallas_call(
        kernel,
        name=name,
        out_shape=[jax.ShapeDtypeStruct(s, d) for s, d in outs],
        in_specs=[pl.BlockSpec(memory_space=m) for m in specs],
        out_specs=[
            pl.BlockSpec(memory_space=m) for m in places or [pltpu.VMEM] * len(outs)
        ],
        scratch_shapes=scratch,
        compiler_params=pltpu.CompilerParams(
            collective_id=number, has_side_effects=True, vmem_limit_bytes=62 << 20
        ),
    )


def shards(
    n,
    pat,
    inputs,
    lengths,
    gain_one,
    shift_one,
    w_query,
    b_query,
    w_key,
    w_value,
    b_value,
    w_out,
    b_out,
    gain_two,
    shift_two,
    w_up,
    b_up,
    w_down,
    b_down,
    d_output,
):
    batches, shard, width = inputs.shape
    cols = w_query.shape[1]
    heads = cols // HD
    units = batches * heads
    chips = n // 2
    half = shard // 2
    quarter = shard // pat
    levels = 1
    while SPAN1 << (levels - 1) < n:
        levels += 1
    perm = jnp.asarray(perm_matrix(shard), BF)
    permt = jnp.asarray(perm_matrix(shard).T, BF)
    qext = jnp.asarray(query_ext(shard), BF)
    ktab = jnp.asarray(key_tables(shard, heads * pat, levels))
    row = lambda v: v.reshape(1, -1)
    by_head = lambda w: w.reshape(w.shape[0], heads, HD)
    pack = lambda a, b: jnp.concatenate([by_head(a), by_head(b)], 2).reshape(a.shape[0], 2 * cols)
    wq = pack(w_query, jnp.zeros_like(w_query))
    wkv = pack(w_key, w_value)
    bq = pack(row(b_query), jnp.zeros((1, cols), F32))
    bkv = pack(jnp.zeros((1, cols), F32), row(b_value))
    vm, sm, anyv = pltpu.VMEM, pltpu.SMEM, pl.ANY
    dma = pltpu.SemaphoreType.DMA
    tiles = units // 2

    xp, n1, qp, kvd, kvt, attf, wofp, attw, den, tab = call(
        functools.partial(forward_kernel, n, pat, levels),
        "attention_forward",
        [
            ((batches, shard, width), BF),
            ((batches, shard, width), BF),
            ((units, shard, 128), BF),
            ((units, SPAN1 * shard, 128), BF),
            ((units, n * half, 128), BF),
            ((pat, tiles, shard, 128), BF),
            ((pat, cols + 2 * HD, width), BF),
            ((tiles, shard, 128), F32),
            ((tiles, shard, 128), F32),
            ((heads, levels, shard, 128), BF),
        ],
        [
            pltpu.VMEM((units, shard, 128), F32),
            dma((heads,)),
            dma((pat - 1,)),
            dma((pat - 1,)),
            dma((tiles, pat - 1)),
            dma((tiles, pat - 1)),
        ]
        + dense_sems(batches)
        + thin_sems(batches, chips),
        [sm] + [vm] * 10 + [anyv],
        0,
    )(lengths, inputs, row(gain_one), row(shift_one), wq, bq, wkv, bkv, w_out, perm, qext, ktab)

    gud, fd, dsf, dst, sto, vecs = call(
        functools.partial(middle_kernel, n, pat),
        "feed_forward",
        [
            ((2 * width, width), BF),
            ((batches, shard, width), BF),
            ((batches, shard, width), BF),
            ((batches, quarter, width), F32),
            ((batches, quarter, width), F32),
            ((8, width), F32),
        ],
        [
            pltpu.VMEM((batches, shard, width), F32),
            pltpu.VMEM((batches, shard, width), BF),
            pltpu.VMEM((batches, shard, width), BF),
            pltpu.VMEM((batches, shard, width), BF),
            pltpu.VMEM((batches, shard, width), BF),
            pltpu.VMEM((batches, pat, quarter, width), BF),
            pltpu.VMEM((batches, quarter, width), F32),
            pltpu.VMEM((batches, pat - 1, quarter, width), BF),
        ]
        + [dma((batches, pat - 1))] * 4,
        [vm] * 11,
        1,
    )(
        xp,
        attf,
        wofp,
        row(b_out),
        row(gain_two),
        row(shift_two),
        w_up,
        row(b_up),
        w_down,
        d_output,
        perm,
    )

    dq, dkv, gout, outputs = call(
        functools.partial(backward_kernel, n, pat, levels),
        "attention_backward",
        [
            ((batches, shard, 2 * cols), BF),
            ((batches, shard, 2 * cols), BF),
            ((cols, width), BF),
            ((batches, shard, width), BF),
        ],
        [
            pltpu.VMEM((units, SPAN1 * shard, 128), BF),
            pltpu.VMEM((units, n * half, 128), BF),
            pltpu.VMEM((SPAN1, 8, shard), F32),
            pltpu.VMEM((n, 8, half), F32),
            pltpu.VMEM((units, shard, 128), BF),
            pltpu.VMEM((units, shard, 128), F32),
            pltpu.VMEM((units, shard, 128), F32),
            pltpu.VMEM((batches, pat - 1, quarter, width), BF),
            pltpu.VMEM((batches, shard, width), BF),
        ]
        + [dma((batches, pat - 1))] * 4
        + dense_sems(batches)
        + thin_sems(batches, chips)
        + [dma((3,))] * 2
        + [dma((chips,))] * 4,
        [sm] + [vm] * 14,
        2,
    )(lengths, dsf, wofp, attf, attw, den, qp, kvd, kvt, tab, qext, fd, sto, row(b_down), permt)

    rows = 2 * width + 4 * cols
    grad_inputs, vout, grads = call(
        functools.partial(tail_kernel, n, pat),
        "input_gradient",
        [
            ((batches, shard, width), BF),
            ((16, width), F32),
            ((rows, width), F32),
        ],
        [
            pltpu.VMEM((batches, pat, quarter, width), BF),
            pltpu.VMEM((batches, pat - 1, quarter, width), BF),
            pltpu.VMEM((batches, shard, width), BF),
            pltpu.VMEM((8, width), F32),
            pltpu.VMEM((pat - 1, 8, width), F32),
        ]
        + [dma((batches, pat - 1))] * 4
        + [dma((pat - 1,))] * 2,
        [vm] * 12,
        3,
    )(xp, n1, dq, dkv, wq, wkv, row(gain_one), dst, vecs, gud, gout, permt)
    vout, grads = lax.psum((vout, grads), "seq")
    base = 2 * width
    g_q, g_k, g_v, g_out = [grads[base + i * cols : base + (i + 1) * cols] for i in range(4)]
    q_row = vout[8, : 2 * cols].reshape(heads, 2, HD)
    v_row = vout[9, : 2 * cols].reshape(heads, 2, HD)
    return (
        outputs,
        grad_inputs,
        vout[0],
        vout[1],
        g_q.T,
        q_row[:, 0].reshape(cols),
        g_k.T,
        g_v.T,
        v_row[:, 1].reshape(cols),
        g_out,
        vout[2],
        vout[3],
        vout[4],
        grads[:width],
        vout[5],
        grads[width:base],
        vout[6],
    )


class LineGather:
    def __init__(self, place, block, send, recv):
        self.p, self.block, self.send, self.recv = place, block, send, recv

    def copy(self, frm, to, sem):
        return remote(
            self.block(frm, self.p.z),
            self.block(frm, to),
            self.send.at[sem],
            self.recv.at[frm],
            (to, self.p.s),
        )

    def got(self, frm):
        here = self.block(frm, self.p.z)
        to = lax.rem(self.p.z + 1, self.p.pat)
        return remote(here, here, self.send.at[0], self.recv.at[frm], (to, self.p.s))

    def direct(self, fn):
        last = self.p.pat - 1
        for z in range(self.p.pat):

            def own(z=z):
                for to in sorted(range(last + 1), key=lambda t: -abs(t - z)):
                    if 0 < abs(to - z) < last:
                        fn(self.copy(z, to, to))

            when(self.p.z == z, own)

    def handed(self, fn):
        last = self.p.pat - 1
        when(self.p.z == last - 1, lambda: fn(0, self.copy(0, last, last + 1)))
        when(self.p.z == 1, lambda: fn(last, self.copy(last, 0, last + 1)))

    def start(self):
        self.direct(lambda copy: copy.start())

    def forward(self):
        def hand(frm, copy):
            self.got(frm).wait_recv()
            copy.start()

        self.handed(hand)

    def arrive(self):
        last = self.p.pat - 1
        for z in range(last + 1):

            def rest(z=z):
                for frm in range(last + 1):
                    if frm != z and (z, frm) not in ((1, last), (last - 1, 0)):
                        self.got(frm).wait_recv()

            when(self.p.z == z, rest)

    def finish(self):
        self.direct(lambda copy: copy.wait_send())
        self.handed(lambda frm, copy: copy.wait_send())


class LineChain:
    def __init__(self, place, block, send, recv):
        self.p, self.block, self.send, self.recv = place, block, send, recv

    def copy(self, frm, up):
        p = self.p
        to = jnp.clip(p.z + (1 if up else -1), 0, p.pat - 1)
        return remote(
            self.block(frm),
            self.block(frm),
            self.send.at[0 if up else 1, frm],
            self.recv.at[frm],
            (to, p.s),
        )

    def start(self):
        p = self.p
        when(p.z < p.pat - 1, lambda: self.copy(p.z, True).start())
        when(p.z > 0, lambda: self.copy(p.z, False).start())

    def inner(self, hop):
        for z in range(1, self.p.pat - 1):
            if z - hop >= 0:
                yield z, z - hop, True
            if z + hop < self.p.pat:
                yield z, z + hop, False

    def got(self, frm):
        p = self.p
        here = self.block(frm)
        to = lax.rem(p.z + 1, p.pat)
        return remote(here, here, self.send.at[0, 0], self.recv.at[frm], (to, p.s))

    def forward(self, hop):
        for z, frm, up in self.inner(hop):

            def hand(frm=frm, up=up):
                self.got(frm).wait_recv()
                self.copy(frm, up).start()

            when(self.p.z == z, hand)

    def arrive(self):
        last = self.p.pat - 1
        for frm in range(self.p.pat):
            if frm > 0:
                when(self.p.z == 0, lambda frm=frm: self.got(frm).wait_recv())
            if frm < last:
                when(self.p.z == last, lambda frm=frm: self.got(frm).wait_recv())

    def finish(self):
        p = self.p
        when(p.z < p.pat - 1, lambda: self.copy(p.z, True).wait_send())
        when(p.z > 0, lambda: self.copy(p.z, False).wait_send())
        for hop in range(1, p.pat - 1):
            for z, frm, up in self.inner(hop):
                when(p.z == z, lambda frm=frm, up=up: self.copy(frm, up).wait_send())


class LineSum:
    def __init__(self, place, part, buf, send, recv):
        self.p, self.part, self.buf, self.send, self.recv = place, part, buf, send, recv

    def copy(self, z, t):
        to = z + 1 if t > z else z - 1
        at = t if (t > z or t < to) else self.p.pat
        return remote(
            self.part(t), self.buf.at[at], self.send.at[t], self.recv.at[at], (to, self.p.s)
        )

    def got(self, at):
        here = self.buf.at[at]
        to = lax.rem(self.p.z + 1, self.p.pat)
        return remote(here, here, self.send.at[0], self.recv.at[at], (to, self.p.s))

    def start(self):
        last = self.p.pat - 1

        def up():
            for t in range(last, 0, -1):
                self.copy(0, t).start()

        def down():
            for t in range(last):
                self.copy(last, t).start()

        when(self.p.z == 0, up)
        when(self.p.z == last, down)

    def inner(self, hop):
        last = self.p.pat - 1
        for z in range(1, last):
            if z == hop:
                for t in range(last, z, -1):
                    yield z, t
            if last - z == hop:
                for t in range(z):
                    yield z, t

    def forward(self, hop):
        for z, t in self.inner(hop):

            def add(z=z, t=t):
                self.got(t).wait_recv()
                part = self.part(t)
                part[...] = (part[...].astype(F32) + self.buf[t].astype(F32)).astype(BF)
                self.copy(z, t).start()

            when(self.p.z == z, add)

    def total(self, out):
        p = self.p
        out[...] = self.part(p.z)[...].astype(F32)

        def below():
            self.got(p.z).wait_recv()
            out[...] += self.buf[p.z].astype(F32)

        def above():
            self.got(p.pat).wait_recv()
            out[...] += self.buf[p.pat].astype(F32)

        when(p.z > 0, below)
        when(p.z < p.pat - 1, above)

    def finish(self):
        last = self.p.pat - 1
        for t in range(last, 0, -1):
            when(self.p.z == 0, lambda t=t: self.copy(0, t).wait_send())
        for t in range(last):
            when(self.p.z == last, lambda t=t: self.copy(last, t).wait_send())
        for hop in range(1, last):
            for z, t in self.inner(hop):
                when(self.p.z == z, lambda z=z, t=t: self.copy(z, t).wait_send())


class PlaneGather:
    def __init__(self, place, piece, sems):
        self.p, self.piece, self.sems = place, piece, sems
        self.chips = place.n // 2

    def direct(self, k, owner):
        p, sems = self.p, self.sems
        to = lax.rem(p.s + 2 * k, p.n)
        return remote(
            self.piece(owner), self.piece(owner), sems[0].at[k - 1], sems[1].at[k - 1], (p.z, to)
        )

    def hand(self, k, owner):
        p, sems = self.p, self.sems
        return remote(
            self.piece(owner), self.piece(owner), sems[2].at[k], sems[3].at[k], (p.z, p.sib)
        )

    def source(self, base, k):
        return lax.rem(base + self.p.n - 2 * k, self.p.n)

    def start(self):
        for k in range(1, self.chips):
            self.direct(k, self.p.s).start()
        self.hand(0, self.p.s).start()

    def pass_on(self):
        for k in range(1, self.chips):
            owner = self.source(self.p.s, k)
            self.direct(k, owner).wait_recv()
            self.hand(k, owner).start()

    def arrive(self):
        for k in range(self.chips):
            self.hand(k, self.source(self.p.sib, k)).wait_recv()

    def finish(self):
        for k in range(1, self.chips):
            self.direct(k, self.p.s).wait_send()
        for k in range(self.chips):
            self.hand(k, self.source(self.p.s, k)).wait_send()


def line_sems(pat):
    return [pltpu.SemaphoreType.DMA((pat + 1,)), pltpu.SemaphoreType.DMA((pat,))]


def chain_sems(pat):
    return [pltpu.SemaphoreType.DMA((2, pat)), pltpu.SemaphoreType.DMA((pat,))]


def sum_sems(pat):
    return [pltpu.SemaphoreType.DMA((pat,)), pltpu.SemaphoreType.DMA((pat + 1,))]


def plane_sems(chips):
    return [pltpu.SemaphoreType.DMA((chips - 1,))] * 2 + [pltpu.SemaphoreType.DMA((chips,))] * 2


def vec_row(ref):
    return ref[...].reshape(1, -1)


def norm_rows(values, gain, shift):
    mean = jnp.mean(values, -1, keepdims=True)
    cen = values - mean
    var = jnp.mean(cen * cen, -1, keepdims=True)
    return cen * lax.rsqrt(var + EPS) * gain + shift


def norm_back(values, grad, gain):
    mean = jnp.mean(values, -1, keepdims=True)
    cen = values - mean
    inv = lax.rsqrt(jnp.mean(cen * cen, -1, keepdims=True) + EPS)
    hat = cen * inv
    dhat = grad * gain
    back = inv * (
        dhat - jnp.mean(dhat, -1, keepdims=True) - hat * jnp.mean(dhat * hat, -1, keepdims=True)
    )
    return (
        back,
        jnp.sum(grad * hat, 0, keepdims=True),
        jnp.sum(grad, 0, keepdims=True),
    )


def live_bias(first, second, base, length, shard):
    ok = jnp.logical_or(
        jnp.logical_and(second < first, second + base < length), second == first
    )
    return jnp.where(ok, 0.0, NEG)


class TreeSum:
    def __init__(self, place, grad, out, bufs, send, recv, keep=False, size=None):
        self.p, self.grad, self.out, self.send, self.recv = place, grad, out, send, recv
        self.keep = keep
        p = place
        bit_x = lax.rem(lax.div(p.s, 2), 2)
        bit_y = lax.div(p.s, 4)
        to_x = p.s + 2 - 4 * bit_x
        to_y = p.s + 4 - 8 * bit_y
        first = p.core == 0
        self.bits = [p.core, jnp.where(first, bit_x, bit_y), jnp.where(first, bit_y, bit_x)]
        self.to = [p.sib, jnp.where(first, to_x, to_y), jnp.where(first, to_y, to_x)]
        self.bufs = bufs
        self.off, self.size = [jnp.int32(0)], [size or grad.shape[0]]
        for d in range(3):
            h = self.size[d] // 2
            self.off.append(self.off[d] + self.bits[d] * h)
            self.size.append(h)

    def half_of(self, d, bit):
        h = self.size[d] // 2
        return rows_of(self.off[d] + bit * h, h)

    def red(self, d):
        src = self.grad.at[self.half_of(d, 1 - self.bits[d]), :]
        return remote(
            src, self.bufs[d], self.send.at[d], self.recv.at[d], (self.p.z, self.to[d])
        )

    def back(self, d, got):
        rows = self.half_of(d, (1 - self.bits[d]) if got else self.bits[d])
        return remote(
            self.out.at[rows, :],
            self.out.at[rows, :],
            self.send.at[3 + d],
            self.recv.at[3 + d],
            (self.p.z, self.to[d]),
        )

    def step(self, d):
        if d == 0:
            self.red(0).start()
        elif d <= 3:
            self.red(d - 1).wait_recv()
            rows = rows_of(self.off[d], self.size[d])
            total = self.grad[rows, :].astype(F32) + self.bufs[d - 1][...].astype(F32)
            if d < 3:
                self.grad[rows, :] = total.astype(BF)
                self.red(d).start()
            elif self.keep:
                self.out[...] = total.astype(BF)
            else:
                self.out[rows, :] = total.astype(BF)
                self.back(2, False).start()
        else:
            self.back(6 - d, True).wait_recv()
            if d < 6:
                self.back(5 - d, False).start()

    def finish(self):
        for d in range(3):
            self.red(d).wait_send()
            if not self.keep:
                self.back(d, False).wait_send()


def layer_kernel(
    n,
    pat,
    levels,
    lens,
    gain1,
    shift1,
    bq,
    bv,
    bout,
    gain2,
    shift2,
    bup,
    bdown,
    wq_hbm,
    wk_hbm,
    wv_hbm,
    wout_hbm,
    perm_hbm,
    qext_hbm,
    ktab,
    x_hbm,
    wup_hbm,
    wdown_hbm,
    dout_hbm,
    outf_hbm,
    gif_hbm,
    gsum1_hbm,
    gsum2_hbm,
    gout_hbm,
    vout,
    perm,
    qext,
    outf,
    gif,
    gsum1,
    gsum2,
    gout,
    grad1,
    xp,
    n1,
    wp,
    qp,
    kvd,
    kvt,
    tab,
    acc,
    ack,
    wqo,
    wko,
    attf,
    attu,
    attw,
    den,
    wor,
    wup,
    wdown,
    sto,
    n2,
    act,
    dop,
    dh,
    dns,
    dnr,
    tot,
    dsl,
    dst,
    dab,
    dat,
    fd,
    fdr,
    qud,
    qut,
    crd,
    crt,
    uext,
    dmr,
    a1,
    a2,
    a3,
    b1,
    b2,
    b3,
    c1,
    c2,
    c3,
    pz,
    pr,
    vecs,
    vz,
    vs,
    *sems,
):
    batches, shard, width = xp.shape
    half = shard // 2
    quarter = shard // pat
    cols = wout_hbm.shape[0]
    heads = cols // HD
    units = batches * heads
    tiles = units // 2
    chips = n // 2
    grad2, grad3 = n2, act
    both = lambda b: slice(b * shard, (b + 1) * shard)
    sems = list(sems)
    take = lambda count: [sems.pop(0) for _ in range(count)]
    p = Place(n, pat)
    bar, greeted = p.greet(True, False, True)
    low, high = lane_masks()

    own_slot = pat - 1
    pairs = [(perm_hbm, perm), (x_hbm.at[0], xp.at[0])]
    for i in range(heads):
        for off, src in ((0, wk_hbm), (HD, wv_hbm)):
            pairs.append((src.at[i * HD : (i + 1) * HD, :], wp.at[pl.ds(i * 128 + off, HD), :]))
    pairs.append((wq_hbm, wp.at[pl.ds(2 * cols, cols), :]))
    at_x = len(pairs)
    pairs += [(x_hbm.at[b], xp.at[b]) for b in range(1, batches)]
    at_out = len(pairs)
    pairs += [(wout_hbm, wor.at[own_slot, pl.ds(0, cols), :])]
    at_tab = len(pairs)
    pairs += [(ktab.at[heads * p.z + i], tab.at[i]) for i in range(heads)] + [(qext_hbm, qext)]
    at_late = len(pairs)
    pairs += [(dout_hbm, dop), (wup_hbm, wup), (wdown_hbm, wdown)]
    load_sem, save_sem = take(2)
    loads = [
        pltpu.make_async_copy(src, dst, load_sem.at[i]) for i, (src, dst) in enumerate(pairs)
    ]
    for copy in loads[:at_x]:
        copy.start()
    saves = [
        pltpu.make_async_copy(src, dst, save_sem.at[i])
        for i, (src, dst) in enumerate(
            (
                (gsum1, gsum1_hbm),
                (outf, outf_hbm),
                (gsum2, gsum2_hbm),
                (gif, gif_hbm),
                (gout, gout_hbm),
            )
        )
    ]

    slot = lambda frm, at: lax.rem(frm - at + 2 * pat - 1, pat)
    out_rows, out_cols = cols // chips, width // 2

    def out_piece(dev, slots):
        chip, core = lax.div(dev, 2), lax.rem(dev, 2)
        return wor.at[
            slots,
            rows_of(chip * out_rows, out_rows),
            pl.ds(pl.multiple_of(core * out_cols, 128), out_cols),
        ]

    def quarters(ref, b):
        return lambda f, *_: ref.at[b, rows_of(f * quarter, quarter), :]

    parity = [lax.rem(heads * p.z + i, 2) for i in range(heads)]

    def share_pair(forward, dense, thin):
        out = []
        sems = take(6)
        for b in range(batches):
            out.append(
                Shares(
                    p,
                    shard,
                    forward,
                    lambda at, b=b: dense.at[
                        pl.ds(heads * b, heads), rows_of(at * shard, shard), :
                    ],
                    lambda dev, b=b: thin.at[pl.ds(heads * b, heads), rows_of(dev * half, half), :],
                    [sem.at[b] for sem in sems[:2]],
                    [sem.at[b] for sem in sems[2:]],
                )
            )
        return out

    rows = range(batches)
    kv_shares = share_pair(True, kvd, kvt)
    qu_shares = share_pair(False, qud, qut)
    cor_sems = take(6)
    cors = [
        Shares(
            p,
            shard,
            False,
            lambda at, b=b: crd.at[b, at],
            lambda dev, b=b: crt.at[b, dev],
            [sem.at[b] for sem in cor_sems[:2]],
            [sem.at[b] for sem in cor_sems[2:]],
        )
        for b in rows
    ]
    wo_line = LineGather(p, lambda f, t: out_piece(p.s, slot(f, t)), *take(2))
    wo_plane = PlaneGather(p, lambda dev: out_piece(dev, pl.ds(0, pat - 1)), take(4))
    att_line = [LineGather(p, lambda f, at, b=b: attf.at[f, b], *take(2)) for b in rows]
    dn_sum = [LineSum(p, lambda t, b=b: dns.at[b, t], dnr.at[b], *take(2)) for b in rows]
    da_send, da_recv = take(2)
    da_spread = [Spread(p, da_send.at[b], da_recv.at[b]) for b in rows]
    fd_sum = [LineSum(p, quarters(fd, b), fdr.at[b], *take(2)) for b in rows]
    out_line = [LineChain(p, quarters(outf, b), *take(2)) for b in rows]
    dm_sum = [LineSum(p, lambda t, b=b: dns.at[b, t], dmr.at[b], *take(2)) for b in rows]
    dqk = dh
    gi_line = [LineChain(p, quarters(gif, b), *take(2)) for b in rows]
    sum1 = TreeSum(p, grad1, gsum1, (a1, a2, a3), *take(2))
    sum2 = TreeSum(p, grad2, gsum2, (b1, b2, b3), *take(2), size=wp.shape[0])
    sum3 = TreeSum(p, grad3, pz, (c1, c2, c3), *take(2), keep=True)
    p_send, p_recv, w_send, w_recv = take(4)
    z_send, z_recv, v_send, v_recv = take(4)
    zsp = Spread(p, z_send, z_recv)

    for r in range(pat):
        wor[r, cols : cols + HD, :] = jnp.zeros((HD, width), BF)
    wp[3 * cols :, :] = jnp.zeros((wp.shape[0] - 3 * cols, width), BF)
    zero_bias = jnp.zeros((1, HD), F32)
    bias_v, bias_q = vec_row(bv), vec_row(bq)
    bias = []
    for i in range(heads):
        bias += [zero_bias, bias_v[:, i * HD : (i + 1) * HD]]
    bias = jnp.concatenate(bias + [bias_q, zero_bias], 1)

    own = rows_of(p.pos * shard, shard)
    zrows = rows_of(p.z * quarter, quarter)
    lane = lax.broadcasted_iota(jnp.int32, (shard, 128), 1)
    for b in rows:
        if b == 0:
            for copy in loads[at_x:at_late]:
                copy.start()
            for copy in loads[:at_x]:
                copy.wait()
        else:
            loads[at_x + b - 1].wait()
        xb = nn(perm[...], xp[b])
        xp[b] = xb.astype(BF)
        n1[b] = norm_rows(xb, vec_row(gain1), vec_row(shift1)).astype(BF)
        qkv = nt(n1[b], wp[...]) + bias
        for i in range(heads):
            kv = qkv[:, i * 128 : (i + 1) * 128].astype(BF)
            kvd[heads * b + i, own, :] = kv
            t = heads + i // 2
            q = qkv[:, t * 128 : (t + 1) * 128]
            if i % 2 == 1:
                q = pltpu.roll(q, HD, 1)
            q = jnp.where(lane < HD, q, 0.0).astype(BF) * jnp.asarray(HD**-0.5, BF)
            qp[heads * b + i] = q
        for i in range(heads):
            kvt[heads * b + i, rows_of(p.s * half, half), :] = kvd[
                heads * b + i, rows_of(p.pos * shard + parity[i] * half, half), :
            ]
        if b == 0:
            pl.semaphore_wait(bar, greeted)
        if b == 0:
            kv_shares[b].start()
            loads[at_out].wait()
            wo_line.start()
            for copy in loads[at_late:]:
                copy.start()
    for copy in loads[at_tab:at_late]:
        copy.wait()

    def attend(qx, kv, ext, bias):
        s = nt(qx, jnp.concatenate([kv, ext], 1))
        if bias is not None:
            s = s + bias
        return nn(jnp.exp(s).astype(BF), kv * high + low)

    first = token_of(lax.broadcasted_iota(jnp.int32, (shard, shard), 0), shard)
    second = token_of(lax.broadcasted_iota(jnp.int32, (shard, shard), 1), shard)

    def attend_own(b):
        bias = live_bias(first, second, p.s * shard, lens[b], shard)
        for i in range(heads):
            u = heads * b + i
            kv = kvd[u, own, :]
            qx = jnp.concatenate([qp[u], qext[...]], 1)
            w = jnp.exp(nt(qx, jnp.concatenate([kv, tab[i, 0]], 1)) + bias).astype(BF)
            wqo[u] = w
            acc[u] = nn(w, kv * high + low)

    def weights_own(b):
        bias = live_bias(second, first, p.s * shard, lens[b], shard)
        for i in range(heads):
            u = heads * b + i
            qx = jnp.concatenate([qp[u], qext[...]], 1)
            kvx = jnp.concatenate([kvd[u, own, :], tab[i, 0]], 1)
            wko[u] = jnp.exp(nt(kvx, qx) + bias).astype(BF)

    def thin_keys(b, i, sg):
        level = level_of(sg, p.seg, levels)
        places = thin_positions(sg * SPAN1, parity[i], shard, SPAN1)
        lenl = length_lane(places, lens[b], SPAN1 * half)
        part = tab[i, level, rows_of(parity[i] * half, half), :]
        ext = jnp.concatenate([part] * SPAN1, 0) + lenl
        return kvt[heads * b + i, rows_of(sg * SPAN1 * half, SPAN1 * half), :], ext

    def attend_rest(b, which):
        def dense(j, carry):
            lenl = length_lane(dense_positions(p.seg * SPAN1 + j, shard), lens[b], shard)
            for i in which:
                u = heads * b + i
                qx = jnp.concatenate([qp[u], qext[...]], 1)
                kv = kvd[u, rows_of(j * shard, shard), :]
                acc[u] += attend(qx, kv, tab[i, 0] + lenl, None)
            return carry

        lax.fori_loop(0, p.pos, dense, 0)

        def thin(sg, carry):
            for i in which:
                u = heads * b + i
                mine = rows_of(parity[i] * half, half)
                kv, ext = thin_keys(b, i, sg)
                qx = jnp.concatenate([qp[u, mine, :], qext[mine, :]], 1)
                acc[u, mine, :] += attend(qx, kv, ext, None)
            return carry

        lax.fori_loop(0, p.seg, thin, 0)

    def send_att(b):
        first_unit = heads * b
        zero, one, two = acc[first_unit], acc[first_unit + 1], acc[first_unit + 2]
        num = jnp.where(lane < HD, pltpu.roll(zero, HD, 1), one)
        dn = jnp.where(lane < HD, zero, pltpu.roll(one, HD, 1))
        wide = num / dn
        den[b, 0] = dn
        attw[b, 0] = wide
        attf[p.z, b, 0:shard, :] = wide.astype(BF)
        dn = jnp.where(lane < HD, two, 1.0)
        wide = jnp.where(lane < HD, pltpu.roll(two, HD, 1), 0.0) / dn
        den[b, 1] = dn
        attw[b, 1] = wide
        packed = wide[0:half] + pltpu.roll(wide[half:shard], HD, 1)
        attf[p.z, b, shard : shard + half, :] = packed.astype(BF)
        att_line[b].start()

    attend_own(0)
    kv_shares[1].start()
    attend_own(1)
    wo_line.forward()
    bdown_sum = jnp.zeros((1, width), F32)
    loads[at_late].wait()
    for b in rows:
        dob = nn(perm[...], dop[b])
        dop[b] = dob.astype(BF)
        bdown_sum = bdown_sum + jnp.sum(dob, 0, keepdims=True)
    weights_own(0)
    weights_own(1)
    kv_shares[0].pass_on()
    wo_line.arrive()
    wo_plane.start()
    kv_shares[0].arrive()
    attend_rest(0, range(heads))
    send_att(0)
    kv_shares[1].pass_on()
    kv_shares[1].arrive()
    attend_rest(1, range(0, 1))
    att_line[0].forward()
    attend_rest(1, range(1, heads))
    send_att(1)
    wo_plane.pass_on()
    for copy in loads[at_late + 1 :]:
        copy.wait()
    wo_plane.arrive()

    def feed_in(b):
        mixed = xp[b].astype(F32) + vec_row(bout)
        for r in range(pat):
            z = lax.rem(p.z + 1 + r, pat)
            packed = attf[z, b, shard : shard + half, :]
            attu[z, b, 0:half, :] = packed
            attu[z, b, half:shard, :] = pltpu.roll(packed.astype(F32), HD, 1).astype(BF)
            pair = jnp.concatenate([attf[z, b, 0:shard, :], attu[z, b]], 1)
            mixed = mixed + nn(pair, wor[r])
        for t in range(width // 128):
            lanes = slice(t * 128, (t + 1) * 128)
            ack[t] = mixed[:, lanes]
            sto[b, :, lanes] = ack[t, zrows, :]
        n2[both(b), :] = norm_rows(mixed, vec_row(gain2), vec_row(shift2)).astype(BF)

    def feed_out(b):
        hid = nn(n2[both(b), :], wup[...]) + vec_row(bup)
        th = jnp.tanh(ROOT * (hid + 0.044715 * (hid * hid * hid)))
        act[both(b), :] = (0.5 * hid * (1.0 + th)).astype(BF)
        slope = 0.5 * (1.0 + th) + 0.5 * hid * (1.0 - th * th) * (
            ROOT * (1.0 + 3.0 * 0.044715 * hid * hid)
        )
        dhid = (nt(dop[b], wdown[...]) * slope).astype(BF)
        dh[b] = dhid
        dn = nt(dhid, wup[...])
        for t in range(pat):
            dns[b, t] = dn[t * quarter : (t + 1) * quarter].astype(BF)
        dn_sum[b].start()
        return jnp.sum(dhid.astype(F32), 0, keepdims=True)

    att_line[0].arrive()
    feed_in(0)
    bup_sum = feed_out(0)
    att_line[1].forward()
    att_line[1].arrive()
    feed_in(1)
    dn_sum[0].forward(1)
    bup_sum = bup_sum + feed_out(1)
    fd[0] = nn(act[both(0), :], wdown[...]).astype(BF)
    dn_sum[0].forward(2)
    up = tn(n2[both(0), :], dh[0])
    for b in range(1, batches):
        up = up + tn(n2[both(b), :], dh[b])
    grad1[0:width, :] = up.astype(BF)
    dn_sum[1].forward(1)
    down = tn(act[both(0), :], dop[0])
    for b in range(1, batches):
        down = down + tn(act[both(b), :], dop[b])
    grad1[width : 2 * width, :] = down.astype(BF)
    sum1.step(0)
    bout_sum = jnp.zeros((1, width), F32)
    gain_sum = jnp.zeros((1, width), F32)
    shift_sum = jnp.zeros((1, width), F32)

    def head_grads(b, r):
        wide = nt(dsl[b], wor[r]).astype(BF)
        return jnp.stack([wide[:, 0:128], wide[:, 128:256]])

    def da_copy(b, k, frm=None):
        at = p.z if frm is None else frm
        return da_spread[b].copy_to(
            k, dab.at[b, k - 1], dat.at[b, :, rows_of(at * quarter, quarter), :]
        )

    def da_arrive(b):
        for k in range(1, pat):
            da_copy(b, k, lax.rem(p.z + pat - k, pat)).wait_recv()

    def state_grad(b, sums):
        dn_sum[b].total(tot)
        back, more_gain, more_shift = norm_back(sto[b], tot[...], vec_row(gain2))
        ds = dop[b, zrows, :].astype(F32) + back
        dst[b] = ds
        dsl[b] = ds.astype(BF)
        for k in range(1, pat):
            dab[b, k - 1] = head_grads(b, k - 1)
            da_copy(b, k).start()
        dat[b, :, zrows, :] = head_grads(b, own_slot)
        return (
            sums[0] + jnp.sum(ds, 0, keepdims=True),
            sums[1] + more_gain,
            sums[2] + more_shift,
        )

    sums = state_grad(0, (bout_sum, gain_sum, shift_sum))
    fd_sum[0].start()
    fd[1] = nn(act[both(1), :], wdown[...]).astype(BF)
    dn_sum[1].forward(2)
    sum1.step(1)
    sums = state_grad(1, sums)
    fd_sum[1].start()
    fd_sum[0].forward(1)
    vecs[...] = jnp.zeros(vecs.shape, F32)
    for r, value in ((2, sums[0]), (3, sums[1]), (4, sums[2]), (5, bup_sum), (6, bdown_sum)):
        vecs[r : r + 1, :] = value

    row8 = lax.broadcasted_iota(jnp.int32, (8, 128), 0)
    lane8 = lax.broadcasted_iota(jnp.int32, (8, 128), 1)
    pick = jnp.where(row8 == lax.div(lane8, HD), 1.0, 0.0).astype(BF)
    ri = lax.broadcasted_iota(jnp.int32, (128, 128), 0)
    ci = lax.broadcasted_iota(jnp.int32, (128, 128), 1)
    same = jnp.where(lax.div(ri, HD) == lax.div(ci, HD), 1.0, 0.0).astype(BF)

    def upstream(b):
        crd[b, p.pos] = jnp.zeros(crd.shape[2:], F32)
        crt[b, p.s] = jnp.zeros(crt.shape[2:], F32)
        for side in range(2):
            datt = dat[b, side].astype(F32)
            dn = den[b, side]
            up = datt / dn
            prod = datt * attw[b, side] / dn
            lead = prod.astype(BF)
            rest = (prod - lead.astype(F32)).astype(BF)
            cor = nn(lead, same) + nn(rest, same)
            cor_rows = nt(pick, lead) + nt(pick, rest)
            for e in range(2):
                i = 2 * side + e
                if i >= heads:
                    continue
                u = heads * b + i
                part = up if e == 1 else pltpu.roll(up, HD, 1)
                qud[u, own, :] = jnp.where(lane < HD, qp[u].astype(F32), part).astype(BF)
                qut[u, rows_of(p.s * half, half), :] = qud[
                    u, rows_of(p.pos * shard + parity[i] * half, half), :
                ]
                cor_row = cor_rows[e : e + 1, :]
                crd[b, p.pos, i : i + 1, :] = cor_row
                col = -cor[:, e * HD : e * HD + 1]
                lead = col.astype(BF).astype(F32)
                uext[u] = (
                    jnp.where(lane == COR_LANE, lead, 0.0)
                    + jnp.where(lane == COR_LANE + 1, col - lead, 0.0)
                ).astype(BF)
                crt[b, p.s, i : i + 1, :] = jnp.where(
                    parity[i] == 0, cor_row[:, 0:half], cor_row[:, half:shard]
                )
        qu_shares[b].start()
        cors[b].start()

    def query_side(qu, qe, ue, kv, ext, bias):
        kvx = jnp.concatenate([kv, ext], 1)
        s = nt(jnp.concatenate([qu * low, qe], 1), kvx)
        if bias is not None:
            s = s + bias
        dp = nt(jnp.concatenate([qu * high, ue], 1), kvx)
        return nn((jnp.exp(s) * dp).astype(BF), kv)

    def key_side(qu, qe, cor, kv, ext, bias):
        s = nt(jnp.concatenate([kv, ext], 1), jnp.concatenate([qu * low, qe], 1))
        if bias is not None:
            s = s + bias
        w = jnp.exp(s)
        dp = nt(kv, qu * high) - cor
        return nn((w * dp).astype(BF), qu * low) + nn(w.astype(BF), qu * high)

    def grads_own(b):
        for i in range(heads):
            u = heads * b + i
            kv, qu = kvd[u, own, :], qud[u, own, :]
            kvx = jnp.concatenate([kv, tab[i, 0]], 1)
            dp = nt(jnp.concatenate([qu * high, uext[u]], 1), kvx)
            acc[u] = nn((wqo[u].astype(F32) * dp).astype(BF), kv)
            dp = nt(kv, qu * high) - crd[b, p.pos, i : i + 1, :]
            ds = (wko[u].astype(F32) * dp).astype(BF)
            ack[u] = nn(ds, qu * low) + nn(wko[u], qu * high)

    def query_rest(b):
        def dense(j, carry):
            lenl = length_lane(dense_positions(p.seg * SPAN1 + j, shard), lens[b], shard)
            for i in range(heads):
                u = heads * b + i
                kv = kvd[u, rows_of(j * shard, shard), :]
                acc[u] += query_side(
                    qud[u, own, :], qext[...], uext[u], kv, tab[i, 0] + lenl, None
                )
            return carry

        lax.fori_loop(0, p.pos, dense, 0)

        def thin(sg, carry):
            for i in range(heads):
                u = heads * b + i
                mine = rows_of(parity[i] * half, half)
                kv, ext = thin_keys(b, i, sg)
                qu = qut[u, rows_of(p.s * half, half), :]
                acc[u, mine, :] += query_side(qu, qext[mine, :], uext[u, mine, :], kv, ext, None)
            return carry

        lax.fori_loop(0, p.seg, thin, 0)

    def key_rest(b):
        lenl = length_lane(dense_positions(p.s, shard), lens[b], shard)

        def dense(j, carry):
            for i in range(heads):
                u = heads * b + i
                qu = qud[u, rows_of(j * shard, shard), :]
                ack[u] += key_side(
                    qu, qext[...], crd[b, j, i : i + 1, :], kvd[u, own, :], tab[i, 0] + lenl, None
                )
            return carry

        lax.fori_loop(p.pos + 1, SPAN1, dense, 0)

        def thin(sg, carry):
            level = level_of(sg, p.seg, levels)
            for i in range(heads):
                u = heads * b + i
                mine = rows_of(parity[i] * half, half)
                ext = tab[i, level, mine, :] + length_lane(
                    thin_positions(p.s, parity[i], shard, 1), lens[b], half
                )
                kv = kvt[u, rows_of(p.s * half, half), :]
                qu = qut[u, rows_of(sg * SPAN1 * half, SPAN1 * half), :]
                qe = jnp.concatenate([qext[mine, :]] * SPAN1, 0)
                cor = jnp.concatenate(
                    [crt[b, sg * SPAN1 + d, i : i + 1, :] for d in range(SPAN1)], 1
                )
                ack[u, mine, :] += key_side(qu, qe, cor, kv, ext, None)
            return carry

        lax.fori_loop(p.seg + 1, n // SPAN1, thin, 0)

    def send_grads(b):
        dn_sum[b].finish()
        for i in range(heads):
            dqk[b, :, i * 128 : (i + 1) * 128] = ack[heads * b + i].astype(BF)
        for t in range((heads + 1) // 2):
            tile = acc[heads * b + 2 * t]
            if 2 * t + 1 < heads:
                other = pltpu.roll(acc[heads * b + 2 * t + 1], HD, 1)
            else:
                other = jnp.zeros((shard, 128), F32)
            tile = jnp.where(lane < HD, tile, other) * HD**-0.5
            at = (heads + t) * 128
            dqk[b, :, at : at + 128] = tile.astype(BF)
        dm = nn(dqk[b, :, 0 : wp.shape[0]], wp[...])
        for t in range(pat):
            dns[b, t] = dm[t * quarter : (t + 1) * quarter].astype(BF)
        dm_sum[b].start()

    def output(b):
        fd_sum[b].total(tot)
        outf[b, zrows, :] = (sto[b] + tot[...] + vec_row(bdown)).astype(BF)
        out_line[b].start()

    da_arrive(0)
    upstream(0)
    for z in range(pat):
        part = jnp.zeros((256, width), F32)
        for b in rows:
            pair = jnp.concatenate([attf[z, b, zrows, :], attu[z, b, zrows, :]], 1)
            part = part + tn(pair, dsl[b])
        grad3[z * cols : (z + 1) * cols, :] = part[0:cols].astype(BF)
    sum3.step(0)
    da_arrive(1)
    upstream(1)
    fd_sum[0].forward(2)
    grads_own(0)
    sum3.step(1)
    fd_sum[1].forward(1)
    output(0)
    grads_own(1)
    sum1.step(2)
    fd_sum[1].forward(2)
    cors[0].pass_on()
    qu_shares[0].pass_on()
    query_rest(0)
    out_line[0].forward(1)
    output(1)
    cors[0].arrive()
    qu_shares[0].arrive()
    key_rest(0)
    send_grads(0)
    out_line[0].forward(2)
    cors[1].pass_on()
    qu_shares[1].pass_on()
    query_rest(1)
    out_line[1].forward(1)
    cors[1].arrive()
    qu_shares[1].arrive()
    key_rest(1)
    send_grads(1)
    dm_sum[0].forward(1)
    out_line[1].forward(2)
    sum3.step(2)
    sum1.step(3)
    dm_sum[0].forward(2)
    sum3.step(3)
    owner = 2 * p.core + sum3.bits[1]
    ahead = lax.rem(owner - p.z + pat, pat)

    def piece_copy(at):
        return remote(pz, pr.at[at], p_send.at[0], p_recv.at[at], (owner, p.s))

    def piece_got(at):
        return remote(
            pr.at[at], pr.at[at], p_send.at[0], p_recv.at[at], (p.other_z(1), p.s)
        )

    when(ahead != 0, lambda: piece_copy(jnp.maximum(ahead - 1, 0)).start())

    packed = tn(dqk[0, :, 0 : 3 * cols], n1[0])
    for b in range(1, batches):
        packed = packed + tn(dqk[b, :, 0 : 3 * cols], n1[b])
    for i in range(heads):
        at = i * 128
        grad2[i * HD : (i + 1) * HD, :] = packed[at : at + HD].astype(BF)
        grad2[cols + i * HD : cols + (i + 1) * HD, :] = packed[at + HD : at + 128].astype(BF)
    grad2[2 * cols : 3 * cols, :] = packed[2 * cols : 3 * cols].astype(BF)
    grad2[3 * cols : wp.shape[0], :] = jnp.zeros((wp.shape[0] - 3 * cols, width), BF)
    sum2.step(0)

    def piece_rows(at):
        return gout.at[rows_of(at * (cols // 2), cols // 2), :]

    def piece_out(k):
        rows = piece_rows(sum3.bits[2])
        to = lax.rem(p.s + k, n)
        return remote(rows, rows, w_send.at[k - 1], w_recv.at[sum3.bits[2]], (p.z, to))

    def piece_in(at):
        rows = piece_rows(at)
        return remote(rows, rows, w_send.at[0], w_recv.at[at], (p.z, p.sib))

    def own_piece():
        total = pz[...].astype(F32)
        for at in range(pat - 1):
            piece_got(at).wait_recv()
            total = total + pr[at].astype(F32)
        piece_rows(sum3.bits[2])[...] = total.astype(BF)
        for k in range(1, n):
            piece_out(k).start()

    dm_sum[1].forward(1)

    def close(b, sums):
        dm_sum[b].total(tot)
        back, more_gain, more_shift = norm_back(
            xp[b, zrows, :].astype(F32), tot[...], vec_row(gain1)
        )
        gif[b, zrows, :] = (dst[b] + back).astype(BF)
        return sums[0] + more_gain, sums[1] + more_shift

    zero = jnp.zeros((1, width), F32)
    sum2.step(1)
    sums = close(0, (zero, zero))
    gi_line[0].start()
    dm_sum[1].forward(2)
    sum2.step(2)
    sum1.step(4)
    gi_line[0].forward(1)
    when(ahead == 0, own_piece)
    qkv_sum = jnp.zeros((1, 3 * cols), F32)
    for b in rows:
        qkv_sum = qkv_sum + jnp.sum(dqk[b, :, 0 : 3 * cols].astype(F32), 0, keepdims=True)
    sums = close(1, sums)
    v0, v1 = vs.at[0], vs.at[1]
    v0[...] = vecs[...]
    v0[0:1, :] = sums[0]
    v0[1:2, :] = sums[1]
    for k in range(1, pat):
        zsp.copy_to(k, v0, vz.at[k - 1]).start()
    gi_line[1].start()
    sum2.step(3)
    gi_line[0].forward(2)
    gi_line[1].forward(1)
    sum2.step(4)
    sum1.step(5)
    gi_line[1].forward(2)
    for k in range(1, pat):
        zsp.copy_to(k, v0, vz.at[k - 1]).wait_recv()
    row = lax.broadcasted_iota(jnp.int32, (8, width), 0)
    extra = vz[0]
    for k in range(2, pat):
        extra = extra + vz[k - 1]
    v1[...] = v0[...] + jnp.where(row < 5, extra, 0.0)
    v1[7:8, 0 : 3 * cols] = qkv_sum

    def vec_copy(k):
        to = lax.rem(p.s + k, n)
        return remote(v1, vs.at[k + 1], v_send.at[k - 1], v_recv.at[k - 1], (p.z, to))

    for k in range(1, n):
        vec_copy(k).start()
    sum1.step(6)
    saves[0].start()
    sum2.step(5)
    for at in range(2):
        mine = jnp.logical_and(ahead == 0, sum3.bits[2] == at)
        when(jnp.logical_not(mine), lambda at=at: piece_in(at).wait_recv())
    saves[4].start()
    for k in range(1, n):
        vec_copy(k).wait_recv()
    allv = v1[...]
    for k in range(1, n):
        allv = allv + vs[k + 1]
    vout[...] = allv
    for b in rows:
        out_line[b].arrive()
    saves[1].start()
    sum2.step(6)
    saves[2].start()
    for b in rows:
        gi_line[b].arrive()
    saves[3].start()
    for copy in saves:
        copy.wait()
    when(ahead != 0, lambda: piece_copy(jnp.maximum(ahead - 1, 0)).wait_send())
    for k in range(1, n):
        when(ahead == 0, lambda k=k: piece_out(k).wait_send())
    for b in rows:
        for k in range(1, pat):
            da_copy(b, k).wait_send()
    sum3.finish()
    for item in [*kv_shares, *qu_shares, *cors, wo_line, wo_plane, *att_line]:
        item.finish()
    for item in [*fd_sum, *out_line, *dm_sum, *gi_line, sum1, sum2]:
        item.finish()
    for k in range(1, pat):
        zsp.copy_to(k, v0, vz.at[k - 1]).wait_send()
    for k in range(1, n):
        vec_copy(k).wait_send()


def finish_kernel(
    vin,
    permt_hbm,
    outf_hbm,
    gif_hbm,
    gsum1_hbm,
    gsum2_hbm,
    gsum3_hbm,
    gain1,
    shift1,
    bq,
    bv,
    bout,
    gain2,
    shift2,
    bup,
    bdown,
    outp_hbm,
    ginp_hbm,
    gup_hbm,
    gdown_hbm,
    gk_hbm,
    gv_hbm,
    gq_hbm,
    gout_hbm,
    permt,
    outf,
    gif,
    gsum1,
    gsum2,
    gsum3,
    outp,
    ginp,
    gup,
    gdown,
    gk,
    gv,
    gq,
    gout,
    load_sem,
    save_sem,
):
    batches = outf.shape[0]
    cols, width = gsum3.shape
    heads = cols // HD
    jobs = []

    def widen(src, dst):
        def run():
            dst[...] = src[...].astype(F32)

        return run

    def turn(src, dst):
        def run():
            dst[...] = nn(permt[...], src[...]).astype(BF)

        return run

    parts = 4
    for src_hbm, src, dst, dst_hbm in (
        (gsum1_hbm.at[0:width], gsum1.at[0:width], gup, gup_hbm),
        (gsum1_hbm.at[width : 2 * width], gsum1.at[width : 2 * width], gdown, gdown_hbm),
    ):
        step = width // parts
        for i in range(parts):
            rows = slice(i * step, (i + 1) * step)
            jobs.append(
                (src_hbm.at[rows], src.at[rows], widen(src.at[rows], dst.at[rows]), dst.at[rows], dst_hbm.at[rows])
            )
    for b in range(batches):
        for src_hbm, src, dst, dst_hbm in (
            (outf_hbm, outf, outp, outp_hbm),
            (gif_hbm, gif, ginp, ginp_hbm),
        ):
            jobs.append((src_hbm.at[b], src.at[b], turn(src.at[b], dst.at[b]), dst.at[b], dst_hbm.at[b]))
    for i, (dst, dst_hbm) in enumerate(((gk, gk_hbm), (gv, gv_hbm), (gq, gq_hbm))):
        rows = slice(i * cols, (i + 1) * cols)
        jobs.append((gsum2_hbm.at[rows], gsum2.at[rows], widen(gsum2.at[rows], dst), dst, dst_hbm))
    jobs.append((gsum3_hbm, gsum3, widen(gsum3, gout), gout, gout_hbm))

    loads = [
        pltpu.make_async_copy(job[0], job[1], load_sem.at[i]) for i, job in enumerate(jobs)
    ]
    perm_load = pltpu.make_async_copy(permt_hbm, permt, load_sem.at[len(jobs)])
    saves = [
        pltpu.make_async_copy(job[3], job[4], save_sem.at[i]) for i, job in enumerate(jobs)
    ]
    for i, copy in enumerate(loads):
        copy.start()
        if i == 0:
            perm_load.start()
    for r, ref in enumerate((gain1, shift1, bout, gain2, shift2, bup, bdown)):
        ref[...] = vin[r : r + 1, :].reshape(width)
    bq[...] = vin[7:8, 2 * cols : 3 * cols].reshape(cols)
    bv[...] = jnp.concatenate(
        [vin[7:8, i * 128 + HD : (i + 1) * 128] for i in range(heads)], 1
    ).reshape(cols)
    perm_load.wait()
    for i, job in enumerate(jobs):
        loads[i].wait()
        job[2]()
        saves[i].start()
    for copy in saves:
        copy.wait()


def plane_program(
    n,
    pat,
    inputs,
    lengths,
    gain_one,
    shift_one,
    w_query,
    b_query,
    w_key,
    w_value,
    b_value,
    w_out,
    b_out,
    gain_two,
    shift_two,
    w_up,
    b_up,
    w_down,
    b_down,
    d_output,
):
    B, S, W = inputs.shape
    cols = w_query.shape[1]
    hidden = w_up.shape[1]
    heads = cols // HD
    units = B * heads
    tiles = units // 2
    chips = n // 2
    half = S // 2
    quarter = S // pat
    levels = 1
    while SPAN1 << (levels - 1) < n:
        levels += 1
    perm = jnp.asarray(perm_matrix(S), BF)
    permt = jnp.asarray(perm_matrix(S).T, BF)
    qext = jnp.asarray(query_ext(S), BF)
    ktab = jnp.asarray(key_tables(S, heads * pat, levels))
    wide = 3 * cols + (-3 * cols) % 128
    assert hidden == W and pat * cols == B * S and units * 128 == W
    r1, r2 = 2 * W, wide
    vm, sm, anyv = pltpu.VMEM, pltpu.SMEM, pl.ANY
    dma = pltpu.SemaphoreType.DMA

    outf, gif, gsum1, gsum2, gout, vout = call(
        functools.partial(layer_kernel, n, pat, levels),
        "layer",
        [
            ((B, S, W), BF),
            ((B, S, W), BF),
            ((r1, W), BF),
            ((r2, W), BF),
            ((cols, W), BF),
            ((8, W), F32),
        ],
        [
            vm((S, S), BF),
            vm((S, 128), BF),
            vm((B, S, W), BF),
            vm((B, S, W), BF),
            vm((r1, W), BF),
            vm((r2, W), BF),
            vm((cols, W), BF),
            vm((r1, W), BF),
            vm((B, S, W), BF),
            vm((B, S, W), BF),
            vm((wide, W), BF),
            vm((units, S, 128), BF),
            vm((units, SPAN1 * S, 128), BF),
            vm((units, n * half, 128), BF),
            vm((heads, levels, S, 128), BF),
            vm((units, S, 128), F32),
            vm((units, S, 128), F32),
            vm((units, S, S), BF),
            vm((units, S, S), BF),
            vm((pat, B, S + half, 128), BF),
            vm((pat, B, S, 128), BF),
            vm((B, 2, S, 128), F32),
            vm((B, 2, S, 128), F32),
            vm((pat, cols + HD, W), BF),
            vm(w_up.shape, BF),
            vm(w_down.shape, BF),
            vm((B, quarter, W), F32),
            vm((B * S, W), BF),
            vm((B * S, hidden), BF),
            vm((B, S, W), BF),
            vm((B, S, hidden), BF),
            vm((B, pat, quarter, W), BF),
            vm((B, pat + 1, quarter, W), BF),
            vm((quarter, W), F32),
            vm((B, quarter, W), BF),
            vm((B, quarter, W), F32),
            vm((B, pat - 1, 2, quarter, 128), BF),
            vm((B, 2, S, 128), BF),
            vm((B, S, W), BF),
            vm((B, pat + 1, quarter, W), BF),
            vm((units, SPAN1 * S, 128), BF),
            vm((units, n * half, 128), BF),
            vm((B, SPAN1, 8, S), F32),
            vm((B, n, 8, half), F32),
            vm((units, S, 128), BF),
            vm((B, pat + 1, quarter, W), BF),
        ]
        + [vm((r1 >> d, W), BF) for d in (1, 2, 3)]
        + [vm((r2 >> d, W), BF) for d in (1, 2, 3)]
        + [vm((pat * cols >> d, W), BF) for d in (1, 2, 3)]
        + [vm((cols // 2, W), BF), vm((pat - 1, cols // 2, W), BF)]
        + [vm((8, W), F32), vm((pat - 1, 8, W), F32), vm((n + 1, 8, W), F32)]
        + [dma((3 * heads + B + 7,)), dma((5,))]
        + (dense_sems(B) + thin_sems(B, chips)) * 3
        + line_sems(pat)
        + plane_sems(chips)
        + line_sems(pat) * B
        + sum_sems(pat) * B
        + [dma((B, pat - 1))] * 2
        + sum_sems(pat) * B
        + chain_sems(pat) * B
        + sum_sems(pat) * B
        + chain_sems(pat) * B
        + [dma((6,))] * 6
        + [dma((1,)), dma((pat - 1,)), dma((n - 1,)), dma((2,))]
        + [dma((pat - 1,))] * 2
        + [dma((n - 1,))] * 2,
        [sm] + [vm] * 9 + [anyv] * 11,
        0,
        [anyv] * 5 + [vm],
    )(
        lengths,
        gain_one,
        shift_one,
        b_query,
        b_value,
        b_out,
        gain_two,
        shift_two,
        b_up,
        b_down,
        w_query.T,
        w_key.T,
        w_value.T,
        w_out,
        perm,
        qext,
        ktab,
        inputs,
        w_up,
        w_down,
        d_output,
    )

    small = [((size,), F32) for size in (W, W, cols, cols, W, W, W, W, W)]
    large = [((B, S, W), BF)] * 2 + [((W, W), F32)] * 2 + [((cols, W), F32)] * 4
    jobs = 8 + 2 * B + 4
    res = pl.pallas_call(
        finish_kernel,
        name="results",
        in_specs=[pl.BlockSpec(memory_space=m) for m in [vm] + [anyv] * 6],
        out_specs=[pl.BlockSpec(memory_space=m) for m in [vm] * len(small) + [anyv] * len(large)],
        out_shape=[jax.ShapeDtypeStruct(s, d) for s, d in small + large],
        scratch_shapes=[
            vm((S, S), BF),
            vm((B, S, W), BF),
            vm((B, S, W), BF),
            vm((r1, W), BF),
            vm((r2, W), BF),
            vm((cols, W), BF),
        ]
        + [vm(s, d) for s, d in large]
        + [dma((jobs + 1,)), dma((jobs,))],
        compiler_params=pltpu.CompilerParams(vmem_limit_bytes=62 << 20),
    )(vout, permt, outf, gif, gsum1, gsum2, gout)
    gain1, shift1, bq, bv, bout, gain2, shift2, bup, bdown = res[:9]
    outputs, grad_inputs, g_up, g_down, g_k, g_v, g_q, g_out = res[9:]
    return (
        outputs,
        grad_inputs,
        gain1,
        shift1,
        g_q.T,
        bq,
        g_k.T,
        g_v.T,
        bv,
        g_out,
        bout,
        gain2,
        shift2,
        g_up,
        bup,
        g_down,
        bdown,
    )


def solution(mesh):
    token = P(None, "seq", None)
    in_specs = (
        token,
        P(),
        P(),
        P(),
        P(None, "pat"),
        P("pat"),
        P(None, "pat"),
        P(None, "pat"),
        P("pat"),
        P("pat", None),
        P(),
        P(),
        P(),
        P(None, "pat"),
        P("pat"),
        P("pat", None),
        P(),
        token,
    )
    out_specs = (
        token,
        token,
        P(),
        P(),
        P(None, "pat"),
        P("pat"),
        P(None, "pat"),
        P(None, "pat"),
        P("pat"),
        P("pat", None),
        P(),
        P(),
        P(),
        P(None, "pat"),
        P("pat"),
        P("pat", None),
        P(),
    )
    n, pat = mesh.shape["seq"], mesh.shape["pat"]
    body = functools.partial(plane_program if n == 8 else shards, n, pat)
    return jax.shard_map(body, mesh=mesh, in_specs=in_specs, out_specs=out_specs, check_vma=False)
```

```python
import functools

import jax
import jax.numpy as jnp
import numpy as np
from jax import lax
from jax.experimental import pallas as pl
from jax.experimental.pallas import tpu as pltpu
from jax.sharding import PartitionSpec as P

HD = 64
SPAN1 = 4
DILATIONS = (1, 2, 4, 6, 12)
CYCLE = 12
EPS = 1e-05
NEG = -1e30
LEN_LANE = 24
COR_LANE = 25
MESH = pl.DeviceIdType.MESH
BF = jnp.bfloat16
F32 = jnp.float32
ROOT = float(np.sqrt(2.0 / np.pi))


def nn(a, b):
    return lax.dot_general(a, b, (((1,), (0,)), ((), ())), preferred_element_type=F32)


def nt(a, b):
    return lax.dot_general(a, b, (((1,), (1,)), ((), ())), preferred_element_type=F32)


def tn(a, b):
    return lax.dot_general(a, b, (((0,), (0,)), ((), ())), preferred_element_type=F32)


def exact_nt(a, b):
    return lax.dot_general(
        a, b, (((1,), (1,)), ((), ())), preferred_element_type=F32, precision=lax.Precision.HIGHEST
    )


def exact_nn(a, b):
    return lax.dot_general(
        a, b, (((1,), (0,)), ((), ())), preferred_element_type=F32, precision=lax.Precision.HIGHEST
    )


def remote(src, dst, send, recv, device):
    return pltpu.make_async_remote_copy(
        src_ref=src,
        dst_ref=dst,
        send_sem=send,
        recv_sem=recv,
        device_id=device,
        device_id_type=MESH,
    )


def when(cond, fn):
    pl.when(cond)(fn)


def rows_of(start, size):
    return pl.ds(pl.multiple_of(start, 16), size)


def orders(shard):
    p = np.arange(shard)
    return 2 * (p % (shard // 2)) + p // (shard // 2)


def perm_matrix(shard):
    token = orders(shard)
    m = np.zeros((shard, shard), np.float32)
    m[np.arange(shard), token] = 1.0
    return m


def query_ext(shard):
    cls = orders(shard) % CYCLE
    m = np.zeros((shard, 128), np.float32)
    m[np.arange(shard), cls] = 1.0
    m[np.arange(shard), CYCLE + cls] = 1.0
    m[:, LEN_LANE] = 1.0
    return m


def key_tables(shard, heads, levels):
    cls = orders(shard) % CYCLE
    out = np.zeros((heads, levels, shard, 128), np.float32)
    for h in range(heads):
        for level in range(levels):
            count = np.zeros((CYCLE, CYCLE))
            for r in DILATIONS[level:]:
                on = (np.arange(CYCLE) % r == h % r).astype(np.float64)
                count += on[:, None] * on[None, :]
            with np.errstate(divide="ignore"):
                log = np.log(count)
            high = np.where(count > 0, log, NEG).astype(np.float32).astype(jnp.bfloat16)
            low = np.where(count > 0, log - high.astype(np.float64), 0.0)
            out[h, level, :, :CYCLE] = high.astype(np.float32)[:, cls].T
            out[h, level, :, CYCLE : 2 * CYCLE] = low[:, cls].T
            out[h, level, :, COR_LANE] = 1.0
            out[h, level, :, COR_LANE + 1] = 1.0
    return out.astype(jnp.bfloat16)


class Place:
    def __init__(self, n, pat):
        self.n, self.pat = n, pat
        self.z = lax.axis_index("pat")
        self.s = lax.axis_index("seq")
        self.core = lax.rem(self.s, 2)
        self.chip = lax.div(self.s, 2)
        self.seg = lax.div(self.s, SPAN1)
        self.pos = lax.rem(self.s, SPAN1)
        self.sib = self.s + 1 - 2 * self.core
        self.even = lax.rem(self.chip, 2) == 0

    def other_z(self, k):
        return lax.rem(self.z + k, self.pat)

    def greet(self, z_axis, same_core, all_seq=False):
        bar = pltpu.get_barrier_semaphore()
        count = 0
        if z_axis:
            for k in range(1, self.pat):
                pl.semaphore_signal(
                    bar, inc=1, device_id=(self.other_z(k), self.s), device_id_type=MESH
                )
                count += 1
        if all_seq:
            for k in range(1, self.n):
                to = lax.rem(self.s + k, self.n)
                pl.semaphore_signal(bar, inc=1, device_id=(self.z, to), device_id_type=MESH)
                count += 1
        elif same_core:
            pl.semaphore_signal(bar, inc=1, device_id=(self.z, self.sib), device_id_type=MESH)
            count += 1
            for k in range(1, self.n // 2):
                to = lax.rem(self.s + 2 * k, self.n)
                pl.semaphore_signal(bar, inc=1, device_id=(self.z, to), device_id_type=MESH)
                count += 1
        return bar, count


def lane_masks():
    lane = lax.broadcasted_iota(jnp.int32, (1, 128), 1)
    low = jnp.where(lane < HD, 1.0, 0.0)
    return low.astype(BF), (1.0 - low).astype(BF)


def token_of(index, shard):
    half = jnp.where(index >= shard // 2, 1, 0)
    return 2 * (index - half * (shard // 2)) + half


def length_lane(positions, length, rows):
    lane = lax.broadcasted_iota(jnp.int32, (rows, 128), 1)
    hit = jnp.logical_and(lane == LEN_LANE, positions >= length)
    return jnp.where(hit, NEG, 0.0).astype(BF)


def dense_positions(device, shard):
    row = lax.broadcasted_iota(jnp.int32, (shard, 128), 0)
    return device * shard + token_of(row, shard)


def thin_positions(first_device, parity, shard, blocks):
    half = shard // 2
    row = lax.broadcasted_iota(jnp.int32, (blocks * half, 128), 0)
    block = lax.div(row, half)
    return (first_device + block) * shard + 2 * (row - block * half) + parity


def level_of(seg_a, seg_b, levels):
    level = jnp.int32(1)
    size = 2
    for _ in range(2, levels):
        apart = lax.div(seg_a, size) != lax.div(seg_b, size)
        level = level + jnp.where(apart, 1, 0)
        size *= 2
    return level


class Shares:
    def __init__(self, place, shard, forward, dense, thin, dense_sems, thin_sems):
        self.p, self.shard, self.forward = place, shard, forward
        self.dense, self.thin = dense, thin
        self.ds, self.ts = dense_sems, thin_sems
        p = place
        self.chips = p.n // 2
        if forward:
            self.sib_sends, self.sib_gets = p.core == 0, p.core == 1
            self.x_sends, self.x_gets = p.even, jnp.logical_not(p.even)
            self.x_to, self.x_slot = p.s + 2, p.pos - 2
        else:
            self.sib_sends, self.sib_gets = p.core == 1, p.core == 0
            self.x_sends, self.x_gets = jnp.logical_not(p.even), p.even
            self.x_to, self.x_slot = p.s - 2, p.pos + 2
        self.sib_pos = p.pos + 1 - 2 * p.core
        self.x_sib_slot = self.x_slot + 1 - 2 * p.core

    def sib_copy(self, slot):
        p = self.p
        return remote(
            self.dense(slot), self.dense(slot), self.ds[0].at[0], self.ds[1].at[0], (p.z, p.sib)
        )

    def x_copy(self, slot):
        p = self.p
        to = jnp.where(self.x_sends, self.x_to, p.sib)
        return remote(
            self.dense(slot), self.dense(slot), self.ds[0].at[1], self.ds[1].at[1], (p.z, to)
        )

    def hand_copy(self, slot):
        p = self.p
        return remote(
            self.dense(slot), self.dense(slot), self.ds[0].at[2], self.ds[1].at[2], (p.z, p.sib)
        )

    def thin_to(self, chip):
        seg = chip // 2
        return (seg > self.p.seg) if self.forward else (seg < self.p.seg)

    def thin_from(self, chip):
        seg = chip // 2
        return (seg < self.p.seg) if self.forward else (seg > self.p.seg)

    def thin_copy(self, chip):
        p = self.p
        return remote(
            self.thin(p.s),
            self.thin(p.s),
            self.ts[0].at[chip],
            self.ts[1].at[p.chip],
            (p.z, 2 * chip + p.core),
        )

    def thin_got(self, chip):
        p = self.p
        slot = 2 * chip + p.core
        return remote(
            self.thin(slot), self.thin(slot), self.ts[0].at[chip], self.ts[1].at[chip], (p.z, p.sib)
        )

    def thin_hand(self, chip, mine):
        p = self.p
        slot = 2 * chip + (p.core if mine else 1 - p.core)
        return remote(
            self.thin(slot), self.thin(slot), self.ts[2].at[chip], self.ts[3].at[chip], (p.z, p.sib)
        )

    def start(self):
        p = self.p
        for chip in range(self.chips - 1, -1, -1) if self.forward else range(self.chips):
            when(self.thin_to(chip), lambda chip=chip: self.thin_copy(chip).start())
        when(self.x_sends, lambda: self.x_copy(p.pos).start())
        when(self.sib_sends, lambda: self.sib_copy(p.pos).start())

    def pass_on(self):
        def dense_part():
            self.x_copy(self.x_slot).wait_recv()
            self.hand_copy(self.x_slot).start()

        when(self.x_gets, dense_part)
        for chip in range(self.chips):

            def thin_part(chip=chip):
                self.thin_got(chip).wait_recv()
                self.thin_hand(chip, True).start()

            when(self.thin_from(chip), thin_part)

    def arrive(self):
        when(self.sib_gets, lambda: self.sib_copy(self.sib_pos).wait_recv())
        when(self.x_gets, lambda: self.hand_copy(self.x_sib_slot).wait_recv())
        for chip in range(self.chips):
            when(
                self.thin_from(chip),
                lambda chip=chip: self.thin_hand(chip, False).wait_recv(),
            )

    def finish(self):
        p = self.p
        when(self.x_sends, lambda: self.x_copy(p.pos).wait_send())
        when(self.sib_sends, lambda: self.sib_copy(p.pos).wait_send())
        when(self.x_gets, lambda: self.hand_copy(self.x_slot).wait_send())
        for chip in range(self.chips):
            when(self.thin_to(chip), lambda chip=chip: self.thin_copy(chip).wait_send())
            when(self.thin_from(chip), lambda chip=chip: self.thin_hand(chip, True).wait_send())


def dense_sems(batches):
    return [pltpu.SemaphoreType.DMA((batches, 3))] * 2


def thin_sems(batches, chips):
    return [pltpu.SemaphoreType.DMA((batches, chips))] * 4


class Spread:
    def __init__(self, place, send, recv):
        self.p, self.send, self.recv = place, send, recv

    def copy_to(self, k, src, dst):
        p = self.p
        return remote(src, dst, self.send.at[k - 1], self.recv.at[k - 1], (p.other_z(k), p.s))


def forward_kernel(
    n,
    pat,
    levels,
    lens,
    x_ref,
    gain,
    shift,
    wq,
    bq,
    wkv,
    bkv,
    wout,
    perm,
    qext,
    ktab,
    xp,
    n1,
    qp,
    kvd,
    kvt,
    attf,
    wofp,
    attw,
    den,
    tab,
    acc,
    tab_sem,
    w_send,
    w_recv,
    a_send,
    a_recv,
    ds0,
    ds1,
    ts0,
    ts1,
    ts2,
    ts3,
):
    batches, shard, width = x_ref.shape
    half = shard // 2
    heads = wout.shape[0] // HD
    units = batches * heads
    p = Place(n, pat)
    bar, greeted = p.greet(True, True)
    low, high = lane_masks()

    def tab_copy(i):
        return pltpu.make_async_copy(ktab.at[heads * p.z + i], tab.at[i], tab_sem.at[i])

    for i in range(heads):
        tab_copy(i).start()
    for z in range(pat):
        wofp[z, 0:HD, :] = jnp.zeros((HD, width), BF)
        wofp[z, HD + heads * HD : 2 * HD + heads * HD, :] = jnp.zeros((HD, width), BF)
    wofp[p.z, HD : HD + heads * HD, :] = wout[...]
    for b in range(batches):
        xb = nn(perm[...], x_ref[b])
        xp[b] = xb.astype(BF)
        mean = jnp.mean(xb, -1, keepdims=True)
        cen = xb - mean
        var = jnp.mean(cen * cen, -1, keepdims=True)
        n1[b] = (cen * lax.rsqrt(var + EPS) * gain[...] + shift[...]).astype(BF)

    shares = [
        Shares(
            p,
            shard,
            True,
            lambda slot, b=b: kvd.at[pl.ds(heads * b, heads), rows_of(slot * shard, shard), :],
            lambda dev, b=b: kvt.at[pl.ds(heads * b, heads), rows_of(dev * half, half), :],
            [ds0.at[b], ds1.at[b]],
            [ts0.at[b], ts1.at[b], ts2.at[b], ts3.at[b]],
        )
        for b in range(batches)
    ]
    parity = [lax.rem(heads * p.z + i, 2) for i in range(heads)]
    for b in range(batches):
        q = ((nn(n1[b], wq[...]) + bq[...]).astype(BF)) * jnp.asarray(HD**-0.5, BF)
        kv = (nn(n1[b], wkv[...]) + bkv[...]).astype(BF)
        for i in range(heads):
            qp[heads * b + i] = q[:, i * 128 : (i + 1) * 128]
            kvd[heads * b + i, rows_of(p.pos * shard, shard), :] = kv[:, i * 128 : (i + 1) * 128]
        for i in range(heads):
            kvt[heads * b + i, rows_of(p.s * half, half), :] = kvd[
                heads * b + i, rows_of(p.pos * shard + parity[i] * half, half), :
            ]
        if b == 0:
            pl.semaphore_wait(bar, greeted)
        shares[b].start()
    w_spread = Spread(p, w_send, w_recv)

    def w_slot(z):
        return wofp.at[z, HD : HD + heads * HD, :]

    for k in range(1, pat):
        w_spread.copy_to(k, w_slot(p.z), w_slot(p.z)).start()
    for i in range(heads):
        tab_copy(i).wait()

    def attend(qx, kv, ext, bias):
        s = nt(qx, jnp.concatenate([kv, ext], 1))
        if bias is not None:
            s = s + bias
        return nn(jnp.exp(s).astype(BF), kv * high + low)

    own = rows_of(p.pos * shard, shard)
    qi = lax.broadcasted_iota(jnp.int32, (shard, shard), 0)
    ki = lax.broadcasted_iota(jnp.int32, (shard, shard), 1)
    qt, kt = token_of(qi, shard), token_of(ki, shard)
    for b in range(batches):
        live = jnp.logical_or(
            jnp.logical_and(kt < qt, kt + p.s * shard < lens[b]), kt == qt
        )
        bias = jnp.where(live, 0.0, NEG)
        for i in range(heads):
            u = heads * b + i
            qx = jnp.concatenate([qp[u], qext[...]], 1)
            acc[u] = attend(qx, kvd[u, own, :], tab[i, 0], bias)

    att_spread = [Spread(p, a_send.at[t], a_recv.at[t]) for t in range(units // 2)]
    lane = lax.broadcasted_iota(jnp.int32, (shard, 128), 1)
    for b in range(batches):
        shares[b].pass_on()
        shares[b].arrive()

        def dense(j, carry, b=b):
            lenl = length_lane(dense_positions(p.seg * SPAN1 + j, shard), lens[b], shard)
            for i in range(heads):
                u = heads * b + i
                qx = jnp.concatenate([qp[u], qext[...]], 1)
                kv = kvd[u, rows_of(j * shard, shard), :]
                acc[u] += attend(qx, kv, tab[i, 0] + lenl, None)
            return carry

        lax.fori_loop(0, p.pos, dense, 0)

        def thin(sg, carry, b=b):
            level = level_of(sg, p.seg, levels)
            for i in range(heads):
                u = heads * b + i
                mine = rows_of(parity[i] * half, half)
                places = thin_positions(sg * SPAN1, parity[i], shard, SPAN1)
                lenl = length_lane(places, lens[b], SPAN1 * half)
                ext = jnp.concatenate([tab[i, level, mine, :]] * SPAN1, 0) + lenl
                qx = jnp.concatenate([qp[u, mine, :], qext[mine, :]], 1)
                kv = kvt[u, rows_of(sg * SPAN1 * half, SPAN1 * half), :]
                acc[u, mine, :] += attend(qx, kv, ext, None)
            return carry

        lax.fori_loop(0, p.seg, thin, 0)
        for t in range(units // 2):
            if (2 * t + 1) // heads != b:
                continue
            even, odd = acc[2 * t], acc[2 * t + 1]
            num = jnp.where(lane < HD, pltpu.roll(even, HD, 1), odd)
            dn = jnp.where(lane < HD, even, pltpu.roll(odd, HD, 1))
            wide = num / dn
            den[t] = dn
            attw[t] = wide
            attf[p.z, t] = wide.astype(BF)
            for k in range(1, pat):
                att_spread[t].copy_to(k, attf.at[p.z, t], attf.at[p.z, t]).start()
    for k in range(1, pat):
        frm = lax.rem(p.z + pat - k, pat)
        w_spread.copy_to(k, w_slot(p.z), w_slot(p.z)).wait_send()
        w_spread.copy_to(k, w_slot(frm), w_slot(frm)).wait_recv()
        for t in range(units // 2):
            att_spread[t].copy_to(k, attf.at[p.z, t], attf.at[p.z, t]).wait_send()
            att_spread[t].copy_to(k, attf.at[frm, t], attf.at[frm, t]).wait_recv()
    for b in range(batches):
        shares[b].finish()


def middle_kernel(
    n,
    pat,
    xp,
    attf,
    wofp,
    bout,
    gain,
    shift,
    wup,
    bup,
    wdown,
    dout,
    perm,
    gud,
    fd,
    dsf,
    dst,
    sto,
    vecs,
    state,
    n2,
    act,
    dop,
    dh,
    dns,
    dno,
    dnr,
    r_send,
    r_recv,
    g_send,
    g_recv,
):
    batches, shard, width = xp.shape
    quarter = shard // pat
    p = Place(n, pat)
    bar, greeted = p.greet(True, False)
    rs = [Spread(p, r_send.at[b], r_recv.at[b]) for b in range(batches)]
    ag = [Spread(p, g_send.at[b], g_recv.at[b]) for b in range(batches)]
    bup_sum = jnp.zeros((1, width), F32)
    bdown_sum = jnp.zeros((1, width), F32)
    for b in range(batches):
        mixed = jnp.zeros((shard, width), F32)
        for z in range(pat):
            pair = jnp.concatenate([attf[z, b], attf[z, b + 1]], 1)
            weight = wofp[z, HD : HD + 256, :] if b == 0 else wofp[z, 0:256, :]
            mixed = mixed + nn(pair, weight)
        st = xp[b].astype(F32) + mixed + bout[...]
        state[b] = st
        mean = jnp.mean(st, -1, keepdims=True)
        cen = st - mean
        var = jnp.mean(cen * cen, -1, keepdims=True)
        norm = (cen * lax.rsqrt(var + EPS) * gain[...] + shift[...]).astype(BF)
        n2[b] = norm
        dob = nn(perm[...], dout[b])
        dop[b] = dob.astype(BF)
        bdown_sum = bdown_sum + jnp.sum(dob, 0, keepdims=True)
        hid = nn(norm, wup[...]) + bup[...]
        cube = hid * hid * hid
        th = jnp.tanh(ROOT * (hid + 0.044715 * cube))
        act[b] = (0.5 * hid * (1.0 + th)).astype(BF)
        slope = 0.5 * (1.0 + th) + 0.5 * hid * (1.0 - th * th) * (
            ROOT * (1.0 + 3.0 * 0.044715 * hid * hid)
        )
        dhid = (nt(dop[b], wdown[...]) * slope).astype(BF)
        dh[b] = dhid
        bup_sum = bup_sum + jnp.sum(dhid.astype(F32), 0, keepdims=True)
        dn = nt(dhid, wup[...])
        for z in range(pat):
            dns[b, z] = dn[z * quarter : (z + 1) * quarter].astype(BF)
        if b == 0:
            pl.semaphore_wait(bar, greeted)
        for k in range(1, pat):
            rs[b].copy_to(k, dns.at[b, p.other_z(k)], dnr.at[b, k - 1]).start()
    vecs[...] = jnp.zeros(vecs.shape, F32)
    for b in range(batches):
        fd[b] = nn(act[b], wdown[...]).astype(BF)
    bout_sum = jnp.zeros((1, width), F32)
    gain_sum = jnp.zeros((1, width), F32)
    shift_sum = jnp.zeros((1, width), F32)
    mine = rows_of(p.z * quarter, quarter)
    for b in range(batches):
        total = dns[b, p.z].astype(F32)
        for k in range(1, pat):
            rs[b].copy_to(k, dns.at[b, p.other_z(k)], dnr.at[b, k - 1]).wait_recv()
            total = total + dnr[b, k - 1].astype(F32)
        st = state[b, mine, :]
        sto[b] = st
        mean = jnp.mean(st, -1, keepdims=True)
        cen = st - mean
        inv = lax.rsqrt(jnp.mean(cen * cen, -1, keepdims=True) + EPS)
        hat = cen * inv
        gain_sum = gain_sum + jnp.sum(total * hat, 0, keepdims=True)
        shift_sum = shift_sum + jnp.sum(total, 0, keepdims=True)
        dhat = total * gain[...]
        back = inv * (
            dhat
            - jnp.mean(dhat, -1, keepdims=True)
            - hat * jnp.mean(dhat * hat, -1, keepdims=True)
        )
        ds = dop[b, mine, :].astype(F32) + back
        dst[b] = ds
        bout_sum = bout_sum + jnp.sum(ds, 0, keepdims=True)
        dsf[b, mine, :] = ds.astype(BF)
        for k in range(1, pat):
            ag[b].copy_to(k, dsf.at[b, mine, :], dsf.at[b, mine, :]).start()
    vecs[2:3, :] = bout_sum
    vecs[3:4, :] = gain_sum
    vecs[4:5, :] = shift_sum
    vecs[5:6, :] = bup_sum
    vecs[6:7, :] = bdown_sum
    up = tn(n2[0], dh[0])
    for b in range(1, batches):
        up = up + tn(n2[b], dh[b])
    gud[0:width, :] = up.astype(BF)
    down = tn(act[0], dop[0])
    for b in range(1, batches):
        down = down + tn(act[b], dop[b])
    gud[width : 2 * width, :] = down.astype(BF)
    for b in range(batches):
        for k in range(1, pat):
            frm = lax.rem(p.z + pat - k, pat)
            theirs = dsf.at[b, rows_of(frm * quarter, quarter), :]
            rs[b].copy_to(k, dns.at[b, p.other_z(k)], dnr.at[b, k - 1]).wait_send()
            ag[b].copy_to(k, dsf.at[b, mine, :], dsf.at[b, mine, :]).wait_send()
            ag[b].copy_to(k, theirs, theirs).wait_recv()


def backward_kernel(
    n,
    pat,
    levels,
    lens,
    dsf,
    wofp,
    attf,
    attw,
    den,
    qp,
    kvd,
    kvt,
    tab,
    qext,
    fd,
    sto,
    bdown,
    permt,
    dq,
    dkv,
    gout,
    outp,
    qud,
    qut,
    crd,
    crt,
    uext,
    acq,
    ack,
    fdr,
    outf,
    f_send,
    f_recv,
    o_send,
    o_recv,
    ds0,
    ds1,
    ts0,
    ts1,
    ts2,
    ts3,
    cd0,
    cd1,
    ct0,
    ct1,
    ct2,
    ct3,
):
    batches, shard, width = dsf.shape
    half = shard // 2
    quarter = shard // pat
    units = qp.shape[0]
    heads = units // batches
    p = Place(n, pat)
    bar, greeted = p.greet(True, True)
    low, high = lane_masks()
    parity = [lax.rem(heads * p.z + i, 2) for i in range(heads)]
    own = rows_of(p.pos * shard, shard)
    lane = lax.broadcasted_iota(jnp.int32, (shard, 128), 1)
    row8 = lax.broadcasted_iota(jnp.int32, (8, 128), 0)
    lane8 = lax.broadcasted_iota(jnp.int32, (8, 128), 1)
    pick = jnp.where(row8 == lax.div(lane8, HD), 1.0, 0.0).astype(F32)
    ri = lax.broadcasted_iota(jnp.int32, (128, 128), 0)
    ci = lax.broadcasted_iota(jnp.int32, (128, 128), 1)
    same = jnp.where(lax.div(ri, HD) == lax.div(ci, HD), 1.0, 0.0).astype(F32)

    wide = [
        nt(dsf[b], wofp[p.z, HD : HD + 256, :] if b == 0 else wofp[p.z, 0:256, :])
        for b in range(batches)
    ]
    tiles = [wide[0][:, 0:128], wide[0][:, 128:256] + wide[1][:, 0:128], wide[1][:, 128:256]]
    crd[p.pos] = jnp.zeros(crd.shape[1:], F32)
    crt[p.s] = jnp.zeros(crt.shape[1:], F32)
    for t in range(units // 2):
        dn = den[t]
        up = tiles[t] / dn
        prod = tiles[t] * attw[t] / dn
        cor = exact_nn(prod, same)
        cor_rows = exact_nt(pick, prod)
        for e in range(2):
            u = 2 * t + e
            i = u % heads
            part = up if e == 1 else pltpu.roll(up, HD, 1)
            mixed = jnp.where(lane < HD, qp[u].astype(F32), part).astype(BF)
            qud[u, own, :] = mixed
            qut[u, rows_of(p.s * half, half), :] = qud[
                u, rows_of(p.pos * shard + parity[i] * half, half), :
            ]
            crd[p.pos, u : u + 1, :] = cor_rows[e : e + 1, :]
            col = -cor[:, e * HD : e * HD + 1]
            first = col.astype(BF).astype(F32)
            ue = jnp.where(lane == COR_LANE, first, 0.0) + jnp.where(
                lane == COR_LANE + 1, col - first, 0.0
            )
            uext[u] = ue.astype(BF)
            thin_cor = jnp.where(parity[i] == 0, cor_rows[e : e + 1, 0:half], cor_rows[e : e + 1, half:shard])
            crt[p.s, u : u + 1, :] = thin_cor
    pl.semaphore_wait(bar, greeted)
    cors = Shares(
        p,
        shard,
        False,
        lambda slot: crd.at[slot],
        lambda dev: crt.at[dev],
        [cd0, cd1],
        [ct0, ct1, ct2, ct3],
    )
    shares = [
        Shares(
            p,
            shard,
            False,
            lambda slot, b=b: qud.at[pl.ds(heads * b, heads), rows_of(slot * shard, shard), :],
            lambda dev, b=b: qut.at[pl.ds(heads * b, heads), rows_of(dev * half, half), :],
            [ds0.at[b], ds1.at[b]],
            [ts0.at[b], ts1.at[b], ts2.at[b], ts3.at[b]],
        )
        for b in range(batches)
    ]
    cors.start()
    for b in range(batches):
        shares[b].start()
    fs = [Spread(p, f_send.at[b], f_recv.at[b]) for b in range(batches)]
    og = [Spread(p, o_send.at[b], o_recv.at[b]) for b in range(batches)]

    def fd_src(b, k):
        return fd.at[b, rows_of(p.other_z(k) * quarter, quarter), :]

    for b in range(batches):
        for k in range(1, pat):
            fs[b].copy_to(k, fd_src(b, k), fdr.at[b, k - 1]).start()

    def query_side(qu, qe, ue, kv, ext, bias):
        kvx = jnp.concatenate([kv, ext], 1)
        s = nt(jnp.concatenate([qu * low, qe], 1), kvx)
        if bias is not None:
            s = s + bias
        dp = nt(jnp.concatenate([qu * high, ue], 1), kvx)
        return nn((jnp.exp(s) * dp).astype(BF), kv)

    def key_side(qu, qe, cor, kv, ext, bias):
        s = nt(jnp.concatenate([kv, ext], 1), jnp.concatenate([qu * low, qe], 1))
        if bias is not None:
            s = s + bias
        w = jnp.exp(s)
        dp = nt(kv, qu * high) - cor
        return nn((w * dp).astype(BF), qu * low) + nn(w.astype(BF), qu * high)

    qi = lax.broadcasted_iota(jnp.int32, (shard, shard), 0)
    ki = lax.broadcasted_iota(jnp.int32, (shard, shard), 1)
    ti, tj = token_of(qi, shard), token_of(ki, shard)
    for b in range(batches):
        bias = jnp.where(
            jnp.logical_or(jnp.logical_and(tj < ti, tj + p.s * shard < lens[b]), tj == ti), 0.0, NEG
        )
        biast = jnp.where(
            jnp.logical_or(jnp.logical_and(ti < tj, ti + p.s * shard < lens[b]), tj == ti), 0.0, NEG
        )
        for i in range(heads):
            u = heads * b + i
            kv = kvd[u, own, :]
            qu = qud[u, own, :]
            acq[u] = query_side(qu, qext[...], uext[u], kv, tab[i, 0], bias)
            ack[u] = key_side(qu, qext[...], crd[p.pos, u : u + 1, :], kv, tab[i, 0], biast)

    for b in range(batches):

        def dense_q(j, carry, b=b):
            lenl = length_lane(dense_positions(p.seg * SPAN1 + j, shard), lens[b], shard)
            for i in range(heads):
                u = heads * b + i
                kv = kvd[u, rows_of(j * shard, shard), :]
                acq[u] += query_side(
                    qud[u, own, :], qext[...], uext[u], kv, tab[i, 0] + lenl, None
                )
            return carry

        lax.fori_loop(0, p.pos, dense_q, 0)

        def thin_q(sg, carry, b=b):
            level = level_of(sg, p.seg, levels)
            for i in range(heads):
                u = heads * b + i
                mine = rows_of(parity[i] * half, half)
                places = thin_positions(sg * SPAN1, parity[i], shard, SPAN1)
                lenl = length_lane(places, lens[b], SPAN1 * half)
                ext = jnp.concatenate([tab[i, level, mine, :]] * SPAN1, 0) + lenl
                kv = kvt[u, rows_of(sg * SPAN1 * half, SPAN1 * half), :]
                qu = qut[u, rows_of(p.s * half, half), :]
                acq[u, mine, :] += query_side(
                    qu, qext[mine, :], uext[u, mine, :], kv, ext, None
                )
            return carry

        lax.fori_loop(0, p.seg, thin_q, 0)

    zrows = rows_of(p.z * quarter, quarter)
    for b in range(batches):
        total = fd[b, zrows, :].astype(F32)
        for k in range(1, pat):
            fs[b].copy_to(k, fd_src(b, k), fdr.at[b, k - 1]).wait_recv()
            total = total + fdr[b, k - 1].astype(F32)
        outf[b, zrows, :] = (sto[b] + total + bdown[...]).astype(BF)
        for k in range(1, pat):
            og[b].copy_to(k, outf.at[b, zrows, :], outf.at[b, zrows, :]).start()
    left = tn(jnp.concatenate([attf[p.z, 0], attf[p.z, 1]], 1), dsf[0])
    right = tn(jnp.concatenate([attf[p.z, 1], attf[p.z, 2]], 1), dsf[1])
    gout[...] = (left[0 : heads * HD] + right[HD : HD + heads * HD]).astype(BF)

    cors.pass_on()
    cors.arrive()
    for b in range(batches):
        shares[b].pass_on()
        shares[b].arrive()
        lenl = length_lane(dense_positions(p.s, shard), lens[b], shard)

        def dense_k(j, carry, b=b, lenl=lenl):
            for i in range(heads):
                u = heads * b + i
                qu = qud[u, rows_of(j * shard, shard), :]
                ack[u] += key_side(
                    qu, qext[...], crd[j, u : u + 1, :], kvd[u, own, :], tab[i, 0] + lenl, None
                )
            return carry

        lax.fori_loop(p.pos + 1, SPAN1, dense_k, 0)

        def thin_k(dev, carry, b=b):
            level = level_of(lax.div(dev, SPAN1), p.seg, levels)
            for i in range(heads):
                u = heads * b + i
                mine = rows_of(parity[i] * half, half)
                ext = tab[i, level, mine, :] + length_lane(
                    thin_positions(p.s, parity[i], shard, 1), lens[b], half
                )
                kv = kvt[u, rows_of(p.s * half, half), :]
                qu = qut[u, rows_of(dev * half, half), :]
                ack[u, mine, :] += key_side(
                    qu, qext[mine, :], crt[dev, u : u + 1, :], kv, ext, None
                )
            return carry

        lax.fori_loop(SPAN1 * (p.seg + 1), n, thin_k, 0)
        for i in range(heads):
            u = heads * b + i
            lanes = slice(i * 128, (i + 1) * 128)
            dq[b, :, lanes] = (acq[u] * HD**-0.5).astype(BF)
            dkv[b, :, lanes] = ack[u].astype(BF)

    for b in range(batches):
        for k in range(1, pat):
            frm = lax.rem(p.z + pat - k, pat)
            theirs = outf.at[b, rows_of(frm * quarter, quarter), :]
            og[b].copy_to(k, theirs, theirs).wait_recv()
            og[b].copy_to(k, outf.at[b, zrows, :], outf.at[b, zrows, :]).wait_send()
            fs[b].copy_to(k, fd_src(b, k), fdr.at[b, k - 1]).wait_send()
        outp[b] = nn(permt[...], outf[b]).astype(BF)
    cors.finish()
    for b in range(batches):
        shares[b].finish()


def tail_kernel(
    n,
    pat,
    xp,
    n1,
    dq,
    dkv,
    wq,
    wkv,
    gain,
    dst,
    vecs,
    gud,
    gout,
    permt,
    ginp,
    vout,
    grad,
    dns,
    dnr,
    gif,
    v0,
    vz,
    r_send,
    r_recv,
    g_send,
    g_recv,
    z_send,
    z_recv,
):
    batches, shard, width = xp.shape
    quarter = shard // pat
    cols = gout.shape[0]
    heads = cols // HD
    p = Place(n, pat)
    bar, greeted = p.greet(True, False)
    rs = [Spread(p, r_send.at[b], r_recv.at[b]) for b in range(batches)]
    ag = [Spread(p, g_send.at[b], g_recv.at[b]) for b in range(batches)]
    for b in range(batches):
        part = nt(dq[b], wq[...]) + nt(dkv[b], wkv[...])
        for z in range(pat):
            dns[b, z] = part[z * quarter : (z + 1) * quarter].astype(BF)
        if b == 0:
            pl.semaphore_wait(bar, greeted)
        for k in range(1, pat):
            rs[b].copy_to(k, dns.at[b, p.other_z(k)], dnr.at[b, k - 1]).start()
    qsum = jnp.zeros((1, heads * 128), F32)
    vsum = jnp.zeros((1, heads * 128), F32)
    for b in range(batches):
        qsum = qsum + jnp.sum(dq[b].astype(F32), 0, keepdims=True)
        vsum = vsum + jnp.sum(dkv[b].astype(F32), 0, keepdims=True)
    grad[0 : 2 * width, :] = gud[...].astype(F32)
    base = 2 * width
    for i in range(heads):
        lanes = slice(i * 128, (i + 1) * 128)
        a = tn(dq[0, :, lanes], n1[0])
        c = tn(dkv[0, :, lanes], n1[0])
        for b in range(1, batches):
            a = a + tn(dq[b, :, lanes], n1[b])
            c = c + tn(dkv[b, :, lanes], n1[b])
        grad[base + i * HD : base + (i + 1) * HD, :] = a[0:HD]
        grad[base + cols + i * HD : base + cols + (i + 1) * HD, :] = c[0:HD]
        grad[base + 2 * cols + i * HD : base + 2 * cols + (i + 1) * HD, :] = c[HD:]
    grad[base + 3 * cols : base + 4 * cols, :] = gout[...].astype(F32)
    zrows = rows_of(p.z * quarter, quarter)
    gain_sum = jnp.zeros((1, width), F32)
    shift_sum = jnp.zeros((1, width), F32)
    for b in range(batches):
        total = dns[b, p.z].astype(F32)
        for k in range(1, pat):
            rs[b].copy_to(k, dns.at[b, p.other_z(k)], dnr.at[b, k - 1]).wait_recv()
            total = total + dnr[b, k - 1].astype(F32)
        back, more_gain, more_shift = norm_back(xp[b, zrows, :].astype(F32), total, gain[...])
        gain_sum = gain_sum + more_gain
        shift_sum = shift_sum + more_shift
        gif[b, zrows, :] = (dst[b] + back).astype(BF)
        for k in range(1, pat):
            ag[b].copy_to(k, gif.at[b, zrows, :], gif.at[b, zrows, :]).start()
    v0[...] = vecs[...]
    v0[0:1, :] = gain_sum
    v0[1:2, :] = shift_sum
    zsp = Spread(p, z_send, z_recv)
    for k in range(1, pat):
        zsp.copy_to(k, v0, vz.at[k - 1]).start()
    for k in range(1, pat):
        zsp.copy_to(k, v0, vz.at[k - 1]).wait_recv()
    row = lax.broadcasted_iota(jnp.int32, (8, width), 0)
    extra = vz[0]
    for k in range(2, pat):
        extra = extra + vz[k - 1]
    vout[0:8, :] = v0[...] + jnp.where(row < 5, extra, 0.0)
    vout[8:16, :] = jnp.zeros((8, width), F32)
    vout[8:9, 0 : heads * 128] = qsum
    vout[9:10, 0 : heads * 128] = vsum
    for b in range(batches):
        for k in range(1, pat):
            frm = lax.rem(p.z + pat - k, pat)
            theirs = gif.at[b, rows_of(frm * quarter, quarter), :]
            ag[b].copy_to(k, theirs, theirs).wait_recv()
        ginp[b] = nn(permt[...], gif[b]).astype(BF)
    for b in range(batches):
        for k in range(1, pat):
            rs[b].copy_to(k, dns.at[b, p.other_z(k)], dnr.at[b, k - 1]).wait_send()
            ag[b].copy_to(k, gif.at[b, zrows, :], gif.at[b, zrows, :]).wait_send()
    for k in range(1, pat):
        zsp.copy_to(k, v0, vz.at[k - 1]).wait_send()


def call(kernel, name, outs, scratch, specs, number, places=None):
    return pl.pallas_call(
        kernel,
        name=name,
        out_shape=[jax.ShapeDtypeStruct(s, d) for s, d in outs],
        in_specs=[pl.BlockSpec(memory_space=m) for m in specs],
        out_specs=[
            pl.BlockSpec(memory_space=m) for m in places or [pltpu.VMEM] * len(outs)
        ],
        scratch_shapes=scratch,
        compiler_params=pltpu.CompilerParams(
            collective_id=number, has_side_effects=True, vmem_limit_bytes=62 << 20
        ),
    )


def shards(
    n,
    pat,
    inputs,
    lengths,
    gain_one,
    shift_one,
    w_query,
    b_query,
    w_key,
    w_value,
    b_value,
    w_out,
    b_out,
    gain_two,
    shift_two,
    w_up,
    b_up,
    w_down,
    b_down,
    d_output,
):
    batches, shard, width = inputs.shape
    cols = w_query.shape[1]
    heads = cols // HD
    units = batches * heads
    chips = n // 2
    half = shard // 2
    quarter = shard // pat
    levels = 1
    while SPAN1 << (levels - 1) < n:
        levels += 1
    perm = jnp.asarray(perm_matrix(shard), BF)
    permt = jnp.asarray(perm_matrix(shard).T, BF)
    qext = jnp.asarray(query_ext(shard), BF)
    ktab = jnp.asarray(key_tables(shard, heads * pat, levels))
    row = lambda v: v.reshape(1, -1)
    by_head = lambda w: w.reshape(w.shape[0], heads, HD)
    pack = lambda a, b: jnp.concatenate([by_head(a), by_head(b)], 2).reshape(a.shape[0], 2 * cols)
    wq = pack(w_query, jnp.zeros_like(w_query))
    wkv = pack(w_key, w_value)
    bq = pack(row(b_query), jnp.zeros((1, cols), F32))
    bkv = pack(jnp.zeros((1, cols), F32), row(b_value))
    vm, sm, anyv = pltpu.VMEM, pltpu.SMEM, pl.ANY
    dma = pltpu.SemaphoreType.DMA
    tiles = units // 2

    xp, n1, qp, kvd, kvt, attf, wofp, attw, den, tab = call(
        functools.partial(forward_kernel, n, pat, levels),
        "attention_forward",
        [
            ((batches, shard, width), BF),
            ((batches, shard, width), BF),
            ((units, shard, 128), BF),
            ((units, SPAN1 * shard, 128), BF),
            ((units, n * half, 128), BF),
            ((pat, tiles, shard, 128), BF),
            ((pat, cols + 2 * HD, width), BF),
            ((tiles, shard, 128), F32),
            ((tiles, shard, 128), F32),
            ((heads, levels, shard, 128), BF),
        ],
        [
            pltpu.VMEM((units, shard, 128), F32),
            dma((heads,)),
            dma((pat - 1,)),
            dma((pat - 1,)),
            dma((tiles, pat - 1)),
            dma((tiles, pat - 1)),
        ]
        + dense_sems(batches)
        + thin_sems(batches, chips),
        [sm] + [vm] * 10 + [anyv],
        0,
    )(lengths, inputs, row(gain_one), row(shift_one), wq, bq, wkv, bkv, w_out, perm, qext, ktab)

    gud, fd, dsf, dst, sto, vecs = call(
        functools.partial(middle_kernel, n, pat),
        "feed_forward",
        [
            ((2 * width, width), BF),
            ((batches, shard, width), BF),
            ((batches, shard, width), BF),
            ((batches, quarter, width), F32),
            ((batches, quarter, width), F32),
            ((8, width), F32),
        ],
        [
            pltpu.VMEM((batches, shard, width), F32),
            pltpu.VMEM((batches, shard, width), BF),
            pltpu.VMEM((batches, shard, width), BF),
            pltpu.VMEM((batches, shard, width), BF),
            pltpu.VMEM((batches, shard, width), BF),
            pltpu.VMEM((batches, pat, quarter, width), BF),
            pltpu.VMEM((batches, quarter, width), F32),
            pltpu.VMEM((batches, pat - 1, quarter, width), BF),
        ]
        + [dma((batches, pat - 1))] * 4,
        [vm] * 11,
        1,
    )(
        xp,
        attf,
        wofp,
        row(b_out),
        row(gain_two),
        row(shift_two),
        w_up,
        row(b_up),
        w_down,
        d_output,
        perm,
    )

    dq, dkv, gout, outputs = call(
        functools.partial(backward_kernel, n, pat, levels),
        "attention_backward",
        [
            ((batches, shard, 2 * cols), BF),
            ((batches, shard, 2 * cols), BF),
            ((cols, width), BF),
            ((batches, shard, width), BF),
        ],
        [
            pltpu.VMEM((units, SPAN1 * shard, 128), BF),
            pltpu.VMEM((units, n * half, 128), BF),
            pltpu.VMEM((SPAN1, 8, shard), F32),
            pltpu.VMEM((n, 8, half), F32),
            pltpu.VMEM((units, shard, 128), BF),
            pltpu.VMEM((units, shard, 128), F32),
            pltpu.VMEM((units, shard, 128), F32),
            pltpu.VMEM((batches, pat - 1, quarter, width), BF),
            pltpu.VMEM((batches, shard, width), BF),
        ]
        + [dma((batches, pat - 1))] * 4
        + dense_sems(batches)
        + thin_sems(batches, chips)
        + [dma((3,))] * 2
        + [dma((chips,))] * 4,
        [sm] + [vm] * 14,
        2,
    )(lengths, dsf, wofp, attf, attw, den, qp, kvd, kvt, tab, qext, fd, sto, row(b_down), permt)

    rows = 2 * width + 4 * cols
    grad_inputs, vout, grads = call(
        functools.partial(tail_kernel, n, pat),
        "input_gradient",
        [
            ((batches, shard, width), BF),
            ((16, width), F32),
            ((rows, width), F32),
        ],
        [
            pltpu.VMEM((batches, pat, quarter, width), BF),
            pltpu.VMEM((batches, pat - 1, quarter, width), BF),
            pltpu.VMEM((batches, shard, width), BF),
            pltpu.VMEM((8, width), F32),
            pltpu.VMEM((pat - 1, 8, width), F32),
        ]
        + [dma((batches, pat - 1))] * 4
        + [dma((pat - 1,))] * 2,
        [vm] * 12,
        3,
    )(xp, n1, dq, dkv, wq, wkv, row(gain_one), dst, vecs, gud, gout, permt)
    vout, grads = lax.psum((vout, grads), "seq")
    base = 2 * width
    g_q, g_k, g_v, g_out = [grads[base + i * cols : base + (i + 1) * cols] for i in range(4)]
    q_row = vout[8, : 2 * cols].reshape(heads, 2, HD)
    v_row = vout[9, : 2 * cols].reshape(heads, 2, HD)
    return (
        outputs,
        grad_inputs,
        vout[0],
        vout[1],
        g_q.T,
        q_row[:, 0].reshape(cols),
        g_k.T,
        g_v.T,
        v_row[:, 1].reshape(cols),
        g_out,
        vout[2],
        vout[3],
        vout[4],
        grads[:width],
        vout[5],
        grads[width:base],
        vout[6],
    )


class LineGather:
    def __init__(self, place, block, send, recv):
        self.p, self.block, self.send, self.recv = place, block, send, recv

    def copy(self, frm, to, sem):
        return remote(
            self.block(frm, self.p.z),
            self.block(frm, to),
            self.send.at[sem],
            self.recv.at[frm],
            (to, self.p.s),
        )

    def got(self, frm):
        here = self.block(frm, self.p.z)
        to = lax.rem(self.p.z + 1, self.p.pat)
        return remote(here, here, self.send.at[0], self.recv.at[frm], (to, self.p.s))

    def direct(self, fn):
        last = self.p.pat - 1
        for z in range(self.p.pat):

            def own(z=z):
                for to in sorted(range(last + 1), key=lambda t: -abs(t - z)):
                    if 0 < abs(to - z) < last:
                        fn(self.copy(z, to, to))

            when(self.p.z == z, own)

    def handed(self, fn):
        last = self.p.pat - 1
        when(self.p.z == last - 1, lambda: fn(0, self.copy(0, last, last + 1)))
        when(self.p.z == 1, lambda: fn(last, self.copy(last, 0, last + 1)))

    def start(self):
        self.direct(lambda copy: copy.start())

    def forward(self):
        def hand(frm, copy):
            self.got(frm).wait_recv()
            copy.start()

        self.handed(hand)

    def arrive(self):
        last = self.p.pat - 1
        for z in range(last + 1):

            def rest(z=z):
                for frm in range(last + 1):
                    if frm != z and (z, frm) not in ((1, last), (last - 1, 0)):
                        self.got(frm).wait_recv()

            when(self.p.z == z, rest)

    def finish(self):
        self.direct(lambda copy: copy.wait_send())
        self.handed(lambda frm, copy: copy.wait_send())


class LineChain:
    def __init__(self, place, block, send, recv):
        self.p, self.block, self.send, self.recv = place, block, send, recv

    def copy(self, frm, up):
        p = self.p
        to = jnp.clip(p.z + (1 if up else -1), 0, p.pat - 1)
        return remote(
            self.block(frm),
            self.block(frm),
            self.send.at[0 if up else 1, frm],
            self.recv.at[frm],
            (to, p.s),
        )

    def start(self):
        p = self.p
        when(p.z < p.pat - 1, lambda: self.copy(p.z, True).start())
        when(p.z > 0, lambda: self.copy(p.z, False).start())

    def inner(self, hop):
        for z in range(1, self.p.pat - 1):
            if z - hop >= 0:
                yield z, z - hop, True
            if z + hop < self.p.pat:
                yield z, z + hop, False

    def got(self, frm):
        p = self.p
        here = self.block(frm)
        to = lax.rem(p.z + 1, p.pat)
        return remote(here, here, self.send.at[0, 0], self.recv.at[frm], (to, p.s))

    def forward(self, hop):
        for z, frm, up in self.inner(hop):

            def hand(frm=frm, up=up):
                self.got(frm).wait_recv()
                self.copy(frm, up).start()

            when(self.p.z == z, hand)

    def arrive(self):
        last = self.p.pat - 1
        for frm in range(self.p.pat):
            if frm > 0:
                when(self.p.z == 0, lambda frm=frm: self.got(frm).wait_recv())
            if frm < last:
                when(self.p.z == last, lambda frm=frm: self.got(frm).wait_recv())

    def finish(self):
        p = self.p
        when(p.z < p.pat - 1, lambda: self.copy(p.z, True).wait_send())
        when(p.z > 0, lambda: self.copy(p.z, False).wait_send())
        for hop in range(1, p.pat - 1):
            for z, frm, up in self.inner(hop):
                when(p.z == z, lambda frm=frm, up=up: self.copy(frm, up).wait_send())


class LineSum:
    def __init__(self, place, part, buf, send, recv):
        self.p, self.part, self.buf, self.send, self.recv = place, part, buf, send, recv

    def copy(self, z, t):
        to = z + 1 if t > z else z - 1
        at = t if (t > z or t < to) else self.p.pat
        return remote(
            self.part(t), self.buf.at[at], self.send.at[t], self.recv.at[at], (to, self.p.s)
        )

    def got(self, at):
        here = self.buf.at[at]
        to = lax.rem(self.p.z + 1, self.p.pat)
        return remote(here, here, self.send.at[0], self.recv.at[at], (to, self.p.s))

    def start(self):
        last = self.p.pat - 1

        def up():
            for t in range(last, 0, -1):
                self.copy(0, t).start()

        def down():
            for t in range(last):
                self.copy(last, t).start()

        when(self.p.z == 0, up)
        when(self.p.z == last, down)

    def inner(self, hop):
        last = self.p.pat - 1
        for z in range(1, last):
            if z == hop:
                for t in range(last, z, -1):
                    yield z, t
            if last - z == hop:
                for t in range(z):
                    yield z, t

    def forward(self, hop):
        for z, t in self.inner(hop):

            def add(z=z, t=t):
                self.got(t).wait_recv()
                part = self.part(t)
                part[...] = (part[...].astype(F32) + self.buf[t].astype(F32)).astype(BF)
                self.copy(z, t).start()

            when(self.p.z == z, add)

    def total(self, out):
        p = self.p
        out[...] = self.part(p.z)[...].astype(F32)

        def below():
            self.got(p.z).wait_recv()
            out[...] += self.buf[p.z].astype(F32)

        def above():
            self.got(p.pat).wait_recv()
            out[...] += self.buf[p.pat].astype(F32)

        when(p.z > 0, below)
        when(p.z < p.pat - 1, above)

    def finish(self):
        last = self.p.pat - 1
        for t in range(last, 0, -1):
            when(self.p.z == 0, lambda t=t: self.copy(0, t).wait_send())
        for t in range(last):
            when(self.p.z == last, lambda t=t: self.copy(last, t).wait_send())
        for hop in range(1, last):
            for z, t in self.inner(hop):
                when(self.p.z == z, lambda z=z, t=t: self.copy(z, t).wait_send())


class PlaneGather:
    def __init__(self, place, piece, sems):
        self.p, self.piece, self.sems = place, piece, sems
        self.chips = place.n // 2

    def direct(self, k, owner):
        p, sems = self.p, self.sems
        to = lax.rem(p.s + 2 * k, p.n)
        return remote(
            self.piece(owner), self.piece(owner), sems[0].at[k - 1], sems[1].at[k - 1], (p.z, to)
        )

    def hand(self, k, owner):
        p, sems = self.p, self.sems
        return remote(
            self.piece(owner), self.piece(owner), sems[2].at[k], sems[3].at[k], (p.z, p.sib)
        )

    def source(self, base, k):
        return lax.rem(base + self.p.n - 2 * k, self.p.n)

    def start(self):
        for k in range(1, self.chips):
            self.direct(k, self.p.s).start()
        self.hand(0, self.p.s).start()

    def pass_on(self):
        for k in range(1, self.chips):
            owner = self.source(self.p.s, k)
            self.direct(k, owner).wait_recv()
            self.hand(k, owner).start()

    def arrive(self):
        for k in range(self.chips):
            self.hand(k, self.source(self.p.sib, k)).wait_recv()

    def finish(self):
        for k in range(1, self.chips):
            self.direct(k, self.p.s).wait_send()
        for k in range(self.chips):
            self.hand(k, self.source(self.p.s, k)).wait_send()


def line_sems(pat):
    return [pltpu.SemaphoreType.DMA((pat + 1,)), pltpu.SemaphoreType.DMA((pat,))]


def chain_sems(pat):
    return [pltpu.SemaphoreType.DMA((2, pat)), pltpu.SemaphoreType.DMA((pat,))]


def sum_sems(pat):
    return [pltpu.SemaphoreType.DMA((pat,)), pltpu.SemaphoreType.DMA((pat + 1,))]


def plane_sems(chips):
    return [pltpu.SemaphoreType.DMA((chips - 1,))] * 2 + [pltpu.SemaphoreType.DMA((chips,))] * 2


def vec_row(ref):
    return ref[...].reshape(1, -1)


def norm_rows(values, gain, shift):
    mean = jnp.mean(values, -1, keepdims=True)
    cen = values - mean
    var = jnp.mean(cen * cen, -1, keepdims=True)
    return cen * lax.rsqrt(var + EPS) * gain + shift


def norm_back(values, grad, gain):
    mean = jnp.mean(values, -1, keepdims=True)
    cen = values - mean
    inv = lax.rsqrt(jnp.mean(cen * cen, -1, keepdims=True) + EPS)
    hat = cen * inv
    dhat = grad * gain
    back = inv * (
        dhat - jnp.mean(dhat, -1, keepdims=True) - hat * jnp.mean(dhat * hat, -1, keepdims=True)
    )
    return (
        back,
        jnp.sum(grad * hat, 0, keepdims=True),
        jnp.sum(grad, 0, keepdims=True),
    )


def live_bias(first, second, base, length, shard):
    ok = jnp.logical_or(
        jnp.logical_and(second < first, second + base < length), second == first
    )
    return jnp.where(ok, 0.0, NEG)


class TreeSum:
    def __init__(self, place, grad, out, bufs, send, recv, keep=False, size=None):
        self.p, self.grad, self.out, self.send, self.recv = place, grad, out, send, recv
        self.keep = keep
        p = place
        bit_x = lax.rem(lax.div(p.s, 2), 2)
        bit_y = lax.div(p.s, 4)
        to_x = p.s + 2 - 4 * bit_x
        to_y = p.s + 4 - 8 * bit_y
        first = p.core == 0
        self.bits = [p.core, jnp.where(first, bit_x, bit_y), jnp.where(first, bit_y, bit_x)]
        self.to = [p.sib, jnp.where(first, to_x, to_y), jnp.where(first, to_y, to_x)]
        self.bufs = bufs
        self.off, self.size = [jnp.int32(0)], [size or grad.shape[0]]
        for d in range(3):
            h = self.size[d] // 2
            self.off.append(self.off[d] + self.bits[d] * h)
            self.size.append(h)

    def half_of(self, d, bit):
        h = self.size[d] // 2
        return rows_of(self.off[d] + bit * h, h)

    def red(self, d):
        src = self.grad.at[self.half_of(d, 1 - self.bits[d]), :]
        return remote(
            src, self.bufs[d], self.send.at[d], self.recv.at[d], (self.p.z, self.to[d])
        )

    def back(self, d, got):
        rows = self.half_of(d, (1 - self.bits[d]) if got else self.bits[d])
        return remote(
            self.out.at[rows, :],
            self.out.at[rows, :],
            self.send.at[3 + d],
            self.recv.at[3 + d],
            (self.p.z, self.to[d]),
        )

    def step(self, d):
        if d == 0:
            self.red(0).start()
        elif d <= 3:
            self.red(d - 1).wait_recv()
            rows = rows_of(self.off[d], self.size[d])
            total = self.grad[rows, :].astype(F32) + self.bufs[d - 1][...].astype(F32)
            if d < 3:
                self.grad[rows, :] = total.astype(BF)
                self.red(d).start()
            elif self.keep:
                self.out[...] = total.astype(BF)
            else:
                self.out[rows, :] = total.astype(BF)
                self.back(2, False).start()
        else:
            self.back(6 - d, True).wait_recv()
            if d < 6:
                self.back(5 - d, False).start()

    def finish(self):
        for d in range(3):
            self.red(d).wait_send()
            if not self.keep:
                self.back(d, False).wait_send()


def layer_kernel(
    n,
    pat,
    levels,
    lens,
    gain1,
    shift1,
    bq,
    bv,
    bout,
    gain2,
    shift2,
    bup,
    bdown,
    wq_hbm,
    wk_hbm,
    wv_hbm,
    wout_hbm,
    perm_hbm,
    qext_hbm,
    ktab,
    x_hbm,
    wup_hbm,
    wdown_hbm,
    dout_hbm,
    outf_hbm,
    gif_hbm,
    gsum1_hbm,
    gsum2_hbm,
    gout_hbm,
    vout,
    perm,
    qext,
    outf,
    gif,
    gsum1,
    gsum2,
    gout,
    grad1,
    xp,
    n1,
    wp,
    qp,
    kvd,
    kvt,
    tab,
    acc,
    ack,
    wqo,
    wko,
    attf,
    attu,
    attw,
    den,
    wor,
    wup,
    wdown,
    sto,
    n2,
    act,
    dop,
    dh,
    dns,
    dnr,
    tot,
    dsl,
    dst,
    dab,
    dat,
    fd,
    fdr,
    qud,
    qut,
    crd,
    crt,
    uext,
    dmr,
    a1,
    a2,
    a3,
    b1,
    b2,
    b3,
    c1,
    c2,
    c3,
    pz,
    pr,
    vecs,
    vz,
    vs,
    *sems,
):
    batches, shard, width = xp.shape
    half = shard // 2
    quarter = shard // pat
    cols = wout_hbm.shape[0]
    heads = cols // HD
    units = batches * heads
    tiles = units // 2
    chips = n // 2
    grad2, grad3 = n2, act
    both = lambda b: slice(b * shard, (b + 1) * shard)
    sems = list(sems)
    take = lambda count: [sems.pop(0) for _ in range(count)]
    p = Place(n, pat)
    bar, greeted = p.greet(True, False, True)
    low, high = lane_masks()

    own_slot = pat - 1
    pairs = [(perm_hbm, perm), (x_hbm.at[0], xp.at[0])]
    for i in range(heads):
        for off, src in ((0, wk_hbm), (HD, wv_hbm)):
            pairs.append((src.at[i * HD : (i + 1) * HD, :], wp.at[pl.ds(i * 128 + off, HD), :]))
    pairs.append((wq_hbm, wp.at[pl.ds(2 * cols, cols), :]))
    at_x = len(pairs)
    pairs += [(x_hbm.at[b], xp.at[b]) for b in range(1, batches)]
    at_out = len(pairs)
    pairs += [(wout_hbm, wor.at[own_slot, pl.ds(0, cols), :])]
    at_tab = len(pairs)
    pairs += [(ktab.at[heads * p.z + i], tab.at[i]) for i in range(heads)] + [(qext_hbm, qext)]
    at_late = len(pairs)
    pairs += [(dout_hbm, dop), (wup_hbm, wup), (wdown_hbm, wdown)]
    load_sem, save_sem = take(2)
    loads = [
        pltpu.make_async_copy(src, dst, load_sem.at[i]) for i, (src, dst) in enumerate(pairs)
    ]
    for copy in loads[:at_x]:
        copy.start()
    saves = [
        pltpu.make_async_copy(src, dst, save_sem.at[i])
        for i, (src, dst) in enumerate(
            (
                (gsum1, gsum1_hbm),
                (outf, outf_hbm),
                (gsum2, gsum2_hbm),
                (gif, gif_hbm),
                (gout, gout_hbm),
            )
        )
    ]

    slot = lambda frm, at: lax.rem(frm - at + 2 * pat - 1, pat)
    out_rows, out_cols = cols // chips, width // 2

    def out_piece(dev, slots):
        chip, core = lax.div(dev, 2), lax.rem(dev, 2)
        return wor.at[
            slots,
            rows_of(chip * out_rows, out_rows),
            pl.ds(pl.multiple_of(core * out_cols, 128), out_cols),
        ]

    def quarters(ref, b):
        return lambda f, *_: ref.at[b, rows_of(f * quarter, quarter), :]

    parity = [lax.rem(heads * p.z + i, 2) for i in range(heads)]

    def share_pair(forward, dense, thin):
        out = []
        sems = take(6)
        for b in range(batches):
            out.append(
                Shares(
                    p,
                    shard,
                    forward,
                    lambda at, b=b: dense.at[
                        pl.ds(heads * b, heads), rows_of(at * shard, shard), :
                    ],
                    lambda dev, b=b: thin.at[pl.ds(heads * b, heads), rows_of(dev * half, half), :],
                    [sem.at[b] for sem in sems[:2]],
                    [sem.at[b] for sem in sems[2:]],
                )
            )
        return out

    rows = range(batches)
    kv_shares = share_pair(True, kvd, kvt)
    qu_shares = share_pair(False, qud, qut)
    cor_sems = take(6)
    cors = [
        Shares(
            p,
            shard,
            False,
            lambda at, b=b: crd.at[b, at],
            lambda dev, b=b: crt.at[b, dev],
            [sem.at[b] for sem in cor_sems[:2]],
            [sem.at[b] for sem in cor_sems[2:]],
        )
        for b in rows
    ]
    wo_line = LineGather(p, lambda f, t: out_piece(p.s, slot(f, t)), *take(2))
    wo_plane = PlaneGather(p, lambda dev: out_piece(dev, pl.ds(0, pat - 1)), take(4))
    att_line = [LineGather(p, lambda f, at, b=b: attf.at[f, b], *take(2)) for b in rows]
    dn_sum = [LineSum(p, lambda t, b=b: dns.at[b, t], dnr.at[b], *take(2)) for b in rows]
    da_send, da_recv = take(2)
    da_spread = [Spread(p, da_send.at[b], da_recv.at[b]) for b in rows]
    fd_sum = [LineSum(p, quarters(fd, b), fdr.at[b], *take(2)) for b in rows]
    out_line = [LineChain(p, quarters(outf, b), *take(2)) for b in rows]
    dm_sum = [LineSum(p, lambda t, b=b: dns.at[b, t], dmr.at[b], *take(2)) for b in rows]
    dqk = dh
    gi_line = [LineChain(p, quarters(gif, b), *take(2)) for b in rows]
    sum1 = TreeSum(p, grad1, gsum1, (a1, a2, a3), *take(2))
    sum2 = TreeSum(p, grad2, gsum2, (b1, b2, b3), *take(2), size=wp.shape[0])
    sum3 = TreeSum(p, grad3, pz, (c1, c2, c3), *take(2), keep=True)
    p_send, p_recv, w_send, w_recv = take(4)
    z_send, z_recv, v_send, v_recv = take(4)
    zsp = Spread(p, z_send, z_recv)

    for r in range(pat):
        wor[r, cols : cols + HD, :] = jnp.zeros((HD, width), BF)
    wp[3 * cols :, :] = jnp.zeros((wp.shape[0] - 3 * cols, width), BF)
    zero_bias = jnp.zeros((1, HD), F32)
    bias_v, bias_q = vec_row(bv), vec_row(bq)
    bias = []
    for i in range(heads):
        bias += [zero_bias, bias_v[:, i * HD : (i + 1) * HD]]
    bias = jnp.concatenate(bias + [bias_q, zero_bias], 1)

    own = rows_of(p.pos * shard, shard)
    zrows = rows_of(p.z * quarter, quarter)
    lane = lax.broadcasted_iota(jnp.int32, (shard, 128), 1)
    for b in rows:
        if b == 0:
            for copy in loads[at_x:at_late]:
                copy.start()
            for copy in loads[:at_x]:
                copy.wait()
        else:
            loads[at_x + b - 1].wait()
        xb = nn(perm[...], xp[b])
        xp[b] = xb.astype(BF)
        n1[b] = norm_rows(xb, vec_row(gain1), vec_row(shift1)).astype(BF)
        qkv = nt(n1[b], wp[...]) + bias
        for i in range(heads):
            kv = qkv[:, i * 128 : (i + 1) * 128].astype(BF)
            kvd[heads * b + i, own, :] = kv
            t = heads + i // 2
            q = qkv[:, t * 128 : (t + 1) * 128]
            if i % 2 == 1:
                q = pltpu.roll(q, HD, 1)
            q = jnp.where(lane < HD, q, 0.0).astype(BF) * jnp.asarray(HD**-0.5, BF)
            qp[heads * b + i] = q
        for i in range(heads):
            kvt[heads * b + i, rows_of(p.s * half, half), :] = kvd[
                heads * b + i, rows_of(p.pos * shard + parity[i] * half, half), :
            ]
        if b == 0:
            pl.semaphore_wait(bar, greeted)
        if b == 0:
            kv_shares[b].start()
            loads[at_out].wait()
            wo_line.start()
            for copy in loads[at_late:]:
                copy.start()
    for copy in loads[at_tab:at_late]:
        copy.wait()

    def attend(qx, kv, ext, bias):
        s = nt(qx, jnp.concatenate([kv, ext], 1))
        if bias is not None:
            s = s + bias
        return nn(jnp.exp(s).astype(BF), kv * high + low)

    first = token_of(lax.broadcasted_iota(jnp.int32, (shard, shard), 0), shard)
    second = token_of(lax.broadcasted_iota(jnp.int32, (shard, shard), 1), shard)

    def attend_own(b):
        bias = live_bias(first, second, p.s * shard, lens[b], shard)
        for i in range(heads):
            u = heads * b + i
            kv = kvd[u, own, :]
            qx = jnp.concatenate([qp[u], qext[...]], 1)
            w = jnp.exp(nt(qx, jnp.concatenate([kv, tab[i, 0]], 1)) + bias).astype(BF)
            wqo[u] = w
            acc[u] = nn(w, kv * high + low)

    def weights_own(b):
        bias = live_bias(second, first, p.s * shard, lens[b], shard)
        for i in range(heads):
            u = heads * b + i
            qx = jnp.concatenate([qp[u], qext[...]], 1)
            kvx = jnp.concatenate([kvd[u, own, :], tab[i, 0]], 1)
            wko[u] = jnp.exp(nt(kvx, qx) + bias).astype(BF)

    def thin_keys(b, i, sg):
        level = level_of(sg, p.seg, levels)
        places = thin_positions(sg * SPAN1, parity[i], shard, SPAN1)
        lenl = length_lane(places, lens[b], SPAN1 * half)
        part = tab[i, level, rows_of(parity[i] * half, half), :]
        ext = jnp.concatenate([part] * SPAN1, 0) + lenl
        return kvt[heads * b + i, rows_of(sg * SPAN1 * half, SPAN1 * half), :], ext

    def attend_rest(b, which):
        def dense(j, carry):
            lenl = length_lane(dense_positions(p.seg * SPAN1 + j, shard), lens[b], shard)
            for i in which:
                u = heads * b + i
                qx = jnp.concatenate([qp[u], qext[...]], 1)
                kv = kvd[u, rows_of(j * shard, shard), :]
                acc[u] += attend(qx, kv, tab[i, 0] + lenl, None)
            return carry

        lax.fori_loop(0, p.pos, dense, 0)

        def thin(sg, carry):
            for i in which:
                u = heads * b + i
                mine = rows_of(parity[i] * half, half)
                kv, ext = thin_keys(b, i, sg)
                qx = jnp.concatenate([qp[u, mine, :], qext[mine, :]], 1)
                acc[u, mine, :] += attend(qx, kv, ext, None)
            return carry

        lax.fori_loop(0, p.seg, thin, 0)

    def send_att(b):
        first_unit = heads * b
        zero, one, two = acc[first_unit], acc[first_unit + 1], acc[first_unit + 2]
        num = jnp.where(lane < HD, pltpu.roll(zero, HD, 1), one)
        dn = jnp.where(lane < HD, zero, pltpu.roll(one, HD, 1))
        wide = num / dn
        den[b, 0] = dn
        attw[b, 0] = wide
        attf[p.z, b, 0:shard, :] = wide.astype(BF)
        dn = jnp.where(lane < HD, two, 1.0)
        wide = jnp.where(lane < HD, pltpu.roll(two, HD, 1), 0.0) / dn
        den[b, 1] = dn
        attw[b, 1] = wide
        packed = wide[0:half] + pltpu.roll(wide[half:shard], HD, 1)
        attf[p.z, b, shard : shard + half, :] = packed.astype(BF)
        att_line[b].start()

    attend_own(0)
    kv_shares[1].start()
    attend_own(1)
    wo_line.forward()
    bdown_sum = jnp.zeros((1, width), F32)
    loads[at_late].wait()
    for b in rows:
        dob = nn(perm[...], dop[b])
        dop[b] = dob.astype(BF)
        bdown_sum = bdown_sum + jnp.sum(dob, 0, keepdims=True)
    weights_own(0)
    weights_own(1)
    kv_shares[0].pass_on()
    wo_line.arrive()
    wo_plane.start()
    kv_shares[0].arrive()
    attend_rest(0, range(heads))
    send_att(0)
    kv_shares[1].pass_on()
    kv_shares[1].arrive()
    attend_rest(1, range(0, 1))
    att_line[0].forward()
    attend_rest(1, range(1, heads))
    send_att(1)
    wo_plane.pass_on()
    for copy in loads[at_late + 1 :]:
        copy.wait()
    wo_plane.arrive()

    def feed_in(b):
        parts = []
        for r in range(pat):
            z = lax.rem(p.z + 1 + r, pat)
            packed = attf[z, b, shard : shard + half, :]
            attu[z, b, 0:half, :] = packed
            attu[z, b, half:shard, :] = pltpu.roll(packed.astype(F32), HD, 1).astype(BF)
            parts += [attf[z, b, 0:shard, :], attu[z, b]]
        weight = wor[...].reshape(-1, width)
        mixed = nn(jnp.concatenate(parts, 1), weight) + xp[b].astype(F32) + vec_row(bout)
        for t in range(width // 128):
            lanes = slice(t * 128, (t + 1) * 128)
            ack[t] = mixed[:, lanes]
            sto[b, :, lanes] = ack[t, zrows, :]
        n2[both(b), :] = norm_rows(mixed, vec_row(gain2), vec_row(shift2)).astype(BF)

    def feed_out(b):
        hid = nn(n2[both(b), :], wup[...]) + vec_row(bup)
        th = jnp.tanh(ROOT * (hid + 0.044715 * (hid * hid * hid)))
        act[both(b), :] = (0.5 * hid * (1.0 + th)).astype(BF)
        slope = 0.5 * (1.0 + th) + 0.5 * hid * (1.0 - th * th) * (
            ROOT * (1.0 + 3.0 * 0.044715 * hid * hid)
        )
        dhid = (nt(dop[b], wdown[...]) * slope).astype(BF)
        dh[b] = dhid
        dn = nt(dhid, wup[...])
        for t in range(pat):
            dns[b, t] = dn[t * quarter : (t + 1) * quarter].astype(BF)
        dn_sum[b].start()
        return jnp.sum(dhid.astype(F32), 0, keepdims=True)

    att_line[0].arrive()
    feed_in(0)
    bup_sum = feed_out(0)
    att_line[1].forward()
    att_line[1].arrive()
    feed_in(1)
    dn_sum[0].forward(1)
    bup_sum = bup_sum + feed_out(1)
    fd[0] = nn(act[both(0), :], wdown[...]).astype(BF)
    dn_sum[0].forward(2)
    up = tn(n2[both(0), :], dh[0])
    for b in range(1, batches):
        up = up + tn(n2[both(b), :], dh[b])
    grad1[0:width, :] = up.astype(BF)
    dn_sum[1].forward(1)
    down = tn(act[both(0), :], dop[0])
    for b in range(1, batches):
        down = down + tn(act[both(b), :], dop[b])
    grad1[width : 2 * width, :] = down.astype(BF)
    sum1.step(0)
    bout_sum = jnp.zeros((1, width), F32)
    gain_sum = jnp.zeros((1, width), F32)
    shift_sum = jnp.zeros((1, width), F32)

    def head_grads(b, r):
        wide = nt(dsl[b], wor[r]).astype(BF)
        return jnp.stack([wide[:, 0:128], wide[:, 128:256]])

    def da_copy(b, k, frm=None):
        at = p.z if frm is None else frm
        return da_spread[b].copy_to(
            k, dab.at[b, k - 1], dat.at[b, :, rows_of(at * quarter, quarter), :]
        )

    def da_arrive(b):
        for k in range(1, pat):
            da_copy(b, k, lax.rem(p.z + pat - k, pat)).wait_recv()

    def state_grad(b, sums):
        dn_sum[b].total(tot)
        back, more_gain, more_shift = norm_back(sto[b], tot[...], vec_row(gain2))
        ds = dop[b, zrows, :].astype(F32) + back
        dst[b] = ds
        dsl[b] = ds.astype(BF)
        for k in range(1, pat):
            dab[b, k - 1] = head_grads(b, k - 1)
            da_copy(b, k).start()
        dat[b, :, zrows, :] = head_grads(b, own_slot)
        return (
            sums[0] + jnp.sum(ds, 0, keepdims=True),
            sums[1] + more_gain,
            sums[2] + more_shift,
        )

    sums = state_grad(0, (bout_sum, gain_sum, shift_sum))
    fd_sum[0].start()
    fd[1] = nn(act[both(1), :], wdown[...]).astype(BF)
    dn_sum[1].forward(2)
    sum1.step(1)
    sums = state_grad(1, sums)
    fd_sum[1].start()
    fd_sum[0].forward(1)
    vecs[...] = jnp.zeros(vecs.shape, F32)
    for r, value in ((2, sums[0]), (3, sums[1]), (4, sums[2]), (5, bup_sum), (6, bdown_sum)):
        vecs[r : r + 1, :] = value

    row8 = lax.broadcasted_iota(jnp.int32, (8, 128), 0)
    lane8 = lax.broadcasted_iota(jnp.int32, (8, 128), 1)
    pick = jnp.where(row8 == lax.div(lane8, HD), 1.0, 0.0).astype(BF)
    ri = lax.broadcasted_iota(jnp.int32, (128, 128), 0)
    ci = lax.broadcasted_iota(jnp.int32, (128, 128), 1)
    same = jnp.where(lax.div(ri, HD) == lax.div(ci, HD), 1.0, 0.0).astype(BF)

    def upstream(b):
        crd[b, p.pos] = jnp.zeros(crd.shape[2:], F32)
        crt[b, p.s] = jnp.zeros(crt.shape[2:], F32)
        for side in range(2):
            datt = dat[b, side].astype(F32)
            dn = den[b, side]
            up = datt / dn
            prod = datt * attw[b, side] / dn
            lead = prod.astype(BF)
            rest = (prod - lead.astype(F32)).astype(BF)
            cor = nn(lead, same) + nn(rest, same)
            cor_rows = nt(pick, lead) + nt(pick, rest)
            for e in range(2):
                i = 2 * side + e
                if i >= heads:
                    continue
                u = heads * b + i
                part = up if e == 1 else pltpu.roll(up, HD, 1)
                qud[u, own, :] = jnp.where(lane < HD, qp[u].astype(F32), part).astype(BF)
                qut[u, rows_of(p.s * half, half), :] = qud[
                    u, rows_of(p.pos * shard + parity[i] * half, half), :
                ]
                cor_row = cor_rows[e : e + 1, :]
                crd[b, p.pos, i : i + 1, :] = cor_row
                col = -cor[:, e * HD : e * HD + 1]
                lead = col.astype(BF).astype(F32)
                uext[u] = (
                    jnp.where(lane == COR_LANE, lead, 0.0)
                    + jnp.where(lane == COR_LANE + 1, col - lead, 0.0)
                ).astype(BF)
                crt[b, p.s, i : i + 1, :] = jnp.where(
                    parity[i] == 0, cor_row[:, 0:half], cor_row[:, half:shard]
                )
        qu_shares[b].start()
        cors[b].start()

    def query_side(qu, qe, ue, kv, ext, bias):
        kvx = jnp.concatenate([kv, ext], 1)
        s = nt(jnp.concatenate([qu * low, qe], 1), kvx)
        if bias is not None:
            s = s + bias
        dp = nt(jnp.concatenate([qu * high, ue], 1), kvx)
        return nn((jnp.exp(s) * dp).astype(BF), kv)

    def key_side(qu, qe, cor, kv, ext, bias):
        s = nt(jnp.concatenate([kv, ext], 1), jnp.concatenate([qu * low, qe], 1))
        if bias is not None:
            s = s + bias
        w = jnp.exp(s)
        dp = nt(kv, qu * high) - cor
        return nn((w * dp).astype(BF), qu * low) + nn(w.astype(BF), qu * high)

    def grads_own(b):
        for i in range(heads):
            u = heads * b + i
            kv, qu = kvd[u, own, :], qud[u, own, :]
            kvx = jnp.concatenate([kv, tab[i, 0]], 1)
            dp = nt(jnp.concatenate([qu * high, uext[u]], 1), kvx)
            acc[u] = nn((wqo[u].astype(F32) * dp).astype(BF), kv)
            dp = nt(kv, qu * high) - crd[b, p.pos, i : i + 1, :]
            ds = (wko[u].astype(F32) * dp).astype(BF)
            ack[u] = nn(ds, qu * low) + nn(wko[u], qu * high)

    def query_rest(b):
        def dense(j, carry):
            lenl = length_lane(dense_positions(p.seg * SPAN1 + j, shard), lens[b], shard)
            for i in range(heads):
                u = heads * b + i
                kv = kvd[u, rows_of(j * shard, shard), :]
                acc[u] += query_side(
                    qud[u, own, :], qext[...], uext[u], kv, tab[i, 0] + lenl, None
                )
            return carry

        lax.fori_loop(0, p.pos, dense, 0)

        def thin(sg, carry):
            for i in range(heads):
                u = heads * b + i
                mine = rows_of(parity[i] * half, half)
                kv, ext = thin_keys(b, i, sg)
                qu = qut[u, rows_of(p.s * half, half), :]
                acc[u, mine, :] += query_side(qu, qext[mine, :], uext[u, mine, :], kv, ext, None)
            return carry

        lax.fori_loop(0, p.seg, thin, 0)

    def key_rest(b):
        lenl = length_lane(dense_positions(p.s, shard), lens[b], shard)

        def dense(j, carry):
            for i in range(heads):
                u = heads * b + i
                qu = qud[u, rows_of(j * shard, shard), :]
                ack[u] += key_side(
                    qu, qext[...], crd[b, j, i : i + 1, :], kvd[u, own, :], tab[i, 0] + lenl, None
                )
            return carry

        lax.fori_loop(p.pos + 1, SPAN1, dense, 0)

        def thin(sg, carry):
            level = level_of(sg, p.seg, levels)
            for i in range(heads):
                u = heads * b + i
                mine = rows_of(parity[i] * half, half)
                ext = tab[i, level, mine, :] + length_lane(
                    thin_positions(p.s, parity[i], shard, 1), lens[b], half
                )
                kv = kvt[u, rows_of(p.s * half, half), :]
                qu = qut[u, rows_of(sg * SPAN1 * half, SPAN1 * half), :]
                qe = jnp.concatenate([qext[mine, :]] * SPAN1, 0)
                cor = jnp.concatenate(
                    [crt[b, sg * SPAN1 + d, i : i + 1, :] for d in range(SPAN1)], 1
                )
                ack[u, mine, :] += key_side(qu, qe, cor, kv, ext, None)
            return carry

        lax.fori_loop(p.seg + 1, n // SPAN1, thin, 0)

    def send_grads(b):
        dn_sum[b].finish()
        for i in range(heads):
            dqk[b, :, i * 128 : (i + 1) * 128] = ack[heads * b + i].astype(BF)
        for t in range((heads + 1) // 2):
            tile = acc[heads * b + 2 * t]
            if 2 * t + 1 < heads:
                other = pltpu.roll(acc[heads * b + 2 * t + 1], HD, 1)
            else:
                other = jnp.zeros((shard, 128), F32)
            tile = jnp.where(lane < HD, tile, other) * HD**-0.5
            at = (heads + t) * 128
            dqk[b, :, at : at + 128] = tile.astype(BF)
        dm = nn(dqk[b, :, 0 : wp.shape[0]], wp[...])
        for t in range(pat):
            dns[b, t] = dm[t * quarter : (t + 1) * quarter].astype(BF)
        dm_sum[b].start()

    def output(b):
        fd_sum[b].total(tot)
        outf[b, zrows, :] = (sto[b] + tot[...] + vec_row(bdown)).astype(BF)
        out_line[b].start()

    da_arrive(0)
    upstream(0)
    for z in range(pat):
        part = jnp.zeros((256, width), F32)
        for b in rows:
            pair = jnp.concatenate([attf[z, b, zrows, :], attu[z, b, zrows, :]], 1)
            part = part + tn(pair, dsl[b])
        grad3[z * cols : (z + 1) * cols, :] = part[0:cols].astype(BF)
    sum3.step(0)
    da_arrive(1)
    upstream(1)
    fd_sum[0].forward(2)
    grads_own(0)
    sum3.step(1)
    fd_sum[1].forward(1)
    output(0)
    grads_own(1)
    sum1.step(2)
    fd_sum[1].forward(2)
    cors[0].pass_on()
    qu_shares[0].pass_on()
    query_rest(0)
    out_line[0].forward(1)
    output(1)
    cors[0].arrive()
    qu_shares[0].arrive()
    key_rest(0)
    send_grads(0)
    out_line[0].forward(2)
    cors[1].pass_on()
    qu_shares[1].pass_on()
    query_rest(1)
    out_line[1].forward(1)
    cors[1].arrive()
    qu_shares[1].arrive()
    key_rest(1)
    send_grads(1)
    dm_sum[0].forward(1)
    out_line[1].forward(2)
    sum3.step(2)
    sum1.step(3)
    dm_sum[0].forward(2)
    sum3.step(3)
    owner = 2 * p.core + sum3.bits[1]
    ahead = lax.rem(owner - p.z + pat, pat)

    def piece_copy(at):
        return remote(pz, pr.at[at], p_send.at[0], p_recv.at[at], (owner, p.s))

    def piece_got(at):
        return remote(
            pr.at[at], pr.at[at], p_send.at[0], p_recv.at[at], (p.other_z(1), p.s)
        )

    when(ahead != 0, lambda: piece_copy(jnp.maximum(ahead - 1, 0)).start())

    packed = tn(dqk[0, :, 0 : 3 * cols], n1[0])
    for b in range(1, batches):
        packed = packed + tn(dqk[b, :, 0 : 3 * cols], n1[b])
    for i in range(heads):
        at = i * 128
        grad2[i * HD : (i + 1) * HD, :] = packed[at : at + HD].astype(BF)
        grad2[cols + i * HD : cols + (i + 1) * HD, :] = packed[at + HD : at + 128].astype(BF)
    grad2[2 * cols : 3 * cols, :] = packed[2 * cols : 3 * cols].astype(BF)
    grad2[3 * cols : wp.shape[0], :] = jnp.zeros((wp.shape[0] - 3 * cols, width), BF)
    sum2.step(0)

    def piece_rows(at):
        return gout.at[rows_of(at * (cols // 2), cols // 2), :]

    def piece_out(k):
        rows = piece_rows(sum3.bits[2])
        to = lax.rem(p.s + k, n)
        return remote(rows, rows, w_send.at[k - 1], w_recv.at[sum3.bits[2]], (p.z, to))

    def piece_in(at):
        rows = piece_rows(at)
        return remote(rows, rows, w_send.at[0], w_recv.at[at], (p.z, p.sib))

    def own_piece():
        total = pz[...].astype(F32)
        for at in range(pat - 1):
            piece_got(at).wait_recv()
            total = total + pr[at].astype(F32)
        piece_rows(sum3.bits[2])[...] = total.astype(BF)
        for k in range(1, n):
            piece_out(k).start()

    dm_sum[1].forward(1)

    def close(b, sums):
        dm_sum[b].total(tot)
        back, more_gain, more_shift = norm_back(
            xp[b, zrows, :].astype(F32), tot[...], vec_row(gain1)
        )
        gif[b, zrows, :] = (dst[b] + back).astype(BF)
        return sums[0] + more_gain, sums[1] + more_shift

    zero = jnp.zeros((1, width), F32)
    sum2.step(1)
    sums = close(0, (zero, zero))
    gi_line[0].start()
    dm_sum[1].forward(2)
    sum2.step(2)
    sum1.step(4)
    gi_line[0].forward(1)
    when(ahead == 0, own_piece)
    qkv_sum = jnp.zeros((1, 3 * cols), F32)
    for b in rows:
        qkv_sum = qkv_sum + jnp.sum(dqk[b, :, 0 : 3 * cols].astype(F32), 0, keepdims=True)
    sums = close(1, sums)
    v0, v1 = vs.at[0], vs.at[1]
    v0[...] = vecs[...]
    v0[0:1, :] = sums[0]
    v0[1:2, :] = sums[1]
    for k in range(1, pat):
        zsp.copy_to(k, v0, vz.at[k - 1]).start()
    gi_line[1].start()
    sum2.step(3)
    gi_line[0].forward(2)
    gi_line[1].forward(1)
    sum2.step(4)
    sum1.step(5)
    gi_line[1].forward(2)
    for k in range(1, pat):
        zsp.copy_to(k, v0, vz.at[k - 1]).wait_recv()
    row = lax.broadcasted_iota(jnp.int32, (8, width), 0)
    extra = vz[0]
    for k in range(2, pat):
        extra = extra + vz[k - 1]
    v1[...] = v0[...] + jnp.where(row < 5, extra, 0.0)
    v1[7:8, 0 : 3 * cols] = qkv_sum

    def vec_copy(k):
        to = lax.rem(p.s + k, n)
        return remote(v1, vs.at[k + 1], v_send.at[k - 1], v_recv.at[k - 1], (p.z, to))

    for k in range(1, n):
        vec_copy(k).start()
    sum1.step(6)
    saves[0].start()
    sum2.step(5)
    for at in range(2):
        mine = jnp.logical_and(ahead == 0, sum3.bits[2] == at)
        when(jnp.logical_not(mine), lambda at=at: piece_in(at).wait_recv())
    saves[4].start()
    for k in range(1, n):
        vec_copy(k).wait_recv()
    allv = v1[...]
    for k in range(1, n):
        allv = allv + vs[k + 1]
    vout[...] = allv
    for b in rows:
        out_line[b].arrive()
    saves[1].start()
    sum2.step(6)
    saves[2].start()
    for b in rows:
        gi_line[b].arrive()
    saves[3].start()
    for copy in saves:
        copy.wait()
    when(ahead != 0, lambda: piece_copy(jnp.maximum(ahead - 1, 0)).wait_send())
    for k in range(1, n):
        when(ahead == 0, lambda k=k: piece_out(k).wait_send())
    for b in rows:
        for k in range(1, pat):
            da_copy(b, k).wait_send()
    sum3.finish()
    for item in [*kv_shares, *qu_shares, *cors, wo_line, wo_plane, *att_line]:
        item.finish()
    for item in [*fd_sum, *out_line, *dm_sum, *gi_line, sum1, sum2]:
        item.finish()
    for k in range(1, pat):
        zsp.copy_to(k, v0, vz.at[k - 1]).wait_send()
    for k in range(1, n):
        vec_copy(k).wait_send()


def finish_kernel(
    vin,
    permt_hbm,
    outf_hbm,
    gif_hbm,
    gsum1_hbm,
    gsum2_hbm,
    gsum3_hbm,
    gain1,
    shift1,
    bq,
    bv,
    bout,
    gain2,
    shift2,
    bup,
    bdown,
    outp_hbm,
    ginp_hbm,
    gup_hbm,
    gdown_hbm,
    gk_hbm,
    gv_hbm,
    gq_hbm,
    gout_hbm,
    permt,
    outf,
    gif,
    gsum1,
    gsum2,
    gsum3,
    outp,
    ginp,
    gup,
    gdown,
    gk,
    gv,
    gq,
    gout,
    load_sem,
    save_sem,
):
    batches = outf.shape[0]
    cols, width = gsum3.shape
    heads = cols // HD
    jobs = []

    def widen(src, dst):
        def run():
            dst[...] = src[...].astype(F32)

        return run

    def turn(src, dst):
        def run():
            dst[...] = nn(permt[...], src[...]).astype(BF)

        return run

    parts = 4
    for src_hbm, src, dst, dst_hbm in (
        (gsum1_hbm.at[0:width], gsum1.at[0:width], gup, gup_hbm),
        (gsum1_hbm.at[width : 2 * width], gsum1.at[width : 2 * width], gdown, gdown_hbm),
    ):
        step = width // parts
        for i in range(parts):
            rows = slice(i * step, (i + 1) * step)
            jobs.append(
                (src_hbm.at[rows], src.at[rows], widen(src.at[rows], dst.at[rows]), dst.at[rows], dst_hbm.at[rows])
            )
    for b in range(batches):
        for src_hbm, src, dst, dst_hbm in (
            (outf_hbm, outf, outp, outp_hbm),
            (gif_hbm, gif, ginp, ginp_hbm),
        ):
            jobs.append((src_hbm.at[b], src.at[b], turn(src.at[b], dst.at[b]), dst.at[b], dst_hbm.at[b]))
    for i, (dst, dst_hbm) in enumerate(((gk, gk_hbm), (gv, gv_hbm), (gq, gq_hbm))):
        rows = slice(i * cols, (i + 1) * cols)
        jobs.append((gsum2_hbm.at[rows], gsum2.at[rows], widen(gsum2.at[rows], dst), dst, dst_hbm))
    jobs.append((gsum3_hbm, gsum3, widen(gsum3, gout), gout, gout_hbm))

    loads = [
        pltpu.make_async_copy(job[0], job[1], load_sem.at[i]) for i, job in enumerate(jobs)
    ]
    perm_load = pltpu.make_async_copy(permt_hbm, permt, load_sem.at[len(jobs)])
    saves = [
        pltpu.make_async_copy(job[3], job[4], save_sem.at[i]) for i, job in enumerate(jobs)
    ]
    for i, copy in enumerate(loads):
        copy.start()
        if i == 0:
            perm_load.start()
    for r, ref in enumerate((gain1, shift1, bout, gain2, shift2, bup, bdown)):
        ref[...] = vin[r : r + 1, :].reshape(width)
    bq[...] = vin[7:8, 2 * cols : 3 * cols].reshape(cols)
    bv[...] = jnp.concatenate(
        [vin[7:8, i * 128 + HD : (i + 1) * 128] for i in range(heads)], 1
    ).reshape(cols)
    for i, job in enumerate(jobs):
        if i == 2 * parts:
            perm_load.wait()
        loads[i].wait()
        job[2]()
        saves[i].start()
    for copy in saves:
        copy.wait()


def plane_program(
    n,
    pat,
    inputs,
    lengths,
    gain_one,
    shift_one,
    w_query,
    b_query,
    w_key,
    w_value,
    b_value,
    w_out,
    b_out,
    gain_two,
    shift_two,
    w_up,
    b_up,
    w_down,
    b_down,
    d_output,
):
    B, S, W = inputs.shape
    cols = w_query.shape[1]
    hidden = w_up.shape[1]
    heads = cols // HD
    units = B * heads
    tiles = units // 2
    chips = n // 2
    half = S // 2
    quarter = S // pat
    levels = 1
    while SPAN1 << (levels - 1) < n:
        levels += 1
    perm = jnp.asarray(perm_matrix(S), BF)
    permt = jnp.asarray(perm_matrix(S).T, BF)
    qext = jnp.asarray(query_ext(S), BF)
    ktab = jnp.asarray(key_tables(S, heads * pat, levels))
    wide = 3 * cols + (-3 * cols) % 128
    assert hidden == W and pat * cols == B * S and units * 128 == W
    r1, r2 = 2 * W, wide
    vm, sm, anyv = pltpu.VMEM, pltpu.SMEM, pl.ANY
    dma = pltpu.SemaphoreType.DMA

    outf, gif, gsum1, gsum2, gout, vout = call(
        functools.partial(layer_kernel, n, pat, levels),
        "layer",
        [
            ((B, S, W), BF),
            ((B, S, W), BF),
            ((r1, W), BF),
            ((r2, W), BF),
            ((cols, W), BF),
            ((8, W), F32),
        ],
        [
            vm((S, S), BF),
            vm((S, 128), BF),
            vm((B, S, W), BF),
            vm((B, S, W), BF),
            vm((r1, W), BF),
            vm((r2, W), BF),
            vm((cols, W), BF),
            vm((r1, W), BF),
            vm((B, S, W), BF),
            vm((B, S, W), BF),
            vm((wide, W), BF),
            vm((units, S, 128), BF),
            vm((units, SPAN1 * S, 128), BF),
            vm((units, n * half, 128), BF),
            vm((heads, levels, S, 128), BF),
            vm((units, S, 128), F32),
            vm((units, S, 128), F32),
            vm((units, S, S), BF),
            vm((units, S, S), BF),
            vm((pat, B, S + half, 128), BF),
            vm((pat, B, S, 128), BF),
            vm((B, 2, S, 128), F32),
            vm((B, 2, S, 128), F32),
            vm((pat, cols + HD, W), BF),
            vm(w_up.shape, BF),
            vm(w_down.shape, BF),
            vm((B, quarter, W), F32),
            vm((B * S, W), BF),
            vm((B * S, hidden), BF),
            vm((B, S, W), BF),
            vm((B, S, hidden), BF),
            vm((B, pat, quarter, W), BF),
            vm((B, pat + 1, quarter, W), BF),
            vm((quarter, W), F32),
            vm((B, quarter, W), BF),
            vm((B, quarter, W), F32),
            vm((B, pat - 1, 2, quarter, 128), BF),
            vm((B, 2, S, 128), BF),
            vm((B, S, W), BF),
            vm((B, pat + 1, quarter, W), BF),
            vm((units, SPAN1 * S, 128), BF),
            vm((units, n * half, 128), BF),
            vm((B, SPAN1, 8, S), F32),
            vm((B, n, 8, half), F32),
            vm((units, S, 128), BF),
            vm((B, pat + 1, quarter, W), BF),
        ]
        + [vm((r1 >> d, W), BF) for d in (1, 2, 3)]
        + [vm((r2 >> d, W), BF) for d in (1, 2, 3)]
        + [vm((pat * cols >> d, W), BF) for d in (1, 2, 3)]
        + [vm((cols // 2, W), BF), vm((pat - 1, cols // 2, W), BF)]
        + [vm((8, W), F32), vm((pat - 1, 8, W), F32), vm((n + 1, 8, W), F32)]
        + [dma((3 * heads + B + 7,)), dma((5,))]
        + (dense_sems(B) + thin_sems(B, chips)) * 3
        + line_sems(pat)
        + plane_sems(chips)
        + line_sems(pat) * B
        + sum_sems(pat) * B
        + [dma((B, pat - 1))] * 2
        + sum_sems(pat) * B
        + chain_sems(pat) * B
        + sum_sems(pat) * B
        + chain_sems(pat) * B
        + [dma((6,))] * 6
        + [dma((1,)), dma((pat - 1,)), dma((n - 1,)), dma((2,))]
        + [dma((pat - 1,))] * 2
        + [dma((n - 1,))] * 2,
        [sm] + [vm] * 9 + [anyv] * 11,
        0,
        [anyv] * 5 + [vm],
    )(
        lengths,
        gain_one,
        shift_one,
        b_query,
        b_value,
        b_out,
        gain_two,
        shift_two,
        b_up,
        b_down,
        w_query.T,
        w_key.T,
        w_value.T,
        w_out,
        perm,
        qext,
        ktab,
        inputs,
        w_up,
        w_down,
        d_output,
    )

    small = [((size,), F32) for size in (W, W, cols, cols, W, W, W, W, W)]
    large = [((B, S, W), BF)] * 2 + [((W, W), F32)] * 2 + [((cols, W), F32)] * 4
    jobs = 8 + 2 * B + 4
    res = pl.pallas_call(
        finish_kernel,
        name="results",
        in_specs=[pl.BlockSpec(memory_space=m) for m in [vm] + [anyv] * 6],
        out_specs=[pl.BlockSpec(memory_space=m) for m in [vm] * len(small) + [anyv] * len(large)],
        out_shape=[jax.ShapeDtypeStruct(s, d) for s, d in small + large],
        scratch_shapes=[
            vm((S, S), BF),
            vm((B, S, W), BF),
            vm((B, S, W), BF),
            vm((r1, W), BF),
            vm((r2, W), BF),
            vm((cols, W), BF),
        ]
        + [vm(s, d) for s, d in large]
        + [dma((jobs + 1,)), dma((jobs,))],
        compiler_params=pltpu.CompilerParams(vmem_limit_bytes=62 << 20),
    )(vout, permt, outf, gif, gsum1, gsum2, gout)
    gain1, shift1, bq, bv, bout, gain2, shift2, bup, bdown = res[:9]
    outputs, grad_inputs, g_up, g_down, g_k, g_v, g_q, g_out = res[9:]
    return (
        outputs,
        grad_inputs,
        gain1,
        shift1,
        g_q.T,
        bq,
        g_k.T,
        g_v.T,
        bv,
        g_out,
        bout,
        gain2,
        shift2,
        g_up,
        bup,
        g_down,
        bdown,
    )


def solution(mesh):
    token = P(None, "seq", None)
    in_specs = (
        token,
        P(),
        P(),
        P(),
        P(None, "pat"),
        P("pat"),
        P(None, "pat"),
        P(None, "pat"),
        P("pat"),
        P("pat", None),
        P(),
        P(),
        P(),
        P(None, "pat"),
        P("pat"),
        P("pat", None),
        P(),
        token,
    )
    out_specs = (
        token,
        token,
        P(),
        P(),
        P(None, "pat"),
        P("pat"),
        P(None, "pat"),
        P(None, "pat"),
        P("pat"),
        P("pat", None),
        P(),
        P(),
        P(),
        P(None, "pat"),
        P("pat"),
        P("pat", None),
        P(),
    )
    n, pat = mesh.shape["seq"], mesh.shape["pat"]
    body = functools.partial(plane_program if n == 8 else shards, n, pat)
    return jax.shard_map(body, mesh=mesh, in_specs=in_specs, out_specs=out_specs, check_vma=False)
```
